32 devices in a mesh: grp: 2 (over x), inst: 2 (over core), tp: 8 (over z, y).
Axes of the slice: x: 2, y: 2, z: 4, core: 2. Of those that a mesh axis runs over, the one named last changes fastest.
Arguments:
- attention_output: bfloat16 [3, 1024, 8192], P(None, ('grp', 'inst'), 'tp'), parts along dimension 1, may hold values from -6 to 6
- output_weight: bfloat16 [8192, 8192], P('tp'), may hold values from -0.09375 to 0.09375
- adapter_down_weight: bfloat16 [192, 64, 8192], P('inst', None, 'tp'), may hold values from -0.0625 to 0.0625
- adapter_up_weight: bfloat16 [192, 64, 8192], P('inst', None, 'tp'), may hold values from -0.75 to 0.75
- adapter_page_table: int32 [192], replicated, may hold values from 0 to 191, each once
- block_adapter_ids: int32 [3, 8, 4], P(None, ('grp', 'inst')), parts along dimension 1, may hold values from 0 to 191, as said below
- row_list_position: int32 [3, 1024], P(None, ('grp', 'inst')), parts along dimension 1, may hold values from 0 to 3
- live_row_count: int32 [3, 4], P(None, ('grp', 'inst')), parts along dimension 1, may hold values from 1 to 256, as said below
Outputs:
- projected: bfloat16 [3, 1024, 8192], P(None, ('grp', 'inst'), 'tp'), parts along dimension 1
The draws below stay inside these ranges and needn't reach their ends.
There are 2 independent parts, one for each index of `grp`. The reference program is written for one: setup_inputs(seed, part) draws one part's arguments, and reference() takes and returns one part's arrays. A program takes and returns all parts, laid end to end along the dimension named above; an argument that names none is the same for every part. Nothing has to cross between parts.
Inputs may be any that keep to these rules, and one draw needn't show every extreme that they name: `block_adapter_ids`: the 4 ids of one block are distinct. `live_row_count`: in every step some instance has all 256 of its rows live.
All inputs are finite; a program needn't handle non-finite values.
Results may differ from the reference program's by a relative error of at most 0.0037.
Values may be sent and summed in bfloat16 or wider, within the bound.
No kernel may reach another device: no remote copies, remote signals or barrier semaphores. Data moves between devices by JAX's collectives and lax.ppermute only.
A program may use at most 192 MiB of HBM per device.

```python
import jax
import jax.numpy as jnp
from jax import lax

MODEL_WIDTH = 8192
ADAPTER_RANK = 64
STEPS = 3
BLOCK = 128
LIST = 4
ROWS_INST = 256
INSTS = 2
ROWS = 512
BLOCKS = 4
GROUP_ADAPTERS = 192


def pick_list(subkey):
    return jax.random.permutation(subkey, GROUP_ADAPTERS)[:LIST]


def draw_block_adapter_ids(key, part):
    key = jax.random.fold_in(key, 11)
    keys = jax.random.split(key, STEPS * BLOCKS)
    lists = jax.vmap(pick_list)(keys)
    return lists.reshape(STEPS, BLOCKS, LIST).astype(jnp.int32)


def draw_live_row_count(key, part):
    key = jax.random.fold_in(key, 23)
    first_key, second_key = jax.random.split(key)
    counts = jax.random.randint(first_key, (STEPS, INSTS), 1, ROWS_INST + 1)
    chosen = jax.random.randint(second_key, (STEPS, 1), 0, INSTS)
    filled = jnp.arange(INSTS, dtype=jnp.int32)[None, :] == chosen
    return jnp.where(filled, ROWS_INST, counts).astype(jnp.int32)


def set_ends(entries, stream_key, low, high):
    spot = [jax.random.randint(jax.random.fold_in(stream_key, axis), (), 0, length) for axis, length in enumerate(entries.shape)]
    longest = entries.shape.index(max(entries.shape))
    beside = spot[:longest] + [(spot[longest] + 1) % entries.shape[longest]] + spot[longest + 1:]
    return entries.at[tuple(spot)].set(low).at[tuple(beside)].set(high)


def with_spikes(drawn, stream_key, source, target, blocks, factor):
    owner, partner = [(jnp.arange(drawn.shape[dim]) // (drawn.shape[dim] // blocks)).reshape([-1 if axis == dim else 1 for axis in range(drawn.ndim)]) for dim in (source, target)]
    chosen = jax.random.permutation(stream_key, blocks)[partner]
    strong = (owner == chosen) | (owner == (partner + blocks // 2) % blocks)
    return jnp.where(strong, factor * drawn, drawn)


def steps_of(own_key, shape, cuts, low, top_value):
    def one(axis_at, shards_of):
        heights = jax.random.uniform(jax.random.fold_in(jax.random.fold_in(own_key, 6), axis_at), (shards_of,), jnp.float32, low / len(cuts), top_value / len(cuts))
        return jnp.repeat(jnp.exp(heights), shape[axis_at] // shards_of).reshape((-1,) + (1,) * (len(shape) - axis_at - 1))

    loudness = one(*cuts[0])
    for cut in cuts[1:]:
        loudness = loudness * one(*cut)
    return loudness


def gaussian(own_key, shape, scale, limit, cuts=(), kind=jnp.bfloat16):
    drawn = scale * jax.random.normal(own_key, shape, jnp.float32)
    if cuts:
        drawn = drawn * steps_of(own_key, shape, cuts, -0.22, 0.18)
    return jnp.clip(drawn, -limit, limit).astype(kind)


def noise_with(key, extent, scale, limit, cuts, heavy, kind=jnp.bfloat16):
    values = scale * jax.random.normal(key, extent, jnp.float32)
    if cuts:
        values = values * steps_of(key, extent, cuts, -0.22, 0.18)
    return jnp.clip(with_spikes(values, jax.random.fold_in(key, 3), *heavy), -limit, limit).astype(kind)


def setup_inputs(seed: int = 0, part: int = 0) -> dict:
    key_list = jax.random.split(jax.random.key(seed), 9)
    own_keys = jax.random.split(jax.random.fold_in(key_list[8], part), 9)
    return {
        "attention_output": gaussian(own_keys[0], (STEPS, ROWS, MODEL_WIDTH), 1.0, 6.0, ((1, 2), (2, 8))),
        "output_weight": noise_with(key_list[1], (MODEL_WIDTH, MODEL_WIDTH), MODEL_WIDTH ** -0.5, 0.09375, ((0, 8),), (0, 1, 8, 2.0)),
        "adapter_down_weight": gaussian(key_list[2], (GROUP_ADAPTERS, ADAPTER_RANK, MODEL_WIDTH), MODEL_WIDTH ** -0.5, 0.0625, ((0, 2), (2, 8))),
        "adapter_up_weight": gaussian(key_list[3], (GROUP_ADAPTERS, ADAPTER_RANK, MODEL_WIDTH), ADAPTER_RANK ** -0.5, 0.75, ((0, 2), (2, 8))),
        "adapter_page_table": jax.random.permutation(key_list[4], GROUP_ADAPTERS).astype(jnp.int32),
        "block_adapter_ids": draw_block_adapter_ids(jax.random.fold_in(jax.random.fold_in(key_list[8], part), 71), part),
        "row_list_position": set_ends(jax.random.randint(own_keys[6], (STEPS, ROWS), 0, LIST), jax.random.fold_in(own_keys[6], 1), 0, LIST - 1).astype(jnp.int32),
        "live_row_count": draw_live_row_count(jax.random.fold_in(jax.random.fold_in(key_list[8], part), 71), part),
    }


def reference(attention_output, output_weight, adapter_down_weight, adapter_up_weight, adapter_page_table, block_adapter_ids, row_list_position, live_row_count):
    results = []
    for current in range(STEPS):
        inputs = attention_output[current]
        base = jnp.dot(inputs, output_weight, preferred_element_type=jnp.float32)
        pages = adapter_page_table[block_adapter_ids[current]]

        def one_block(pieces):
            block_in, block_page_ids, slots = pieces
            down_matrices = adapter_down_weight[block_page_ids].astype(jnp.float32)
            up_matrices = adapter_up_weight[block_page_ids].astype(jnp.float32)
            low_all = jnp.einsum('rd,lkd->rlk', block_in.astype(jnp.float32), down_matrices)
            picked = (slots[:, None] == jnp.arange(LIST, dtype=jnp.int32)[None, :]).astype(jnp.float32)
            low = jnp.sum(low_all * picked[:, :, None], axis=1)
            low_b = lax.optimization_barrier(low.astype(jnp.bfloat16)).astype(jnp.float32)
            expanded = picked[:, :, None] * low_b[:, None, :]
            return jnp.einsum('rlk,lkd->rd', expanded, up_matrices)

        delta = lax.map(one_block, (inputs.reshape(BLOCKS, BLOCK, MODEL_WIDTH), pages, row_list_position[current].reshape(BLOCKS, BLOCK)))
        delta = delta.reshape(ROWS, MODEL_WIDTH)
        row_index = jnp.arange(ROWS, dtype=jnp.int32)
        limits = live_row_count[current][row_index // ROWS_INST]
        alive = (row_index % ROWS_INST) < limits
        results.append(jnp.where(alive[:, None], base + delta, 0.0).astype(jnp.bfloat16))
    return jnp.stack(results)
```

```python
import functools

import jax
import jax.numpy as jnp
from jax import lax
from jax.experimental import pallas as pl
from jax.experimental.pallas import tpu as pltpu
from jax.sharding import PartitionSpec as P

VMEM_LIMIT = 40 * 1024 * 1024


def ring_order(size):
    if size == 8:
        return list(range(0, size, 2)) + list(range(size - 1, 0, -2))
    return list(range(size))


def params():
    return pltpu.CompilerParams(vmem_limit_bytes=VMEM_LIMIT)


def hop_kernel(with_received, dests, x_ref, w_ref, *refs):
    total = jnp.dot(x_ref[...], w_ref[...], preferred_element_type=jnp.float32)
    if with_received:
        total = total + refs[0][...].astype(jnp.float32)
    refs[-1][...] = total.astype(refs[-1].dtype)


def hop(dests, offset, half, x, weight, received):
    rows, depth = x.shape
    block_cols = weight.shape[1] // dests.shape[0]
    half_cols = block_cols // 2
    tile = min(256, half_cols)
    tiles = half_cols // tile
    in_specs = [
        pl.BlockSpec((rows, depth), lambda j, d: (0, 0)),
        pl.BlockSpec(
            (depth, tile), lambda j, d: (0, (d[offset] * 2 + half) * tiles + j)
        ),
    ]
    operands = [x, weight]
    if received is not None:
        in_specs.append(pl.BlockSpec((rows, tile), lambda j, d: (0, j)))
        operands.append(received)
    return pl.pallas_call(
        functools.partial(hop_kernel, received is not None),
        grid_spec=pltpu.PrefetchScalarGridSpec(
            num_scalar_prefetch=1,
            grid=(tiles,),
            in_specs=in_specs,
            out_specs=pl.BlockSpec((rows, tile), lambda j, d: (0, j)),
        ),
        out_shape=jax.ShapeDtypeStruct((rows, half_cols), jnp.bfloat16),
        compiler_params=params(),
        cost_estimate=pl.CostEstimate(
            flops=2 * rows * depth * half_cols,
            bytes_accessed=2 * (rows * depth + depth * half_cols + 2 * rows * half_cols),
            transcendentals=0,
        ),
    )(dests, *operands)


def collect_kernel(count, index, table_ref, out_ref, sems):
    for slot in range(count):
        pltpu.make_async_copy(
            table_ref.at[index[slot]], out_ref.at[slot], sems.at[slot]
        ).start()
    for slot in range(count):
        pltpu.make_async_copy(
            table_ref.at[index[slot]], out_ref.at[slot], sems.at[slot]
        ).wait()


def collect(index, table):
    count = index.shape[0]
    shape = (count,) + table.shape[1:]
    return pl.pallas_call(
        functools.partial(collect_kernel, count),
        grid_spec=pltpu.PrefetchScalarGridSpec(
            num_scalar_prefetch=1,
            grid=(1,),
            in_specs=[pl.BlockSpec(memory_space=pl.ANY)],
            out_specs=pl.BlockSpec(memory_space=pl.ANY),
            scratch_shapes=[pltpu.SemaphoreType.DMA((count,))],
        ),
        out_shape=jax.ShapeDtypeStruct(shape, table.dtype),
        compiler_params=params(),
        cost_estimate=pl.CostEstimate(
            flops=0, bytes_accessed=4 * shape[0] * shape[1] * shape[2], transcendentals=0
        ),
    )(index, table)


def load_pages(count, local, index, table_ref, got_ref, pages, sems):
    for slot in range(count):
        own = local[slot] == 1

        @pl.when(own)
        def _():
            pltpu.make_async_copy(
                table_ref.at[index[slot]], pages.at[slot], sems.at[slot]
            ).start()

        @pl.when(jnp.logical_not(own))
        def _():
            pltpu.make_async_copy(got_ref.at[slot], pages.at[slot], sems.at[slot]).start()

    for slot in range(count):
        pltpu.make_async_copy(got_ref.at[slot], pages.at[slot], sems.at[slot]).wait()


def low_kernel(sizes, local, index, x_ref, place_ref, table_ref, got_ref, out_ref, pages, sems):
    steps, blocks, listed, rank, block_rows = sizes
    load_pages(steps * blocks * listed, local, index, table_ref, got_ref, pages, sems)
    column = lax.broadcasted_iota(jnp.int32, (block_rows, listed * rank), 1) // rank
    for step in range(steps):
        for block in range(blocks):
            at = step * blocks + block
            rows = pl.ds(at * block_rows, block_rows)
            listing = pages[at * listed : (at + 1) * listed].reshape(listed * rank, -1)
            every = lax.dot_general(
                x_ref[rows, :], listing, (((1,), (1,)), ((), ())),
                preferred_element_type=jnp.float32,
            )
            every = jnp.where(column == place_ref[rows, :], every, 0.0)
            low = every[:, :rank]
            for entry in range(1, listed):
                low = low + every[:, entry * rank : (entry + 1) * rank]
            out_ref[step, :, block * rank : (block + 1) * rank] = low


def low_rank(sizes, local, index, x, place, table, got):
    steps, blocks, listed, rank, block_rows = sizes
    count = steps * blocks * listed
    depth = x.shape[1]
    whole = pl.BlockSpec(memory_space=pltpu.VMEM)
    return pl.pallas_call(
        functools.partial(low_kernel, sizes),
        grid_spec=pltpu.PrefetchScalarGridSpec(
            num_scalar_prefetch=2,
            grid=(1,),
            in_specs=[
                whole, whole, pl.BlockSpec(memory_space=pl.ANY), pl.BlockSpec(memory_space=pl.ANY)
            ],
            out_specs=whole,
            scratch_shapes=[
                pltpu.VMEM((count, rank, depth), table.dtype),
                pltpu.SemaphoreType.DMA((count,)),
            ],
        ),
        out_shape=jax.ShapeDtypeStruct((steps, block_rows, blocks * rank), jnp.float32),
        compiler_params=params(),
        cost_estimate=pl.CostEstimate(
            flops=2 * x.shape[0] * depth * listed * rank,
            bytes_accessed=2 * (x.shape[0] * depth + count * rank * depth),
            transcendentals=0,
        ),
    )(local, index, x, place, table, got)


def own_kernel(
    sizes, dests, local, index, x_ref, w_ref, place_ref, low_ref, table_ref, got_ref, out_ref,
    pages, sems,
):
    steps, blocks, listed, rank, block_rows = sizes
    tile = w_ref.shape[1]
    now = pl.program_id(0)

    @pl.when(now == 0)
    def _():
        load_pages(steps * blocks * listed, local, index, table_ref, got_ref, pages, sems)

    columns = pl.ds(pl.multiple_of(now * tile, tile), tile)
    out_ref[...] = jnp.dot(x_ref[...], w_ref[...], preferred_element_type=jnp.float32)
    column = lax.broadcasted_iota(jnp.int32, (block_rows, listed * rank), 1) // rank
    for step in range(steps):
        for block in range(blocks):
            at = step * blocks + block
            rows = pl.ds(at * block_rows, block_rows)
            low = low_ref[step, :, block * rank : (block + 1) * rank]
            spread = jnp.concatenate([low] * listed, axis=1)
            spread = jnp.where(column == place_ref[rows, :], spread, 0.0).astype(jnp.bfloat16)
            listing = pages[at * listed : (at + 1) * listed, :, columns]
            out_ref[rows, :] += jnp.dot(
                spread, listing.reshape(listed * rank, tile), preferred_element_type=jnp.float32
            )


def own_terms(sizes, dests, local, index, x, weight, place, low, table, got):
    steps, blocks, listed, rank, block_rows = sizes
    count = steps * blocks * listed
    rows, depth = x.shape
    cols = weight.shape[1] // dests.shape[0]
    tile = min(256, cols)
    tiles = cols // tile
    whole = pl.BlockSpec(memory_space=pltpu.VMEM)
    return pl.pallas_call(
        functools.partial(own_kernel, sizes),
        grid_spec=pltpu.PrefetchScalarGridSpec(
            num_scalar_prefetch=3,
            grid=(tiles,),
            in_specs=[
                whole,
                pl.BlockSpec((depth, tile), lambda j, d, l, i: (0, d[0] * tiles + j)),
                whole,
                whole,
                pl.BlockSpec(memory_space=pl.ANY),
                pl.BlockSpec(memory_space=pl.ANY),
            ],
            out_specs=pl.BlockSpec((rows, tile), lambda j, d, l, i: (0, j)),
            scratch_shapes=[
                pltpu.VMEM((count, rank, cols), table.dtype),
                pltpu.SemaphoreType.DMA((count,)),
            ],
        ),
        out_shape=jax.ShapeDtypeStruct((rows, cols), jnp.float32),
        compiler_params=params(),
        cost_estimate=pl.CostEstimate(
            flops=2 * rows * cols * (depth + listed * rank),
            bytes_accessed=2 * (rows * depth + depth * cols + count * rank * cols) + 4 * rows * cols,
            transcendentals=0,
        ),
    )(dests, local, index, x, weight, place, low, table, got)


def sum_over(value, axis, size):
    if size & (size - 1):
        return lax.psum(value, axis)
    apart = 1
    while apart < size:
        value = value + lax.ppermute(value, axis, [(i, i ^ apart) for i in range(size)])
        apart *= 2
    return value


def per_device(
    ring,
    attention_output,
    output_weight,
    adapter_down_weight,
    adapter_up_weight,
    adapter_page_table,
    block_adapter_ids,
    row_list_position,
    live_row_count,
):
    size = len(ring)
    steps, row_count, depth = attention_output.shape
    resident, rank, _ = adapter_down_weight.shape
    _, blocks, listed = block_adapter_ids.shape
    sizes = (steps, blocks, listed, rank, row_count // blocks)
    rows = steps * row_count
    x = attention_output.reshape(rows, depth)

    instance = lax.axis_index("inst")
    tp = lax.axis_index("tp")
    ring_at = jnp.array(ring, dtype=jnp.int32)
    place_of = [0] * size
    for at, index in enumerate(ring):
        place_of[index] = at
    place = jnp.array(place_of, dtype=jnp.int32)[tp]
    dests = ring_at[(place + jnp.arange(size, dtype=jnp.int32)) % size]

    swap = [(0, 1), (1, 0)]
    ids = block_adapter_ids.reshape(-1)
    ids_there = lax.ppermute(ids, "inst", swap)
    pages = adapter_page_table[ids]
    index = pages % resident
    local = (pages // resident == instance).astype(jnp.int32)
    index_there = adapter_page_table[ids_there] % resident
    got_down = lax.ppermute(collect(index_there, adapter_down_weight), "inst", swap)
    got_up = lax.ppermute(collect(index_there, adapter_up_weight), "inst", swap)

    forward = [(ring[i], ring[(i + 1) % size]) for i in range(size)]
    backward = [(ring[i], ring[i - 1]) for i in range(size)]
    far = size // 2
    chains = [
        (0, 1, forward, far),
        (1, -1, backward, far),
        (1, 1, forward, size - 1 - far),
        (0, -1, backward, size - 1 - far),
    ]
    arrived = [None] * len(chains)
    for left in range(far, 0, -1):
        for chain, (half, sign, moves, length) in enumerate(chains):
            if left <= length:
                partial = hop(
                    dests, (sign * left) % size, half, x, output_weight, arrived[chain]
                )
                arrived[chain] = lax.ppermute(partial, "tp", moves)

    slots = row_list_position.reshape(rows, 1)
    low = low_rank(sizes, local, index, x, slots, adapter_down_weight, got_down)
    low = sum_over(low, "tp", size)
    own = own_terms(
        sizes, dests, local, index, x, output_weight, slots, low, adapter_up_weight, got_up
    )
    halves = []
    for half in range(2):
        there = [a for a, c in zip(arrived, chains) if c[0] == half]
        halves.append(sum(a.astype(jnp.float32) for a in there))
    total = own + jnp.concatenate(halves, axis=1)
    alive = jnp.arange(row_count, dtype=jnp.int32)[None, :] < live_row_count
    total = jnp.where(alive[:, :, None], total.reshape(steps, row_count, -1), 0.0)
    return total.astype(jnp.bfloat16)


def solution(mesh):
    in_specs = (
        P(None, ("grp", "inst"), "tp"),
        P("tp", None),
        P("inst", None, "tp"),
        P("inst", None, "tp"),
        P(),
        P(None, ("grp", "inst"), None),
        P(None, ("grp", "inst")),
        P(None, ("grp", "inst")),
    )
    out_specs = P(None, ("grp", "inst"), "tp")
    ring = ring_order(mesh.shape["tp"])
    return jax.shard_map(
        functools.partial(per_device, ring),
        mesh=mesh, in_specs=in_specs, out_specs=out_specs, check_vma=False,
    )
```

```python
import functools

import jax
import jax.numpy as jnp
from jax import lax
from jax.experimental import pallas as pl
from jax.experimental.pallas import tpu as pltpu
from jax.sharding import PartitionSpec as P

VMEM_LIMIT = 40 * 1024 * 1024


def ring_order(size):
    if size == 8:
        return list(range(0, size, 2)) + list(range(size - 1, 0, -2))
    return list(range(size))


def params():
    return pltpu.CompilerParams(vmem_limit_bytes=VMEM_LIMIT)


def hop_kernel(with_received, dests, x_ref, w_ref, *refs):
    total = jnp.dot(x_ref[...], w_ref[...], preferred_element_type=jnp.float32)
    if with_received:
        total = total + refs[0][...].astype(jnp.float32)
    refs[-1][...] = total.astype(refs[-1].dtype)


def hop(dests, offset, half, x, weight, received):
    rows, depth = x.shape
    block_cols = weight.shape[1] // dests.shape[0]
    half_cols = block_cols // 2
    tile = min(256, half_cols)
    tiles = half_cols // tile
    in_specs = [
        pl.BlockSpec((rows, depth), lambda j, d: (0, 0)),
        pl.BlockSpec(
            (depth, tile), lambda j, d: (0, (d[offset] * 2 + half) * tiles + j)
        ),
    ]
    operands = [x, weight]
    if received is not None:
        in_specs.append(pl.BlockSpec((rows, tile), lambda j, d: (0, j)))
        operands.append(received)
    return pl.pallas_call(
        functools.partial(hop_kernel, received is not None),
        grid_spec=pltpu.PrefetchScalarGridSpec(
            num_scalar_prefetch=1,
            grid=(tiles,),
            in_specs=in_specs,
            out_specs=pl.BlockSpec((rows, tile), lambda j, d: (0, j)),
        ),
        out_shape=jax.ShapeDtypeStruct((rows, half_cols), jnp.bfloat16),
        compiler_params=params(),
        cost_estimate=pl.CostEstimate(
            flops=2 * rows * depth * half_cols,
            bytes_accessed=2 * (rows * depth + depth * half_cols + 2 * rows * half_cols),
            transcendentals=0,
        ),
    )(dests, *operands)


def collect_kernel(count, index, table_ref, out_ref, sems):
    for slot in range(count):
        pltpu.make_async_copy(
            table_ref.at[index[slot]], out_ref.at[slot], sems.at[slot]
        ).start()
    for slot in range(count):
        pltpu.make_async_copy(
            table_ref.at[index[slot]], out_ref.at[slot], sems.at[slot]
        ).wait()


def collect(index, table):
    count = index.shape[0]
    shape = (count,) + table.shape[1:]
    return pl.pallas_call(
        functools.partial(collect_kernel, count),
        grid_spec=pltpu.PrefetchScalarGridSpec(
            num_scalar_prefetch=1,
            grid=(1,),
            in_specs=[pl.BlockSpec(memory_space=pl.ANY)],
            out_specs=pl.BlockSpec(memory_space=pltpu.VMEM),
            scratch_shapes=[pltpu.SemaphoreType.DMA((count,))],
        ),
        out_shape=jax.ShapeDtypeStruct(shape, table.dtype),
        compiler_params=params(),
        cost_estimate=pl.CostEstimate(
            flops=0, bytes_accessed=4 * shape[0] * shape[1] * shape[2], transcendentals=0
        ),
    )(index, table)


def load_pages(count, local, index, table_ref, got_ref, pages, sems):
    for slot in range(count):
        own = local[slot] == 1

        @pl.when(own)
        def _():
            pltpu.make_async_copy(
                table_ref.at[index[slot]], pages.at[slot], sems.at[slot]
            ).start()

        @pl.when(jnp.logical_not(own))
        def _():
            pltpu.make_async_copy(got_ref.at[slot], pages.at[slot], sems.at[slot]).start()

    for slot in range(count):
        pltpu.make_async_copy(got_ref.at[slot], pages.at[slot], sems.at[slot]).wait()


def low_kernel(sizes, local, index, x_ref, place_ref, table_ref, got_ref, out_ref, pages, sems):
    steps, blocks, listed, rank, block_rows = sizes
    load_pages(steps * blocks * listed, local, index, table_ref, got_ref, pages, sems)
    column = lax.broadcasted_iota(jnp.int32, (block_rows, listed * rank), 1) // rank
    for step in range(steps):
        for block in range(blocks):
            at = step * blocks + block
            rows = pl.ds(at * block_rows, block_rows)
            listing = pages[at * listed : (at + 1) * listed].reshape(listed * rank, -1)
            every = lax.dot_general(
                x_ref[rows, :], listing, (((1,), (1,)), ((), ())),
                preferred_element_type=jnp.float32,
            )
            every = jnp.where(column == place_ref[rows, :], every, 0.0)
            low = every[:, :rank]
            for entry in range(1, listed):
                low = low + every[:, entry * rank : (entry + 1) * rank]
            out_ref[step, :, block * rank : (block + 1) * rank] = low


def low_rank(sizes, local, index, x, place, table, got):
    steps, blocks, listed, rank, block_rows = sizes
    count = steps * blocks * listed
    depth = x.shape[1]
    whole = pl.BlockSpec(memory_space=pltpu.VMEM)
    return pl.pallas_call(
        functools.partial(low_kernel, sizes),
        grid_spec=pltpu.PrefetchScalarGridSpec(
            num_scalar_prefetch=2,
            grid=(1,),
            in_specs=[
                whole, whole, pl.BlockSpec(memory_space=pl.ANY), pl.BlockSpec(memory_space=pl.ANY)
            ],
            out_specs=whole,
            scratch_shapes=[
                pltpu.VMEM((count, rank, depth), table.dtype),
                pltpu.SemaphoreType.DMA((count,)),
            ],
        ),
        out_shape=jax.ShapeDtypeStruct((steps, block_rows, blocks * rank), jnp.float32),
        compiler_params=params(),
        cost_estimate=pl.CostEstimate(
            flops=2 * x.shape[0] * depth * listed * rank,
            bytes_accessed=2 * (x.shape[0] * depth + count * rank * depth),
            transcendentals=0,
        ),
    )(local, index, x, place, table, got)


def own_kernel(
    sizes, dests, local, index, x_ref, w_ref, place_ref, low_ref, table_ref, got_ref, out_ref,
    pages, sems,
):
    steps, blocks, listed, rank, block_rows = sizes
    tile = w_ref.shape[1]
    now = pl.program_id(0)

    @pl.when(now == 0)
    def _():
        load_pages(steps * blocks * listed, local, index, table_ref, got_ref, pages, sems)

    columns = pl.ds(pl.multiple_of(now * tile, tile), tile)
    out_ref[...] = jnp.dot(x_ref[...], w_ref[...], preferred_element_type=jnp.float32)
    column = lax.broadcasted_iota(jnp.int32, (block_rows, listed * rank), 1) // rank
    for step in range(steps):
        for block in range(blocks):
            at = step * blocks + block
            rows = pl.ds(at * block_rows, block_rows)
            low = low_ref[step, :, block * rank : (block + 1) * rank]
            spread = jnp.concatenate([low] * listed, axis=1)
            spread = jnp.where(column == place_ref[rows, :], spread, 0.0).astype(jnp.bfloat16)
            listing = pages[at * listed : (at + 1) * listed, :, columns]
            out_ref[rows, :] += jnp.dot(
                spread, listing.reshape(listed * rank, tile), preferred_element_type=jnp.float32
            )


def own_terms(sizes, dests, local, index, x, weight, place, low, table, got):
    steps, blocks, listed, rank, block_rows = sizes
    count = steps * blocks * listed
    rows, depth = x.shape
    cols = weight.shape[1] // dests.shape[0]
    tile = min(256, cols)
    tiles = cols // tile
    whole = pl.BlockSpec(memory_space=pltpu.VMEM)
    return pl.pallas_call(
        functools.partial(own_kernel, sizes),
        grid_spec=pltpu.PrefetchScalarGridSpec(
            num_scalar_prefetch=3,
            grid=(tiles,),
            in_specs=[
                whole,
                pl.BlockSpec((depth, tile), lambda j, d, l, i: (0, d[0] * tiles + j)),
                whole,
                whole,
                pl.BlockSpec(memory_space=pl.ANY),
                pl.BlockSpec(memory_space=pl.ANY),
            ],
            out_specs=pl.BlockSpec((rows, tile), lambda j, d, l, i: (0, j)),
            scratch_shapes=[
                pltpu.VMEM((count, rank, cols), table.dtype),
                pltpu.SemaphoreType.DMA((count,)),
            ],
        ),
        out_shape=jax.ShapeDtypeStruct((rows, cols), jnp.float32),
        compiler_params=params(),
        cost_estimate=pl.CostEstimate(
            flops=2 * rows * cols * (depth + listed * rank),
            bytes_accessed=2 * (rows * depth + depth * cols + count * rank * cols) + 4 * rows * cols,
            transcendentals=0,
        ),
    )(dests, local, index, x, weight, place, low, table, got)


def sum_over(value, axis, size):
    if size & (size - 1):
        return lax.psum(value, axis)
    apart = 1
    while apart < size:
        value = value + lax.ppermute(value, axis, [(i, i ^ apart) for i in range(size)])
        apart *= 2
    return value


def per_device(
    ring,
    attention_output,
    output_weight,
    adapter_down_weight,
    adapter_up_weight,
    adapter_page_table,
    block_adapter_ids,
    row_list_position,
    live_row_count,
):
    size = len(ring)
    steps, row_count, depth = attention_output.shape
    resident, rank, _ = adapter_down_weight.shape
    _, blocks, listed = block_adapter_ids.shape
    sizes = (steps, blocks, listed, rank, row_count // blocks)
    rows = steps * row_count
    x = attention_output.reshape(rows, depth)

    instance = lax.axis_index("inst")
    tp = lax.axis_index("tp")
    ring_at = jnp.array(ring, dtype=jnp.int32)
    place_of = [0] * size
    for at, index in enumerate(ring):
        place_of[index] = at
    place = jnp.array(place_of, dtype=jnp.int32)[tp]
    dests = ring_at[(place + jnp.arange(size, dtype=jnp.int32)) % size]

    swap = [(0, 1), (1, 0)]
    ids = block_adapter_ids.reshape(-1)
    ids_there = lax.ppermute(ids, "inst", swap)
    pages = adapter_page_table[ids]
    index = pages % resident
    local = (pages // resident == instance).astype(jnp.int32)
    index_there = adapter_page_table[ids_there] % resident
    got_down = lax.ppermute(collect(index_there, adapter_down_weight), "inst", swap)
    got_up = lax.ppermute(collect(index_there, adapter_up_weight), "inst", swap)

    forward = [(ring[i], ring[(i + 1) % size]) for i in range(size)]
    backward = [(ring[i], ring[i - 1]) for i in range(size)]
    far = size // 2
    chains = [
        (0, 1, forward, far),
        (1, -1, backward, far),
        (1, 1, forward, size - 1 - far),
        (0, -1, backward, size - 1 - far),
    ]
    arrived = [None] * len(chains)
    for left in range(far, 0, -1):
        for chain, (half, sign, moves, length) in enumerate(chains):
            if left <= length:
                partial = hop(
                    dests, (sign * left) % size, half, x, output_weight, arrived[chain]
                )
                arrived[chain] = lax.ppermute(partial, "tp", moves)

    slots = row_list_position.reshape(rows, 1)
    low = low_rank(sizes, local, index, x, slots, adapter_down_weight, got_down)
    low = sum_over(low, "tp", size)
    own = own_terms(
        sizes, dests, local, index, x, output_weight, slots, low, adapter_up_weight, got_up
    )
    halves = []
    for half in range(2):
        there = [a for a, c in zip(arrived, chains) if c[0] == half]
        halves.append(sum(a.astype(jnp.float32) for a in there))
    total = own + jnp.concatenate(halves, axis=1)
    alive = jnp.arange(row_count, dtype=jnp.int32)[None, :] < live_row_count
    total = jnp.where(alive[:, :, None], total.reshape(steps, row_count, -1), 0.0)
    return total.astype(jnp.bfloat16)


def solution(mesh):
    in_specs = (
        P(None, ("grp", "inst"), "tp"),
        P("tp", None),
        P("inst", None, "tp"),
        P("inst", None, "tp"),
        P(),
        P(None, ("grp", "inst"), None),
        P(None, ("grp", "inst")),
        P(None, ("grp", "inst")),
    )
    out_specs = P(None, ("grp", "inst"), "tp")
    ring = ring_order(mesh.shape["tp"])
    return jax.shard_map(
        functools.partial(per_device, ring),
        mesh=mesh, in_specs=in_specs, out_specs=out_specs, check_vma=False,
    )
```

```python
import functools

import jax
import jax.numpy as jnp
from jax import lax
from jax.experimental import pallas as pl
from jax.experimental.pallas import tpu as pltpu
from jax.sharding import PartitionSpec as P

VMEM_LIMIT = 48 * 1024 * 1024
GRAIN = 16
SWAP = [(0, 1), (1, 0)]
WHOLE = pl.BlockSpec(memory_space=pltpu.VMEM)
ANYWHERE = pl.BlockSpec(memory_space=pl.ANY)


def ring_order(size):
    if size == 8:
        return list(range(0, size, 2)) + list(range(size - 1, 0, -2))
    return list(range(size))


def row_buckets(rows):
    grain = max(4 * GRAIN, rows // 24)
    return list(range(rows * 2 // 3, rows, grain)) + [rows]


def params():
    return pltpu.CompilerParams(vmem_limit_bytes=VMEM_LIMIT)


def cost(flops, size):
    return pl.CostEstimate(flops=flops, bytes_accessed=size, transcendentals=0)


def padded(count):
    return (count + (GRAIN - 1)) // GRAIN * GRAIN


def place_of_step(live, step, full_rows):
    start = 0
    for before in range(step):
        start = start + padded(live[2 * before]) + padded(live[2 * before + 1])
    full = jnp.where(live[2 * step + 1] == full_rows, 1, 0)
    short = padded(jnp.where(full == 1, live[2 * step], live[2 * step + 1]))
    return start, short, full


def pack_kernel(live, me, own_ref, there_ref, out_ref, sems):
    steps, count, _ = own_ref.shape

    def copies(full_ones, run):
        for step in range(steps):
            start, short, full = place_of_step(live, step, count)
            at = start + short if full_ones else start
            at = pl.multiple_of(at, GRAIN)
            mine = (full == me[0]) if full_ones else (full != me[0])
            target = out_ref.at[pl.ds(at, count)]
            sem = sems.at[step]

            @pl.when(mine)
            def _():
                run(pltpu.make_async_copy(own_ref.at[step], target, sem))

            @pl.when(jnp.logical_not(mine))
            def _():
                run(pltpu.make_async_copy(there_ref.at[step], target, sem))

    for full_ones in (False, True):
        copies(full_ones, lambda copy: copy.start())
        copies(full_ones, lambda copy: copy.wait())


def pack(live, me, own, there):
    steps, count, depth = own.shape
    rows = 2 * steps * count
    return pl.pallas_call(
        pack_kernel,
        grid_spec=pltpu.PrefetchScalarGridSpec(
            num_scalar_prefetch=2,
            grid=(1,),
            in_specs=[ANYWHERE, ANYWHERE],
            out_specs=WHOLE,
            scratch_shapes=[pltpu.SemaphoreType.DMA((steps,))],
        ),
        out_shape=jax.ShapeDtypeStruct((rows, depth), own.dtype),
        compiler_params=params(),
        cost_estimate=cost(0, 4 * rows * depth),
    )(live, me, own, there)


def hop_kernel(with_received, columns, x_ref, w_ref, *refs):
    total = jnp.dot(x_ref[...], w_ref[...], preferred_element_type=jnp.float32)
    if with_received:
        total = total + refs[0][...].astype(jnp.float32)
    refs[-1][...] = total.astype(refs[-1].dtype)


def hop(rows, columns, offset, part, x, weight, received):
    depth = x.shape[1]
    width = weight.shape[1] // columns.shape[0] // 4
    tile = rows // 4
    in_specs = [
        pl.BlockSpec((tile, depth), lambda i, c: (i, 0)),
        pl.BlockSpec((depth, width), lambda i, c: (0, c[offset] + part)),
    ]
    operands = [x, weight]
    if received is not None:
        in_specs.append(pl.BlockSpec((tile, width), lambda i, c: (i, 0)))
        operands.append(received)
    return pl.pallas_call(
        functools.partial(hop_kernel, received is not None),
        grid_spec=pltpu.PrefetchScalarGridSpec(
            num_scalar_prefetch=1,
            grid=(rows // tile,),
            in_specs=in_specs,
            out_specs=pl.BlockSpec((tile, width), lambda i, c: (i, 0)),
        ),
        out_shape=jax.ShapeDtypeStruct((rows, width), jnp.bfloat16),
        compiler_params=params(),
        cost_estimate=cost(
            2 * rows * depth * width, 2 * (rows * depth + depth * width + 2 * rows * width)
        ),
    )(columns, *operands)


def collect_kernel(count, index, me, table_ref, out_ref, sems):
    half = out_ref.shape[2]
    columns = pl.ds(pl.multiple_of((1 - me[0]) * half, 128), half)
    copies = [
        pltpu.make_async_copy(
            table_ref.at[index[slot], :, columns], out_ref.at[slot], sems.at[slot]
        )
        for slot in range(count)
    ]
    for copy in copies:
        copy.start()
    for copy in copies:
        copy.wait()


def collect(index, me, table):
    count = index.shape[0]
    shape = (count, table.shape[1], table.shape[2] // 2)
    return pl.pallas_call(
        functools.partial(collect_kernel, count),
        grid_spec=pltpu.PrefetchScalarGridSpec(
            num_scalar_prefetch=2,
            grid=(1,),
            in_specs=[ANYWHERE],
            out_specs=WHOLE,
            scratch_shapes=[pltpu.SemaphoreType.DMA((count,))],
        ),
        out_shape=jax.ShapeDtypeStruct(shape, table.dtype),
        compiler_params=params(),
        cost_estimate=cost(0, 4 * shape[0] * shape[1] * shape[2]),
    )(index, me, table)


def low_kernel(
    sizes, local, index, own_ref, there_ref, own_place_ref, there_place_ref, table_ref,
    own_out, there_out, pages, sems,
):
    steps, blocks, listed, rank, block_rows = sizes
    count = 2 * steps * blocks * listed

    def each(run):
        for slot in range(count):

            @pl.when(local[slot] == 1)
            def _():
                run(
                    pltpu.make_async_copy(
                        table_ref.at[index[slot]], pages.at[slot], sems.at[slot]
                    )
                )

    each(lambda copy: copy.start())
    each(lambda copy: copy.wait())
    sides = ((own_ref, own_place_ref, own_out), (there_ref, there_place_ref, there_out))
    for side, (x_ref, place_ref, out_ref) in enumerate(sides):
        for step in range(steps):
            for block in range(blocks):
                at = ((side * steps + step) * blocks + block) * listed
                listing = pages[at : at + listed].reshape(listed * rank, -1)
                rows = slice(block * block_rows, (block + 1) * block_rows)
                every = lax.dot_general(
                    listing, x_ref[step, rows, :], (((1,), (1,)), ((), ())),
                    preferred_element_type=jnp.float32,
                )
                place = place_ref[step : step + 1, rows]
                low = jnp.zeros((rank, block_rows), jnp.float32)
                for entry in range(listed):
                    wanted = jnp.where(local[at + entry] == 1, entry, -1)
                    low = jnp.where(
                        place == wanted, every[entry * rank : (entry + 1) * rank], low
                    )
                start = (step * blocks + block) * block_rows
                out_ref[:, start : start + block_rows] = low


def low_rank(sizes, local, index, own, there, own_place, there_place, table):
    steps, blocks, listed, rank, block_rows = sizes
    count = 2 * steps * blocks * listed
    depth = own.shape[2]
    rows = steps * blocks * block_rows
    return pl.pallas_call(
        functools.partial(low_kernel, sizes),
        grid_spec=pltpu.PrefetchScalarGridSpec(
            num_scalar_prefetch=2,
            grid=(1,),
            in_specs=[WHOLE] * 4 + [ANYWHERE],
            out_specs=[WHOLE] * 2,
            scratch_shapes=[
                pltpu.VMEM((count, rank, depth), table.dtype),
                pltpu.SemaphoreType.DMA((count,)),
            ],
        ),
        out_shape=[jax.ShapeDtypeStruct((rank, rows), jnp.float32)] * 2,
        compiler_params=params(),
        cost_estimate=cost(
            4 * rows * depth * listed * rank, 4 * rows * depth + count * rank * depth
        ),
    )(local, index, own, there, own_place, there_place, table)


def own_kernel(
    sizes, columns, local, index, me, own_ref, there_ref, w_ref, own_place_ref, there_place_ref,
    own_low_ref, there_low_ref, table_ref, got_ref, own_out, there_out, pages, sems,
):
    steps, blocks, listed, rank, block_rows = sizes
    count = 2 * steps * blocks * listed
    half = pages.shape[2]
    tile = w_ref.shape[1]
    now = pl.program_id(0)

    @pl.when(now == 0)
    def _():
        mine = pl.ds(pl.multiple_of(me[0] * half, 128), half)
        for slot in range(count):
            held = local[slot] == 1

            @pl.when(held)
            def _():
                pltpu.make_async_copy(
                    table_ref.at[index[slot], :, mine], pages.at[slot], sems.at[slot]
                ).start()

            @pl.when(jnp.logical_not(held))
            def _():
                pltpu.make_async_copy(got_ref.at[slot], pages.at[slot], sems.at[slot]).start()

        for slot in range(count):
            pltpu.make_async_copy(got_ref.at[slot], pages.at[slot], sems.at[slot]).wait()

    tile_at = pl.ds(pl.multiple_of(now * tile, tile), tile)
    entry_of = lax.broadcasted_iota(jnp.int32, (listed * rank, block_rows), 0) // rank
    sides = (
        (own_ref, own_place_ref, own_low_ref, own_out),
        (there_ref, there_place_ref, there_low_ref, there_out),
    )
    for side, (x_ref, place_ref, low_ref, out_ref) in enumerate(sides):
        for step in range(steps):
            for block in range(blocks):
                at = ((side * steps + step) * blocks + block) * listed
                rows = slice(block * block_rows, (block + 1) * block_rows)
                start = (step * blocks + block) * block_rows
                low = low_ref[:, start : start + block_rows].astype(jnp.float32)
                spread = jnp.concatenate([low] * listed, axis=0)
                spread = jnp.where(entry_of == place_ref[step : step + 1, rows], spread, 0.0)
                listing = pages[at : at + listed, :, tile_at].reshape(listed * rank, tile)
                out_ref[start : start + block_rows, :] = jnp.dot(
                    x_ref[step, rows, :], w_ref[...], preferred_element_type=jnp.float32
                ) + jnp.dot(
                    spread.T.astype(jnp.bfloat16), listing, preferred_element_type=jnp.float32
                )


def own_terms(
    sizes, columns, local, index, me, own, there, weight, own_place, there_place, own_low,
    there_low, table, got,
):
    steps, blocks, listed, rank, block_rows = sizes
    count = 2 * steps * blocks * listed
    depth = own.shape[2]
    rows = steps * blocks * block_rows
    half = weight.shape[1] // columns.shape[0] // 2
    tile = half // 2
    return pl.pallas_call(
        functools.partial(own_kernel, sizes),
        grid_spec=pltpu.PrefetchScalarGridSpec(
            num_scalar_prefetch=4,
            grid=(2,),
            in_specs=[
                WHOLE,
                WHOLE,
                pl.BlockSpec((depth, tile), lambda j, c, l, i, m: (0, c[0] + j)),
            ]
            + [WHOLE] * 4
            + [ANYWHERE] * 2,
            out_specs=[pl.BlockSpec((rows, tile), lambda j, c, l, i, m: (0, j))] * 2,
            scratch_shapes=[
                pltpu.VMEM((count, rank, half), table.dtype),
                pltpu.SemaphoreType.DMA((count,)),
            ],
        ),
        out_shape=[jax.ShapeDtypeStruct((rows, half), jnp.float32)] * 2,
        compiler_params=params(),
        cost_estimate=cost(
            4 * rows * half * (depth + listed * rank),
            4 * rows * depth + 2 * depth * half + 2 * count * rank * half + 8 * rows * half,
        ),
    )(
        columns, local, index, me, own, there, weight, own_place, there_place, own_low, there_low,
        table, got,
    )


def finish_kernel(steps, live, me, own_ref, there_ref, one_ref, two_ref, own_out, there_out):
    count = own_ref.shape[0] // steps
    row = lax.broadcasted_iota(jnp.int32, (count, own_ref.shape[1]), 0)
    sides = ((own_ref, own_out, me[0]), (there_ref, there_out, 1 - me[0]))
    for step in range(steps):
        start, short, full = place_of_step(live, step, count)
        for terms_ref, out_ref, instance in sides:
            at = jnp.where(full == instance, start + short, start)
            packed = pl.ds(pl.multiple_of(at, GRAIN), count)
            rows = slice(step * count, (step + 1) * count)
            total = (
                terms_ref[rows, :]
                + one_ref[packed, :].astype(jnp.float32)
                + two_ref[packed, :].astype(jnp.float32)
            )
            alive = row < live[2 * step + instance]
            out_ref[rows, :] = jnp.where(alive, total, 0.0).astype(out_ref.dtype)


def finish(steps, live, me, part, own, there, one, two):
    rows = own.shape[0]
    width = one.shape[1]
    terms = pl.BlockSpec((rows, width), lambda i, l, m: (0, part))
    return pl.pallas_call(
        functools.partial(finish_kernel, steps),
        grid_spec=pltpu.PrefetchScalarGridSpec(
            num_scalar_prefetch=2,
            grid=(1,),
            in_specs=[terms, terms, WHOLE, WHOLE],
            out_specs=[WHOLE] * 2,
        ),
        out_shape=[jax.ShapeDtypeStruct((rows, width), jnp.bfloat16)] * 2,
        compiler_params=params(),
        cost_estimate=cost(0, rows * width * 12 + 4 * one.shape[0] * width),
    )(live, me, own, there, one, two)


def sum_over(value, axis, size):
    if size & (size - 1):
        return lax.psum(value, axis)
    apart = 1
    while apart < size:
        value = value + lax.ppermute(value, axis, [(i, i ^ apart) for i in range(size)])
        apart *= 2
    return value


def ring_and_adapters(
    rows, ring, sizes, packed, own, there, output_weight, adapter_down_weight, adapter_up_weight,
    columns, local, index, me, live, own_place, there_place,
):
    size = len(ring)
    steps = sizes[0]

    forward = [(ring[i], ring[(i + 1) % size]) for i in range(size)]
    backward = [(ring[i], ring[i - 1]) for i in range(size)]
    far = size // 2
    chains = [
        (0, 1, forward, far),
        (1, -1, backward, far),
        (1, 1, forward, size - 1 - far),
        (0, -1, backward, size - 1 - far),
    ]
    arrived = [None] * len(chains)
    for left in range(far, 0, -1):
        for chain, (part, sign, moves, length) in enumerate(chains):
            if left <= length:
                partial = hop(
                    rows, columns, (sign * left) % size, part, packed, output_weight,
                    arrived[chain],
                )
                arrived[chain] = lax.ppermute(partial, "tp", moves)

    own_low, there_low = low_rank(
        sizes, local, index, own, there, own_place, there_place, adapter_down_weight
    )
    own_low = own_low + lax.ppermute(there_low, "inst", SWAP)
    own_low = sum_over(own_low, "tp", size).astype(jnp.bfloat16)
    there_low = lax.ppermute(own_low, "inst", SWAP)
    count = index.shape[0] // 2
    index_there = jnp.concatenate([index[count:], index[:count]])
    got_up = lax.ppermute(collect(index_there, me, adapter_up_weight), "inst", SWAP)
    own_sum, there_sum = own_terms(
        sizes, columns, local, index, me, own, there, output_weight, own_place, there_place,
        own_low, there_low, adapter_up_weight, got_up,
    )
    here, away = [], []
    for part in range(2):
        one, two = [a for a, c in zip(arrived, chains) if c[0] == part]
        mine, theirs = finish(steps, live, me, part, own_sum, there_sum, one, two)
        here.append(mine)
        away.append(lax.ppermute(theirs, "inst", SWAP))
    return (*here, *away)


def per_device(
    ring,
    attention_output,
    output_weight,
    adapter_down_weight,
    adapter_up_weight,
    adapter_page_table,
    block_adapter_ids,
    row_list_position,
    live_row_count,
):
    size = len(ring)
    steps, row_count, depth = attention_output.shape
    resident, rank, _ = adapter_down_weight.shape
    _, blocks, listed = block_adapter_ids.shape
    sizes = (steps, blocks, listed, rank, row_count // blocks)

    instance = lax.axis_index("inst")
    tp = lax.axis_index("tp")
    place_of = [0] * size
    for at, tp_index in enumerate(ring):
        place_of[tp_index] = at
    place = jnp.array(place_of, dtype=jnp.int32)[tp]
    dests = jnp.array(ring, dtype=jnp.int32)[(place + jnp.arange(size, dtype=jnp.int32)) % size]
    columns = dests * 4 + instance * 2

    there = lax.ppermute(attention_output, "inst", SWAP)
    ids = block_adapter_ids.reshape(-1)
    numbers = jnp.concatenate([ids, live_row_count.reshape(-1), row_list_position.reshape(-1)])
    numbers_there = lax.ppermute(numbers, "inst", SWAP)
    listings = ids.shape[0]
    there_place = numbers_there[listings + steps :].reshape(steps, row_count)
    live_pair = jnp.stack(
        [live_row_count.reshape(-1), numbers_there[listings : listings + steps]], axis=1
    )
    live = jnp.where(instance == 0, live_pair, live_pair[:, ::-1]).reshape(-1)
    pages = adapter_page_table[jnp.concatenate([ids, numbers_there[:listings]])]
    index = pages % resident
    local = (pages // resident == instance).astype(jnp.int32)
    me = instance.reshape(1)

    packed = pack(live, me, attention_output, there)
    buckets = row_buckets(2 * steps * row_count)
    needed = jnp.sum(padded(live))
    branch = jnp.sum((needed > jnp.array(buckets, dtype=jnp.int32)).astype(jnp.int32))
    parts = lax.switch(
        branch,
        [functools.partial(ring_and_adapters, rows, ring, sizes) for rows in buckets],
        packed, attention_output, there, output_weight, adapter_down_weight, adapter_up_weight,
        columns, local, index, me, live, row_list_position, there_place,
    )
    here, away = parts[:2], parts[2:]
    result = jnp.where(
        instance == 0,
        jnp.concatenate([*here, *away], axis=1),
        jnp.concatenate([*away, *here], axis=1),
    )
    return result.reshape(steps, row_count, -1)


def solution(mesh):
    in_specs = (
        P(None, ("grp", "inst"), "tp"),
        P("tp", None),
        P("inst", None, "tp"),
        P("inst", None, "tp"),
        P(),
        P(None, ("grp", "inst"), None),
        P(None, ("grp", "inst")),
        P(None, ("grp", "inst")),
    )
    out_specs = P(None, ("grp", "inst"), "tp")
    ring = ring_order(mesh.shape["tp"])
    return jax.shard_map(
        functools.partial(per_device, ring),
        mesh=mesh, in_specs=in_specs, out_specs=out_specs, check_vma=False,
    )
```

```python
import functools

import jax
import jax.numpy as jnp
from jax import lax
from jax.experimental import pallas as pl
from jax.experimental.pallas import tpu as pltpu
from jax.sharding import PartitionSpec as P

VMEM_LIMIT = 40 * 1024 * 1024
SWAP = [(0, 1), (1, 0)]
WHOLE = pl.BlockSpec(memory_space=pltpu.VMEM)
ANYWHERE = pl.BlockSpec(memory_space=pl.ANY)


def serpentine(size):
    return size == 8


def ring_index(place, size):
    if not serpentine(size):
        return place
    return jnp.where(place < size // 2, 2 * place, 2 * (size - 1 - place) + 1)


def ring_place(index, size):
    if not serpentine(size):
        return index
    return jnp.where(index & 1 == 0, index >> 1, size - 1 - (index >> 1))


def ring_order(size):
    if not serpentine(size):
        return list(range(size))
    return list(range(0, size, 2)) + list(range(size - 1, 0, -2))


def params():
    return pltpu.CompilerParams(vmem_limit_bytes=VMEM_LIMIT)


def cost(flops, size):
    return pl.CostEstimate(flops=flops, bytes_accessed=size, transcendentals=0)


def hop_kernel(with_received, dests, x_ref, w_ref, *refs):
    total = jnp.dot(x_ref[...], w_ref[...], preferred_element_type=jnp.float32)
    if with_received:
        total = total + refs[0][...].astype(jnp.float32)
    refs[-1][...] = total.astype(refs[-1].dtype)


def hop(dests, offset, half, x, weight, received, after):
    rows, depth = x.shape
    half_cols = weight.shape[1] // dests.shape[0] // 2
    tile = min(256, half_cols)
    tiles = half_cols // tile
    in_specs = [
        pl.BlockSpec((rows, depth), lambda j, d: (0, 0)),
        pl.BlockSpec(
            (depth, tile), lambda j, d: (0, (d[offset] * 2 + half) * tiles + j)
        ),
    ]
    operands = [x, weight]
    if received is not None:
        in_specs.append(pl.BlockSpec((rows, tile), lambda j, d: (0, j)))
        operands.append(received)
    if after is not None:
        in_specs.append(ANYWHERE)
        operands.append(after)
    return pl.pallas_call(
        functools.partial(hop_kernel, received is not None),
        grid_spec=pltpu.PrefetchScalarGridSpec(
            num_scalar_prefetch=1,
            grid=(tiles,),
            in_specs=in_specs,
            out_specs=pl.BlockSpec((rows, tile), lambda j, d: (0, j)),
        ),
        out_shape=jax.ShapeDtypeStruct((rows, half_cols), jnp.bfloat16),
        compiler_params=params(),
        cost_estimate=cost(
            2 * rows * depth * half_cols,
            2 * (rows * depth + depth * half_cols + 2 * rows * half_cols),
        ),
    )(dests, *operands)


def collect_kernel(count, index, table_ref, after_ref, out_ref, sems):
    copies = [
        pltpu.make_async_copy(table_ref.at[index[slot]], out_ref.at[slot], sems.at[slot])
        for slot in range(count)
    ]
    for copy in copies:
        copy.start()
    for copy in copies:
        copy.wait()


def collect(index, table, after):
    count = index.shape[0]
    shape = (count,) + table.shape[1:]
    return pl.pallas_call(
        functools.partial(collect_kernel, count),
        grid_spec=pltpu.PrefetchScalarGridSpec(
            num_scalar_prefetch=1,
            grid=(1,),
            in_specs=[ANYWHERE, ANYWHERE],
            out_specs=WHOLE,
            scratch_shapes=[pltpu.SemaphoreType.DMA((count,))],
        ),
        out_shape=jax.ShapeDtypeStruct(shape, table.dtype),
        compiler_params=params(),
        cost_estimate=cost(0, 4 * shape[0] * shape[1] * shape[2]),
    )(index, table, after)


def load_pages(count, local, index, table_ref, got_ref, pages, sems):
    for slot in range(count):
        own = local[slot] == 1

        @pl.when(own)
        def _():
            pltpu.make_async_copy(
                table_ref.at[index[slot]], pages.at[slot], sems.at[slot]
            ).start()

        @pl.when(jnp.logical_not(own))
        def _():
            pltpu.make_async_copy(got_ref.at[slot], pages.at[slot], sems.at[slot]).start()

    for slot in range(count):
        pltpu.make_async_copy(got_ref.at[slot], pages.at[slot], sems.at[slot]).wait()


def low_kernel(
    sizes, local, index, x_ref, place_ref, table_ref, got_ref, after_ref, out_ref, pages, sems
):
    steps, blocks, listed, rank, block_rows = sizes
    load_pages(steps * blocks * listed, local, index, table_ref, got_ref, pages, sems)
    for step in range(steps):
        for block in range(blocks):
            at = step * blocks + block
            rows = slice(at * block_rows, (at + 1) * block_rows)
            listing = pages[at * listed : (at + 1) * listed].reshape(listed * rank, -1)
            every = lax.dot_general(
                listing, x_ref[rows, :], (((1,), (1,)), ((), ())),
                preferred_element_type=jnp.float32,
            )
            place = place_ref[step : step + 1, block * block_rows : (block + 1) * block_rows]
            low = jnp.zeros((rank, block_rows), jnp.float32)
            for entry in range(listed):
                low = jnp.where(place == entry, every[entry * rank : (entry + 1) * rank], low)
            out_ref[:, rows] = low


def low_rank(sizes, local, index, x, place, table, got, after):
    steps, blocks, listed, rank, block_rows = sizes
    count = steps * blocks * listed
    rows, depth = x.shape
    return pl.pallas_call(
        functools.partial(low_kernel, sizes),
        grid_spec=pltpu.PrefetchScalarGridSpec(
            num_scalar_prefetch=2,
            grid=(1,),
            in_specs=[WHOLE, WHOLE, ANYWHERE, ANYWHERE, ANYWHERE],
            out_specs=WHOLE,
            scratch_shapes=[
                pltpu.VMEM((count, rank, depth), table.dtype),
                pltpu.SemaphoreType.DMA((count,)),
            ],
        ),
        out_shape=jax.ShapeDtypeStruct((rank, rows), jnp.float32),
        compiler_params=params(),
        cost_estimate=cost(
            2 * rows * depth * listed * rank, 2 * (rows * depth + count * rank * depth)
        ),
    )(local, index, x, place, table, got, after)


def add_kernel(one_ref, two_ref, after_ref, out_ref):
    out_ref[...] = one_ref[...] + two_ref[...]


def add(one, two, after):
    return pl.pallas_call(
        add_kernel,
        in_specs=[WHOLE, WHOLE, ANYWHERE],
        out_specs=WHOLE,
        out_shape=jax.ShapeDtypeStruct(one.shape, one.dtype),
        compiler_params=params(),
        cost_estimate=cost(one.size, 12 * one.size),
    )(one, two, after)


def own_kernel(
    sizes, dests, local, index, x_ref, w_ref, place_ref, low_ref, table_ref, got_ref, after_ref,
    out_ref, pages, sems,
):
    steps, blocks, listed, rank, block_rows = sizes
    tile = w_ref.shape[1]
    now = pl.program_id(0)

    @pl.when(now == 0)
    def _():
        load_pages(steps * blocks * listed, local, index, table_ref, got_ref, pages, sems)

    columns = pl.ds(pl.multiple_of(now * tile, tile), tile)
    entry_of = lax.broadcasted_iota(jnp.int32, (listed * rank, block_rows), 0) // rank
    for step in range(steps):
        for block in range(blocks):
            at = step * blocks + block
            rows = slice(at * block_rows, (at + 1) * block_rows)
            low = low_ref[:, rows]
            spread = jnp.concatenate([low] * listed, axis=0)
            place = place_ref[step : step + 1, block * block_rows : (block + 1) * block_rows]
            spread = jnp.where(entry_of == place, spread, 0.0)
            listing = pages[at * listed : (at + 1) * listed, :, columns]
            out_ref[rows, :] = jnp.dot(
                x_ref[rows, :], w_ref[...], preferred_element_type=jnp.float32
            ) + jnp.dot(
                spread.T.astype(jnp.bfloat16),
                listing.reshape(listed * rank, tile),
                preferred_element_type=jnp.float32,
            )


def own_terms(sizes, dests, local, index, x, weight, place, low, table, got, after):
    steps, blocks, listed, rank, block_rows = sizes
    count = steps * blocks * listed
    rows, depth = x.shape
    cols = weight.shape[1] // dests.shape[0]
    tile = min(256, cols)
    tiles = cols // tile
    return pl.pallas_call(
        functools.partial(own_kernel, sizes),
        grid_spec=pltpu.PrefetchScalarGridSpec(
            num_scalar_prefetch=3,
            grid=(tiles,),
            in_specs=[
                WHOLE,
                pl.BlockSpec((depth, tile), lambda j, d, l, i: (0, d[0] * tiles + j)),
                WHOLE,
                WHOLE,
                ANYWHERE,
                ANYWHERE,
                ANYWHERE,
            ],
            out_specs=pl.BlockSpec((rows, tile), lambda j, d, l, i: (0, j)),
            scratch_shapes=[
                pltpu.VMEM((count, rank, cols), table.dtype),
                pltpu.SemaphoreType.DMA((count,)),
            ],
        ),
        out_shape=jax.ShapeDtypeStruct((rows, cols), jnp.float32),
        compiler_params=params(),
        cost_estimate=cost(
            2 * rows * cols * (depth + listed * rank),
            2 * (rows * depth + depth * cols + count * rank * cols) + 4 * rows * cols,
        ),
    )(dests, local, index, x, weight, place, low, table, got, after)


def finish_kernel(live, own_ref, one_ref, two_ref, *refs):
    out_ref = refs[-1]
    total = (
        own_ref[...] + one_ref[...].astype(jnp.float32) + two_ref[...].astype(jnp.float32)
    )
    row = lax.broadcasted_iota(jnp.int32, total.shape, 0)
    out_ref[...] = jnp.where(row < live[pl.program_id(0)], total, 0.0).astype(out_ref.dtype)


def finish(live, half, own, one, two, result):
    rows, cols = own.shape
    steps = live.shape[0]
    block = (rows // steps, cols // 2)
    in_specs = [
        pl.BlockSpec(block, lambda s, l: (s, half)),
        pl.BlockSpec(block, lambda s, l: (s, 0)),
        pl.BlockSpec(block, lambda s, l: (s, 0)),
    ]
    operands = [own, one, two]
    aliases = {}
    if result is not None:
        in_specs.append(ANYWHERE)
        operands.append(result)
        aliases = {4: 0}
    return pl.pallas_call(
        finish_kernel,
        grid_spec=pltpu.PrefetchScalarGridSpec(
            num_scalar_prefetch=1,
            grid=(steps,),
            in_specs=in_specs,
            out_specs=pl.BlockSpec(block, lambda s, l: (s, half)),
        ),
        out_shape=jax.ShapeDtypeStruct((rows, cols), jnp.bfloat16),
        input_output_aliases=aliases,
        compiler_params=params(),
        cost_estimate=cost(0, rows * cols * 5),
    )(live, *operands)


def per_device(
    size,
    attention_output,
    output_weight,
    adapter_down_weight,
    adapter_up_weight,
    adapter_page_table,
    block_adapter_ids,
    row_list_position,
    live_row_count,
):
    steps, row_count, depth = attention_output.shape
    resident, rank, _ = adapter_down_weight.shape
    _, blocks, listed = block_adapter_ids.shape
    sizes = (steps, blocks, listed, rank, row_count // blocks)
    x = attention_output.reshape(steps * row_count, depth)
    ring = ring_order(size)

    instance = lax.axis_index("inst")
    place = ring_place(lax.axis_index("tp"), size)
    dests = ring_index(lax.rem(place + jnp.arange(size, dtype=jnp.int32), size), size)

    forward = [(ring[i], ring[(i + 1) % size]) for i in range(size)]
    backward = [(ring[i], ring[i - 1]) for i in range(size)]
    far = size // 2
    pairs = [[(0, 1, forward), (1, -1, backward)], [(1, 1, forward), (0, -1, backward)]]
    arrived = {}
    last = None

    def turn(number, last):
        left = far - (number + 1) // 2
        for half, sign, moves in pairs[number % 2]:
            last = hop(
                dests, (sign * left) % size, half, x, output_weight,
                arrived.get((half, sign)), last,
            )
            arrived[half, sign] = lax.ppermute(last, "tp", moves)
        return last

    ids = block_adapter_ids.reshape(-1)
    ids_there = lax.ppermute(ids, "inst", SWAP)
    last = turn(0, last)
    pages = adapter_page_table[jnp.concatenate([ids, ids_there])]
    places = pages % resident
    index, index_there = places[: ids.shape[0]], places[ids.shape[0] :]
    local = (pages[: ids.shape[0]] // resident == instance).astype(jnp.int32)
    last = collect(index_there, adapter_down_weight, last)
    got_down = lax.ppermute(last, "inst", SWAP)
    last = turn(1, last)
    last = collect(index_there, adapter_up_weight, last)
    got_up = lax.ppermute(last, "inst", SWAP)
    low = last = low_rank(
        sizes, local, index, x, row_list_position, adapter_down_weight, got_down, last
    )

    last = turn(2, last)
    number, turns = 3, 2 * far - 1
    if size & (size - 1):
        low = lax.psum(low, "tp")
    else:
        apart = 1
        while apart < size:
            sent = lax.ppermute(low, "tp", [(i, i ^ apart) for i in range(size)])
            if number < turns:
                last = turn(number, last)
                number += 1
            low = last = add(low, sent, last)
            apart *= 2
    while number < turns:
        last = turn(number, last)
        number += 1
    low = low.astype(jnp.bfloat16).astype(jnp.float32)
    own = own_terms(
        sizes, dests, local, index, x, output_weight, row_list_position, low,
        adapter_up_weight, got_up, last,
    )
    result = None
    for half in range(2):
        result = finish(
            live_row_count.reshape(-1), half, own, arrived[half, 1], arrived[half, -1], result
        )
    return result.reshape(steps, row_count, -1)


def solution(mesh):
    in_specs = (
        P(None, ("grp", "inst"), "tp"),
        P("tp", None),
        P("inst", None, "tp"),
        P("inst", None, "tp"),
        P(),
        P(None, ("grp", "inst"), None),
        P(None, ("grp", "inst")),
        P(None, ("grp", "inst")),
    )
    out_specs = P(None, ("grp", "inst"), "tp")
    return jax.shard_map(
        functools.partial(per_device, mesh.shape["tp"]),
        mesh=mesh, in_specs=in_specs, out_specs=out_specs, check_vma=False,
    )
```

```python
import functools

import jax
import jax.numpy as jnp
from jax import lax
from jax.experimental import pallas as pl
from jax.experimental.pallas import tpu as pltpu
from jax.sharding import PartitionSpec as P

VMEM_LIMIT = 40 * 1024 * 1024
SWAP = [(0, 1), (1, 0)]
WHOLE = pl.BlockSpec(memory_space=pltpu.VMEM)
ANYWHERE = pl.BlockSpec(memory_space=pl.ANY)


def serpentine(size):
    return size == 8


def ring_index(place, size):
    if not serpentine(size):
        return place
    return jnp.where(place < size // 2, 2 * place, 2 * (size - 1 - place) + 1)


def ring_place(index, size):
    if not serpentine(size):
        return index
    return jnp.where(index & 1 == 0, index >> 1, size - 1 - (index >> 1))


def ring_order(size):
    if not serpentine(size):
        return list(range(size))
    return list(range(0, size, 2)) + list(range(size - 1, 0, -2))


def params():
    return pltpu.CompilerParams(vmem_limit_bytes=VMEM_LIMIT)


def cost(flops, size):
    return pl.CostEstimate(flops=30 * flops, bytes_accessed=size, transcendentals=0)


def hop_kernel(with_received, dests, x_ref, w_ref, *refs):
    total = jnp.dot(x_ref[...], w_ref[...], preferred_element_type=jnp.float32)
    if with_received:
        total = total + refs[0][...].astype(jnp.float32)
    refs[-1][...] = total.astype(refs[-1].dtype)


def hop(dests, offset, half, x, weight, received, after):
    rows, depth = x.shape
    half_cols = weight.shape[1] // dests.shape[0] // 2
    tile = min(256, half_cols)
    tiles = half_cols // tile
    in_specs = [
        pl.BlockSpec((rows, depth), lambda j, d: (0, 0)),
        pl.BlockSpec(
            (depth, tile), lambda j, d: (0, (d[offset] * 2 + half) * tiles + j)
        ),
    ]
    operands = [x, weight]
    if received is not None:
        in_specs.append(pl.BlockSpec((rows, tile), lambda j, d: (0, j)))
        operands.append(received)
    if after is not None:
        in_specs.append(ANYWHERE)
        operands.append(after)
    return pl.pallas_call(
        functools.partial(hop_kernel, received is not None),
        grid_spec=pltpu.PrefetchScalarGridSpec(
            num_scalar_prefetch=1,
            grid=(tiles,),
            in_specs=in_specs,
            out_specs=pl.BlockSpec((rows, tile), lambda j, d: (0, j)),
        ),
        out_shape=jax.ShapeDtypeStruct((rows, half_cols), jnp.bfloat16),
        compiler_params=params(),
        cost_estimate=cost(
            2 * rows * depth * half_cols,
            2 * (rows * depth + depth * half_cols + 2 * rows * half_cols),
        ),
    )(dests, *operands)


def collect_kernel(count, index, table_ref, after_ref, out_ref, sems):
    copies = [
        pltpu.make_async_copy(table_ref.at[index[slot]], out_ref.at[slot], sems.at[slot])
        for slot in range(count)
    ]
    for copy in copies:
        copy.start()
    for copy in copies:
        copy.wait()


def collect(index, table, after):
    count = index.shape[0]
    shape = (count,) + table.shape[1:]
    return pl.pallas_call(
        functools.partial(collect_kernel, count),
        grid_spec=pltpu.PrefetchScalarGridSpec(
            num_scalar_prefetch=1,
            grid=(1,),
            in_specs=[ANYWHERE, ANYWHERE],
            out_specs=WHOLE,
            scratch_shapes=[pltpu.SemaphoreType.DMA((count,))],
        ),
        out_shape=jax.ShapeDtypeStruct(shape, table.dtype),
        compiler_params=params(),
        cost_estimate=cost(0, 4 * shape[0] * shape[1] * shape[2]),
    )(index, table, after)


def load_pages(count, local, index, table_ref, got_ref, pages, sems):
    for slot in range(count):
        own = local[slot] == 1

        @pl.when(own)
        def _():
            pltpu.make_async_copy(
                table_ref.at[index[slot]], pages.at[slot], sems.at[slot]
            ).start()

        @pl.when(jnp.logical_not(own))
        def _():
            pltpu.make_async_copy(got_ref.at[slot], pages.at[slot], sems.at[slot]).start()

    for slot in range(count):
        pltpu.make_async_copy(got_ref.at[slot], pages.at[slot], sems.at[slot]).wait()


def low_kernel(
    sizes, local, index, x_ref, place_ref, table_ref, got_ref, after_ref, out_ref, pages, sems
):
    steps, blocks, listed, rank, block_rows = sizes
    load_pages(steps * blocks * listed, local, index, table_ref, got_ref, pages, sems)
    for step in range(steps):
        for block in range(blocks):
            at = step * blocks + block
            rows = slice(at * block_rows, (at + 1) * block_rows)
            listing = pages[at * listed : (at + 1) * listed].reshape(listed * rank, -1)
            every = lax.dot_general(
                listing, x_ref[rows, :], (((1,), (1,)), ((), ())),
                preferred_element_type=jnp.float32,
            )
            place = place_ref[step : step + 1, block * block_rows : (block + 1) * block_rows]
            low = jnp.zeros((rank, block_rows), jnp.float32)
            for entry in range(listed):
                low = jnp.where(place == entry, every[entry * rank : (entry + 1) * rank], low)
            out_ref[:, rows] = low


def low_rank(sizes, local, index, x, place, table, got, after):
    steps, blocks, listed, rank, block_rows = sizes
    count = steps * blocks * listed
    rows, depth = x.shape
    return pl.pallas_call(
        functools.partial(low_kernel, sizes),
        grid_spec=pltpu.PrefetchScalarGridSpec(
            num_scalar_prefetch=2,
            grid=(1,),
            in_specs=[WHOLE, WHOLE, ANYWHERE, ANYWHERE, ANYWHERE],
            out_specs=WHOLE,
            scratch_shapes=[
                pltpu.VMEM((count, rank, depth), table.dtype),
                pltpu.SemaphoreType.DMA((count,)),
            ],
        ),
        out_shape=jax.ShapeDtypeStruct((rank, rows), jnp.float32),
        compiler_params=params(),
        cost_estimate=cost(
            2 * rows * depth * listed * rank, 2 * (rows * depth + count * rank * depth)
        ),
    )(local, index, x, place, table, got, after)


def add_kernel(one_ref, two_ref, after_ref, out_ref):
    out_ref[...] = one_ref[...] + two_ref[...]


def add(one, two, after):
    return pl.pallas_call(
        add_kernel,
        in_specs=[WHOLE, WHOLE, ANYWHERE],
        out_specs=WHOLE,
        out_shape=jax.ShapeDtypeStruct(one.shape, one.dtype),
        compiler_params=params(),
        cost_estimate=cost(one.size, 12 * one.size),
    )(one, two, after)


def own_kernel(
    sizes, dests, local, index, x_ref, w_ref, place_ref, low_ref, table_ref, got_ref, after_ref,
    out_ref, pages, sems,
):
    steps, blocks, listed, rank, block_rows = sizes
    tile = w_ref.shape[1]
    now = pl.program_id(0)

    @pl.when(now == 0)
    def _():
        load_pages(steps * blocks * listed, local, index, table_ref, got_ref, pages, sems)

    columns = pl.ds(pl.multiple_of(now * tile, tile), tile)
    entry_of = lax.broadcasted_iota(jnp.int32, (listed * rank, block_rows), 0) // rank
    for step in range(steps):
        for block in range(blocks):
            at = step * blocks + block
            rows = slice(at * block_rows, (at + 1) * block_rows)
            low = low_ref[:, rows]
            spread = jnp.concatenate([low] * listed, axis=0)
            place = place_ref[step : step + 1, block * block_rows : (block + 1) * block_rows]
            spread = jnp.where(entry_of == place, spread, 0.0)
            listing = pages[at * listed : (at + 1) * listed, :, columns]
            out_ref[rows, :] = jnp.dot(
                x_ref[rows, :], w_ref[...], preferred_element_type=jnp.float32
            ) + jnp.dot(
                spread.T.astype(jnp.bfloat16),
                listing.reshape(listed * rank, tile),
                preferred_element_type=jnp.float32,
            )


def own_terms(sizes, dests, local, index, x, weight, place, low, table, got, after):
    steps, blocks, listed, rank, block_rows = sizes
    count = steps * blocks * listed
    rows, depth = x.shape
    cols = weight.shape[1] // dests.shape[0]
    tile = min(256, cols)
    tiles = cols // tile
    return pl.pallas_call(
        functools.partial(own_kernel, sizes),
        grid_spec=pltpu.PrefetchScalarGridSpec(
            num_scalar_prefetch=3,
            grid=(tiles,),
            in_specs=[
                WHOLE,
                pl.BlockSpec((depth, tile), lambda j, d, l, i: (0, d[0] * tiles + j)),
                WHOLE,
                WHOLE,
                ANYWHERE,
                ANYWHERE,
                ANYWHERE,
            ],
            out_specs=pl.BlockSpec((rows, tile), lambda j, d, l, i: (0, j)),
            scratch_shapes=[
                pltpu.VMEM((count, rank, cols), table.dtype),
                pltpu.SemaphoreType.DMA((count,)),
            ],
        ),
        out_shape=jax.ShapeDtypeStruct((rows, cols), jnp.float32),
        compiler_params=params(),
        cost_estimate=cost(
            2 * rows * cols * (depth + listed * rank),
            2 * (rows * depth + depth * cols + count * rank * cols) + 4 * rows * cols,
        ),
    )(dests, local, index, x, weight, place, low, table, got, after)


def finish_kernel(live, own_ref, one_ref, two_ref, *refs):
    out_ref = refs[-1]
    total = (
        own_ref[...] + one_ref[...].astype(jnp.float32) + two_ref[...].astype(jnp.float32)
    )
    row = lax.broadcasted_iota(jnp.int32, total.shape, 0)
    out_ref[...] = jnp.where(row < live[pl.program_id(0)], total, 0.0).astype(out_ref.dtype)


def finish(live, half, own, one, two, result):
    rows, cols = own.shape
    steps = live.shape[0]
    block = (rows // steps, cols // 2)
    in_specs = [
        pl.BlockSpec(block, lambda s, l: (s, half)),
        pl.BlockSpec(block, lambda s, l: (s, 0)),
        pl.BlockSpec(block, lambda s, l: (s, 0)),
    ]
    operands = [own, one, two]
    aliases = {}
    if result is not None:
        in_specs.append(ANYWHERE)
        operands.append(result)
        aliases = {4: 0}
    return pl.pallas_call(
        finish_kernel,
        grid_spec=pltpu.PrefetchScalarGridSpec(
            num_scalar_prefetch=1,
            grid=(steps,),
            in_specs=in_specs,
            out_specs=pl.BlockSpec(block, lambda s, l: (s, half)),
        ),
        out_shape=jax.ShapeDtypeStruct((rows, cols), jnp.bfloat16),
        input_output_aliases=aliases,
        compiler_params=params(),
        cost_estimate=cost(0, rows * cols * 5),
    )(live, *operands)


def per_device(
    size,
    attention_output,
    output_weight,
    adapter_down_weight,
    adapter_up_weight,
    adapter_page_table,
    block_adapter_ids,
    row_list_position,
    live_row_count,
):
    steps, row_count, depth = attention_output.shape
    resident, rank, _ = adapter_down_weight.shape
    _, blocks, listed = block_adapter_ids.shape
    sizes = (steps, blocks, listed, rank, row_count // blocks)
    x = attention_output.reshape(steps * row_count, depth)
    ring = ring_order(size)

    instance = lax.axis_index("inst")
    place = ring_place(lax.axis_index("tp"), size)
    dests = ring_index(lax.rem(place + jnp.arange(size, dtype=jnp.int32), size), size)

    forward = [(ring[i], ring[(i + 1) % size]) for i in range(size)]
    backward = [(ring[i], ring[i - 1]) for i in range(size)]
    far = size // 2
    pairs = [[(0, 1, forward), (1, -1, backward)], [(1, 1, forward), (0, -1, backward)]]
    arrived = {}
    last = None

    def turn(number, last):
        left = far - (number + 1) // 2
        for half, sign, moves in pairs[number % 2]:
            last = hop(
                dests, (sign * left) % size, half, x, output_weight,
                arrived.get((half, sign)), last,
            )
            arrived[half, sign] = lax.ppermute(last, "tp", moves)
        return last

    ids = block_adapter_ids.reshape(-1)
    ids_there = lax.ppermute(ids, "inst", SWAP)
    last = turn(0, last)
    pages = adapter_page_table[jnp.concatenate([ids, ids_there])]
    places = pages % resident
    index, index_there = places[: ids.shape[0]], places[ids.shape[0] :]
    local = (pages[: ids.shape[0]] // resident == instance).astype(jnp.int32)
    last = collect(index_there, adapter_down_weight, last)
    got_down = lax.ppermute(last, "inst", SWAP)
    last = turn(1, last)
    last = collect(index_there, adapter_up_weight, last)
    got_up = lax.ppermute(last, "inst", SWAP)
    low = last = low_rank(
        sizes, local, index, x, row_list_position, adapter_down_weight, got_down, last
    )

    last = turn(2, last)
    number, turns = 3, 2 * far - 1
    if size & (size - 1):
        low = lax.psum(low, "tp")
    else:
        apart = 1
        while apart < size:
            sent = lax.ppermute(low, "tp", [(i, i ^ apart) for i in range(size)])
            if number < turns:
                last = turn(number, last)
                number += 1
            low = last = add(low, sent, last)
            apart *= 2
    while number < turns:
        last = turn(number, last)
        number += 1
    low = low.astype(jnp.bfloat16).astype(jnp.float32)
    own = own_terms(
        sizes, dests, local, index, x, output_weight, row_list_position, low,
        adapter_up_weight, got_up, last,
    )
    result = None
    for half in range(2):
        result = finish(
            live_row_count.reshape(-1), half, own, arrived[half, 1], arrived[half, -1], result
        )
    return result.reshape(steps, row_count, -1)


def solution(mesh):
    in_specs = (
        P(None, ("grp", "inst"), "tp"),
        P("tp", None),
        P("inst", None, "tp"),
        P("inst", None, "tp"),
        P(),
        P(None, ("grp", "inst"), None),
        P(None, ("grp", "inst")),
        P(None, ("grp", "inst")),
    )
    out_specs = P(None, ("grp", "inst"), "tp")
    return jax.shard_map(
        functools.partial(per_device, mesh.shape["tp"]),
        mesh=mesh, in_specs=in_specs, out_specs=out_specs, check_vma=False,
    )
```

```python
import functools

import jax
import jax.numpy as jnp
from jax import lax
from jax.experimental import pallas as pl
from jax.experimental.pallas import tpu as pltpu
from jax.sharding import PartitionSpec as P

VMEM_LIMIT = 40 * 1024 * 1024
SWAP = [(0, 1), (1, 0)]
WHOLE = pl.BlockSpec(memory_space=pltpu.VMEM)
ANYWHERE = pl.BlockSpec(memory_space=pl.ANY)


def serpentine(size):
    return size == 8


def ring_index(place, size):
    if not serpentine(size):
        return place
    return jnp.where(place < size // 2, 2 * place, 2 * (size - 1 - place) + 1)


def ring_place(index, size):
    if not serpentine(size):
        return index
    return jnp.where(index & 1 == 0, index >> 1, size - 1 - (index >> 1))


def ring_order(size):
    if not serpentine(size):
        return list(range(size))
    return list(range(0, size, 2)) + list(range(size - 1, 0, -2))


def params():
    return pltpu.CompilerParams(vmem_limit_bytes=VMEM_LIMIT)


def cost(flops, size):
    return pl.CostEstimate(flops=30 * flops, bytes_accessed=size, transcendentals=0)


def hop_kernel(with_received, dests, x_ref, w_ref, *refs):
    tile = w_ref.shape[1]
    columns = pl.ds(pl.multiple_of(pl.program_id(0) * tile, tile), tile)
    total = jnp.dot(x_ref[...], w_ref[...], preferred_element_type=jnp.float32)
    if with_received:
        total = total + refs[0][:, columns].astype(jnp.float32)
    refs[-1][:, columns] = total.astype(refs[-1].dtype)


def hop(dests, offset, half, x, weight, received, after):
    rows, depth = x.shape
    half_cols = weight.shape[1] // dests.shape[0] // 2
    tile = min(256, half_cols)
    tiles = half_cols // tile
    in_specs = [
        WHOLE,
        pl.BlockSpec(
            (depth, tile), lambda j, d: (0, (d[offset] * 2 + half) * tiles + j)
        ),
    ]
    operands = [x, weight]
    if received is not None:
        in_specs.append(WHOLE)
        operands.append(received)
    if after is not None:
        in_specs.append(ANYWHERE)
        operands.append(after)
    return pl.pallas_call(
        functools.partial(hop_kernel, received is not None),
        grid_spec=pltpu.PrefetchScalarGridSpec(
            num_scalar_prefetch=1,
            grid=(tiles,),
            in_specs=in_specs,
            out_specs=WHOLE,
        ),
        out_shape=jax.ShapeDtypeStruct((rows, half_cols), jnp.bfloat16),
        compiler_params=params(),
        cost_estimate=cost(
            2 * rows * depth * half_cols,
            2 * (rows * depth + depth * half_cols + 2 * rows * half_cols),
        ),
    )(dests, *operands)


def collect_kernel(count, index, table_ref, after_ref, out_ref, sems):
    copies = [
        pltpu.make_async_copy(table_ref.at[index[slot]], out_ref.at[slot], sems.at[slot])
        for slot in range(count)
    ]
    for copy in copies:
        copy.start()
    for copy in copies:
        copy.wait()


def collect(index, table, after):
    count = index.shape[0]
    shape = (count,) + table.shape[1:]
    return pl.pallas_call(
        functools.partial(collect_kernel, count),
        grid_spec=pltpu.PrefetchScalarGridSpec(
            num_scalar_prefetch=1,
            grid=(1,),
            in_specs=[ANYWHERE, ANYWHERE],
            out_specs=WHOLE,
            scratch_shapes=[pltpu.SemaphoreType.DMA((count,))],
        ),
        out_shape=jax.ShapeDtypeStruct(shape, table.dtype),
        compiler_params=params(),
        cost_estimate=cost(0, 4 * shape[0] * shape[1] * shape[2]),
    )(index, table, after)


def load_pages(count, local, index, table_ref, got_ref, pages, sems):
    for slot in range(count):
        own = local[slot] == 1

        @pl.when(own)
        def _():
            pltpu.make_async_copy(
                table_ref.at[index[slot]], pages.at[slot], sems.at[slot]
            ).start()

        @pl.when(jnp.logical_not(own))
        def _():
            pltpu.make_async_copy(got_ref.at[slot], pages.at[slot], sems.at[slot]).start()

    for slot in range(count):
        pltpu.make_async_copy(got_ref.at[slot], pages.at[slot], sems.at[slot]).wait()


def low_kernel(
    sizes, local, index, x_ref, place_ref, table_ref, got_ref, after_ref, out_ref, pages, sems
):
    steps, blocks, listed, rank, block_rows = sizes
    load_pages(steps * blocks * listed, local, index, table_ref, got_ref, pages, sems)
    for step in range(steps):
        for block in range(blocks):
            at = step * blocks + block
            rows = slice(at * block_rows, (at + 1) * block_rows)
            listing = pages[at * listed : (at + 1) * listed].reshape(listed * rank, -1)
            every = lax.dot_general(
                listing, x_ref[rows, :], (((1,), (1,)), ((), ())),
                preferred_element_type=jnp.float32,
            )
            place = place_ref[step : step + 1, block * block_rows : (block + 1) * block_rows]
            low = jnp.zeros((rank, block_rows), jnp.float32)
            for entry in range(listed):
                low = jnp.where(place == entry, every[entry * rank : (entry + 1) * rank], low)
            out_ref[:, rows] = low


def low_rank(sizes, local, index, x, place, table, got, after):
    steps, blocks, listed, rank, block_rows = sizes
    count = steps * blocks * listed
    rows, depth = x.shape
    return pl.pallas_call(
        functools.partial(low_kernel, sizes),
        grid_spec=pltpu.PrefetchScalarGridSpec(
            num_scalar_prefetch=2,
            grid=(1,),
            in_specs=[WHOLE, WHOLE, ANYWHERE, ANYWHERE, ANYWHERE],
            out_specs=WHOLE,
            scratch_shapes=[
                pltpu.VMEM((count, rank, depth), table.dtype),
                pltpu.SemaphoreType.DMA((count,)),
            ],
        ),
        out_shape=jax.ShapeDtypeStruct((rank, rows), jnp.float32),
        compiler_params=params(),
        cost_estimate=cost(
            2 * rows * depth * listed * rank, 2 * (rows * depth + count * rank * depth)
        ),
    )(local, index, x, place, table, got, after)


def add_kernel(one_ref, two_ref, after_ref, out_ref):
    out_ref[...] = one_ref[...] + two_ref[...]


def add(one, two, after):
    return pl.pallas_call(
        add_kernel,
        in_specs=[WHOLE, WHOLE, ANYWHERE],
        out_specs=WHOLE,
        out_shape=jax.ShapeDtypeStruct(one.shape, one.dtype),
        compiler_params=params(),
        cost_estimate=cost(one.size, 12 * one.size),
    )(one, two, after)


def own_kernel(
    local, index, dests, x_ref, w_ref, table_ref, got_ref, after_ref, out_ref, pages, sems
):
    tile = w_ref.shape[1]
    now = pl.program_id(0)
    count = pages.shape[0]

    @pl.when(now == 0)
    def _():
        load_pages(count, local, index, table_ref, got_ref, pages, sems)

    columns = pl.ds(pl.multiple_of(now * tile, tile), tile)
    out_ref[:, columns] = jnp.dot(x_ref[...], w_ref[...], preferred_element_type=jnp.float32)


def own_terms(dests, local, index, x, weight, table, got, after):
    count, rank, cols = got.shape
    rows, depth = x.shape
    tile = min(256, cols)
    tiles = cols // tile
    return pl.pallas_call(
        own_kernel,
        grid_spec=pltpu.PrefetchScalarGridSpec(
            num_scalar_prefetch=3,
            grid=(tiles,),
            in_specs=[
                WHOLE,
                pl.BlockSpec((depth, tile), lambda j, l, i, d: (0, d[0] * tiles + j)),
                ANYWHERE,
                ANYWHERE,
                ANYWHERE,
            ],
            out_specs=[WHOLE, WHOLE],
            scratch_shapes=[pltpu.SemaphoreType.DMA((count,))],
        ),
        out_shape=[
            jax.ShapeDtypeStruct((rows, cols), jnp.float32),
            jax.ShapeDtypeStruct((count, rank, cols), table.dtype),
        ],
        compiler_params=params(),
        cost_estimate=cost(
            2 * rows * cols * depth,
            2 * (rows * depth + depth * cols + 2 * count * rank * cols) + 4 * rows * cols,
        ),
    )(local, index, dests, x, weight, table, got, after)


def delta_kernel(sizes, own_ref, pages_ref, place_ref, low_ref, after_ref, out_ref):
    steps, blocks, listed, rank, block_rows = sizes
    entry_of = lax.broadcasted_iota(jnp.int32, (listed * rank, block_rows), 0) // rank
    for step in range(steps):
        for block in range(blocks):
            at = step * blocks + block
            rows = slice(at * block_rows, (at + 1) * block_rows)
            low = low_ref[:, rows]
            spread = jnp.concatenate([low] * listed, axis=0)
            place = place_ref[step : step + 1, block * block_rows : (block + 1) * block_rows]
            spread = jnp.where(entry_of == place, spread, 0.0)
            listing = pages_ref[at * listed : (at + 1) * listed].reshape(listed * rank, -1)
            out_ref[rows, :] = own_ref[rows, :] + jnp.dot(
                spread.T.astype(jnp.bfloat16), listing, preferred_element_type=jnp.float32
            )


def add_delta(sizes, own, pages, place, low, after):
    rows, cols = own.shape
    return pl.pallas_call(
        functools.partial(delta_kernel, sizes),
        in_specs=[WHOLE, WHOLE, WHOLE, WHOLE, ANYWHERE],
        out_specs=WHOLE,
        out_shape=jax.ShapeDtypeStruct(own.shape, own.dtype),
        compiler_params=params(),
        cost_estimate=cost(
            2 * rows * cols * sizes[2] * sizes[3], 8 * rows * cols + 2 * pages.size
        ),
    )(own, pages, place, low, after)


def finish_kernel(live, own_ref, one_ref, two_ref, *refs):
    out_ref = refs[-1]
    total = (
        own_ref[...] + one_ref[...].astype(jnp.float32) + two_ref[...].astype(jnp.float32)
    )
    row = lax.broadcasted_iota(jnp.int32, total.shape, 0)
    out_ref[...] = jnp.where(row < live[pl.program_id(0)], total, 0.0).astype(out_ref.dtype)


def finish(live, half, own, one, two, result):
    rows, cols = own.shape
    steps = live.shape[0]
    block = (rows // steps, cols // 2)
    in_specs = [
        pl.BlockSpec(block, lambda s, l: (s, half)),
        pl.BlockSpec(block, lambda s, l: (s, 0)),
        pl.BlockSpec(block, lambda s, l: (s, 0)),
    ]
    operands = [own, one, two]
    aliases = {}
    if result is not None:
        in_specs.append(ANYWHERE)
        operands.append(result)
        aliases = {4: 0}
    return pl.pallas_call(
        finish_kernel,
        grid_spec=pltpu.PrefetchScalarGridSpec(
            num_scalar_prefetch=1,
            grid=(steps,),
            in_specs=in_specs,
            out_specs=pl.BlockSpec(block, lambda s, l: (s, half)),
        ),
        out_shape=jax.ShapeDtypeStruct((rows, cols), jnp.bfloat16),
        input_output_aliases=aliases,
        compiler_params=params(),
        cost_estimate=cost(0, rows * cols * 5),
    )(live, *operands)


def per_device(
    size,
    attention_output,
    output_weight,
    adapter_down_weight,
    adapter_up_weight,
    adapter_page_table,
    block_adapter_ids,
    row_list_position,
    live_row_count,
):
    steps, row_count, depth = attention_output.shape
    resident, rank, _ = adapter_down_weight.shape
    _, blocks, listed = block_adapter_ids.shape
    sizes = (steps, blocks, listed, rank, row_count // blocks)
    x = attention_output.reshape(steps * row_count, depth)
    ring = ring_order(size)

    instance = lax.axis_index("inst")
    place = ring_place(lax.axis_index("tp"), size)
    dests = ring_index(lax.rem(place + jnp.arange(size, dtype=jnp.int32), size), size)

    forward = [(ring[i], ring[(i + 1) % size]) for i in range(size)]
    backward = [(ring[i], ring[i - 1]) for i in range(size)]
    far = size // 2
    pairs = [[(0, 1, forward), (1, -1, backward)], [(1, 1, forward), (0, -1, backward)]]
    arrived = {}
    last = None

    def turn(number, last):
        left = far - (number + 1) // 2
        for half, sign, moves in pairs[number % 2]:
            last = hop(
                dests, (sign * left) % size, half, x, output_weight,
                arrived.get((half, sign)), last,
            )
            arrived[half, sign] = lax.ppermute(last, "tp", moves)
        return last

    ids = block_adapter_ids.reshape(-1)
    ids_there = lax.ppermute(ids, "inst", SWAP)
    last = turn(0, last)
    pages = adapter_page_table[jnp.concatenate([ids, ids_there])]
    places = pages % resident
    index, index_there = places[: ids.shape[0]], places[ids.shape[0] :]
    local = (pages[: ids.shape[0]] // resident == instance).astype(jnp.int32)
    last = collect(index_there, adapter_down_weight, last)
    got_down = lax.ppermute(last, "inst", SWAP)
    last = turn(1, last)
    last = collect(index_there, adapter_up_weight, last)
    got_up = lax.ppermute(last, "inst", SWAP)
    low = last = low_rank(
        sizes, local, index, x, row_list_position, adapter_down_weight, got_down, last
    )

    last = turn(2, last)
    own, up_pages = own_terms(
        dests, local, index, x, output_weight, adapter_up_weight, got_up, last
    )
    last = own
    number, turns = 3, 2 * far - 1
    if size & (size - 1):
        low = lax.psum(low, "tp")
    else:
        apart = 1
        while apart < size:
            sent = lax.ppermute(low, "tp", [(i, i ^ apart) for i in range(size)])
            apart *= 2
            for _ in range(1 if apart < size else 2):
                if number < turns:
                    last = turn(number, last)
                    number += 1
            low = last = add(low, sent, last)
    while number < turns:
        last = turn(number, last)
        number += 1
    low = low.astype(jnp.bfloat16).astype(jnp.float32)
    own = add_delta(sizes, own, up_pages, row_list_position, low, last)
    result = None
    for half in range(2):
        result = finish(
            live_row_count.reshape(-1), half, own, arrived[half, 1], arrived[half, -1], result
        )
    return result.reshape(steps, row_count, -1)


def solution(mesh):
    in_specs = (
        P(None, ("grp", "inst"), "tp"),
        P("tp", None),
        P("inst", None, "tp"),
        P("inst", None, "tp"),
        P(),
        P(None, ("grp", "inst"), None),
        P(None, ("grp", "inst")),
        P(None, ("grp", "inst")),
    )
    out_specs = P(None, ("grp", "inst"), "tp")
    return jax.shard_map(
        functools.partial(per_device, mesh.shape["tp"]),
        mesh=mesh, in_specs=in_specs, out_specs=out_specs, check_vma=False,
    )
```

```python
import functools

import jax
import jax.numpy as jnp
from jax import lax
from jax.experimental import pallas as pl
from jax.experimental.pallas import tpu as pltpu
from jax.sharding import PartitionSpec as P

VMEM_LIMIT = 40 * 1024 * 1024
SWAP = [(0, 1), (1, 0)]
WHOLE = pl.BlockSpec(memory_space=pltpu.VMEM)
ANYWHERE = pl.BlockSpec(memory_space=pl.ANY)


def serpentine(size):
    return size == 8


def ring_index(place, size):
    if not serpentine(size):
        return place
    return jnp.where(place < size // 2, 2 * place, 2 * (size - 1 - place) + 1)


def ring_place(index, size):
    if not serpentine(size):
        return index
    return jnp.where(index & 1 == 0, index >> 1, size - 1 - (index >> 1))


def ring_order(size):
    if not serpentine(size):
        return list(range(size))
    return list(range(0, size, 2)) + list(range(size - 1, 0, -2))


def params():
    return pltpu.CompilerParams(vmem_limit_bytes=VMEM_LIMIT)


def cost(flops, size):
    return pl.CostEstimate(flops=30 * flops, bytes_accessed=size, transcendentals=0)


def hop_kernel(with_received, dests, x_ref, w_ref, *refs):
    tile = w_ref.shape[1]
    columns = pl.ds(pl.multiple_of(pl.program_id(0) * tile, tile), tile)
    total = jnp.dot(x_ref[...], w_ref[...], preferred_element_type=jnp.float32)
    if with_received:
        total = total + refs[0][:, columns].astype(jnp.float32)
    refs[-1][:, columns] = total.astype(refs[-1].dtype)


def hop(dests, offset, half, x, weight, received, after):
    rows, depth = x.shape
    half_cols = weight.shape[1] // dests.shape[0] // 2
    tile = min(256, half_cols)
    tiles = half_cols // tile
    in_specs = [
        WHOLE,
        pl.BlockSpec(
            (depth, tile), lambda j, d: (0, (d[offset] * 2 + half) * tiles + j)
        ),
    ]
    operands = [x, weight]
    if received is not None:
        in_specs.append(WHOLE)
        operands.append(received)
    if after is not None:
        in_specs.append(ANYWHERE)
        operands.append(after)
    return pl.pallas_call(
        functools.partial(hop_kernel, received is not None),
        grid_spec=pltpu.PrefetchScalarGridSpec(
            num_scalar_prefetch=1,
            grid=(tiles,),
            in_specs=in_specs,
            out_specs=WHOLE,
        ),
        out_shape=jax.ShapeDtypeStruct((rows, half_cols), jnp.bfloat16),
        compiler_params=params(),
        cost_estimate=cost(
            2 * rows * depth * half_cols,
            2 * (rows * depth + depth * half_cols + 2 * rows * half_cols),
        ),
    )(dests, *operands)


def collect_kernel(count, index, table_ref, after_ref, out_ref, sems):
    copies = [
        pltpu.make_async_copy(table_ref.at[index[slot]], out_ref.at[slot], sems.at[slot])
        for slot in range(count)
    ]
    for copy in copies:
        copy.start()
    for copy in copies:
        copy.wait()


def collect(index, table, after):
    count = index.shape[0]
    shape = (count,) + table.shape[1:]
    return pl.pallas_call(
        functools.partial(collect_kernel, count),
        grid_spec=pltpu.PrefetchScalarGridSpec(
            num_scalar_prefetch=1,
            grid=(1,),
            in_specs=[ANYWHERE, ANYWHERE],
            out_specs=WHOLE,
            scratch_shapes=[pltpu.SemaphoreType.DMA((count,))],
        ),
        out_shape=jax.ShapeDtypeStruct(shape, table.dtype),
        compiler_params=params(),
        cost_estimate=cost(0, 4 * shape[0] * shape[1] * shape[2]),
    )(index, table, after)


def load_pages(count, local, index, table_ref, got_ref, pages, sems):
    for slot in range(count):
        own = local[slot] == 1

        @pl.when(own)
        def _():
            pltpu.make_async_copy(
                table_ref.at[index[slot]], pages.at[slot], sems.at[slot]
            ).start()

        @pl.when(jnp.logical_not(own))
        def _():
            pltpu.make_async_copy(got_ref.at[slot], pages.at[slot], sems.at[slot]).start()

    for slot in range(count):
        pltpu.make_async_copy(got_ref.at[slot], pages.at[slot], sems.at[slot]).wait()


def low_kernel(
    sizes, local, index, side, x_ref, place_ref, table_ref, got_ref, after_ref, keep_ref, give_ref,
    pages, sems,
):
    steps, blocks, listed, rank, block_rows = sizes
    half = steps * blocks // 2
    load_pages(steps * blocks * listed, local, index, table_ref, got_ref, pages, sems)
    for step in range(steps):
        for block in range(blocks):
            at = step * blocks + block
            listing = pages[at * listed : (at + 1) * listed].reshape(listed * rank, -1)
            every = lax.dot_general(
                listing, x_ref[at * block_rows : (at + 1) * block_rows, :],
                (((1,), (1,)), ((), ())), preferred_element_type=jnp.float32,
            )
            place = place_ref[step : step + 1, block * block_rows : (block + 1) * block_rows]
            low = jnp.zeros((rank, block_rows), jnp.float32)
            for entry in range(listed):
                low = jnp.where(place == entry, every[entry * rank : (entry + 1) * rank], low)
            rows = slice(at % half * block_rows, (at % half + 1) * block_rows)
            mine = side[0] == at // half

            @pl.when(mine)
            def _():
                keep_ref[:, rows] = low

            @pl.when(jnp.logical_not(mine))
            def _():
                give_ref[:, rows] = low


def low_rank(sizes, local, index, side, x, place, table, got, after):
    steps, blocks, listed, rank, block_rows = sizes
    count = steps * blocks * listed
    rows, depth = x.shape
    return pl.pallas_call(
        functools.partial(low_kernel, sizes),
        grid_spec=pltpu.PrefetchScalarGridSpec(
            num_scalar_prefetch=3,
            grid=(1,),
            in_specs=[WHOLE, WHOLE, ANYWHERE, ANYWHERE, ANYWHERE],
            out_specs=[WHOLE, WHOLE],
            scratch_shapes=[
                pltpu.VMEM((count, rank, depth), table.dtype),
                pltpu.SemaphoreType.DMA((count,)),
            ],
        ),
        out_shape=[jax.ShapeDtypeStruct((rank, rows // 2), jnp.float32)] * 2,
        compiler_params=params(),
        cost_estimate=cost(
            2 * rows * depth * listed * rank, 2 * (rows * depth + count * rank * depth)
        ),
    )(local, index, side, x, place, table, got, after)


def add_kernel(low_ref, sent_ref, after_ref, out_ref):
    out_ref[...] = (low_ref[...] + sent_ref[...]).astype(out_ref.dtype)


def add(low, sent, dtype, after):
    return pl.pallas_call(
        add_kernel,
        in_specs=[WHOLE, WHOLE, ANYWHERE],
        out_specs=WHOLE,
        out_shape=jax.ShapeDtypeStruct(low.shape, dtype),
        compiler_params=params(),
        cost_estimate=cost(low.size, 12 * low.size),
    )(low, sent, after)


def own_kernel(
    local, index, dests, x_ref, w_ref, table_ref, got_ref, after_ref, out_ref, pages, sems
):
    tile = w_ref.shape[1]
    now = pl.program_id(0)
    count = pages.shape[0]

    @pl.when(now == 0)
    def _():
        load_pages(count, local, index, table_ref, got_ref, pages, sems)

    columns = pl.ds(pl.multiple_of(now * tile, tile), tile)
    out_ref[:, columns] = jnp.dot(x_ref[...], w_ref[...], preferred_element_type=jnp.float32)


def own_terms(dests, local, index, x, weight, table, got, after):
    count, rank, cols = got.shape
    rows, depth = x.shape
    tile = min(256, cols)
    tiles = cols // tile
    return pl.pallas_call(
        own_kernel,
        grid_spec=pltpu.PrefetchScalarGridSpec(
            num_scalar_prefetch=3,
            grid=(tiles,),
            in_specs=[
                WHOLE,
                pl.BlockSpec((depth, tile), lambda j, l, i, d: (0, d[0] * tiles + j)),
                ANYWHERE,
                ANYWHERE,
                ANYWHERE,
            ],
            out_specs=[WHOLE, WHOLE],
            scratch_shapes=[pltpu.SemaphoreType.DMA((count,))],
        ),
        out_shape=[
            jax.ShapeDtypeStruct((rows, cols), jnp.float32),
            jax.ShapeDtypeStruct((count, rank, cols), table.dtype),
        ],
        compiler_params=params(),
        cost_estimate=cost(
            2 * rows * cols * depth,
            2 * (rows * depth + depth * cols + 2 * count * rank * cols) + 4 * rows * cols,
        ),
    )(local, index, dests, x, weight, table, got, after)


def delta_kernel(
    sizes, side, own_ref, pages_ref, place_ref, low_ref, other_ref, after_ref, out_ref
):
    steps, blocks, listed, rank, block_rows = sizes
    half = steps * blocks // 2
    entry_of = lax.broadcasted_iota(jnp.int32, (listed * rank, block_rows), 0) // rank
    for step in range(steps):
        for block in range(blocks):
            at = step * blocks + block
            rows = slice(at * block_rows, (at + 1) * block_rows)
            in_half = slice(at % half * block_rows, (at % half + 1) * block_rows)
            low = jnp.where(
                side[0] == at // half,
                low_ref[:, in_half].astype(jnp.float32),
                other_ref[:, in_half].astype(jnp.float32),
            )
            spread = jnp.concatenate([low] * listed, axis=0)
            place = place_ref[step : step + 1, block * block_rows : (block + 1) * block_rows]
            spread = jnp.where(entry_of == place, spread, 0.0)
            listing = pages_ref[at * listed : (at + 1) * listed].reshape(listed * rank, -1)
            out_ref[rows, :] = own_ref[rows, :] + jnp.dot(
                spread.T.astype(jnp.bfloat16), listing, preferred_element_type=jnp.float32
            )


def add_delta(sizes, side, own, pages, place, low, other, after):
    rows, cols = own.shape
    return pl.pallas_call(
        functools.partial(delta_kernel, sizes),
        grid_spec=pltpu.PrefetchScalarGridSpec(
            num_scalar_prefetch=1,
            grid=(1,),
            in_specs=[WHOLE] * 5 + [ANYWHERE],
            out_specs=WHOLE,
        ),
        out_shape=jax.ShapeDtypeStruct(own.shape, own.dtype),
        compiler_params=params(),
        cost_estimate=cost(
            2 * rows * cols * sizes[2] * sizes[3], 8 * rows * cols + 2 * pages.size
        ),
    )(side, own, pages, place, low, other, after)


def finish_kernel(half, live, own_ref, one_ref, two_ref, *refs):
    out_ref = refs[-1]
    count, cols = out_ref.shape
    step = pl.program_id(0)
    rows = pl.ds(pl.multiple_of(step * count, count), count)
    total = (
        own_ref[rows, half * cols : (half + 1) * cols]
        + one_ref[rows, :].astype(jnp.float32)
        + two_ref[rows, :].astype(jnp.float32)
    )
    row = lax.broadcasted_iota(jnp.int32, total.shape, 0)
    out_ref[...] = jnp.where(row < live[step], total, 0.0).astype(out_ref.dtype)


def finish(live, half, own, one, two, result):
    rows, cols = own.shape
    steps = live.shape[0]
    in_specs = [WHOLE, WHOLE, WHOLE]
    operands = [own, one, two]
    aliases = {}
    if result is not None:
        in_specs.append(ANYWHERE)
        operands.append(result)
        aliases = {4: 0}
    return pl.pallas_call(
        functools.partial(finish_kernel, half),
        grid_spec=pltpu.PrefetchScalarGridSpec(
            num_scalar_prefetch=1,
            grid=(steps,),
            in_specs=in_specs,
            out_specs=pl.BlockSpec((rows // steps, cols // 2), lambda s, l: (s, half)),
        ),
        out_shape=jax.ShapeDtypeStruct((rows, cols), jnp.bfloat16),
        input_output_aliases=aliases,
        compiler_params=params(),
        cost_estimate=cost(0, rows * cols * 5),
    )(live, *operands)


def per_device(
    size,
    attention_output,
    output_weight,
    adapter_down_weight,
    adapter_up_weight,
    adapter_page_table,
    block_adapter_ids,
    row_list_position,
    live_row_count,
):
    steps, row_count, depth = attention_output.shape
    resident, rank, _ = adapter_down_weight.shape
    _, blocks, listed = block_adapter_ids.shape
    sizes = (steps, blocks, listed, rank, row_count // blocks)
    x = attention_output.reshape(steps * row_count, depth)
    ring = ring_order(size)

    instance = lax.axis_index("inst")
    place = ring_place(lax.axis_index("tp"), size)
    dests = ring_index(lax.rem(place + jnp.arange(size, dtype=jnp.int32), size), size)

    forward = [(ring[i], ring[(i + 1) % size]) for i in range(size)]
    backward = [(ring[i], ring[i - 1]) for i in range(size)]
    far = size // 2
    pairs = [[(0, 1, forward), (1, -1, backward)], [(1, 1, forward), (0, -1, backward)]]
    arrived = {}
    last = None

    def turn(number, last):
        left = far - (number + 1) // 2
        for half, sign, moves in pairs[number % 2]:
            last = hop(
                dests, (sign * left) % size, half, x, output_weight,
                arrived.get((half, sign)), last,
            )
            arrived[half, sign] = lax.ppermute(last, "tp", moves)
        return last

    ids = block_adapter_ids.reshape(-1)
    ids_there = lax.ppermute(ids, "inst", SWAP)
    last = turn(0, last)
    pages = adapter_page_table[jnp.concatenate([ids, ids_there])]
    places = pages % resident
    index, index_there = places[: ids.shape[0]], places[ids.shape[0] :]
    local = (pages[: ids.shape[0]] // resident == instance).astype(jnp.int32)
    last = collect(index_there, adapter_down_weight, last)
    got_down = lax.ppermute(last, "inst", SWAP)
    last = turn(1, last)
    last = collect(index_there, adapter_up_weight, last)
    got_up = lax.ppermute(last, "inst", SWAP)
    side = (lax.axis_index("tp") & 1).reshape(1)
    low, give = low_rank(
        sizes, local, index, side, x, row_list_position, adapter_down_weight, got_down, last
    )
    last = low

    def over(value, apart):
        return lax.ppermute(value, "tp", [(i, i ^ apart) for i in range(size)])

    number, turns = 2, 2 * far - 1
    apart = 1
    while apart < size:
        sent = over(give if apart == 1 else low, apart)
        last = turn(number, last)
        number += 1
        if apart == 1:
            own, up_pages = own_terms(
                dests, local, index, x, output_weight, adapter_up_weight, got_up, last
            )
            last = own
        apart *= 2
        while apart == size and number < turns - 1:
            last = turn(number, last)
            number += 1
        low = last = add(low, sent, jnp.float32 if apart < size else jnp.bfloat16, last)
    other = over(low, 1)
    last = turn(number, last)
    own = add_delta(sizes, side, own, up_pages, row_list_position, low, other, last)
    result = None
    for half in range(2):
        result = finish(
            live_row_count.reshape(-1), half, own, arrived[half, 1], arrived[half, -1], result
        )
    return result.reshape(steps, row_count, -1)


def solution(mesh):
    in_specs = (
        P(None, ("grp", "inst"), "tp"),
        P("tp", None),
        P("inst", None, "tp"),
        P("inst", None, "tp"),
        P(),
        P(None, ("grp", "inst"), None),
        P(None, ("grp", "inst")),
        P(None, ("grp", "inst")),
    )
    out_specs = P(None, ("grp", "inst"), "tp")
    return jax.shard_map(
        functools.partial(per_device, mesh.shape["tp"]),
        mesh=mesh, in_specs=in_specs, out_specs=out_specs, check_vma=False,
    )
```

```python
import functools

import jax
import jax.numpy as jnp
from jax import lax
from jax.experimental import pallas as pl
from jax.experimental.pallas import tpu as pltpu
from jax.sharding import PartitionSpec as P

VMEM_LIMIT = 40 * 1024 * 1024
FIRST_VMEM_LIMIT = 60 * 1024 * 1024
SWAP = [(0, 1), (1, 0)]
WHOLE = pl.BlockSpec(memory_space=pltpu.VMEM)
ANYWHERE = pl.BlockSpec(memory_space=pl.ANY)


def serpentine(size):
    return size == 8


def ring_index(place, size):
    if not serpentine(size):
        return place
    return jnp.where(place < size // 2, 2 * place, 2 * (size - 1 - place) + 1)


def ring_place(index, size):
    if not serpentine(size):
        return index
    return jnp.where(index & 1 == 0, index >> 1, size - 1 - (index >> 1))


def ring_order(size):
    if not serpentine(size):
        return list(range(size))
    return list(range(0, size, 2)) + list(range(size - 1, 0, -2))


def params():
    return pltpu.CompilerParams(vmem_limit_bytes=VMEM_LIMIT)


def cost(flops, size):
    return pl.CostEstimate(flops=30 * flops, bytes_accessed=size, transcendentals=0)


def hop_kernel(with_received, dests, x_ref, w_ref, *refs):
    tile = w_ref.shape[1]
    columns = pl.ds(pl.multiple_of(pl.program_id(0) * tile, tile), tile)
    total = jnp.dot(x_ref[...], w_ref[...], preferred_element_type=jnp.float32)
    if with_received:
        total = total + refs[0][:, columns].astype(jnp.float32)
    refs[-1][:, columns] = total.astype(refs[-1].dtype)


def hop(dests, offset, half, x, weight, received, after):
    rows, depth = x.shape
    half_cols = weight.shape[1] // dests.shape[0] // 2
    tile = min(256, half_cols)
    tiles = half_cols // tile
    in_specs = [
        WHOLE,
        pl.BlockSpec(
            (depth, tile), lambda j, d: (0, (d[offset] * 2 + half) * tiles + j)
        ),
    ]
    operands = [x, weight]
    if received is not None:
        in_specs.append(WHOLE)
        operands.append(received)
    if after is not None:
        in_specs.append(ANYWHERE)
        operands.append(after)
    return pl.pallas_call(
        functools.partial(hop_kernel, received is not None),
        grid_spec=pltpu.PrefetchScalarGridSpec(
            num_scalar_prefetch=1,
            grid=(tiles,),
            in_specs=in_specs,
            out_specs=WHOLE,
        ),
        out_shape=jax.ShapeDtypeStruct((rows, half_cols), jnp.bfloat16),
        compiler_params=params(),
        cost_estimate=cost(
            2 * rows * depth * half_cols,
            2 * (rows * depth + depth * half_cols + 2 * rows * half_cols),
        ),
    )(dests, *operands)


def first_hop_kernel(dests, x_ref, w_ref, out_ref, token_ref):
    token_ref[...] = jnp.zeros_like(token_ref)
    out_ref[...] = jnp.dot(
        x_ref[...], w_ref[...], preferred_element_type=jnp.float32
    ).astype(out_ref.dtype)


def first_hop(dests, offset, half, x, weight):
    rows, depth = x.shape
    half_cols = weight.shape[1] // dests.shape[0] // 2
    tile = min(256, half_cols)
    tiles = half_cols // tile
    row_tile = rows // 4
    return pl.pallas_call(
        first_hop_kernel,
        grid_spec=pltpu.PrefetchScalarGridSpec(
            num_scalar_prefetch=1,
            grid=(tiles, rows // row_tile),
            in_specs=[
                pl.BlockSpec((row_tile, depth), lambda j, i, d: (i, 0)),
                pl.BlockSpec(
                    (depth, tile), lambda j, i, d: (0, (d[offset] * 2 + half) * tiles + j)
                ),
            ],
            out_specs=[
                pl.BlockSpec((row_tile, tile), lambda j, i, d: (i, j)),
                pl.BlockSpec((8, 128), lambda j, i, d: (0, 0)),
            ],
        ),
        out_shape=[
            jax.ShapeDtypeStruct((rows, half_cols), jnp.bfloat16),
            jax.ShapeDtypeStruct((8, 128), jnp.float32),
        ],
        compiler_params=pltpu.CompilerParams(vmem_limit_bytes=FIRST_VMEM_LIMIT),
        cost_estimate=cost(
            2 * rows * depth * half_cols, 2 * (rows * depth + depth * half_cols)
        ),
    )(dests, x, weight)


def collect_kernel(count, index, table_ref, after_ref, out_ref, sems):
    copies = [
        pltpu.make_async_copy(table_ref.at[index[slot]], out_ref.at[slot], sems.at[slot])
        for slot in range(count)
    ]
    for copy in copies:
        copy.start()
    for copy in copies:
        copy.wait()


def collect(index, table, after):
    count = index.shape[0]
    shape = (count,) + table.shape[1:]
    return pl.pallas_call(
        functools.partial(collect_kernel, count),
        grid_spec=pltpu.PrefetchScalarGridSpec(
            num_scalar_prefetch=1,
            grid=(1,),
            in_specs=[ANYWHERE, ANYWHERE],
            out_specs=WHOLE,
            scratch_shapes=[pltpu.SemaphoreType.DMA((count,))],
        ),
        out_shape=jax.ShapeDtypeStruct(shape, table.dtype),
        compiler_params=params(),
        cost_estimate=cost(0, 4 * shape[0] * shape[1] * shape[2]),
    )(index, table, after)


def start_pages(count, local, index, table_ref, got_ref, pages, sems):
    for slot in range(count):
        own = local[slot] == 1

        @pl.when(own)
        def _():
            pltpu.make_async_copy(
                table_ref.at[index[slot]], pages.at[slot], sems.at[slot]
            ).start()

        @pl.when(jnp.logical_not(own))
        def _():
            pltpu.make_async_copy(got_ref.at[slot], pages.at[slot], sems.at[slot]).start()


def wait_pages(slots, got_ref, pages, sems):
    for slot in slots:
        pltpu.make_async_copy(got_ref.at[slot], pages.at[slot], sems.at[slot]).wait()


def low_kernel(
    sizes, local, index, side, x_ref, place_ref, table_ref, got_ref, after_ref, keep_ref, give_ref,
    pages, sems,
):
    steps, blocks, listed, rank, block_rows = sizes
    half = steps * blocks // 2
    start_pages(steps * blocks * listed, local, index, table_ref, got_ref, pages, sems)
    for step in range(steps):
        for block in range(blocks):
            at = step * blocks + block
            wait_pages(range(at * listed, (at + 1) * listed), got_ref, pages, sems)
            listing = pages[at * listed : (at + 1) * listed].reshape(listed * rank, -1)
            every = lax.dot_general(
                listing, x_ref[at * block_rows : (at + 1) * block_rows, :],
                (((1,), (1,)), ((), ())), preferred_element_type=jnp.float32,
            )
            place = place_ref[step : step + 1, block * block_rows : (block + 1) * block_rows]
            low = jnp.zeros((rank, block_rows), jnp.float32)
            for entry in range(listed):
                low = jnp.where(place == entry, every[entry * rank : (entry + 1) * rank], low)
            rows = slice(at % half * block_rows, (at % half + 1) * block_rows)
            mine = side[0] == at // half

            @pl.when(mine)
            def _():
                keep_ref[:, rows] = low

            @pl.when(jnp.logical_not(mine))
            def _():
                give_ref[:, rows] = low


def low_rank(sizes, local, index, side, x, place, table, got, after):
    steps, blocks, listed, rank, block_rows = sizes
    count = steps * blocks * listed
    rows, depth = x.shape
    return pl.pallas_call(
        functools.partial(low_kernel, sizes),
        grid_spec=pltpu.PrefetchScalarGridSpec(
            num_scalar_prefetch=3,
            grid=(1,),
            in_specs=[WHOLE, WHOLE, ANYWHERE, ANYWHERE, ANYWHERE],
            out_specs=[WHOLE, WHOLE],
            scratch_shapes=[
                pltpu.VMEM((count, rank, depth), table.dtype),
                pltpu.SemaphoreType.DMA((count,)),
            ],
        ),
        out_shape=[jax.ShapeDtypeStruct((rank, rows // 2), jnp.float32)] * 2,
        compiler_params=params(),
        cost_estimate=cost(
            2 * rows * depth * listed * rank, 2 * (rows * depth + count * rank * depth)
        ),
    )(local, index, side, x, place, table, got, after)


def add_kernel(low_ref, sent_ref, after_ref, out_ref):
    out_ref[...] = (low_ref[...] + sent_ref[...]).astype(out_ref.dtype)


def add(low, sent, dtype, after):
    return pl.pallas_call(
        add_kernel,
        in_specs=[WHOLE, WHOLE, ANYWHERE],
        out_specs=WHOLE,
        out_shape=jax.ShapeDtypeStruct(low.shape, dtype),
        compiler_params=params(),
        cost_estimate=cost(low.size, 12 * low.size),
    )(low, sent, after)


def own_kernel(
    local, index, dests, x_ref, w_ref, table_ref, got_ref, after_ref, out_ref, pages, sems
):
    tile = w_ref.shape[1]
    now = pl.program_id(0)
    count = pages.shape[0]

    @pl.when(now == 0)
    def _():
        start_pages(count, local, index, table_ref, got_ref, pages, sems)

    columns = pl.ds(pl.multiple_of(now * tile, tile), tile)
    out_ref[:, columns] = jnp.dot(x_ref[...], w_ref[...], preferred_element_type=jnp.float32)

    @pl.when(now == pl.num_programs(0) - 1)
    def _():
        wait_pages(range(count), got_ref, pages, sems)


def own_terms(dests, local, index, x, weight, table, got, after):
    count, rank, cols = got.shape
    rows, depth = x.shape
    tile = min(256, cols)
    tiles = cols // tile
    return pl.pallas_call(
        own_kernel,
        grid_spec=pltpu.PrefetchScalarGridSpec(
            num_scalar_prefetch=3,
            grid=(tiles,),
            in_specs=[
                WHOLE,
                pl.BlockSpec((depth, tile), lambda j, l, i, d: (0, d[0] * tiles + j)),
                ANYWHERE,
                ANYWHERE,
                ANYWHERE,
            ],
            out_specs=[WHOLE, WHOLE],
            scratch_shapes=[pltpu.SemaphoreType.DMA((count,))],
        ),
        out_shape=[
            jax.ShapeDtypeStruct((rows, cols), jnp.float32),
            jax.ShapeDtypeStruct((count, rank, cols), table.dtype),
        ],
        compiler_params=params(),
        cost_estimate=cost(
            2 * rows * cols * depth,
            2 * (rows * depth + depth * cols + 2 * count * rank * cols) + 4 * rows * cols,
        ),
    )(local, index, dests, x, weight, table, got, after)


def delta_kernel(
    sizes, side, own_ref, pages_ref, place_ref, low_ref, other_ref, after_ref, out_ref
):
    steps, blocks, listed, rank, block_rows = sizes
    half = steps * blocks // 2
    entry_of = lax.broadcasted_iota(jnp.int32, (listed * rank, block_rows), 0) // rank
    for step in range(steps):
        for block in range(blocks):
            at = step * blocks + block
            rows = slice(at * block_rows, (at + 1) * block_rows)
            in_half = slice(at % half * block_rows, (at % half + 1) * block_rows)
            low = jnp.where(
                side[0] == at // half,
                low_ref[:, in_half].astype(jnp.float32),
                other_ref[:, in_half].astype(jnp.float32),
            )
            spread = jnp.concatenate([low] * listed, axis=0)
            place = place_ref[step : step + 1, block * block_rows : (block + 1) * block_rows]
            spread = jnp.where(entry_of == place, spread, 0.0)
            listing = pages_ref[at * listed : (at + 1) * listed].reshape(listed * rank, -1)
            out_ref[rows, :] = own_ref[rows, :] + jnp.dot(
                spread.T.astype(jnp.bfloat16), listing, preferred_element_type=jnp.float32
            )


def add_delta(sizes, side, own, pages, place, low, other, after):
    rows, cols = own.shape
    return pl.pallas_call(
        functools.partial(delta_kernel, sizes),
        grid_spec=pltpu.PrefetchScalarGridSpec(
            num_scalar_prefetch=1,
            grid=(1,),
            in_specs=[WHOLE] * 5 + [ANYWHERE],
            out_specs=WHOLE,
        ),
        out_shape=jax.ShapeDtypeStruct(own.shape, own.dtype),
        compiler_params=params(),
        cost_estimate=cost(
            2 * rows * cols * sizes[2] * sizes[3], 8 * rows * cols + 2 * pages.size
        ),
    )(side, own, pages, place, low, other, after)


def finish_kernel(half, live, own_ref, one_ref, two_ref, *refs):
    out_ref = refs[-1]
    count, cols = out_ref.shape
    step = pl.program_id(0)
    rows = pl.ds(pl.multiple_of(step * count, count), count)
    total = (
        own_ref[rows, half * cols : (half + 1) * cols]
        + one_ref[rows, :].astype(jnp.float32)
        + two_ref[rows, :].astype(jnp.float32)
    )
    row = lax.broadcasted_iota(jnp.int32, total.shape, 0)
    out_ref[...] = jnp.where(row < live[step], total, 0.0).astype(out_ref.dtype)


def finish(live, half, own, one, two, result):
    rows, cols = own.shape
    steps = live.shape[0]
    in_specs = [WHOLE, WHOLE, WHOLE]
    operands = [own, one, two]
    aliases = {}
    if result is not None:
        in_specs.append(ANYWHERE)
        operands.append(result)
        aliases = {4: 0}
    return pl.pallas_call(
        functools.partial(finish_kernel, half),
        grid_spec=pltpu.PrefetchScalarGridSpec(
            num_scalar_prefetch=1,
            grid=(steps,),
            in_specs=in_specs,
            out_specs=pl.BlockSpec((rows // steps, cols // 2), lambda s, l: (s, half)),
        ),
        out_shape=jax.ShapeDtypeStruct((rows, cols), jnp.bfloat16),
        input_output_aliases=aliases,
        compiler_params=params(),
        cost_estimate=cost(0, rows * cols * 5),
    )(live, *operands)


def per_device(
    size,
    attention_output,
    output_weight,
    adapter_down_weight,
    adapter_up_weight,
    adapter_page_table,
    block_adapter_ids,
    row_list_position,
    live_row_count,
):
    steps, row_count, depth = attention_output.shape
    resident, rank, _ = adapter_down_weight.shape
    _, blocks, listed = block_adapter_ids.shape
    sizes = (steps, blocks, listed, rank, row_count // blocks)
    x = attention_output.reshape(steps * row_count, depth)
    ring = ring_order(size)

    instance = lax.axis_index("inst")
    place = ring_place(lax.axis_index("tp"), size)
    dests = ring_index(lax.rem(place + jnp.arange(size, dtype=jnp.int32), size), size)

    forward = [(ring[i], ring[(i + 1) % size]) for i in range(size)]
    backward = [(ring[i], ring[i - 1]) for i in range(size)]
    far = size // 2
    pairs = [[(0, 1, forward), (1, -1, backward)], [(1, 1, forward), (0, -1, backward)]]
    arrived = {}
    half, sign, moves = pairs[0][0]
    first, token = first_hop(dests, (sign * far) % size, half, x, output_weight)
    arrived[half, sign] = lax.ppermute(first, "tp", moves)

    def turn(number, last):
        left = far - (number + 1) // 2
        for half, sign, moves in pairs[number % 2]:
            last = hop(
                dests, (sign * left) % size, half, x, output_weight,
                arrived.get((half, sign)), last,
            )
            arrived[half, sign] = lax.ppermute(last, "tp", moves)
        return last

    ids = block_adapter_ids.reshape(-1)
    ids_there = lax.ppermute(block_adapter_ids, "inst", SWAP).reshape(-1)
    half, sign, moves = pairs[0][1]
    last = hop(dests, (sign * far) % size, half, x, output_weight, None, token)
    arrived[half, sign] = lax.ppermute(last, "tp", moves)
    pages = adapter_page_table[jnp.concatenate([ids, ids_there])]
    places = pages % resident
    index, index_there = places[: ids.shape[0]], places[ids.shape[0] :]
    local = (pages[: ids.shape[0]] // resident == instance).astype(jnp.int32)
    last = collect(index_there, adapter_down_weight, last)
    got_down = lax.ppermute(last, "inst", SWAP)
    last = turn(1, last)
    last = collect(index_there, adapter_up_weight, last)
    got_up = lax.ppermute(last, "inst", SWAP)
    side = (lax.axis_index("tp") & 1).reshape(1)
    low, give = low_rank(
        sizes, local, index, side, x, row_list_position, adapter_down_weight, got_down, last
    )
    last = low

    def over(value, apart):
        return lax.ppermute(value, "tp", [(i, i ^ apart) for i in range(size)])

    number, turns = 2, 2 * far - 1
    apart = 1
    while apart < size:
        sent = over(give if apart == 1 else low, apart)
        last = turn(number, last)
        number += 1
        if apart == 1:
            own, up_pages = own_terms(
                dests, local, index, x, output_weight, adapter_up_weight, got_up, last
            )
            last = own
        apart *= 2
        while apart == size and number < turns - 1:
            last = turn(number, last)
            number += 1
        low = last = add(low, sent, jnp.float32 if apart < size else jnp.bfloat16, last)
    other = over(low, 1)
    last = turn(number, last)
    own = add_delta(sizes, side, own, up_pages, row_list_position, low, other, last)
    result = None
    for half in range(2):
        result = finish(
            live_row_count.reshape(-1), half, own, arrived[half, 1], arrived[half, -1], result
        )
    return result.reshape(steps, row_count, -1)


def solution(mesh):
    in_specs = (
        P(None, ("grp", "inst"), "tp"),
        P("tp", None),
        P("inst", None, "tp"),
        P("inst", None, "tp"),
        P(),
        P(None, ("grp", "inst"), None),
        P(None, ("grp", "inst")),
        P(None, ("grp", "inst")),
    )
    out_specs = P(None, ("grp", "inst"), "tp")
    return jax.shard_map(
        functools.partial(per_device, mesh.shape["tp"]),
        mesh=mesh, in_specs=in_specs, out_specs=out_specs, check_vma=False,
    )
```

```python
import functools

import jax
import jax.numpy as jnp
from jax import lax
from jax.experimental import pallas as pl
from jax.experimental.pallas import tpu as pltpu
from jax.sharding import PartitionSpec as P

VMEM_LIMIT = 40 * 1024 * 1024
FIRST_VMEM_LIMIT = 60 * 1024 * 1024
SWAP = [(0, 1), (1, 0)]
WHOLE = pl.BlockSpec(memory_space=pltpu.VMEM)
ANYWHERE = pl.BlockSpec(memory_space=pl.ANY)


def serpentine(size):
    return size == 8


def ring_index(place, size):
    if not serpentine(size):
        return place
    return jnp.where(place < size // 2, 2 * place, 2 * (size - 1 - place) + 1)


def ring_place(index, size):
    if not serpentine(size):
        return index
    return jnp.where(index & 1 == 0, index >> 1, size - 1 - (index >> 1))


def ring_order(size):
    if not serpentine(size):
        return list(range(size))
    return list(range(0, size, 2)) + list(range(size - 1, 0, -2))


def params():
    return pltpu.CompilerParams(vmem_limit_bytes=VMEM_LIMIT)


def cost(flops, size):
    return pl.CostEstimate(flops=30 * flops, bytes_accessed=size, transcendentals=0)


def hop_kernel(with_received, dests, x_ref, w_ref, *refs):
    tile = w_ref.shape[1]
    columns = pl.ds(pl.multiple_of(pl.program_id(0) * tile, tile), tile)
    total = jnp.dot(x_ref[...], w_ref[...], preferred_element_type=jnp.float32)
    if with_received:
        total = total + refs[0][:, columns].astype(jnp.float32)
    refs[-1][:, columns] = total.astype(refs[-1].dtype)


def hop(dests, offset, half, x, weight, received, after):
    rows, depth = x.shape
    half_cols = weight.shape[1] // dests.shape[0] // 2
    tile = min(256, half_cols)
    tiles = half_cols // tile
    in_specs = [
        WHOLE,
        pl.BlockSpec(
            (depth, tile), lambda j, d: (0, (d[offset] * 2 + half) * tiles + j)
        ),
    ]
    operands = [x, weight]
    if received is not None:
        in_specs.append(WHOLE)
        operands.append(received)
    if after is not None:
        in_specs.append(ANYWHERE)
        operands.append(after)
    return pl.pallas_call(
        functools.partial(hop_kernel, received is not None),
        grid_spec=pltpu.PrefetchScalarGridSpec(
            num_scalar_prefetch=1,
            grid=(tiles,),
            in_specs=in_specs,
            out_specs=WHOLE,
        ),
        out_shape=jax.ShapeDtypeStruct((rows, half_cols), jnp.bfloat16),
        compiler_params=params(),
        cost_estimate=cost(
            2 * rows * depth * half_cols,
            2 * (rows * depth + depth * half_cols + 2 * rows * half_cols),
        ),
    )(dests, *operands)


def first_hop_kernel(dests, x_ref, w_ref, out_ref, token_ref, total_ref):
    now = pl.program_id(0)
    product = jnp.dot(x_ref[...], w_ref[...], preferred_element_type=jnp.float32)

    @pl.when(now == 0)
    def _():
        total_ref[...] = product

    @pl.when((now > 0) & (now < pl.num_programs(0) - 1))
    def _():
        total_ref[...] += product

    @pl.when(now == pl.num_programs(0) - 1)
    def _():
        out_ref[...] = (total_ref[...] + product).astype(out_ref.dtype)
        token_ref[...] = jnp.zeros_like(token_ref)


def first_hop(dests, offset, half, x, weight):
    rows, depth = x.shape
    half_cols = weight.shape[1] // dests.shape[0] // 2
    piece = max(256, depth // 4)
    return pl.pallas_call(
        first_hop_kernel,
        grid_spec=pltpu.PrefetchScalarGridSpec(
            num_scalar_prefetch=1,
            grid=(depth // piece,),
            in_specs=[
                pl.BlockSpec((rows, piece), lambda k, d: (0, k)),
                pl.BlockSpec((piece, half_cols), lambda k, d: (k, d[offset] * 2 + half)),
            ],
            out_specs=[
                pl.BlockSpec((rows, half_cols), lambda k, d: (0, 0)),
                pl.BlockSpec((8, 128), lambda k, d: (0, 0)),
            ],
            scratch_shapes=[pltpu.VMEM((rows, half_cols), jnp.float32)],
        ),
        out_shape=[
            jax.ShapeDtypeStruct((rows, half_cols), jnp.bfloat16),
            jax.ShapeDtypeStruct((8, 128), jnp.float32),
        ],
        compiler_params=pltpu.CompilerParams(vmem_limit_bytes=FIRST_VMEM_LIMIT),
        cost_estimate=cost(
            2 * rows * depth * half_cols, 2 * (rows * depth + depth * half_cols)
        ),
    )(dests, x, weight)


def touch_kernel(arrived_ref, after_ref, out_ref):
    out_ref[...] = jnp.zeros_like(out_ref)


def touch(arrived, after):
    return pl.pallas_call(
        touch_kernel,
        in_specs=[ANYWHERE, ANYWHERE],
        out_specs=WHOLE,
        out_shape=jax.ShapeDtypeStruct((8, 128), jnp.float32),
        compiler_params=params(),
    )(arrived, after)


def collect_kernel(count, index, table_ref, after_ref, out_ref, sems):
    copies = [
        pltpu.make_async_copy(table_ref.at[index[slot]], out_ref.at[slot], sems.at[slot])
        for slot in range(count)
    ]
    for copy in copies:
        copy.start()
    for copy in copies:
        copy.wait()


def collect(index, table, after):
    count = index.shape[0]
    shape = (count,) + table.shape[1:]
    return pl.pallas_call(
        functools.partial(collect_kernel, count),
        grid_spec=pltpu.PrefetchScalarGridSpec(
            num_scalar_prefetch=1,
            grid=(1,),
            in_specs=[ANYWHERE, ANYWHERE],
            out_specs=WHOLE,
            scratch_shapes=[pltpu.SemaphoreType.DMA((count,))],
        ),
        out_shape=jax.ShapeDtypeStruct(shape, table.dtype),
        compiler_params=params(),
        cost_estimate=cost(0, 4 * shape[0] * shape[1] * shape[2]),
    )(index, table, after)


def start_pages(count, local, index, table_ref, got_ref, pages, sems):
    for slot in range(count):
        own = local[slot] == 1

        @pl.when(own)
        def _():
            pltpu.make_async_copy(
                table_ref.at[index[slot]], pages.at[slot], sems.at[slot]
            ).start()

        @pl.when(jnp.logical_not(own))
        def _():
            pltpu.make_async_copy(got_ref.at[slot], pages.at[slot], sems.at[slot]).start()


def wait_pages(slots, got_ref, pages, sems):
    for slot in slots:
        pltpu.make_async_copy(got_ref.at[slot], pages.at[slot], sems.at[slot]).wait()


def low_kernel(
    sizes, local, index, side, x_ref, place_ref, table_ref, got_ref, after_ref, keep_ref, give_ref,
    pages, sems,
):
    steps, blocks, listed, rank, block_rows = sizes
    half = steps * blocks // 2
    start_pages(steps * blocks * listed, local, index, table_ref, got_ref, pages, sems)
    for step in range(steps):
        for block in range(blocks):
            at = step * blocks + block
            wait_pages(range(at * listed, (at + 1) * listed), got_ref, pages, sems)
            listing = pages[at * listed : (at + 1) * listed].reshape(listed * rank, -1)
            every = lax.dot_general(
                listing, x_ref[at * block_rows : (at + 1) * block_rows, :],
                (((1,), (1,)), ((), ())), preferred_element_type=jnp.float32,
            )
            place = place_ref[step : step + 1, block * block_rows : (block + 1) * block_rows]
            low = jnp.zeros((rank, block_rows), jnp.float32)
            for entry in range(listed):
                low = jnp.where(place == entry, every[entry * rank : (entry + 1) * rank], low)
            rows = slice(at % half * block_rows, (at % half + 1) * block_rows)
            mine = side[0] == at // half

            @pl.when(mine)
            def _():
                keep_ref[:, rows] = low

            @pl.when(jnp.logical_not(mine))
            def _():
                give_ref[:, rows] = low


def low_rank(sizes, local, index, side, x, place, table, got, after):
    steps, blocks, listed, rank, block_rows = sizes
    count = steps * blocks * listed
    rows, depth = x.shape
    return pl.pallas_call(
        functools.partial(low_kernel, sizes),
        grid_spec=pltpu.PrefetchScalarGridSpec(
            num_scalar_prefetch=3,
            grid=(1,),
            in_specs=[WHOLE, WHOLE, ANYWHERE, ANYWHERE, ANYWHERE],
            out_specs=[WHOLE, WHOLE],
            scratch_shapes=[
                pltpu.VMEM((count, rank, depth), table.dtype),
                pltpu.SemaphoreType.DMA((count,)),
            ],
        ),
        out_shape=[jax.ShapeDtypeStruct((rank, rows // 2), jnp.float32)] * 2,
        compiler_params=params(),
        cost_estimate=cost(
            2 * rows * depth * listed * rank, 2 * (rows * depth + count * rank * depth)
        ),
    )(local, index, side, x, place, table, got, after)


def add_kernel(low_ref, sent_ref, after_ref, out_ref):
    out_ref[...] = (low_ref[...] + sent_ref[...]).astype(out_ref.dtype)


def add(low, sent, dtype, after):
    return pl.pallas_call(
        add_kernel,
        in_specs=[WHOLE, WHOLE, ANYWHERE],
        out_specs=WHOLE,
        out_shape=jax.ShapeDtypeStruct(low.shape, dtype),
        compiler_params=params(),
        cost_estimate=cost(low.size, 12 * low.size),
    )(low, sent, after)


def own_kernel(
    local, index, dests, x_ref, w_ref, table_ref, got_ref, after_ref, out_ref, pages, sems
):
    tile = w_ref.shape[1]
    now = pl.program_id(0)
    count = pages.shape[0]

    @pl.when(now == 0)
    def _():
        start_pages(count, local, index, table_ref, got_ref, pages, sems)

    columns = pl.ds(pl.multiple_of(now * tile, tile), tile)
    out_ref[:, columns] = jnp.dot(x_ref[...], w_ref[...], preferred_element_type=jnp.float32)

    @pl.when(now == pl.num_programs(0) - 1)
    def _():
        wait_pages(range(count), got_ref, pages, sems)


def own_terms(dests, local, index, x, weight, table, got, after):
    count, rank, cols = got.shape
    rows, depth = x.shape
    tile = min(256, cols)
    tiles = cols // tile
    return pl.pallas_call(
        own_kernel,
        grid_spec=pltpu.PrefetchScalarGridSpec(
            num_scalar_prefetch=3,
            grid=(tiles,),
            in_specs=[
                WHOLE,
                pl.BlockSpec((depth, tile), lambda j, l, i, d: (0, d[0] * tiles + j)),
                ANYWHERE,
                ANYWHERE,
                ANYWHERE,
            ],
            out_specs=[WHOLE, WHOLE],
            scratch_shapes=[pltpu.SemaphoreType.DMA((count,))],
        ),
        out_shape=[
            jax.ShapeDtypeStruct((rows, cols), jnp.float32),
            jax.ShapeDtypeStruct((count, rank, cols), table.dtype),
        ],
        compiler_params=params(),
        cost_estimate=cost(
            2 * rows * cols * depth,
            2 * (rows * depth + depth * cols + 2 * count * rank * cols) + 4 * rows * cols,
        ),
    )(local, index, dests, x, weight, table, got, after)


def delta_kernel(
    sizes, side, own_ref, pages_ref, place_ref, low_ref, other_ref, after_ref, out_ref
):
    steps, blocks, listed, rank, block_rows = sizes
    half = steps * blocks // 2
    entry_of = lax.broadcasted_iota(jnp.int32, (listed * rank, block_rows), 0) // rank
    for step in range(steps):
        for block in range(blocks):
            at = step * blocks + block
            rows = slice(at * block_rows, (at + 1) * block_rows)
            in_half = slice(at % half * block_rows, (at % half + 1) * block_rows)
            low = jnp.where(
                side[0] == at // half,
                low_ref[:, in_half].astype(jnp.float32),
                other_ref[:, in_half].astype(jnp.float32),
            )
            spread = jnp.concatenate([low] * listed, axis=0)
            place = place_ref[step : step + 1, block * block_rows : (block + 1) * block_rows]
            spread = jnp.where(entry_of == place, spread, 0.0)
            listing = pages_ref[at * listed : (at + 1) * listed].reshape(listed * rank, -1)
            out_ref[rows, :] = own_ref[rows, :] + jnp.dot(
                spread.T.astype(jnp.bfloat16), listing, preferred_element_type=jnp.float32
            )


def add_delta(sizes, side, own, pages, place, low, other, after):
    rows, cols = own.shape
    return pl.pallas_call(
        functools.partial(delta_kernel, sizes),
        grid_spec=pltpu.PrefetchScalarGridSpec(
            num_scalar_prefetch=1,
            grid=(1,),
            in_specs=[WHOLE] * 5 + [ANYWHERE],
            out_specs=WHOLE,
        ),
        out_shape=jax.ShapeDtypeStruct(own.shape, own.dtype),
        compiler_params=params(),
        cost_estimate=cost(
            2 * rows * cols * sizes[2] * sizes[3], 8 * rows * cols + 2 * pages.size
        ),
    )(side, own, pages, place, low, other, after)


def finish_kernel(half, live, own_ref, one_ref, two_ref, *refs):
    out_ref = refs[-1]
    count, cols = out_ref.shape
    step = pl.program_id(0)
    rows = pl.ds(pl.multiple_of(step * count, count), count)
    total = (
        own_ref[rows, half * cols : (half + 1) * cols]
        + one_ref[rows, :].astype(jnp.float32)
        + two_ref[rows, :].astype(jnp.float32)
    )
    row = lax.broadcasted_iota(jnp.int32, total.shape, 0)
    out_ref[...] = jnp.where(row < live[step], total, 0.0).astype(out_ref.dtype)


def finish(live, half, own, one, two, result):
    rows, cols = own.shape
    steps = live.shape[0]
    in_specs = [WHOLE, WHOLE, WHOLE]
    operands = [own, one, two]
    aliases = {}
    if result is not None:
        in_specs.append(ANYWHERE)
        operands.append(result)
        aliases = {4: 0}
    return pl.pallas_call(
        functools.partial(finish_kernel, half),
        grid_spec=pltpu.PrefetchScalarGridSpec(
            num_scalar_prefetch=1,
            grid=(steps,),
            in_specs=in_specs,
            out_specs=pl.BlockSpec((rows // steps, cols // 2), lambda s, l: (s, half)),
        ),
        out_shape=jax.ShapeDtypeStruct((rows, cols), jnp.bfloat16),
        input_output_aliases=aliases,
        compiler_params=params(),
        cost_estimate=cost(0, rows * cols * 5),
    )(live, *operands)


def per_device(
    size,
    attention_output,
    output_weight,
    adapter_down_weight,
    adapter_up_weight,
    adapter_page_table,
    block_adapter_ids,
    row_list_position,
    live_row_count,
):
    steps, row_count, depth = attention_output.shape
    resident, rank, _ = adapter_down_weight.shape
    _, blocks, listed = block_adapter_ids.shape
    sizes = (steps, blocks, listed, rank, row_count // blocks)
    x = attention_output.reshape(steps * row_count, depth)
    ring = ring_order(size)

    instance = lax.axis_index("inst")
    place = ring_place(lax.axis_index("tp"), size)
    dests = ring_index(lax.rem(place + jnp.arange(size, dtype=jnp.int32), size), size)

    forward = [(ring[i], ring[(i + 1) % size]) for i in range(size)]
    backward = [(ring[i], ring[i - 1]) for i in range(size)]
    far = size // 2
    pairs = [[(0, 1, forward), (1, -1, backward)], [(1, 1, forward), (0, -1, backward)]]
    arrived = {}
    half, sign, moves = pairs[0][0]
    first, token = first_hop(dests, (sign * far) % size, half, x, output_weight)
    arrived[half, sign] = lax.ppermute(first, "tp", moves)

    def turn(number, last):
        left = far - (number + 1) // 2
        for half, sign, moves in pairs[number % 2]:
            last = hop(
                dests, (sign * left) % size, half, x, output_weight,
                arrived.get((half, sign)), last,
            )
            arrived[half, sign] = lax.ppermute(last, "tp", moves)
        return last

    ids = block_adapter_ids.reshape(-1)
    ids_there = lax.ppermute(block_adapter_ids, "inst", SWAP).reshape(-1)
    half, sign, moves = pairs[0][1]
    last = hop(dests, (sign * far) % size, half, x, output_weight, None, token)
    arrived[half, sign] = lax.ppermute(last, "tp", moves)
    pages = adapter_page_table[jnp.concatenate([ids, ids_there])]
    places = pages % resident
    index, index_there = places[: ids.shape[0]], places[ids.shape[0] :]
    local = (pages[: ids.shape[0]] // resident == instance).astype(jnp.int32)
    last = collect(index_there, adapter_down_weight, last)
    got_down = lax.ppermute(last, "inst", SWAP)
    last = turn(1, last)
    last = collect(index_there, adapter_up_weight, last)
    got_up = lax.ppermute(last, "inst", SWAP)
    side = (lax.axis_index("tp") & 1).reshape(1)
    low, give = low_rank(
        sizes, local, index, side, x, row_list_position, adapter_down_weight, got_down, last
    )
    last = low

    def over(value, apart):
        return lax.ppermute(value, "tp", [(i, i ^ apart) for i in range(size)])

    number, turns = 2, 2 * far - 1
    apart = 1
    while apart < size:
        sent = over(give if apart == 1 else low, apart)
        until = turns - 1 if 2 * apart == size else number + (1 if apart == 1 else 2)
        while number < min(until, turns - 1):
            last = turn(number, last)
            if number == 2:
                last = touch(got_up, last)
            if number == 3:
                own, up_pages = own_terms(
                    dests, local, index, x, output_weight, adapter_up_weight, got_up, last
                )
                last = own
            number += 1
        apart *= 2
        low = last = add(low, sent, jnp.float32 if apart < size else jnp.bfloat16, last)
    other = over(low, 1)
    last = turn(number, last)
    own = add_delta(sizes, side, own, up_pages, row_list_position, low, other, last)
    result = None
    for half in range(2):
        result = finish(
            live_row_count.reshape(-1), half, own, arrived[half, 1], arrived[half, -1], result
        )
    return result.reshape(steps, row_count, -1)


def solution(mesh):
    in_specs = (
        P(None, ("grp", "inst"), "tp"),
        P("tp", None),
        P("inst", None, "tp"),
        P("inst", None, "tp"),
        P(),
        P(None, ("grp", "inst"), None),
        P(None, ("grp", "inst")),
        P(None, ("grp", "inst")),
    )
    out_specs = P(None, ("grp", "inst"), "tp")
    return jax.shard_map(
        functools.partial(per_device, mesh.shape["tp"]),
        mesh=mesh, in_specs=in_specs, out_specs=out_specs, check_vma=False,
    )
```

```python
import functools

import jax
import jax.numpy as jnp
from jax import lax
from jax.experimental import pallas as pl
from jax.experimental.pallas import tpu as pltpu
from jax.sharding import PartitionSpec as P

VMEM_LIMIT = 40 * 1024 * 1024
LOW_SCALE = 16.0
SWAP = [(0, 1), (1, 0)]
WHOLE = pl.BlockSpec(memory_space=pltpu.VMEM)
ANYWHERE = pl.BlockSpec(memory_space=pl.ANY)


def serpentine(size):
    return size == 8


def ring_index(place, size):
    if not serpentine(size):
        return place
    return jnp.where(place < size // 2, 2 * place, 2 * (size - 1 - place) + 1)


def ring_place(index, size):
    if not serpentine(size):
        return index
    return jnp.where(index & 1 == 0, index >> 1, size - 1 - (index >> 1))


def ring_order(size):
    if not serpentine(size):
        return list(range(size))
    return list(range(0, size, 2)) + list(range(size - 1, 0, -2))


def params():
    return pltpu.CompilerParams(vmem_limit_bytes=VMEM_LIMIT)


def cost(flops, size):
    return pl.CostEstimate(flops=30 * flops, bytes_accessed=size, transcendentals=0)


def hop_kernel(pieces, dests, x_ref, w_ref, *refs):
    tile = w_ref.shape[1]
    now = pl.program_id(0)
    columns = pl.ds(pl.multiple_of(now * tile, tile), tile)
    total = jnp.dot(x_ref[...], w_ref[...], preferred_element_type=jnp.float32)
    out_ref = refs[-1]
    if len(pieces) == 1:
        out_ref[:, columns] = (total + refs[0][:, columns].astype(jnp.float32)).astype(
            out_ref.dtype
        )
    elif pieces:
        for piece, received_ref in zip(pieces, refs):

            @pl.when(now == piece)
            def _():
                out_ref[:, columns] = (total + received_ref[...].astype(jnp.float32)).astype(
                    out_ref.dtype
                )

    else:
        out_ref[:, columns] = total.astype(out_ref.dtype)


def tiling(dests, weight):
    half_cols = weight.shape[1] // dests.shape[0] // 2
    tile = min(256, half_cols)
    return half_cols, tile, half_cols // tile


def hop(dests, offset, half, x, weight, received, after):
    rows, depth = x.shape
    half_cols, tile, tiles = tiling(dests, weight)
    return pl.pallas_call(
        functools.partial(hop_kernel, tuple(range(len(received)))),
        grid_spec=pltpu.PrefetchScalarGridSpec(
            num_scalar_prefetch=1,
            grid=(tiles,),
            in_specs=[
                WHOLE,
                pl.BlockSpec(
                    (depth, tile), lambda j, d: (0, (d[offset] * 2 + half) * tiles + j)
                ),
            ]
            + [WHOLE] * len(received)
            + [ANYWHERE],
            out_specs=WHOLE,
        ),
        out_shape=jax.ShapeDtypeStruct((rows, half_cols), jnp.bfloat16),
        compiler_params=params(),
        cost_estimate=cost(
            2 * rows * depth * half_cols,
            2 * (rows * depth + depth * half_cols + 2 * rows * half_cols),
        ),
    )(dests, x, weight, *received, after)


def first_kernel(with_after, dests, x_ref, w_ref, *refs):
    total = jnp.dot(x_ref[...], w_ref[...], preferred_element_type=jnp.float32)
    for chain, out_ref in enumerate(refs[-2:]):

        @pl.when(pl.program_id(0) == chain)
        def _():
            out_ref[...] = total.astype(out_ref.dtype)


def first_pieces(dests, offset, piece, x, weight, after):
    rows, depth = x.shape
    _, tile, tiles = tiling(dests, weight)
    size = dests.shape[0]

    def place(j, d):
        one = d[offset] * 2 * tiles + piece
        two = (d[(size - offset) % size] * 2 + 1) * tiles + piece
        return (0, jnp.where(j == 0, one, two))

    tail = [] if after is None else [after]
    return pl.pallas_call(
        functools.partial(first_kernel, after is not None),
        grid_spec=pltpu.PrefetchScalarGridSpec(
            num_scalar_prefetch=1,
            grid=(2,),
            in_specs=[WHOLE, pl.BlockSpec((depth, tile), place)] + [ANYWHERE] * len(tail),
            out_specs=[WHOLE, WHOLE],
        ),
        out_shape=[jax.ShapeDtypeStruct((rows, tile), jnp.bfloat16)] * 2,
        compiler_params=params(),
        cost_estimate=cost(
            4 * rows * depth * tile, 2 * (rows * depth + 2 * depth * tile + 2 * rows * tile)
        ),
    )(dests, x, weight, *tail)


def touch_kernel(*refs):
    refs[-1][...] = jnp.zeros_like(refs[-1])


def touch(*arrays):
    return pl.pallas_call(
        touch_kernel,
        in_specs=[ANYWHERE] * len(arrays),
        out_specs=WHOLE,
        out_shape=jax.ShapeDtypeStruct((8, 128), jnp.float32),
        compiler_params=params(),
    )(*arrays)


def collect_kernel(count, index, table_ref, after_ref, out_ref, sems):
    copies = [
        pltpu.make_async_copy(table_ref.at[index[slot]], out_ref.at[slot], sems.at[slot])
        for slot in range(count)
    ]
    for copy in copies:
        copy.start()
    for copy in copies:
        copy.wait()


def collect(index, table, after):
    count = index.shape[0]
    shape = (count,) + table.shape[1:]
    return pl.pallas_call(
        functools.partial(collect_kernel, count),
        grid_spec=pltpu.PrefetchScalarGridSpec(
            num_scalar_prefetch=1,
            grid=(1,),
            in_specs=[ANYWHERE, ANYWHERE],
            out_specs=WHOLE,
            scratch_shapes=[pltpu.SemaphoreType.DMA((count,))],
        ),
        out_shape=jax.ShapeDtypeStruct(shape, table.dtype),
        compiler_params=params(),
        cost_estimate=cost(0, 4 * shape[0] * shape[1] * shape[2]),
    )(index, table, after)


def start_pages(count, local, index, table_ref, got_ref, pages, sems):
    for slot in range(count):
        own = local[slot] == 1

        @pl.when(own)
        def _():
            pltpu.make_async_copy(
                table_ref.at[index[slot]], pages.at[slot], sems.at[slot]
            ).start()

        @pl.when(jnp.logical_not(own))
        def _():
            pltpu.make_async_copy(got_ref.at[slot], pages.at[slot], sems.at[slot]).start()


def wait_pages(slots, got_ref, pages, sems):
    for slot in slots:
        pltpu.make_async_copy(got_ref.at[slot], pages.at[slot], sems.at[slot]).wait()


def low_kernel(
    sizes, local, index, side, x_ref, place_ref, table_ref, got_ref, after_ref, keep_ref, give_ref,
    pages, sems,
):
    steps, blocks, listed, rank, block_rows = sizes
    half = steps * blocks // 2
    start_pages(steps * blocks * listed, local, index, table_ref, got_ref, pages, sems)
    for step in range(steps):
        for block in range(blocks):
            at = step * blocks + block
            wait_pages(range(at * listed, (at + 1) * listed), got_ref, pages, sems)
            listing = pages[at * listed : (at + 1) * listed].reshape(listed * rank, -1)
            every = lax.dot_general(
                listing, x_ref[at * block_rows : (at + 1) * block_rows, :],
                (((1,), (1,)), ((), ())), preferred_element_type=jnp.float32,
            )
            place = place_ref[step : step + 1, block * block_rows : (block + 1) * block_rows]
            low = jnp.zeros((rank, block_rows), jnp.float32)
            for entry in range(listed):
                low = jnp.where(place == entry, every[entry * rank : (entry + 1) * rank], low)
            rows = slice(at % half * block_rows, (at % half + 1) * block_rows)
            mine = side[0] == at // half

            @pl.when(mine)
            def _():
                keep_ref[:, rows] = low

            @pl.when(jnp.logical_not(mine))
            def _():
                give_ref[:, rows] = low


def low_rank(sizes, local, index, side, x, place, table, got, after):
    steps, blocks, listed, rank, block_rows = sizes
    count = steps * blocks * listed
    rows, depth = x.shape
    return pl.pallas_call(
        functools.partial(low_kernel, sizes),
        grid_spec=pltpu.PrefetchScalarGridSpec(
            num_scalar_prefetch=3,
            grid=(1,),
            in_specs=[WHOLE, WHOLE, ANYWHERE, ANYWHERE, ANYWHERE],
            out_specs=[WHOLE, WHOLE],
            scratch_shapes=[
                pltpu.VMEM((count, rank, depth), table.dtype),
                pltpu.SemaphoreType.DMA((count,)),
            ],
        ),
        out_shape=[jax.ShapeDtypeStruct((rank, rows // 2), jnp.float32)] * 2,
        compiler_params=params(),
        cost_estimate=cost(
            2 * rows * depth * listed * rank, 2 * (rows * depth + count * rank * depth)
        ),
    )(local, index, side, x, place, table, got, after)


def add_kernel(low_ref, sent_ref, after_ref, out_ref):
    out_ref[...] = (low_ref[...] + sent_ref[...]).astype(out_ref.dtype)


def add(low, sent, dtype, after):
    return pl.pallas_call(
        add_kernel,
        in_specs=[WHOLE, WHOLE, ANYWHERE],
        out_specs=WHOLE,
        out_shape=jax.ShapeDtypeStruct(low.shape, dtype),
        compiler_params=params(),
        cost_estimate=cost(low.size, 12 * low.size),
    )(low, sent, after)


def own_kernel(
    local, index, dests, x_ref, w_ref, table_ref, got_ref, after_ref, out_ref, pages, sems
):
    tile = w_ref.shape[1]
    now = pl.program_id(0)
    count = pages.shape[0]

    @pl.when(now == 0)
    def _():
        start_pages(count, local, index, table_ref, got_ref, pages, sems)

    columns = pl.ds(pl.multiple_of(now * tile, tile), tile)
    out_ref[:, columns] = jnp.dot(x_ref[...], w_ref[...], preferred_element_type=jnp.float32)

    @pl.when(now == pl.num_programs(0) - 1)
    def _():
        wait_pages(range(count), got_ref, pages, sems)


def own_terms(dests, local, index, x, weight, table, got, after):
    count, rank, cols = got.shape
    rows, depth = x.shape
    tile = min(256, cols)
    tiles = cols // tile
    return pl.pallas_call(
        own_kernel,
        grid_spec=pltpu.PrefetchScalarGridSpec(
            num_scalar_prefetch=3,
            grid=(tiles,),
            in_specs=[
                WHOLE,
                pl.BlockSpec((depth, tile), lambda j, l, i, d: (0, d[0] * tiles + j)),
                ANYWHERE,
                ANYWHERE,
                ANYWHERE,
            ],
            out_specs=[WHOLE, WHOLE],
            scratch_shapes=[pltpu.SemaphoreType.DMA((count,))],
        ),
        out_shape=[
            jax.ShapeDtypeStruct((rows, cols), jnp.float32),
            jax.ShapeDtypeStruct((count, rank, cols), table.dtype),
        ],
        compiler_params=params(),
        cost_estimate=cost(
            2 * rows * cols * depth,
            2 * (rows * depth + depth * cols + 2 * count * rank * cols) + 4 * rows * cols,
        ),
    )(local, index, dests, x, weight, table, got, after)


def delta_kernel(
    sizes, side, own_ref, pages_ref, place_ref, low_ref, other_ref, after_ref, out_ref
):
    steps, blocks, listed, rank, block_rows = sizes
    half = steps * blocks // 2
    entry_of = lax.broadcasted_iota(jnp.int32, (listed * rank, block_rows), 0) // rank
    for step in range(steps):
        for block in range(blocks):
            at = step * blocks + block
            rows = slice(at * block_rows, (at + 1) * block_rows)
            in_half = slice(at % half * block_rows, (at % half + 1) * block_rows)
            low = jnp.where(
                side[0] == at // half,
                low_ref[:, in_half].astype(jnp.float32),
                other_ref[:, in_half].astype(jnp.float32),
            )
            spread = jnp.concatenate([low] * listed, axis=0)
            place = place_ref[step : step + 1, block * block_rows : (block + 1) * block_rows]
            spread = jnp.where(entry_of == place, spread, 0.0)
            listing = pages_ref[at * listed : (at + 1) * listed].reshape(listed * rank, -1)
            out_ref[rows, :] = own_ref[rows, :] + jnp.dot(
                spread.T.astype(jnp.bfloat16), listing, preferred_element_type=jnp.float32
            )


def add_delta(sizes, side, own, pages, place, low, other, after):
    rows, cols = own.shape
    return pl.pallas_call(
        functools.partial(delta_kernel, sizes),
        grid_spec=pltpu.PrefetchScalarGridSpec(
            num_scalar_prefetch=1,
            grid=(1,),
            in_specs=[WHOLE] * 5 + [ANYWHERE],
            out_specs=WHOLE,
        ),
        out_shape=jax.ShapeDtypeStruct(own.shape, own.dtype),
        compiler_params=params(),
        cost_estimate=cost(
            2 * rows * cols * sizes[2] * sizes[3], 8 * rows * cols + 2 * pages.size
        ),
    )(side, own, pages, place, low, other, after)


def finish_kernel(half, live, own_ref, one_ref, two_ref, *refs):
    out_ref = refs[-1]
    count, cols = out_ref.shape
    step = pl.program_id(0)
    rows = pl.ds(pl.multiple_of(step * count, count), count)
    total = (
        own_ref[rows, half * cols : (half + 1) * cols]
        + one_ref[rows, :].astype(jnp.float32)
        + two_ref[rows, :].astype(jnp.float32)
    )
    row = lax.broadcasted_iota(jnp.int32, total.shape, 0)
    out_ref[...] = jnp.where(row < live[step], total, 0.0).astype(out_ref.dtype)


def finish(live, half, own, one, two, result):
    rows, cols = own.shape
    steps = live.shape[0]
    in_specs = [WHOLE, WHOLE, WHOLE]
    operands = [own, one, two]
    aliases = {}
    if result is not None:
        in_specs.append(ANYWHERE)
        operands.append(result)
        aliases = {4: 0}
    return pl.pallas_call(
        functools.partial(finish_kernel, half),
        grid_spec=pltpu.PrefetchScalarGridSpec(
            num_scalar_prefetch=1,
            grid=(steps,),
            in_specs=in_specs,
            out_specs=pl.BlockSpec((rows // steps, cols // 2), lambda s, l: (s, half)),
        ),
        out_shape=jax.ShapeDtypeStruct((rows, cols), jnp.bfloat16),
        input_output_aliases=aliases,
        compiler_params=params(),
        cost_estimate=cost(0, rows * cols * 5),
    )(live, *operands)


def per_device(
    size,
    attention_output,
    output_weight,
    adapter_down_weight,
    adapter_up_weight,
    adapter_page_table,
    block_adapter_ids,
    row_list_position,
    live_row_count,
):
    steps, row_count, depth = attention_output.shape
    resident, rank, _ = adapter_down_weight.shape
    _, blocks, listed = block_adapter_ids.shape
    sizes = (steps, blocks, listed, rank, row_count // blocks)
    x = attention_output.reshape(steps * row_count, depth)
    ring = ring_order(size)

    instance = lax.axis_index("inst")
    place = ring_place(lax.axis_index("tp"), size)
    dests = ring_index(lax.rem(place + jnp.arange(size, dtype=jnp.int32), size), size)

    forward = [(ring[i], ring[(i + 1) % size]) for i in range(size)]
    backward = [(ring[i], ring[i - 1]) for i in range(size)]
    far = size // 2
    pairs = [[(0, 1, forward), (1, -1, backward)], [(1, 1, forward), (0, -1, backward)]]
    arrived = {}
    def turn(number, last):
        left = far - (number + 1) // 2
        for half, sign, moves in pairs[number % 2]:
            last = hop(
                dests, (sign * left) % size, half, x, output_weight,
                arrived.get((half, sign), []), last,
            )
            arrived[half, sign] = [lax.ppermute(last, "tp", moves)]
        return last

    ids = block_adapter_ids.reshape(-1)
    ids_there = lax.ppermute(block_adapter_ids, "inst", SWAP).reshape(-1)
    last = None
    for piece in range(tiling(dests, output_weight)[2]):
        both = first_pieces(dests, far % size, piece, x, output_weight, last)
        for (half, sign, moves), part in zip(pairs[0], both):
            arrived.setdefault((half, sign), []).append(lax.ppermute(part, "tp", moves))
        last = both[1]
    pages = adapter_page_table[jnp.concatenate([ids, ids_there])]
    places = pages % resident
    index, index_there = places[: ids.shape[0]], places[ids.shape[0] :]
    local = (pages[: ids.shape[0]] // resident == instance).astype(jnp.int32)
    last = collect(index_there, adapter_down_weight, last)
    got_down = lax.ppermute(last, "inst", SWAP)
    last = touch(last, *(arrived[half, sign][0] for half, sign, _ in pairs[0]))
    last = turn(1, last)
    last = collect(index_there, adapter_up_weight, last)
    got_up = lax.ppermute(last, "inst", SWAP)
    side = (lax.axis_index("tp") & 1).reshape(1)
    low, give = low_rank(
        sizes, local, index, side, x, row_list_position, adapter_down_weight, got_down, last
    )
    last = low

    def over(value, apart):
        return lax.ppermute(value, "tp", [(i, i ^ apart) for i in range(size)])

    number, turns = 2, 2 * far - 1
    apart = 1
    while apart < size:
        sent = over(((give if apart == 1 else low) * LOW_SCALE).astype(jnp.float16), apart)
        until = turns - 1 if 2 * apart == size else number + (1 if apart == 1 else 2)
        while number < min(until, turns - 1):
            last = turn(number, last)
            if number == 2:
                last = touch(got_up, last)
            if number == 3:
                own, up_pages = own_terms(
                    dests, local, index, x, output_weight, adapter_up_weight, got_up, last
                )
                last = own
            number += 1
        apart *= 2
        zero = touch(last)[0, 0]
        sent = sent.astype(jnp.float32) * (1.0 / LOW_SCALE) + zero
        low = last = add(low, sent, jnp.float32 if apart < size else jnp.bfloat16, last)
    other = over(low, 1)
    last = turn(number, last)
    own = add_delta(sizes, side, own, up_pages, row_list_position, low, other, last)
    result = None
    for half in range(2):
        result = finish(
            live_row_count.reshape(-1), half, own, arrived[half, 1][0], arrived[half, -1][0], result
        )
    return result.reshape(steps, row_count, -1)


def solution(mesh):
    in_specs = (
        P(None, ("grp", "inst"), "tp"),
        P("tp", None),
        P("inst", None, "tp"),
        P("inst", None, "tp"),
        P(),
        P(None, ("grp", "inst"), None),
        P(None, ("grp", "inst")),
        P(None, ("grp", "inst")),
    )
    out_specs = P(None, ("grp", "inst"), "tp")
    return jax.shard_map(
        functools.partial(per_device, mesh.shape["tp"]),
        mesh=mesh, in_specs=in_specs, out_specs=out_specs, check_vma=False,
    )
```

```python
import functools

import jax
import jax.numpy as jnp
from jax import lax
from jax.experimental import pallas as pl
from jax.experimental.pallas import tpu as pltpu
from jax.sharding import PartitionSpec as P

VMEM_LIMIT = 40 * 1024 * 1024
LOW_SCALE = 16.0
SWAP = [(0, 1), (1, 0)]
WHOLE = pl.BlockSpec(memory_space=pltpu.VMEM)
ANYWHERE = pl.BlockSpec(memory_space=pl.ANY)


def serpentine(size):
    return size == 8


def ring_index(place, size):
    if not serpentine(size):
        return place
    return jnp.where(place < size // 2, 2 * place, 2 * (size - 1 - place) + 1)


def ring_place(index, size):
    if not serpentine(size):
        return index
    return jnp.where(index & 1 == 0, index >> 1, size - 1 - (index >> 1))


def ring_order(size):
    if not serpentine(size):
        return list(range(size))
    return list(range(0, size, 2)) + list(range(size - 1, 0, -2))


def params():
    return pltpu.CompilerParams(vmem_limit_bytes=VMEM_LIMIT)


def cost(flops, size):
    return pl.CostEstimate(flops=30 * flops, bytes_accessed=size, transcendentals=0)


def hop_kernel(pieces, dests, x_ref, w_ref, *refs):
    tile = w_ref.shape[1]
    now = pl.program_id(0)
    columns = pl.ds(pl.multiple_of(now * tile, tile), tile)
    total = jnp.dot(x_ref[...], w_ref[...], preferred_element_type=jnp.float32)
    out_ref = refs[-1]
    if len(pieces) == 1:
        out_ref[:, columns] = (total + refs[0][:, columns].astype(jnp.float32)).astype(
            out_ref.dtype
        )
    elif pieces:
        for piece, received_ref in zip(pieces, refs):

            @pl.when(now == piece)
            def _():
                out_ref[:, columns] = (total + received_ref[...].astype(jnp.float32)).astype(
                    out_ref.dtype
                )

    else:
        out_ref[:, columns] = total.astype(out_ref.dtype)


def tiling(dests, weight):
    half_cols = weight.shape[1] // dests.shape[0] // 2
    tile = min(256, half_cols)
    return half_cols, tile, half_cols // tile


def hop(dests, offset, half, x, weight, received, after):
    rows, depth = x.shape
    half_cols, tile, tiles = tiling(dests, weight)
    return pl.pallas_call(
        functools.partial(hop_kernel, tuple(range(len(received)))),
        grid_spec=pltpu.PrefetchScalarGridSpec(
            num_scalar_prefetch=1,
            grid=(tiles,),
            in_specs=[
                WHOLE,
                pl.BlockSpec(
                    (depth, tile), lambda j, d: (0, (d[offset] * 2 + half) * tiles + j)
                ),
            ]
            + [WHOLE] * len(received)
            + [ANYWHERE],
            out_specs=WHOLE,
        ),
        out_shape=jax.ShapeDtypeStruct((rows, half_cols), jnp.bfloat16),
        compiler_params=params(),
        cost_estimate=cost(
            2 * rows * depth * half_cols,
            2 * (rows * depth + depth * half_cols + 2 * rows * half_cols),
        ),
    )(dests, x, weight, *received, after)


def first_kernel(with_after, dests, x_ref, w_ref, *refs):
    total = jnp.dot(x_ref[...], w_ref[...], preferred_element_type=jnp.float32)
    for chain, out_ref in enumerate(refs[-2:]):

        @pl.when(pl.program_id(0) == chain)
        def _():
            out_ref[...] = total.astype(out_ref.dtype)


def first_pieces(dests, offset, piece, x, weight, after):
    rows, depth = x.shape
    _, tile, tiles = tiling(dests, weight)
    size = dests.shape[0]

    def place(j, d):
        one = d[offset] * 2 * tiles + piece
        two = (d[(size - offset) % size] * 2 + 1) * tiles + piece
        return (0, jnp.where(j == 0, one, two))

    tail = [] if after is None else [after]
    return pl.pallas_call(
        functools.partial(first_kernel, after is not None),
        grid_spec=pltpu.PrefetchScalarGridSpec(
            num_scalar_prefetch=1,
            grid=(2,),
            in_specs=[WHOLE, pl.BlockSpec((depth, tile), place)] + [ANYWHERE] * len(tail),
            out_specs=[WHOLE, WHOLE],
        ),
        out_shape=[jax.ShapeDtypeStruct((rows, tile), jnp.bfloat16)] * 2,
        compiler_params=params(),
        cost_estimate=cost(
            4 * rows * depth * tile, 2 * (rows * depth + 2 * depth * tile + 2 * rows * tile)
        ),
    )(dests, x, weight, *tail)


def touch_kernel(*refs):
    refs[-1][...] = jnp.zeros_like(refs[-1])


def touch(*arrays):
    return pl.pallas_call(
        touch_kernel,
        in_specs=[ANYWHERE] * len(arrays),
        out_specs=WHOLE,
        out_shape=jax.ShapeDtypeStruct((8, 128), jnp.float32),
        compiler_params=params(),
    )(*arrays)


def collect_kernel(count, index, table_ref, after_ref, out_ref, sems):
    copies = [
        pltpu.make_async_copy(table_ref.at[index[slot]], out_ref.at[slot], sems.at[slot])
        for slot in range(count)
    ]
    for copy in copies:
        copy.start()
    for copy in copies:
        copy.wait()


def collect(index, table, after):
    count = index.shape[0]
    shape = (count,) + table.shape[1:]
    return pl.pallas_call(
        functools.partial(collect_kernel, count),
        grid_spec=pltpu.PrefetchScalarGridSpec(
            num_scalar_prefetch=1,
            grid=(1,),
            in_specs=[ANYWHERE, ANYWHERE],
            out_specs=WHOLE,
            scratch_shapes=[pltpu.SemaphoreType.DMA((count,))],
        ),
        out_shape=jax.ShapeDtypeStruct(shape, table.dtype),
        compiler_params=params(),
        cost_estimate=cost(0, 4 * shape[0] * shape[1] * shape[2]),
    )(index, table, after)


def start_pages(count, local, index, table_ref, got_ref, pages, sems):
    for slot in range(count):
        own = local[slot] == 1

        @pl.when(own)
        def _():
            pltpu.make_async_copy(
                table_ref.at[index[slot]], pages.at[slot], sems.at[slot]
            ).start()

        @pl.when(jnp.logical_not(own))
        def _():
            pltpu.make_async_copy(got_ref.at[slot], pages.at[slot], sems.at[slot]).start()


def wait_pages(slots, got_ref, pages, sems):
    for slot in slots:
        pltpu.make_async_copy(got_ref.at[slot], pages.at[slot], sems.at[slot]).wait()


def low_kernel(
    sizes, local, index, side, x_ref, place_ref, table_ref, got_ref, after_ref, keep_ref, give_ref,
    pages, sems,
):
    steps, blocks, listed, rank, block_rows = sizes
    half = steps * blocks // 2
    start_pages(steps * blocks * listed, local, index, table_ref, got_ref, pages, sems)
    for step in range(steps):
        for block in range(blocks):
            at = step * blocks + block
            wait_pages(range(at * listed, (at + 1) * listed), got_ref, pages, sems)
            listing = pages[at * listed : (at + 1) * listed].reshape(listed * rank, -1)
            every = lax.dot_general(
                listing, x_ref[at * block_rows : (at + 1) * block_rows, :],
                (((1,), (1,)), ((), ())), preferred_element_type=jnp.float32,
            )
            place = place_ref[step : step + 1, block * block_rows : (block + 1) * block_rows]
            low = jnp.zeros((rank, block_rows), jnp.float32)
            for entry in range(listed):
                low = jnp.where(place == entry, every[entry * rank : (entry + 1) * rank], low)
            rows = slice(at % half * block_rows, (at % half + 1) * block_rows)
            mine = side[0] == at // half

            @pl.when(mine)
            def _():
                keep_ref[:, rows] = low

            @pl.when(jnp.logical_not(mine))
            def _():
                give_ref[:, rows] = low


def low_rank(sizes, local, index, side, x, place, table, got, after):
    steps, blocks, listed, rank, block_rows = sizes
    count = steps * blocks * listed
    rows, depth = x.shape
    return pl.pallas_call(
        functools.partial(low_kernel, sizes),
        grid_spec=pltpu.PrefetchScalarGridSpec(
            num_scalar_prefetch=3,
            grid=(1,),
            in_specs=[WHOLE, WHOLE, ANYWHERE, ANYWHERE, ANYWHERE],
            out_specs=[WHOLE, WHOLE],
            scratch_shapes=[
                pltpu.VMEM((count, rank, depth), table.dtype),
                pltpu.SemaphoreType.DMA((count,)),
            ],
        ),
        out_shape=[jax.ShapeDtypeStruct((rank, rows // 2), jnp.float32)] * 2,
        compiler_params=params(),
        cost_estimate=cost(
            2 * rows * depth * listed * rank, 2 * (rows * depth + count * rank * depth)
        ),
    )(local, index, side, x, place, table, got, after)


def add_kernel(low_ref, sent_ref, after_ref, out_ref):
    out_ref[...] = (low_ref[...] + sent_ref[...]).astype(out_ref.dtype)


def add(low, sent, dtype, after):
    return pl.pallas_call(
        add_kernel,
        in_specs=[WHOLE, WHOLE, ANYWHERE],
        out_specs=WHOLE,
        out_shape=jax.ShapeDtypeStruct(low.shape, dtype),
        compiler_params=params(),
        cost_estimate=cost(low.size, 12 * low.size),
    )(low, sent, after)


def own_kernel(
    local, index, dests, x_ref, w_ref, table_ref, got_ref, after_ref, out_ref, pages, sems
):
    tile = w_ref.shape[1]
    now = pl.program_id(0)
    count = pages.shape[0]

    @pl.when(now == 0)
    def _():
        start_pages(count, local, index, table_ref, got_ref, pages, sems)

    columns = pl.ds(pl.multiple_of(now * tile, tile), tile)
    out_ref[:, columns] = jnp.dot(x_ref[...], w_ref[...], preferred_element_type=jnp.float32)

    @pl.when(now == pl.num_programs(0) - 1)
    def _():
        wait_pages(range(count), got_ref, pages, sems)


def own_terms(dests, local, index, x, weight, table, got, after):
    count, rank, cols = got.shape
    rows, depth = x.shape
    tile = min(256, cols)
    tiles = cols // tile
    return pl.pallas_call(
        own_kernel,
        grid_spec=pltpu.PrefetchScalarGridSpec(
            num_scalar_prefetch=3,
            grid=(tiles,),
            in_specs=[
                WHOLE,
                pl.BlockSpec((depth, tile), lambda j, l, i, d: (0, d[0] * tiles + j)),
                ANYWHERE,
                ANYWHERE,
                ANYWHERE,
            ],
            out_specs=[WHOLE, WHOLE],
            scratch_shapes=[pltpu.SemaphoreType.DMA((count,))],
        ),
        out_shape=[
            jax.ShapeDtypeStruct((rows, cols), jnp.float32),
            jax.ShapeDtypeStruct((count, rank, cols), table.dtype),
        ],
        compiler_params=params(),
        cost_estimate=cost(
            2 * rows * cols * depth,
            2 * (rows * depth + depth * cols + 2 * count * rank * cols) + 4 * rows * cols,
        ),
    )(local, index, dests, x, weight, table, got, after)


def delta_kernel(
    sizes, side, own_ref, pages_ref, place_ref, low_ref, other_ref, after_ref, out_ref
):
    steps, blocks, listed, rank, block_rows = sizes
    half = steps * blocks // 2
    entry_of = lax.broadcasted_iota(jnp.int32, (listed * rank, block_rows), 0) // rank
    for step in range(steps):
        for block in range(blocks):
            at = step * blocks + block
            rows = slice(at * block_rows, (at + 1) * block_rows)
            in_half = slice(at % half * block_rows, (at % half + 1) * block_rows)
            low = jnp.where(
                side[0] == at // half,
                low_ref[:, in_half].astype(jnp.float32),
                other_ref[:, in_half].astype(jnp.float32),
            )
            spread = jnp.concatenate([low] * listed, axis=0)
            place = place_ref[step : step + 1, block * block_rows : (block + 1) * block_rows]
            spread = jnp.where(entry_of == place, spread, 0.0)
            listing = pages_ref[at * listed : (at + 1) * listed].reshape(listed * rank, -1)
            out_ref[rows, :] = own_ref[rows, :] + jnp.dot(
                spread.T.astype(jnp.bfloat16), listing, preferred_element_type=jnp.float32
            )


def add_delta(sizes, side, own, pages, place, low, other, after):
    rows, cols = own.shape
    return pl.pallas_call(
        functools.partial(delta_kernel, sizes),
        grid_spec=pltpu.PrefetchScalarGridSpec(
            num_scalar_prefetch=1,
            grid=(1,),
            in_specs=[WHOLE] * 5 + [ANYWHERE],
            out_specs=WHOLE,
        ),
        out_shape=jax.ShapeDtypeStruct(own.shape, own.dtype),
        compiler_params=params(),
        cost_estimate=cost(
            2 * rows * cols * sizes[2] * sizes[3], 8 * rows * cols + 2 * pages.size
        ),
    )(side, own, pages, place, low, other, after)


def finish_kernel(half, live, own_ref, one_ref, two_ref, *refs):
    out_ref = refs[-1]
    count, cols = out_ref.shape
    step = pl.program_id(0)
    rows = pl.ds(pl.multiple_of(step * count, count), count)
    total = (
        own_ref[rows, half * cols : (half + 1) * cols]
        + one_ref[rows, :].astype(jnp.float32)
        + two_ref[rows, :].astype(jnp.float32)
    )
    row = lax.broadcasted_iota(jnp.int32, total.shape, 0)
    out_ref[...] = jnp.where(row < live[step], total, 0.0).astype(out_ref.dtype)


def finish(live, half, own, one, two, result):
    rows, cols = own.shape
    steps = live.shape[0]
    in_specs = [WHOLE, WHOLE, WHOLE]
    operands = [own, one, two]
    aliases = {}
    if result is not None:
        in_specs.append(ANYWHERE)
        operands.append(result)
        aliases = {4: 0}
    return pl.pallas_call(
        functools.partial(finish_kernel, half),
        grid_spec=pltpu.PrefetchScalarGridSpec(
            num_scalar_prefetch=1,
            grid=(steps,),
            in_specs=in_specs,
            out_specs=pl.BlockSpec((rows // steps, cols // 2), lambda s, l: (s, half)),
        ),
        out_shape=jax.ShapeDtypeStruct((rows, cols), jnp.bfloat16),
        input_output_aliases=aliases,
        compiler_params=params(),
        cost_estimate=cost(0, rows * cols * 5),
    )(live, *operands)


def per_device(
    size,
    attention_output,
    output_weight,
    adapter_down_weight,
    adapter_up_weight,
    adapter_page_table,
    block_adapter_ids,
    row_list_position,
    live_row_count,
):
    steps, row_count, depth = attention_output.shape
    resident, rank, _ = adapter_down_weight.shape
    _, blocks, listed = block_adapter_ids.shape
    sizes = (steps, blocks, listed, rank, row_count // blocks)
    x = attention_output.reshape(steps * row_count, depth)
    ring = ring_order(size)

    instance = lax.axis_index("inst")
    place = ring_place(lax.axis_index("tp"), size)
    dests = ring_index(lax.rem(place + jnp.arange(size, dtype=jnp.int32), size), size)

    forward = [(ring[i], ring[(i + 1) % size]) for i in range(size)]
    backward = [(ring[i], ring[i - 1]) for i in range(size)]
    far = size // 2
    pairs = [[(0, 1, forward), (1, -1, backward)], [(1, 1, forward), (0, -1, backward)]]
    arrived = {}

    def turn(number, last, between=None):
        left = far - (number + 1) // 2
        for half, sign, moves in pairs[number % 2]:
            last = hop(
                dests, (sign * left) % size, half, x, output_weight,
                arrived.get((half, sign), []), last,
            )
            arrived[half, sign] = [lax.ppermute(last, "tp", moves)]
            if between is not None:
                last, between = touch(between, last), None
        return last

    ids = block_adapter_ids.reshape(-1)
    ids_there = lax.ppermute(block_adapter_ids, "inst", SWAP).reshape(-1)
    last = None
    for piece in range(tiling(dests, output_weight)[2]):
        both = first_pieces(dests, far % size, piece, x, output_weight, last)
        for (half, sign, moves), part in zip(pairs[0], both):
            arrived.setdefault((half, sign), []).append(lax.ppermute(part, "tp", moves))
        last = both[1]
    pages = adapter_page_table[jnp.concatenate([ids, ids_there])]
    places = pages % resident
    index, index_there = places[: ids.shape[0]], places[ids.shape[0] :]
    local = (pages[: ids.shape[0]] // resident == instance).astype(jnp.int32)
    last = collect(index_there, adapter_down_weight, last)
    got_down = lax.ppermute(last, "inst", SWAP)
    last = touch(last, *(arrived[half, sign][0] for half, sign, _ in pairs[0]))
    last = turn(1, last)
    last = collect(index_there, adapter_up_weight, last)
    got_up = lax.ppermute(last, "inst", SWAP)
    last = turn(2, last, got_down)
    side = (lax.axis_index("tp") & 1).reshape(1)
    low, give = low_rank(
        sizes, local, index, side, x, row_list_position, adapter_down_weight, got_down, last
    )
    last = touch(got_up, low)

    def over(value, apart):
        return lax.ppermute(value, "tp", [(i, i ^ apart) for i in range(size)])

    number, turns = 3, 2 * far - 1
    apart = 1
    while apart < size:
        sent = over(((give if apart == 1 else low) * LOW_SCALE).astype(jnp.float16), apart)
        until = turns - 1 if 2 * apart == size else number + 1
        while number < min(until, turns - 1):
            last = turn(number, last)
            if number == 3:
                own, up_pages = own_terms(
                    dests, local, index, x, output_weight, adapter_up_weight, got_up, last
                )
                last = own
            number += 1
        apart *= 2
        zero = touch(last)[0, 0]
        sent = sent.astype(jnp.float32) * (1.0 / LOW_SCALE) + zero
        low = last = add(low, sent, jnp.float32 if apart < size else jnp.bfloat16, last)
    other = over(low, 1)
    last = turn(number, last)
    own = add_delta(sizes, side, own, up_pages, row_list_position, low, other, last)
    result = None
    for half in range(2):
        result = finish(
            live_row_count.reshape(-1), half, own, arrived[half, 1][0], arrived[half, -1][0], result
        )
    return result.reshape(steps, row_count, -1)


def solution(mesh):
    in_specs = (
        P(None, ("grp", "inst"), "tp"),
        P("tp", None),
        P("inst", None, "tp"),
        P("inst", None, "tp"),
        P(),
        P(None, ("grp", "inst"), None),
        P(None, ("grp", "inst")),
        P(None, ("grp", "inst")),
    )
    out_specs = P(None, ("grp", "inst"), "tp")
    return jax.shard_map(
        functools.partial(per_device, mesh.shape["tp"]),
        mesh=mesh, in_specs=in_specs, out_specs=out_specs, check_vma=False,
    )
```

```python
import functools

import jax
import jax.numpy as jnp
from jax import lax
from jax.experimental import pallas as pl
from jax.experimental.pallas import tpu as pltpu
from jax.sharding import PartitionSpec as P

VMEM_LIMIT = 40 * 1024 * 1024
LOW_SCALE = 16.0
GRAIN = 16
SWAP = [(0, 1), (1, 0)]
WHOLE = pl.BlockSpec(memory_space=pltpu.VMEM)
ANYWHERE = pl.BlockSpec(memory_space=pl.ANY)


def serpentine(size):
    return size == 8


def ring_index(place, size):
    if not serpentine(size):
        return place
    return jnp.where(place < size // 2, 2 * place, 2 * (size - 1 - place) + 1)


def ring_place(index, size):
    if not serpentine(size):
        return index
    return jnp.where(index & 1 == 0, index >> 1, size - 1 - (index >> 1))


def ring_order(size):
    if not serpentine(size):
        return list(range(size))
    return list(range(0, size, 2)) + list(range(size - 1, 0, -2))


def params():
    return pltpu.CompilerParams(vmem_limit_bytes=VMEM_LIMIT)


def cost(flops, size):
    return pl.CostEstimate(flops=30 * flops, bytes_accessed=size, transcendentals=0)


def hop_kernel(pieces, dests, x_ref, w_ref, *refs):
    tile = w_ref.shape[1]
    now = pl.program_id(0)
    columns = pl.ds(pl.multiple_of(now * tile, tile), tile)
    total = jnp.dot(x_ref[...], w_ref[...], preferred_element_type=jnp.float32)
    out_ref = refs[-1]
    if len(pieces) == 1:
        out_ref[:, columns] = (total + refs[0][:, columns].astype(jnp.float32)).astype(
            out_ref.dtype
        )
    elif pieces:
        for piece, received_ref in zip(pieces, refs):

            @pl.when(now == piece)
            def _():
                out_ref[:, columns] = (total + received_ref[...].astype(jnp.float32)).astype(
                    out_ref.dtype
                )

    else:
        out_ref[:, columns] = total.astype(out_ref.dtype)


def tiling(dests, weight):
    half_cols = weight.shape[1] // dests.shape[0] // 2
    tile = min(256, half_cols)
    return half_cols, tile, half_cols // tile


def hop(dests, offset, half, x, weight, received, after):
    rows, depth = x.shape
    half_cols, tile, tiles = tiling(dests, weight)
    return pl.pallas_call(
        functools.partial(hop_kernel, tuple(range(len(received)))),
        grid_spec=pltpu.PrefetchScalarGridSpec(
            num_scalar_prefetch=1,
            grid=(tiles,),
            in_specs=[
                WHOLE,
                pl.BlockSpec(
                    (depth, tile), lambda j, d: (0, (d[offset] * 2 + half) * tiles + j)
                ),
            ]
            + [WHOLE] * len(received)
            + [ANYWHERE],
            out_specs=WHOLE,
        ),
        out_shape=jax.ShapeDtypeStruct((rows, half_cols), jnp.bfloat16),
        compiler_params=params(),
        cost_estimate=cost(
            2 * rows * depth * half_cols,
            2 * (rows * depth + depth * half_cols + 2 * rows * half_cols),
        ),
    )(dests, x, weight, *received, after)


def first_kernel(with_after, dests, x_ref, w_ref, *refs):
    total = jnp.dot(x_ref[...], w_ref[...], preferred_element_type=jnp.float32)
    for chain, out_ref in enumerate(refs[-2:]):

        @pl.when(pl.program_id(0) == chain)
        def _():
            out_ref[...] = total.astype(out_ref.dtype)


def first_pieces(dests, offset, piece, x, weight, after):
    rows, depth = x.shape
    _, tile, tiles = tiling(dests, weight)
    size = dests.shape[0]

    def place(j, d):
        one = d[offset] * 2 * tiles + piece
        two = (d[(size - offset) % size] * 2 + 1) * tiles + piece
        return (0, jnp.where(j == 0, one, two))

    tail = [] if after is None else [after]
    return pl.pallas_call(
        functools.partial(first_kernel, after is not None),
        grid_spec=pltpu.PrefetchScalarGridSpec(
            num_scalar_prefetch=1,
            grid=(2,),
            in_specs=[WHOLE, pl.BlockSpec((depth, tile), place)] + [ANYWHERE] * len(tail),
            out_specs=[WHOLE, WHOLE],
        ),
        out_shape=[jax.ShapeDtypeStruct((rows, tile), jnp.bfloat16)] * 2,
        compiler_params=params(),
        cost_estimate=cost(
            4 * rows * depth * tile, 2 * (rows * depth + 2 * depth * tile + 2 * rows * tile)
        ),
    )(dests, x, weight, *tail)


def touch_kernel(*refs):
    refs[-1][...] = jnp.zeros_like(refs[-1])


def touch(*arrays):
    return pl.pallas_call(
        touch_kernel,
        in_specs=[ANYWHERE] * len(arrays),
        out_specs=WHOLE,
        out_shape=jax.ShapeDtypeStruct((8, 128), jnp.float32),
        compiler_params=params(),
    )(*arrays)


def collect_kernel(count, index, table_ref, after_ref, out_ref, sems):
    copies = [
        pltpu.make_async_copy(table_ref.at[index[slot]], out_ref.at[slot], sems.at[slot])
        for slot in range(count)
    ]
    for copy in copies:
        copy.start()
    for copy in copies:
        copy.wait()


def collect(index, table, after):
    count = index.shape[0]
    shape = (count,) + table.shape[1:]
    return pl.pallas_call(
        functools.partial(collect_kernel, count),
        grid_spec=pltpu.PrefetchScalarGridSpec(
            num_scalar_prefetch=1,
            grid=(1,),
            in_specs=[ANYWHERE, ANYWHERE],
            out_specs=WHOLE,
            scratch_shapes=[pltpu.SemaphoreType.DMA((count,))],
        ),
        out_shape=jax.ShapeDtypeStruct(shape, table.dtype),
        compiler_params=params(),
        cost_estimate=cost(0, 4 * shape[0] * shape[1] * shape[2]),
    )(index, table, after)


def start_pages(count, local, index, table_ref, got_ref, pages, sems):
    for slot in range(count):
        own = local[slot] == 1

        @pl.when(own)
        def _():
            pltpu.make_async_copy(
                table_ref.at[index[slot]], pages.at[slot], sems.at[slot]
            ).start()

        @pl.when(jnp.logical_not(own))
        def _():
            pltpu.make_async_copy(got_ref.at[slot], pages.at[slot], sems.at[slot]).start()


def wait_pages(slots, got_ref, pages, sems):
    for slot in slots:
        pltpu.make_async_copy(got_ref.at[slot], pages.at[slot], sems.at[slot]).wait()


def low_kernel(
    sizes, local, index, side, x_ref, place_ref, table_ref, got_ref, after_ref, keep_ref, give_ref,
    pages, sems,
):
    steps, blocks, listed, rank, block_rows = sizes
    half = steps * blocks // 2
    start_pages(steps * blocks * listed, local, index, table_ref, got_ref, pages, sems)
    for step in range(steps):
        for block in range(blocks):
            at = step * blocks + block
            wait_pages(range(at * listed, (at + 1) * listed), got_ref, pages, sems)
            listing = pages[at * listed : (at + 1) * listed].reshape(listed * rank, -1)
            every = lax.dot_general(
                listing, x_ref[at * block_rows : (at + 1) * block_rows, :],
                (((1,), (1,)), ((), ())), preferred_element_type=jnp.float32,
            )
            place = place_ref[step : step + 1, block * block_rows : (block + 1) * block_rows]
            low = jnp.zeros((rank, block_rows), jnp.float32)
            for entry in range(listed):
                low = jnp.where(place == entry, every[entry * rank : (entry + 1) * rank], low)
            rows = slice(at % half * block_rows, (at % half + 1) * block_rows)
            mine = side[0] == at // half

            @pl.when(mine)
            def _():
                keep_ref[:, rows] = low

            @pl.when(jnp.logical_not(mine))
            def _():
                give_ref[:, rows] = low


def low_rank(sizes, local, index, side, x, place, table, got, after):
    steps, blocks, listed, rank, block_rows = sizes
    count = steps * blocks * listed
    rows, depth = x.shape
    return pl.pallas_call(
        functools.partial(low_kernel, sizes),
        grid_spec=pltpu.PrefetchScalarGridSpec(
            num_scalar_prefetch=3,
            grid=(1,),
            in_specs=[WHOLE, WHOLE, ANYWHERE, ANYWHERE, ANYWHERE],
            out_specs=[WHOLE, WHOLE],
            scratch_shapes=[
                pltpu.VMEM((count, rank, depth), table.dtype),
                pltpu.SemaphoreType.DMA((count,)),
            ],
        ),
        out_shape=[jax.ShapeDtypeStruct((rank, rows // 2), jnp.float32)] * 2,
        compiler_params=params(),
        cost_estimate=cost(
            2 * rows * depth * listed * rank, 2 * (rows * depth + count * rank * depth)
        ),
    )(local, index, side, x, place, table, got, after)


def add_kernel(low_ref, sent_ref, after_ref, out_ref):
    out_ref[...] = (low_ref[...] + sent_ref[...]).astype(out_ref.dtype)


def add(low, sent, dtype, after):
    return pl.pallas_call(
        add_kernel,
        in_specs=[WHOLE, WHOLE, ANYWHERE],
        out_specs=WHOLE,
        out_shape=jax.ShapeDtypeStruct(low.shape, dtype),
        compiler_params=params(),
        cost_estimate=cost(low.size, 12 * low.size),
    )(low, sent, after)


def own_kernel(
    local, index, dests, x_ref, w_ref, table_ref, got_ref, after_ref, out_ref, pages, sems
):
    tile = w_ref.shape[1]
    now = pl.program_id(0)
    count = pages.shape[0]

    @pl.when(now == 0)
    def _():
        start_pages(count, local, index, table_ref, got_ref, pages, sems)

    columns = pl.ds(pl.multiple_of(now * tile, tile), tile)
    out_ref[:, columns] = jnp.dot(x_ref[...], w_ref[...], preferred_element_type=jnp.float32)

    @pl.when(now == pl.num_programs(0) - 1)
    def _():
        wait_pages(range(count), got_ref, pages, sems)


def own_terms(dests, local, index, x, weight, table, got, after):
    count, rank, cols = got.shape
    rows, depth = x.shape
    tile = min(256, cols)
    tiles = cols // tile
    return pl.pallas_call(
        own_kernel,
        grid_spec=pltpu.PrefetchScalarGridSpec(
            num_scalar_prefetch=3,
            grid=(tiles,),
            in_specs=[
                WHOLE,
                pl.BlockSpec((depth, tile), lambda j, l, i, d: (0, d[0] * tiles + j)),
                ANYWHERE,
                ANYWHERE,
                ANYWHERE,
            ],
            out_specs=[WHOLE, WHOLE],
            scratch_shapes=[pltpu.SemaphoreType.DMA((count,))],
        ),
        out_shape=[
            jax.ShapeDtypeStruct((rows, cols), jnp.float32),
            jax.ShapeDtypeStruct((count, rank, cols), table.dtype),
        ],
        compiler_params=params(),
        cost_estimate=cost(
            2 * rows * cols * depth,
            2 * (rows * depth + depth * cols + 2 * count * rank * cols) + 4 * rows * cols,
        ),
    )(local, index, dests, x, weight, table, got, after)


def delta_kernel(
    sizes, side, own_ref, pages_ref, place_ref, low_ref, other_ref, after_ref, out_ref
):
    steps, blocks, listed, rank, block_rows = sizes
    half = steps * blocks // 2
    entry_of = lax.broadcasted_iota(jnp.int32, (listed * rank, block_rows), 0) // rank
    for step in range(steps):
        for block in range(blocks):
            at = step * blocks + block
            rows = slice(at * block_rows, (at + 1) * block_rows)
            in_half = slice(at % half * block_rows, (at % half + 1) * block_rows)
            low = jnp.where(
                side[0] == at // half,
                low_ref[:, in_half].astype(jnp.float32),
                other_ref[:, in_half].astype(jnp.float32),
            )
            spread = jnp.concatenate([low] * listed, axis=0)
            place = place_ref[step : step + 1, block * block_rows : (block + 1) * block_rows]
            spread = jnp.where(entry_of == place, spread, 0.0)
            listing = pages_ref[at * listed : (at + 1) * listed].reshape(listed * rank, -1)
            out_ref[rows, :] = own_ref[rows, :] + jnp.dot(
                spread.T.astype(jnp.bfloat16), listing, preferred_element_type=jnp.float32
            )


def add_delta(sizes, side, own, pages, place, low, other, after):
    rows, cols = own.shape
    return pl.pallas_call(
        functools.partial(delta_kernel, sizes),
        grid_spec=pltpu.PrefetchScalarGridSpec(
            num_scalar_prefetch=1,
            grid=(1,),
            in_specs=[WHOLE] * 5 + [ANYWHERE],
            out_specs=WHOLE,
        ),
        out_shape=jax.ShapeDtypeStruct(own.shape, own.dtype),
        compiler_params=params(),
        cost_estimate=cost(
            2 * rows * cols * sizes[2] * sizes[3], 8 * rows * cols + 2 * pages.size
        ),
    )(side, own, pages, place, low, other, after)


def chunks(count):
    size = 32 if count % 32 == 0 else GRAIN
    return [slice(at, at + size) for at in range(0, count, size)]


def join_kernel(own_ref, left_ref, right_ref, out_ref):
    cols = left_ref.shape[1]
    for rows in chunks(own_ref.shape[0]):
        for at, part_ref in ((0, left_ref), (cols, right_ref)):
            out_ref[rows, at : at + cols] = own_ref[rows, at : at + cols] + part_ref[
                rows, :
            ].astype(jnp.float32)


def join(own, left, right):
    return pl.pallas_call(
        join_kernel,
        in_specs=[WHOLE] * 3,
        out_specs=WHOLE,
        out_shape=jax.ShapeDtypeStruct(own.shape, own.dtype),
        compiler_params=params(),
        cost_estimate=cost(own.size, 10 * own.size),
    )(own, left, right)


def finish_kernel(half, live, own_ref, last_ref, *refs):
    out_ref = refs[-1]
    count, cols = out_ref.shape
    step = pl.program_id(0)
    start = pl.multiple_of(step * count, count)
    columns = slice(half * cols, (half + 1) * cols)
    for rows in chunks(count):
        here = pl.ds(start + rows.start, rows.stop - rows.start)
        total = own_ref[here, columns] + last_ref[here, :].astype(jnp.float32)
        row = rows.start + lax.broadcasted_iota(jnp.int32, total.shape, 0)
        out_ref[rows, :] = jnp.where(row < live[step], total, 0.0).astype(out_ref.dtype)


def finish(live, half, own, last, result):
    rows, cols = own.shape
    steps = live.shape[0]
    in_specs = [WHOLE, WHOLE]
    operands = [own, last]
    aliases = {}
    if result is not None:
        in_specs.append(ANYWHERE)
        operands.append(result)
        aliases = {3: 0}
    return pl.pallas_call(
        functools.partial(finish_kernel, half),
        grid_spec=pltpu.PrefetchScalarGridSpec(
            num_scalar_prefetch=1,
            grid=(steps,),
            in_specs=in_specs,
            out_specs=pl.BlockSpec((rows // steps, cols // 2), lambda s, l: (s, half)),
        ),
        out_shape=jax.ShapeDtypeStruct((rows, cols), jnp.bfloat16),
        input_output_aliases=aliases,
        compiler_params=params(),
        cost_estimate=cost(0, rows * cols * 5),
    )(live, *operands)


def per_device(
    size,
    attention_output,
    output_weight,
    adapter_down_weight,
    adapter_up_weight,
    adapter_page_table,
    block_adapter_ids,
    row_list_position,
    live_row_count,
):
    steps, row_count, depth = attention_output.shape
    resident, rank, _ = adapter_down_weight.shape
    _, blocks, listed = block_adapter_ids.shape
    sizes = (steps, blocks, listed, rank, row_count // blocks)
    x = attention_output.reshape(steps * row_count, depth)
    ring = ring_order(size)

    instance = lax.axis_index("inst")
    place = ring_place(lax.axis_index("tp"), size)
    dests = ring_index(lax.rem(place + jnp.arange(size, dtype=jnp.int32), size), size)

    forward = [(ring[i], ring[(i + 1) % size]) for i in range(size)]
    backward = [(ring[i], ring[i - 1]) for i in range(size)]
    far = size // 2
    pairs = [[(0, 1, forward), (1, -1, backward)], [(1, 1, forward), (0, -1, backward)]]
    arrived = {}

    def turn(number, last, between=None):
        left = far - (number + 1) // 2
        for half, sign, moves in pairs[number % 2]:
            last = hop(
                dests, (sign * left) % size, half, x, output_weight,
                arrived.get((half, sign), []), last,
            )
            arrived[half, sign] = [lax.ppermute(last, "tp", moves)]
            if between is not None:
                last, between = touch(between, last), None
        return last

    ids = block_adapter_ids.reshape(-1)
    ids_there = lax.ppermute(block_adapter_ids, "inst", SWAP).reshape(-1)
    last = None
    for piece in range(tiling(dests, output_weight)[2]):
        both = first_pieces(dests, far % size, piece, x, output_weight, last)
        for (half, sign, moves), part in zip(pairs[0], both):
            arrived.setdefault((half, sign), []).append(lax.ppermute(part, "tp", moves))
        last = both[1]
    pages = adapter_page_table[jnp.concatenate([ids, ids_there])]
    places = pages % resident
    index, index_there = places[: ids.shape[0]], places[ids.shape[0] :]
    local = (pages[: ids.shape[0]] // resident == instance).astype(jnp.int32)
    last = collect(index_there, adapter_down_weight, last)
    got_down = lax.ppermute(last, "inst", SWAP)
    last = touch(last, *(arrived[half, sign][0] for half, sign, _ in pairs[0]))
    last = turn(1, last)
    last = collect(index_there, adapter_up_weight, last)
    got_up = lax.ppermute(last, "inst", SWAP)
    last = turn(2, last, got_down)
    side = (lax.axis_index("tp") & 1).reshape(1)
    low, give = low_rank(
        sizes, local, index, side, x, row_list_position, adapter_down_weight, got_down, last
    )
    last = touch(got_up, low)

    def over(value, apart):
        return lax.ppermute(value, "tp", [(i, i ^ apart) for i in range(size)])

    number, turns = 3, 2 * far - 1
    apart = 1
    while apart < size:
        sent = over(((give if apart == 1 else low) * LOW_SCALE).astype(jnp.float16), apart)
        until = turns - 1 if 2 * apart == size else number + 1
        while number < min(until, turns - 1):
            last = turn(number, last)
            if number == 3:
                own, up_pages = own_terms(
                    dests, local, index, x, output_weight, adapter_up_weight, got_up, last
                )
                last = own
            number += 1
        apart *= 2
        zero = touch(last)[0, 0]
        sent = sent.astype(jnp.float32) * (1.0 / LOW_SCALE) + zero
        low = last = add(low, sent, jnp.float32 if apart < size else jnp.bfloat16, last)
    other = over(low, 1)
    last = turn(number, last)
    own = add_delta(sizes, side, own, up_pages, row_list_position, low, other, last)
    own = join(own, arrived[0, -1][0], arrived[1, 1][0])
    result = None
    for half, sign, _ in pairs[0]:
        result = finish(live_row_count.reshape(-1), half, own, arrived[half, sign][0], result)
    return result.reshape(steps, row_count, -1)


def solution(mesh):
    in_specs = (
        P(None, ("grp", "inst"), "tp"),
        P("tp", None),
        P("inst", None, "tp"),
        P("inst", None, "tp"),
        P(),
        P(None, ("grp", "inst"), None),
        P(None, ("grp", "inst")),
        P(None, ("grp", "inst")),
    )
    out_specs = P(None, ("grp", "inst"), "tp")
    return jax.shard_map(
        functools.partial(per_device, mesh.shape["tp"]),
        mesh=mesh, in_specs=in_specs, out_specs=out_specs, check_vma=False,
    )
```

```python
import functools

import jax
import jax.numpy as jnp
from jax import lax
from jax.experimental import pallas as pl
from jax.experimental.pallas import tpu as pltpu
from jax.sharding import PartitionSpec as P

VMEM_LIMIT = 40 * 1024 * 1024
FIRST_VMEM_LIMIT = 62 * 1024 * 1024
LOW_SCALE = 16.0
GRAIN = 16
SWAP = [(0, 1), (1, 0)]
WHOLE = pl.BlockSpec(memory_space=pltpu.VMEM)
ANYWHERE = pl.BlockSpec(memory_space=pl.ANY)


def serpentine(size):
    return size == 8


def ring_index(place, size):
    if not serpentine(size):
        return place
    return jnp.where(place < size // 2, 2 * place, 2 * (size - 1 - place) + 1)


def ring_place(index, size):
    if not serpentine(size):
        return index
    return jnp.where(index & 1 == 0, index >> 1, size - 1 - (index >> 1))


def ring_order(size):
    if not serpentine(size):
        return list(range(size))
    return list(range(0, size, 2)) + list(range(size - 1, 0, -2))


def params(limit=VMEM_LIMIT):
    return pltpu.CompilerParams(vmem_limit_bytes=limit)


def cost(flops, size):
    return pl.CostEstimate(flops=30 * flops, bytes_accessed=size, transcendentals=0)


def hop_kernel(pieces, dests, x_ref, w_ref, *refs):
    tile = w_ref.shape[1]
    now = pl.program_id(0)
    columns = pl.ds(pl.multiple_of(now * tile, tile), tile)
    total = jnp.dot(x_ref[...], w_ref[...], preferred_element_type=jnp.float32)
    out_ref = refs[-1]
    if len(pieces) == 1:
        out_ref[:, columns] = (total + refs[0][:, columns].astype(jnp.float32)).astype(
            out_ref.dtype
        )
    elif pieces:
        for piece, received_ref in zip(pieces, refs):

            @pl.when(now == piece)
            def _():
                out_ref[:, columns] = (total + received_ref[...].astype(jnp.float32)).astype(
                    out_ref.dtype
                )

    else:
        out_ref[:, columns] = total.astype(out_ref.dtype)


def tiling(dests, weight):
    half_cols = weight.shape[1] // dests.shape[0] // 2
    tile = min(256, half_cols)
    return half_cols, tile, half_cols // tile


def hop(dests, offset, half, x, weight, received, after):
    rows, depth = x.shape
    half_cols, tile, tiles = tiling(dests, weight)
    return pl.pallas_call(
        functools.partial(hop_kernel, tuple(range(len(received)))),
        grid_spec=pltpu.PrefetchScalarGridSpec(
            num_scalar_prefetch=1,
            grid=(tiles,),
            in_specs=[
                WHOLE,
                pl.BlockSpec(
                    (depth, tile), lambda j, d: (0, (d[offset] * 2 + half) * tiles + j)
                ),
            ]
            + [WHOLE] * len(received)
            + [ANYWHERE],
            out_specs=WHOLE,
        ),
        out_shape=jax.ShapeDtypeStruct((rows, half_cols), jnp.bfloat16),
        compiler_params=params(),
        cost_estimate=cost(
            2 * rows * depth * half_cols,
            2 * (rows * depth + depth * half_cols + 2 * rows * half_cols),
        ),
    )(dests, x, weight, *received, after)


def first_kernel(with_after, dests, x_ref, w_ref, *refs):
    total = jnp.dot(x_ref[...], w_ref[...], preferred_element_type=jnp.float32)
    refs[-1][...] = jnp.zeros_like(refs[-1])
    for chain, out_ref in enumerate(refs[-3:-1]):

        @pl.when(pl.program_id(0) == chain)
        def _():
            out_ref[...] = total.astype(out_ref.dtype)


def first_pieces(dests, offset, piece, x, weight, after):
    rows, depth = x.shape
    _, tile, tiles = tiling(dests, weight)
    size = dests.shape[0]

    def place(j, d):
        one = d[offset] * 2 * tiles + piece
        two = (d[(size - offset) % size] * 2 + 1) * tiles + piece
        return (0, jnp.where(j == 0, one, two))

    tail = [] if after is None else [after]
    return pl.pallas_call(
        functools.partial(first_kernel, after is not None),
        grid_spec=pltpu.PrefetchScalarGridSpec(
            num_scalar_prefetch=1,
            grid=(2,),
            in_specs=[
                pl.BlockSpec((rows, depth), lambda j, d: (0, 0)) if after is None else WHOLE,
                pl.BlockSpec((depth, tile), place),
            ]
            + [ANYWHERE] * len(tail),
            out_specs=[WHOLE, WHOLE, pl.BlockSpec((8, 128), lambda j, d: (0, 0))],
        ),
        out_shape=[jax.ShapeDtypeStruct((rows, tile), jnp.bfloat16)] * 2
        + [jax.ShapeDtypeStruct((8, 128), jnp.float32)],
        compiler_params=params(FIRST_VMEM_LIMIT if after is None else VMEM_LIMIT),
        cost_estimate=cost(
            4 * rows * depth * tile, 2 * (rows * depth + 2 * depth * tile + 2 * rows * tile)
        ),
    )(dests, x, weight, *tail)


def touch_kernel(*refs):
    refs[-1][...] = jnp.zeros_like(refs[-1])


def touch(*arrays):
    return pl.pallas_call(
        touch_kernel,
        in_specs=[ANYWHERE] * len(arrays),
        out_specs=WHOLE,
        out_shape=jax.ShapeDtypeStruct((8, 128), jnp.float32),
        compiler_params=params(),
    )(*arrays)


def collect_kernel(count, index, table_ref, after_ref, out_ref, sems):
    copies = [
        pltpu.make_async_copy(table_ref.at[index[slot]], out_ref.at[slot], sems.at[slot])
        for slot in range(count)
    ]
    for copy in copies:
        copy.start()
    for copy in copies:
        copy.wait()


def collect(index, table, after):
    count = index.shape[0]
    shape = (count,) + table.shape[1:]
    return pl.pallas_call(
        functools.partial(collect_kernel, count),
        grid_spec=pltpu.PrefetchScalarGridSpec(
            num_scalar_prefetch=1,
            grid=(1,),
            in_specs=[ANYWHERE, ANYWHERE],
            out_specs=WHOLE,
            scratch_shapes=[pltpu.SemaphoreType.DMA((count,))],
        ),
        out_shape=jax.ShapeDtypeStruct(shape, table.dtype),
        compiler_params=params(),
        cost_estimate=cost(0, 4 * shape[0] * shape[1] * shape[2]),
    )(index, table, after)


def start_pages(count, local, index, table_ref, got_ref, pages, sems):
    for slot in range(count):
        own = local[slot] == 1

        @pl.when(own)
        def _():
            pltpu.make_async_copy(
                table_ref.at[index[slot]], pages.at[slot], sems.at[slot]
            ).start()

        @pl.when(jnp.logical_not(own))
        def _():
            pltpu.make_async_copy(got_ref.at[slot], pages.at[slot], sems.at[slot]).start()


def wait_pages(slots, got_ref, pages, sems):
    for slot in slots:
        pltpu.make_async_copy(got_ref.at[slot], pages.at[slot], sems.at[slot]).wait()


def low_kernel(
    sizes, local, index, side, x_ref, place_ref, table_ref, got_ref, after_ref, keep_ref, give_ref,
    pages, sems,
):
    steps, blocks, listed, rank, block_rows = sizes
    half = steps * blocks // 2
    start_pages(steps * blocks * listed, local, index, table_ref, got_ref, pages, sems)
    for step in range(steps):
        for block in range(blocks):
            at = step * blocks + block
            wait_pages(range(at * listed, (at + 1) * listed), got_ref, pages, sems)
            listing = pages[at * listed : (at + 1) * listed].reshape(listed * rank, -1)
            every = lax.dot_general(
                listing, x_ref[at * block_rows : (at + 1) * block_rows, :],
                (((1,), (1,)), ((), ())), preferred_element_type=jnp.float32,
            )
            place = place_ref[step : step + 1, block * block_rows : (block + 1) * block_rows]
            low = jnp.zeros((rank, block_rows), jnp.float32)
            for entry in range(listed):
                low = jnp.where(place == entry, every[entry * rank : (entry + 1) * rank], low)
            rows = slice(at % half * block_rows, (at % half + 1) * block_rows)
            mine = side[0] == at // half

            @pl.when(mine)
            def _():
                keep_ref[:, rows] = low

            @pl.when(jnp.logical_not(mine))
            def _():
                give_ref[:, rows] = low


def low_rank(sizes, local, index, side, x, place, table, got, after):
    steps, blocks, listed, rank, block_rows = sizes
    count = steps * blocks * listed
    rows, depth = x.shape
    return pl.pallas_call(
        functools.partial(low_kernel, sizes),
        grid_spec=pltpu.PrefetchScalarGridSpec(
            num_scalar_prefetch=3,
            grid=(1,),
            in_specs=[WHOLE, WHOLE, ANYWHERE, ANYWHERE, ANYWHERE],
            out_specs=[WHOLE, WHOLE],
            scratch_shapes=[
                pltpu.VMEM((count, rank, depth), table.dtype),
                pltpu.SemaphoreType.DMA((count,)),
            ],
        ),
        out_shape=[jax.ShapeDtypeStruct((rank, rows // 2), jnp.float32)] * 2,
        compiler_params=params(),
        cost_estimate=cost(
            2 * rows * depth * listed * rank, 2 * (rows * depth + count * rank * depth)
        ),
    )(local, index, side, x, place, table, got, after)


def add_kernel(low_ref, sent_ref, after_ref, out_ref):
    out_ref[...] = (low_ref[...] + sent_ref[...]).astype(out_ref.dtype)


def add(low, sent, dtype, after):
    return pl.pallas_call(
        add_kernel,
        in_specs=[WHOLE, WHOLE, ANYWHERE],
        out_specs=WHOLE,
        out_shape=jax.ShapeDtypeStruct(low.shape, dtype),
        compiler_params=params(),
        cost_estimate=cost(low.size, 12 * low.size),
    )(low, sent, after)


def own_kernel(
    local, index, dests, x_ref, w_ref, table_ref, got_ref, after_ref, out_ref, pages, sems
):
    tile = w_ref.shape[1]
    now = pl.program_id(0)
    count = pages.shape[0]

    @pl.when(now == 0)
    def _():
        start_pages(count, local, index, table_ref, got_ref, pages, sems)

    columns = pl.ds(pl.multiple_of(now * tile, tile), tile)
    out_ref[:, columns] = jnp.dot(x_ref[...], w_ref[...], preferred_element_type=jnp.float32)

    @pl.when(now == pl.num_programs(0) - 1)
    def _():
        wait_pages(range(count), got_ref, pages, sems)


def own_terms(dests, local, index, x, weight, table, got, after):
    count, rank, cols = got.shape
    rows, depth = x.shape
    tile = min(256, cols)
    tiles = cols // tile
    return pl.pallas_call(
        own_kernel,
        grid_spec=pltpu.PrefetchScalarGridSpec(
            num_scalar_prefetch=3,
            grid=(tiles,),
            in_specs=[
                WHOLE,
                pl.BlockSpec((depth, tile), lambda j, l, i, d: (0, d[0] * tiles + j)),
                ANYWHERE,
                ANYWHERE,
                ANYWHERE,
            ],
            out_specs=[WHOLE, WHOLE],
            scratch_shapes=[pltpu.SemaphoreType.DMA((count,))],
        ),
        out_shape=[
            jax.ShapeDtypeStruct((rows, cols), jnp.float32),
            jax.ShapeDtypeStruct((count, rank, cols), table.dtype),
        ],
        compiler_params=params(),
        cost_estimate=cost(
            2 * rows * cols * depth,
            2 * (rows * depth + depth * cols + 2 * count * rank * cols) + 4 * rows * cols,
        ),
    )(local, index, dests, x, weight, table, got, after)


def delta_kernel(
    sizes, side, own_ref, pages_ref, place_ref, low_ref, other_ref, after_ref, out_ref
):
    steps, blocks, listed, rank, block_rows = sizes
    half = steps * blocks // 2
    entry_of = lax.broadcasted_iota(jnp.int32, (listed * rank, block_rows), 0) // rank
    for step in range(steps):
        for block in range(blocks):
            at = step * blocks + block
            rows = slice(at * block_rows, (at + 1) * block_rows)
            in_half = slice(at % half * block_rows, (at % half + 1) * block_rows)
            low = jnp.where(
                side[0] == at // half,
                low_ref[:, in_half].astype(jnp.float32),
                other_ref[:, in_half].astype(jnp.float32),
            )
            spread = jnp.concatenate([low] * listed, axis=0)
            place = place_ref[step : step + 1, block * block_rows : (block + 1) * block_rows]
            spread = jnp.where(entry_of == place, spread, 0.0)
            listing = pages_ref[at * listed : (at + 1) * listed].reshape(listed * rank, -1)
            out_ref[rows, :] = own_ref[rows, :] + jnp.dot(
                spread.T.astype(jnp.bfloat16), listing, preferred_element_type=jnp.float32
            )


def add_delta(sizes, side, own, pages, place, low, other, after):
    rows, cols = own.shape
    return pl.pallas_call(
        functools.partial(delta_kernel, sizes),
        grid_spec=pltpu.PrefetchScalarGridSpec(
            num_scalar_prefetch=1,
            grid=(1,),
            in_specs=[WHOLE] * 5 + [ANYWHERE],
            out_specs=WHOLE,
        ),
        out_shape=jax.ShapeDtypeStruct(own.shape, own.dtype),
        compiler_params=params(),
        cost_estimate=cost(
            2 * rows * cols * sizes[2] * sizes[3], 8 * rows * cols + 2 * pages.size
        ),
    )(side, own, pages, place, low, other, after)


def chunks(count):
    size = 32 if count % 32 == 0 else GRAIN
    return [slice(at, at + size) for at in range(0, count, size)]


def join_kernel(own_ref, left_ref, right_ref, out_ref):
    cols = left_ref.shape[1]
    for rows in chunks(own_ref.shape[0]):
        for at, part_ref in ((0, left_ref), (cols, right_ref)):
            out_ref[rows, at : at + cols] = own_ref[rows, at : at + cols] + part_ref[
                rows, :
            ].astype(jnp.float32)


def join(own, left, right):
    return pl.pallas_call(
        join_kernel,
        in_specs=[WHOLE] * 3,
        out_specs=WHOLE,
        out_shape=jax.ShapeDtypeStruct(own.shape, own.dtype),
        compiler_params=params(),
        cost_estimate=cost(own.size, 10 * own.size),
    )(own, left, right)


def finish_kernel(half, live, own_ref, last_ref, *refs):
    out_ref, held, sems = refs[-3:]
    rows, cols = held.shape
    count = rows // live.shape[0]
    columns = slice(half * cols, (half + 1) * cols)
    part = rows // sems.shape[0]
    copies = []
    for at in range(sems.shape[0]):
        for chunk in chunks(part):
            here = slice(at * part + chunk.start, at * part + chunk.stop)
            total = own_ref[here, columns] + last_ref[here, :].astype(jnp.float32)
            row = here.start % count + lax.broadcasted_iota(jnp.int32, total.shape, 0)
            alive = row < live[here.start // count]
            held[here, :] = jnp.where(alive, total, 0.0).astype(held.dtype)
        rows_at = pl.ds(at * part, part)
        copies.append(
            pltpu.make_async_copy(held.at[rows_at], out_ref.at[rows_at, columns], sems.at[at])
        )
        copies[-1].start()
    for copy in copies:
        copy.wait()


def finish(live, half, own, last, result):
    rows, cols = own.shape
    steps = live.shape[0]
    in_specs = [WHOLE, WHOLE]
    operands = [own, last]
    aliases = {}
    if result is not None:
        in_specs.append(ANYWHERE)
        operands.append(result)
        aliases = {3: 0}
    return pl.pallas_call(
        functools.partial(finish_kernel, half),
        grid_spec=pltpu.PrefetchScalarGridSpec(
            num_scalar_prefetch=1,
            grid=(1,),
            in_specs=in_specs,
            out_specs=ANYWHERE,
            scratch_shapes=[
                pltpu.VMEM((rows, cols // 2), jnp.bfloat16),
                pltpu.SemaphoreType.DMA((2 * steps,)),
            ],
        ),
        out_shape=jax.ShapeDtypeStruct((rows, cols), jnp.bfloat16),
        input_output_aliases=aliases,
        compiler_params=params(),
        cost_estimate=cost(0, rows * cols * 5),
    )(live, *operands)


def per_device(
    size,
    attention_output,
    output_weight,
    adapter_down_weight,
    adapter_up_weight,
    adapter_page_table,
    block_adapter_ids,
    row_list_position,
    live_row_count,
):
    steps, row_count, depth = attention_output.shape
    resident, rank, _ = adapter_down_weight.shape
    _, blocks, listed = block_adapter_ids.shape
    sizes = (steps, blocks, listed, rank, row_count // blocks)
    x = attention_output.reshape(steps * row_count, depth)
    ring = ring_order(size)

    instance = lax.axis_index("inst")
    place = ring_place(lax.axis_index("tp"), size)
    dests = ring_index(lax.rem(place + jnp.arange(size, dtype=jnp.int32), size), size)

    forward = [(ring[i], ring[(i + 1) % size]) for i in range(size)]
    backward = [(ring[i], ring[i - 1]) for i in range(size)]
    far = size // 2
    pairs = [[(0, 1, forward), (1, -1, backward)], [(1, 1, forward), (0, -1, backward)]]
    arrived = {}

    def turn(number, last, between=None):
        left = far - (number + 1) // 2
        for half, sign, moves in pairs[number % 2]:
            last = hop(
                dests, (sign * left) % size, half, x, output_weight,
                arrived.get((half, sign), []), last,
            )
            arrived[half, sign] = [lax.ppermute(last, "tp", moves)]
            if between is not None:
                last, between = touch(between, last), None
        return last

    ids = block_adapter_ids.reshape(-1)
    ids_there = lax.ppermute(block_adapter_ids, "inst", SWAP).reshape(-1)
    last = None
    for piece in range(tiling(dests, output_weight)[2]):
        *both, last = first_pieces(dests, far % size, piece, x, output_weight, last)
        for (half, sign, moves), part in zip(pairs[0], both):
            arrived.setdefault((half, sign), []).append(lax.ppermute(part, "tp", moves))
    pages = adapter_page_table[jnp.concatenate([ids, ids_there])]
    places = pages % resident
    index, index_there = places[: ids.shape[0]], places[ids.shape[0] :]
    local = (pages[: ids.shape[0]] // resident == instance).astype(jnp.int32)
    last = collect(index_there, adapter_down_weight, last)
    got_down = lax.ppermute(last, "inst", SWAP)
    last = touch(last, *(arrived[half, sign][0] for half, sign, _ in pairs[0]))
    last = turn(1, last)
    last = collect(index_there, adapter_up_weight, last)
    got_up = lax.ppermute(last, "inst", SWAP)
    last = turn(2, last, got_down)
    side = (lax.axis_index("tp") & 1).reshape(1)
    low, give = low_rank(
        sizes, local, index, side, x, row_list_position, adapter_down_weight, got_down, last
    )
    last = touch(got_up, low)

    def over(value, apart):
        return lax.ppermute(value, "tp", [(i, i ^ apart) for i in range(size)])

    number, turns = 3, 2 * far - 1
    apart = 1
    while apart < size:
        sent = over(((give if apart == 1 else low) * LOW_SCALE).astype(jnp.float16), apart)
        until = turns - 1 if 2 * apart == size else number + 1
        while number < min(until, turns - 1):
            last = turn(number, last)
            if number == 3:
                own, up_pages = own_terms(
                    dests, local, index, x, output_weight, adapter_up_weight, got_up, last
                )
                last = own
            number += 1
        apart *= 2
        zero = touch(last)[0, 0]
        sent = sent.astype(jnp.float32) * (1.0 / LOW_SCALE) + zero
        low = last = add(low, sent, jnp.float32 if apart < size else jnp.bfloat16, last)
    other = over(low, 1)
    last = turn(number, last)
    own = add_delta(sizes, side, own, up_pages, row_list_position, low, other, last)
    own = join(own, arrived[0, -1][0], arrived[1, 1][0])
    result = None
    for half, sign, _ in pairs[0]:
        result = finish(live_row_count.reshape(-1), half, own, arrived[half, sign][0], result)
    return result.reshape(steps, row_count, -1)


def solution(mesh):
    in_specs = (
        P(None, ("grp", "inst"), "tp"),
        P("tp", None),
        P("inst", None, "tp"),
        P("inst", None, "tp"),
        P(),
        P(None, ("grp", "inst"), None),
        P(None, ("grp", "inst")),
        P(None, ("grp", "inst")),
    )
    out_specs = P(None, ("grp", "inst"), "tp")
    return jax.shard_map(
        functools.partial(per_device, mesh.shape["tp"]),
        mesh=mesh, in_specs=in_specs, out_specs=out_specs, check_vma=False,
    )
```

```python
import functools

import jax
import jax.numpy as jnp
from jax import lax
from jax.experimental import pallas as pl
from jax.experimental.pallas import tpu as pltpu
from jax.sharding import PartitionSpec as P

VMEM_LIMIT = 40 * 1024 * 1024
FIRST_VMEM_LIMIT = 62 * 1024 * 1024
LOW_SCALE = 16.0
GRAIN = 16
SWAP = [(0, 1), (1, 0)]
WHOLE = pl.BlockSpec(memory_space=pltpu.VMEM)
ANYWHERE = pl.BlockSpec(memory_space=pl.ANY)


def serpentine(size):
    return size == 8


def ring_index(place, size):
    if not serpentine(size):
        return place
    return jnp.where(place < size // 2, 2 * place, 2 * (size - 1 - place) + 1)


def ring_place(index, size):
    if not serpentine(size):
        return index
    return jnp.where(index & 1 == 0, index >> 1, size - 1 - (index >> 1))


def ring_order(size):
    if not serpentine(size):
        return list(range(size))
    return list(range(0, size, 2)) + list(range(size - 1, 0, -2))


def params(limit=VMEM_LIMIT):
    return pltpu.CompilerParams(vmem_limit_bytes=limit)


def cost(flops, size):
    return pl.CostEstimate(flops=30 * flops, bytes_accessed=size, transcendentals=0)


def hop_kernel(pieces, dests, x_ref, w_ref, *refs):
    tile = w_ref.shape[1]
    now = pl.program_id(0)
    columns = pl.ds(pl.multiple_of(now * tile, tile), tile)
    total = jnp.dot(x_ref[...], w_ref[...], preferred_element_type=jnp.float32)
    out_ref = refs[-1]
    if len(pieces) == 1:
        out_ref[:, columns] = (total + refs[0][:, columns].astype(jnp.float32)).astype(
            out_ref.dtype
        )
    elif pieces:
        for piece, received_ref in zip(pieces, refs):

            @pl.when(now == piece)
            def _():
                out_ref[:, columns] = (total + received_ref[...].astype(jnp.float32)).astype(
                    out_ref.dtype
                )

    else:
        out_ref[:, columns] = total.astype(out_ref.dtype)


def tiling(dests, weight):
    half_cols = weight.shape[1] // dests.shape[0] // 2
    tile = min(256, half_cols)
    return half_cols, tile, half_cols // tile


def hop(dests, offset, half, x, weight, received, after):
    rows, depth = x.shape
    half_cols, tile, tiles = tiling(dests, weight)
    return pl.pallas_call(
        functools.partial(hop_kernel, tuple(range(len(received)))),
        grid_spec=pltpu.PrefetchScalarGridSpec(
            num_scalar_prefetch=1,
            grid=(tiles,),
            in_specs=[
                WHOLE,
                pl.BlockSpec(
                    (depth, tile), lambda j, d: (0, (d[offset] * 2 + half) * tiles + j)
                ),
            ]
            + [WHOLE] * len(received)
            + [ANYWHERE],
            out_specs=WHOLE,
        ),
        out_shape=jax.ShapeDtypeStruct((rows, half_cols), jnp.bfloat16),
        compiler_params=params(),
        cost_estimate=cost(
            2 * rows * depth * half_cols,
            2 * (rows * depth + depth * half_cols + 2 * rows * half_cols),
        ),
    )(dests, x, weight, *received, after)


def first_kernel(with_after, dests, x_ref, w_ref, *refs):
    total = jnp.dot(x_ref[...], w_ref[...], preferred_element_type=jnp.float32)
    refs[-1][...] = jnp.zeros_like(refs[-1])
    for chain, out_ref in enumerate(refs[-3:-1]):

        @pl.when(pl.program_id(0) == chain)
        def _():
            out_ref[...] = total.astype(out_ref.dtype)


def first_pieces(dests, offset, piece, x, weight, after):
    rows, depth = x.shape
    _, tile, tiles = tiling(dests, weight)
    size = dests.shape[0]

    def place(j, d):
        one = d[offset] * 2 * tiles + piece
        two = (d[(size - offset) % size] * 2 + 1) * tiles + piece
        return (0, jnp.where(j == 0, one, two))

    tail = [] if after is None else [after]
    return pl.pallas_call(
        functools.partial(first_kernel, after is not None),
        grid_spec=pltpu.PrefetchScalarGridSpec(
            num_scalar_prefetch=1,
            grid=(2,),
            in_specs=[
                pl.BlockSpec((rows, depth), lambda j, d: (0, 0)) if after is None else WHOLE,
                pl.BlockSpec((depth, tile), place),
            ]
            + [ANYWHERE] * len(tail),
            out_specs=[WHOLE, WHOLE, pl.BlockSpec((8, 128), lambda j, d: (0, 0))],
        ),
        out_shape=[jax.ShapeDtypeStruct((rows, tile), jnp.bfloat16)] * 2
        + [jax.ShapeDtypeStruct((8, 128), jnp.float32)],
        compiler_params=params(FIRST_VMEM_LIMIT if after is None else VMEM_LIMIT),
        cost_estimate=cost(
            4 * rows * depth * tile, 2 * (rows * depth + 2 * depth * tile + 2 * rows * tile)
        ),
    )(dests, x, weight, *tail)


def touch_kernel(*refs):
    refs[-1][...] = jnp.zeros_like(refs[-1])


def touch(*arrays):
    return pl.pallas_call(
        touch_kernel,
        in_specs=[ANYWHERE] * len(arrays),
        out_specs=WHOLE,
        out_shape=jax.ShapeDtypeStruct((8, 128), jnp.float32),
        compiler_params=params(),
    )(*arrays)


def collect_kernel(count, index, table_ref, after_ref, out_ref, sems):
    copies = [
        pltpu.make_async_copy(table_ref.at[index[slot]], out_ref.at[slot], sems.at[slot])
        for slot in range(count)
    ]
    for copy in copies:
        copy.start()
    for copy in copies:
        copy.wait()


def collect(index, table, after):
    count = index.shape[0]
    shape = (count,) + table.shape[1:]
    return pl.pallas_call(
        functools.partial(collect_kernel, count),
        grid_spec=pltpu.PrefetchScalarGridSpec(
            num_scalar_prefetch=1,
            grid=(1,),
            in_specs=[ANYWHERE, ANYWHERE],
            out_specs=WHOLE,
            scratch_shapes=[pltpu.SemaphoreType.DMA((count,))],
        ),
        out_shape=jax.ShapeDtypeStruct(shape, table.dtype),
        compiler_params=params(),
        cost_estimate=cost(0, 4 * shape[0] * shape[1] * shape[2]),
    )(index, table, after)


def start_pages(count, local, index, table_ref, got_ref, pages, sems):
    for slot in range(count):
        own = local[slot] == 1

        @pl.when(own)
        def _():
            pltpu.make_async_copy(
                table_ref.at[index[slot]], pages.at[slot], sems.at[slot]
            ).start()

        @pl.when(jnp.logical_not(own))
        def _():
            pltpu.make_async_copy(got_ref.at[slot], pages.at[slot], sems.at[slot]).start()


def wait_pages(slots, got_ref, pages, sems):
    for slot in slots:
        pltpu.make_async_copy(got_ref.at[slot], pages.at[slot], sems.at[slot]).wait()


def low_kernel(
    sizes, local, index, side, x_ref, place_ref, table_ref, got_ref, after_ref, keep_ref, give_ref,
    pages, sems,
):
    steps, blocks, listed, rank, block_rows = sizes
    half = steps * blocks // 2
    start_pages(steps * blocks * listed, local, index, table_ref, got_ref, pages, sems)
    for step in range(steps):
        for block in range(blocks):
            at = step * blocks + block
            wait_pages(range(at * listed, (at + 1) * listed), got_ref, pages, sems)
            listing = pages[at * listed : (at + 1) * listed].reshape(listed * rank, -1)
            every = lax.dot_general(
                listing, x_ref[at * block_rows : (at + 1) * block_rows, :],
                (((1,), (1,)), ((), ())), preferred_element_type=jnp.float32,
            )
            place = place_ref[step : step + 1, block * block_rows : (block + 1) * block_rows]
            low = jnp.zeros((rank, block_rows), jnp.float32)
            for entry in range(listed):
                low = jnp.where(place == entry, every[entry * rank : (entry + 1) * rank], low)
            rows = slice(at % half * block_rows, (at % half + 1) * block_rows)
            mine = side[0] == at // half

            @pl.when(mine)
            def _():
                keep_ref[:, rows] = low

            @pl.when(jnp.logical_not(mine))
            def _():
                give_ref[:, rows] = low


def low_rank(sizes, local, index, side, x, place, table, got, after):
    steps, blocks, listed, rank, block_rows = sizes
    count = steps * blocks * listed
    rows, depth = x.shape
    return pl.pallas_call(
        functools.partial(low_kernel, sizes),
        grid_spec=pltpu.PrefetchScalarGridSpec(
            num_scalar_prefetch=3,
            grid=(1,),
            in_specs=[WHOLE, WHOLE, ANYWHERE, ANYWHERE, ANYWHERE],
            out_specs=[WHOLE, WHOLE],
            scratch_shapes=[
                pltpu.VMEM((count, rank, depth), table.dtype),
                pltpu.SemaphoreType.DMA((count,)),
            ],
        ),
        out_shape=[jax.ShapeDtypeStruct((rank, rows // 2), jnp.float32)] * 2,
        compiler_params=params(),
        cost_estimate=cost(
            2 * rows * depth * listed * rank, 2 * (rows * depth + count * rank * depth)
        ),
    )(local, index, side, x, place, table, got, after)


def add_kernel(low_ref, sent_ref, after_ref, out_ref):
    out_ref[...] = (low_ref[...] + sent_ref[...]).astype(out_ref.dtype)


def add(low, sent, dtype, after):
    return pl.pallas_call(
        add_kernel,
        in_specs=[WHOLE, WHOLE, ANYWHERE],
        out_specs=WHOLE,
        out_shape=jax.ShapeDtypeStruct(low.shape, dtype),
        compiler_params=params(),
        cost_estimate=cost(low.size, 12 * low.size),
    )(low, sent, after)


def own_kernel(
    local, index, dests, x_ref, w_ref, table_ref, got_ref, after_ref, out_ref, pages, sems
):
    tile = w_ref.shape[1]
    now = pl.program_id(0)
    count = pages.shape[0]

    @pl.when(now == 0)
    def _():
        start_pages(count, local, index, table_ref, got_ref, pages, sems)

    columns = pl.ds(pl.multiple_of(now * tile, tile), tile)
    out_ref[:, columns] = jnp.dot(x_ref[...], w_ref[...], preferred_element_type=jnp.float32)

    @pl.when(now == pl.num_programs(0) - 1)
    def _():
        wait_pages(range(count), got_ref, pages, sems)


def own_terms(dests, local, index, x, weight, table, got, after):
    count, rank, cols = got.shape
    rows, depth = x.shape
    tile = min(256, cols)
    tiles = cols // tile
    return pl.pallas_call(
        own_kernel,
        grid_spec=pltpu.PrefetchScalarGridSpec(
            num_scalar_prefetch=3,
            grid=(tiles,),
            in_specs=[
                WHOLE,
                pl.BlockSpec((depth, tile), lambda j, l, i, d: (0, d[0] * tiles + j)),
                ANYWHERE,
                ANYWHERE,
                ANYWHERE,
            ],
            out_specs=[WHOLE, WHOLE],
            scratch_shapes=[pltpu.SemaphoreType.DMA((count,))],
        ),
        out_shape=[
            jax.ShapeDtypeStruct((rows, cols), jnp.float32),
            jax.ShapeDtypeStruct((count, rank, cols), table.dtype),
        ],
        compiler_params=params(),
        cost_estimate=cost(
            2 * rows * cols * depth,
            2 * (rows * depth + depth * cols + 2 * count * rank * cols) + 4 * rows * cols,
        ),
    )(local, index, dests, x, weight, table, got, after)


def delta_kernel(
    sizes, side, own_ref, pages_ref, place_ref, low_ref, other_ref, after_ref, out_ref
):
    steps, blocks, listed, rank, block_rows = sizes
    half = steps * blocks // 2
    entry_of = lax.broadcasted_iota(jnp.int32, (listed * rank, block_rows), 0) // rank
    for step in range(steps):
        for block in range(blocks):
            at = step * blocks + block
            rows = slice(at * block_rows, (at + 1) * block_rows)
            in_half = slice(at % half * block_rows, (at % half + 1) * block_rows)
            low = jnp.where(
                side[0] == at // half,
                low_ref[:, in_half].astype(jnp.float32),
                other_ref[:, in_half].astype(jnp.float32),
            )
            spread = jnp.concatenate([low] * listed, axis=0)
            place = place_ref[step : step + 1, block * block_rows : (block + 1) * block_rows]
            spread = jnp.where(entry_of == place, spread, 0.0)
            listing = pages_ref[at * listed : (at + 1) * listed].reshape(listed * rank, -1)
            out_ref[rows, :] = own_ref[rows, :] + jnp.dot(
                spread.T.astype(jnp.bfloat16), listing, preferred_element_type=jnp.float32
            )


def add_delta(sizes, side, own, pages, place, low, other, after):
    rows, cols = own.shape
    return pl.pallas_call(
        functools.partial(delta_kernel, sizes),
        grid_spec=pltpu.PrefetchScalarGridSpec(
            num_scalar_prefetch=1,
            grid=(1,),
            in_specs=[WHOLE] * 5 + [ANYWHERE],
            out_specs=WHOLE,
        ),
        out_shape=jax.ShapeDtypeStruct(own.shape, own.dtype),
        compiler_params=params(),
        cost_estimate=cost(
            2 * rows * cols * sizes[2] * sizes[3], 8 * rows * cols + 2 * pages.size
        ),
    )(side, own, pages, place, low, other, after)


def chunks(count):
    size = 32 if count % 32 == 0 else GRAIN
    return [slice(at, at + size) for at in range(0, count, size)]


def join_kernel(own_ref, left_ref, right_ref, out_ref):
    cols = left_ref.shape[1]
    for rows in chunks(own_ref.shape[0]):
        for at, part_ref in ((0, left_ref), (cols, right_ref)):
            out_ref[rows, at : at + cols] = own_ref[rows, at : at + cols] + part_ref[
                rows, :
            ].astype(jnp.float32)


def join(own, left, right):
    return pl.pallas_call(
        join_kernel,
        in_specs=[WHOLE] * 3,
        out_specs=WHOLE,
        out_shape=jax.ShapeDtypeStruct(own.shape, own.dtype),
        compiler_params=params(),
        cost_estimate=cost(own.size, 10 * own.size),
    )(own, left, right)


def finish_kernel(half, live, own_ref, last_ref, *refs):
    out_ref, held, sems = refs[-3:]
    rows, cols = held.shape
    count = rows // live.shape[0]
    columns = slice(half * cols, (half + 1) * cols)
    part = rows // sems.shape[0]
    copies = []
    for at in range(sems.shape[0]):
        for chunk in chunks(part):
            here = slice(at * part + chunk.start, at * part + chunk.stop)
            total = own_ref[here, columns] + last_ref[here, :].astype(jnp.float32)
            row = here.start % count + lax.broadcasted_iota(jnp.int32, total.shape, 0)
            alive = row < live[here.start // count]
            held[here, :] = jnp.where(alive, total, 0.0).astype(held.dtype)
        rows_at = pl.ds(at * part, part)
        copies.append(
            pltpu.make_async_copy(held.at[rows_at], out_ref.at[rows_at, columns], sems.at[at])
        )
        copies[-1].start()
    for copy in copies:
        copy.wait()


def finish(live, half, own, last, result):
    rows, cols = own.shape
    steps = live.shape[0]
    in_specs = [WHOLE, WHOLE]
    operands = [own, last]
    aliases = {}
    if result is not None:
        in_specs.append(ANYWHERE)
        operands.append(result)
        aliases = {3: 0}
    return pl.pallas_call(
        functools.partial(finish_kernel, half),
        grid_spec=pltpu.PrefetchScalarGridSpec(
            num_scalar_prefetch=1,
            grid=(1,),
            in_specs=in_specs,
            out_specs=ANYWHERE,
            scratch_shapes=[
                pltpu.VMEM((rows, cols // 2), jnp.bfloat16),
                pltpu.SemaphoreType.DMA((2 * steps,)),
            ],
        ),
        out_shape=jax.ShapeDtypeStruct((rows, cols), jnp.bfloat16),
        input_output_aliases=aliases,
        compiler_params=params(),
        cost_estimate=cost(0, rows * cols * 5),
    )(live, *operands)


def per_device(
    size,
    attention_output,
    output_weight,
    adapter_down_weight,
    adapter_up_weight,
    adapter_page_table,
    block_adapter_ids,
    row_list_position,
    live_row_count,
):
    steps, row_count, depth = attention_output.shape
    resident, rank, _ = adapter_down_weight.shape
    _, blocks, listed = block_adapter_ids.shape
    sizes = (steps, blocks, listed, rank, row_count // blocks)
    x = attention_output.reshape(steps * row_count, depth)
    ring = ring_order(size)

    instance = lax.axis_index("inst")
    place = ring_place(lax.axis_index("tp"), size)
    dests = ring_index(lax.rem(place + jnp.arange(size, dtype=jnp.int32), size), size)

    forward = [(ring[i], ring[(i + 1) % size]) for i in range(size)]
    backward = [(ring[i], ring[i - 1]) for i in range(size)]
    far = size // 2
    pairs = [[(0, 1, forward), (1, -1, backward)], [(1, 1, forward), (0, -1, backward)]]
    arrived = {}

    def turn(number, last, between=None):
        left = far - (number + 1) // 2
        for half, sign, moves in pairs[number % 2]:
            last = hop(
                dests, (sign * left) % size, half, x, output_weight,
                arrived.get((half, sign), []), last,
            )
            arrived[half, sign] = [lax.ppermute(last, "tp", moves)]
            if between is not None:
                last, between = touch(between, last), None
        return last

    ids = block_adapter_ids.reshape(-1)
    ids_there = lax.ppermute(block_adapter_ids, "inst", SWAP).reshape(-1)
    last = None
    for piece in range(tiling(dests, output_weight)[2]):
        *both, last = first_pieces(dests, far % size, piece, x, output_weight, last)
        for (half, sign, moves), part in zip(pairs[0], both):
            arrived.setdefault((half, sign), []).append(lax.ppermute(part, "tp", moves))
    pages = adapter_page_table[jnp.concatenate([ids, ids_there])]
    places = pages % resident
    index, index_there = places[: ids.shape[0]], places[ids.shape[0] :]
    local = (pages[: ids.shape[0]] // resident == instance).astype(jnp.int32)
    last = collect(index_there, adapter_down_weight, last)
    got_down = lax.ppermute(last, "inst", SWAP)
    last = touch(last, *(arrived[half, sign][0] for half, sign, _ in pairs[0]))
    last = turn(1, last)
    side = (lax.axis_index("tp") & 1).reshape(1)
    low, give = low_rank(
        sizes, local, index, side, x, row_list_position, adapter_down_weight, got_down, last
    )
    last = low

    def over(value, apart):
        return lax.ppermute(value, "tp", [(i, i ^ apart) for i in range(size)])

    number, turns = 2, 2 * far - 1
    apart = 1
    while apart < size:
        sent = over(((give if apart == 1 else low) * LOW_SCALE).astype(jnp.float16), apart)
        until = turns - 1 if 2 * apart == size else number + 1
        while number < min(until, turns - 1):
            last = turn(number, last)
            if number == 4:
                last = collect(index_there, adapter_up_weight, last)
                got_up = lax.ppermute(last, "inst", SWAP)
            if number == 5:
                own, up_pages = own_terms(
                    dests, local, index, x, output_weight, adapter_up_weight, got_up, last
                )
                last = own
            number += 1
        apart *= 2
        zero = touch(last)[0, 0]
        sent = sent.astype(jnp.float32) * (1.0 / LOW_SCALE) + zero
        low = last = add(low, sent, jnp.float32 if apart < size else jnp.bfloat16, last)
    other = over(low, 1)
    last = turn(number, last)
    own = add_delta(sizes, side, own, up_pages, row_list_position, low, other, last)
    own = join(own, arrived[0, -1][0], arrived[1, 1][0])
    result = None
    for half, sign, _ in pairs[0]:
        result = finish(live_row_count.reshape(-1), half, own, arrived[half, sign][0], result)
    return result.reshape(steps, row_count, -1)


def solution(mesh):
    in_specs = (
        P(None, ("grp", "inst"), "tp"),
        P("tp", None),
        P("inst", None, "tp"),
        P("inst", None, "tp"),
        P(),
        P(None, ("grp", "inst"), None),
        P(None, ("grp", "inst")),
        P(None, ("grp", "inst")),
    )
    out_specs = P(None, ("grp", "inst"), "tp")
    return jax.shard_map(
        functools.partial(per_device, mesh.shape["tp"]),
        mesh=mesh, in_specs=in_specs, out_specs=out_specs, check_vma=False,
    )
```

```python
import functools

import jax
import jax.numpy as jnp
from jax import lax
from jax.experimental import pallas as pl
from jax.experimental.pallas import tpu as pltpu
from jax.sharding import PartitionSpec as P

VMEM_LIMIT = 40 * 1024 * 1024
FIRST_VMEM_LIMIT = 62 * 1024 * 1024
LOW_SCALE = 16.0
GRAIN = 16
SWAP = [(0, 1), (1, 0)]
WHOLE = pl.BlockSpec(memory_space=pltpu.VMEM)
ANYWHERE = pl.BlockSpec(memory_space=pl.ANY)


def serpentine(size):
    return size == 8


def ring_index(place, size):
    if not serpentine(size):
        return place
    return jnp.where(place < size // 2, 2 * place, 2 * (size - 1 - place) + 1)


def ring_place(index, size):
    if not serpentine(size):
        return index
    return jnp.where(index & 1 == 0, index >> 1, size - 1 - (index >> 1))


def ring_order(size):
    if not serpentine(size):
        return list(range(size))
    return list(range(0, size, 2)) + list(range(size - 1, 0, -2))


def params(limit=VMEM_LIMIT):
    return pltpu.CompilerParams(vmem_limit_bytes=limit)


def cost(flops, size):
    return pl.CostEstimate(flops=30 * flops, bytes_accessed=size, transcendentals=0)


def hop_kernel(pieces, dests, x_ref, w_ref, *refs):
    tile = w_ref.shape[1]
    now = pl.program_id(0)
    columns = pl.ds(pl.multiple_of(now * tile, tile), tile)
    total = jnp.dot(x_ref[...], w_ref[...], preferred_element_type=jnp.float32)
    out_ref = refs[-1]
    if len(pieces) == 1:
        out_ref[:, columns] = (total + refs[0][:, columns].astype(jnp.float32)).astype(
            out_ref.dtype
        )
    elif pieces:
        for piece, received_ref in zip(pieces, refs):

            @pl.when(now == piece)
            def _():
                out_ref[:, columns] = (total + received_ref[...].astype(jnp.float32)).astype(
                    out_ref.dtype
                )

    else:
        out_ref[:, columns] = total.astype(out_ref.dtype)


def tiling(dests, weight):
    half_cols = weight.shape[1] // dests.shape[0] // 2
    tile = min(256, half_cols)
    return half_cols, tile, half_cols // tile


def hop(dests, offset, half, x, weight, received, after):
    rows, depth = x.shape
    half_cols, tile, tiles = tiling(dests, weight)
    return pl.pallas_call(
        functools.partial(hop_kernel, tuple(range(len(received)))),
        grid_spec=pltpu.PrefetchScalarGridSpec(
            num_scalar_prefetch=1,
            grid=(tiles,),
            in_specs=[
                WHOLE,
                pl.BlockSpec(
                    (depth, tile), lambda j, d: (0, (d[offset] * 2 + half) * tiles + j)
                ),
            ]
            + [WHOLE] * len(received)
            + [ANYWHERE],
            out_specs=WHOLE,
        ),
        out_shape=jax.ShapeDtypeStruct((rows, half_cols), jnp.bfloat16),
        compiler_params=params(),
        cost_estimate=cost(
            2 * rows * depth * half_cols,
            2 * (rows * depth + depth * half_cols + 2 * rows * half_cols),
        ),
    )(dests, x, weight, *received, after)


def first_kernel(dests, x_ref, w_ref, *refs):
    *out_refs, token_ref, held = refs
    total = jnp.dot(x_ref[...], w_ref[...], preferred_element_type=jnp.float32)
    token_ref[...] = jnp.zeros_like(token_ref)
    part, chain = pl.program_id(0), pl.program_id(1)

    @pl.when(part == 0)
    def _():
        held[chain] = total

    for number, out_ref in enumerate(out_refs):

        @pl.when((part == 1) & (chain == number))
        def _():
            out_ref[...] = (held[number] + total).astype(out_ref.dtype)


def first_pieces(dests, offset, x, weight):
    rows, depth = x.shape
    _, tile, tiles = tiling(dests, weight)
    size = dests.shape[0]

    def place(k, j, d):
        one = d[offset] * 2 * tiles
        two = (d[(size - offset) % size] * 2 + 1) * tiles
        return (k, jnp.where(j == 0, one, two))

    return pl.pallas_call(
        first_kernel,
        grid_spec=pltpu.PrefetchScalarGridSpec(
            num_scalar_prefetch=1,
            grid=(2, 2),
            in_specs=[
                pl.BlockSpec((rows, depth // 2), lambda k, j, d: (0, k)),
                pl.BlockSpec((depth // 2, tile), place),
            ],
            out_specs=[WHOLE, WHOLE, pl.BlockSpec((8, 128), lambda k, j, d: (0, 0))],
            scratch_shapes=[pltpu.VMEM((2, rows, tile), jnp.float32)],
        ),
        out_shape=[jax.ShapeDtypeStruct((rows, tile), jnp.bfloat16)] * 2
        + [jax.ShapeDtypeStruct((8, 128), jnp.float32)],
        compiler_params=params(FIRST_VMEM_LIMIT),
        cost_estimate=cost(
            4 * rows * depth * tile, 2 * (rows * depth + 2 * depth * tile + 2 * rows * tile)
        ),
    )(dests, x, weight)


def next_kernel(dests, x_ref, w_ref, after_ref, *out_refs):
    total = jnp.dot(x_ref[...], w_ref[...], preferred_element_type=jnp.float32)
    for chain, out_ref in enumerate(out_refs):

        @pl.when(pl.program_id(0) == chain)
        def _():
            out_ref[...] = total.astype(out_ref.dtype)


def next_pieces(dests, offset, piece, x, weight, after):
    rows, depth = x.shape
    _, tile, tiles = tiling(dests, weight)
    size = dests.shape[0]

    def place(j, d):
        one = d[offset] * 2 * tiles + piece
        two = (d[(size - offset) % size] * 2 + 1) * tiles + piece
        return (0, jnp.where(j == 0, one, two))

    return pl.pallas_call(
        next_kernel,
        grid_spec=pltpu.PrefetchScalarGridSpec(
            num_scalar_prefetch=1,
            grid=(2,),
            in_specs=[WHOLE, pl.BlockSpec((depth, tile), place), ANYWHERE],
            out_specs=[WHOLE, WHOLE],
        ),
        out_shape=[jax.ShapeDtypeStruct((rows, tile), jnp.bfloat16)] * 2,
        compiler_params=params(),
        cost_estimate=cost(
            4 * rows * depth * tile, 2 * (rows * depth + 2 * depth * tile + 2 * rows * tile)
        ),
    )(dests, x, weight, after)


def touch_kernel(*refs):
    refs[-1][...] = jnp.zeros_like(refs[-1])


def touch(*arrays):
    return pl.pallas_call(
        touch_kernel,
        in_specs=[ANYWHERE] * len(arrays),
        out_specs=WHOLE,
        out_shape=jax.ShapeDtypeStruct((8, 128), jnp.float32),
        compiler_params=params(),
    )(*arrays)


def collect_kernel(count, index, table_ref, after_ref, out_ref, sems):
    copies = [
        pltpu.make_async_copy(table_ref.at[index[slot]], out_ref.at[slot], sems.at[slot])
        for slot in range(count)
    ]
    for copy in copies:
        copy.start()
    for copy in copies:
        copy.wait()


def collect(index, table, after):
    count = index.shape[0]
    shape = (count,) + table.shape[1:]
    return pl.pallas_call(
        functools.partial(collect_kernel, count),
        grid_spec=pltpu.PrefetchScalarGridSpec(
            num_scalar_prefetch=1,
            grid=(1,),
            in_specs=[ANYWHERE, ANYWHERE],
            out_specs=WHOLE,
            scratch_shapes=[pltpu.SemaphoreType.DMA((count,))],
        ),
        out_shape=jax.ShapeDtypeStruct(shape, table.dtype),
        compiler_params=params(),
        cost_estimate=cost(0, 4 * shape[0] * shape[1] * shape[2]),
    )(index, table, after)


def start_pages(count, local, index, table_ref, got_ref, pages, sems):
    for slot in range(count):
        own = local[slot] == 1

        @pl.when(own)
        def _():
            pltpu.make_async_copy(
                table_ref.at[index[slot]], pages.at[slot], sems.at[slot]
            ).start()

        @pl.when(jnp.logical_not(own))
        def _():
            pltpu.make_async_copy(got_ref.at[slot], pages.at[slot], sems.at[slot]).start()


def wait_pages(slots, got_ref, pages, sems):
    for slot in slots:
        pltpu.make_async_copy(got_ref.at[slot], pages.at[slot], sems.at[slot]).wait()


def low_kernel(
    sizes, local, index, side, x_ref, place_ref, table_ref, got_ref, after_ref, keep_ref, give_ref,
    pages, sems,
):
    steps, blocks, listed, rank, block_rows = sizes
    half = steps * blocks // 2
    start_pages(steps * blocks * listed, local, index, table_ref, got_ref, pages, sems)
    for step in range(steps):
        for block in range(blocks):
            at = step * blocks + block
            wait_pages(range(at * listed, (at + 1) * listed), got_ref, pages, sems)
            listing = pages[at * listed : (at + 1) * listed].reshape(listed * rank, -1)
            every = lax.dot_general(
                listing, x_ref[at * block_rows : (at + 1) * block_rows, :],
                (((1,), (1,)), ((), ())), preferred_element_type=jnp.float32,
            )
            place = place_ref[step : step + 1, block * block_rows : (block + 1) * block_rows]
            low = jnp.zeros((rank, block_rows), jnp.float32)
            for entry in range(listed):
                low = jnp.where(place == entry, every[entry * rank : (entry + 1) * rank], low)
            rows = slice(at % half * block_rows, (at % half + 1) * block_rows)
            mine = side[0] == at // half

            @pl.when(mine)
            def _():
                keep_ref[:, rows] = low

            @pl.when(jnp.logical_not(mine))
            def _():
                give_ref[:, rows] = low


def low_rank(sizes, local, index, side, x, place, table, got, after):
    steps, blocks, listed, rank, block_rows = sizes
    count = steps * blocks * listed
    rows, depth = x.shape
    return pl.pallas_call(
        functools.partial(low_kernel, sizes),
        grid_spec=pltpu.PrefetchScalarGridSpec(
            num_scalar_prefetch=3,
            grid=(1,),
            in_specs=[WHOLE, WHOLE, ANYWHERE, ANYWHERE, ANYWHERE],
            out_specs=[WHOLE, WHOLE],
            scratch_shapes=[
                pltpu.VMEM((count, rank, depth), table.dtype),
                pltpu.SemaphoreType.DMA((count,)),
            ],
        ),
        out_shape=[jax.ShapeDtypeStruct((rank, rows // 2), jnp.float32)] * 2,
        compiler_params=params(),
        cost_estimate=cost(
            2 * rows * depth * listed * rank, 2 * (rows * depth + count * rank * depth)
        ),
    )(local, index, side, x, place, table, got, after)


def add_kernel(low_ref, sent_ref, after_ref, out_ref):
    out_ref[...] = (low_ref[...] + sent_ref[...]).astype(out_ref.dtype)


def add(low, sent, dtype, after):
    return pl.pallas_call(
        add_kernel,
        in_specs=[WHOLE, WHOLE, ANYWHERE],
        out_specs=WHOLE,
        out_shape=jax.ShapeDtypeStruct(low.shape, dtype),
        compiler_params=params(),
        cost_estimate=cost(low.size, 12 * low.size),
    )(low, sent, after)


def own_kernel(
    local, index, dests, x_ref, w_ref, table_ref, got_ref, after_ref, out_ref, pages, sems
):
    tile = w_ref.shape[1]
    now = pl.program_id(0)
    count = pages.shape[0]

    @pl.when(now == 0)
    def _():
        start_pages(count, local, index, table_ref, got_ref, pages, sems)

    columns = pl.ds(pl.multiple_of(now * tile, tile), tile)
    out_ref[:, columns] = jnp.dot(x_ref[...], w_ref[...], preferred_element_type=jnp.float32)

    @pl.when(now == pl.num_programs(0) - 1)
    def _():
        wait_pages(range(count), got_ref, pages, sems)


def own_terms(dests, local, index, x, weight, table, got, after):
    count, rank, cols = got.shape
    rows, depth = x.shape
    tile = min(256, cols)
    tiles = cols // tile
    return pl.pallas_call(
        own_kernel,
        grid_spec=pltpu.PrefetchScalarGridSpec(
            num_scalar_prefetch=3,
            grid=(tiles,),
            in_specs=[
                WHOLE,
                pl.BlockSpec((depth, tile), lambda j, l, i, d: (0, d[0] * tiles + j)),
                ANYWHERE,
                ANYWHERE,
                ANYWHERE,
            ],
            out_specs=[WHOLE, WHOLE],
            scratch_shapes=[pltpu.SemaphoreType.DMA((count,))],
        ),
        out_shape=[
            jax.ShapeDtypeStruct((rows, cols), jnp.float32),
            jax.ShapeDtypeStruct((count, rank, cols), table.dtype),
        ],
        compiler_params=params(),
        cost_estimate=cost(
            2 * rows * cols * depth,
            2 * (rows * depth + depth * cols + 2 * count * rank * cols) + 4 * rows * cols,
        ),
    )(local, index, dests, x, weight, table, got, after)


def delta_kernel(
    sizes, side, own_ref, pages_ref, place_ref, low_ref, other_ref, after_ref, out_ref
):
    steps, blocks, listed, rank, block_rows = sizes
    half = steps * blocks // 2
    entry_of = lax.broadcasted_iota(jnp.int32, (listed * rank, block_rows), 0) // rank
    for step in range(steps):
        for block in range(blocks):
            at = step * blocks + block
            rows = slice(at * block_rows, (at + 1) * block_rows)
            in_half = slice(at % half * block_rows, (at % half + 1) * block_rows)
            low = jnp.where(
                side[0] == at // half,
                low_ref[:, in_half].astype(jnp.float32),
                other_ref[:, in_half].astype(jnp.float32),
            )
            spread = jnp.concatenate([low] * listed, axis=0)
            place = place_ref[step : step + 1, block * block_rows : (block + 1) * block_rows]
            spread = jnp.where(entry_of == place, spread, 0.0)
            listing = pages_ref[at * listed : (at + 1) * listed].reshape(listed * rank, -1)
            out_ref[rows, :] = own_ref[rows, :] + jnp.dot(
                spread.T.astype(jnp.bfloat16), listing, preferred_element_type=jnp.float32
            )


def add_delta(sizes, side, own, pages, place, low, other, after):
    rows, cols = own.shape
    return pl.pallas_call(
        functools.partial(delta_kernel, sizes),
        grid_spec=pltpu.PrefetchScalarGridSpec(
            num_scalar_prefetch=1,
            grid=(1,),
            in_specs=[WHOLE] * 5 + [ANYWHERE],
            out_specs=WHOLE,
        ),
        out_shape=jax.ShapeDtypeStruct(own.shape, own.dtype),
        compiler_params=params(),
        cost_estimate=cost(
            2 * rows * cols * sizes[2] * sizes[3], 8 * rows * cols + 2 * pages.size
        ),
    )(side, own, pages, place, low, other, after)


def chunks(count):
    size = 32 if count % 32 == 0 else GRAIN
    return [slice(at, at + size) for at in range(0, count, size)]


def join_kernel(own_ref, left_ref, right_ref, out_ref):
    cols = left_ref.shape[1]
    for rows in chunks(own_ref.shape[0]):
        for at, part_ref in ((0, left_ref), (cols, right_ref)):
            out_ref[rows, at : at + cols] = own_ref[rows, at : at + cols] + part_ref[
                rows, :
            ].astype(jnp.float32)


def join(own, left, right):
    return pl.pallas_call(
        join_kernel,
        in_specs=[WHOLE] * 3,
        out_specs=WHOLE,
        out_shape=jax.ShapeDtypeStruct(own.shape, own.dtype),
        compiler_params=params(),
        cost_estimate=cost(own.size, 10 * own.size),
    )(own, left, right)


def finish_kernel(live, own_ref, left_ref, right_ref, out_ref, held, sems):
    rows, cols = held.shape
    half = cols // 2
    count = rows // live.shape[0]
    part = rows // sems.shape[0]
    copies = []
    for at in range(sems.shape[0]):
        for chunk in chunks(part):
            here = slice(at * part + chunk.start, at * part + chunk.stop)
            row = here.start % count + lax.broadcasted_iota(
                jnp.int32, (here.stop - here.start, half), 0
            )
            alive = row < live[here.start // count]
            for columns, last_ref in ((slice(0, half), left_ref), (slice(half, cols), right_ref)):
                total = own_ref[here, columns] + last_ref[here, :].astype(jnp.float32)
                held[here, columns] = jnp.where(alive, total, 0.0).astype(held.dtype)
        rows_at = pl.ds(at * part, part)
        copies.append(pltpu.make_async_copy(held.at[rows_at], out_ref.at[rows_at], sems.at[at]))
        copies[-1].start()
    for copy in copies:
        copy.wait()


def finish(live, own, left, right):
    rows, cols = own.shape
    return pl.pallas_call(
        finish_kernel,
        grid_spec=pltpu.PrefetchScalarGridSpec(
            num_scalar_prefetch=1,
            grid=(1,),
            in_specs=[WHOLE] * 3,
            out_specs=ANYWHERE,
            scratch_shapes=[
                pltpu.VMEM((rows, cols), jnp.bfloat16),
                pltpu.SemaphoreType.DMA((4 * live.shape[0],)),
            ],
        ),
        out_shape=jax.ShapeDtypeStruct((rows, cols), jnp.bfloat16),
        compiler_params=params(),
        cost_estimate=cost(0, rows * cols * 10),
    )(live, own, left, right)


def per_device(
    size,
    attention_output,
    output_weight,
    adapter_down_weight,
    adapter_up_weight,
    adapter_page_table,
    block_adapter_ids,
    row_list_position,
    live_row_count,
):
    steps, row_count, depth = attention_output.shape
    resident, rank, _ = adapter_down_weight.shape
    _, blocks, listed = block_adapter_ids.shape
    sizes = (steps, blocks, listed, rank, row_count // blocks)
    x = attention_output.reshape(steps * row_count, depth)
    ring = ring_order(size)

    instance = lax.axis_index("inst")
    place = ring_place(lax.axis_index("tp"), size)
    dests = ring_index(lax.rem(place + jnp.arange(size, dtype=jnp.int32), size), size)

    forward = [(ring[i], ring[(i + 1) % size]) for i in range(size)]
    backward = [(ring[i], ring[i - 1]) for i in range(size)]
    far = size // 2
    pairs = [[(0, 1, forward), (1, -1, backward)], [(1, 1, forward), (0, -1, backward)]]
    arrived = {}

    def turn(number, last, between=None):
        left = far - (number + 1) // 2
        for half, sign, moves in pairs[number % 2]:
            last = hop(
                dests, (sign * left) % size, half, x, output_weight,
                arrived.get((half, sign), []), last,
            )
            arrived[half, sign] = [lax.ppermute(last, "tp", moves)]
            if between is not None:
                last, between = touch(between, last), None
        return last

    ids = block_adapter_ids.reshape(-1)
    ids_there = lax.ppermute(block_adapter_ids, "inst", SWAP).reshape(-1)
    last = None
    for piece in range(tiling(dests, output_weight)[2]):
        if piece == 0:
            *both, last = first_pieces(dests, far % size, x, output_weight)
        else:
            both = next_pieces(dests, far % size, piece, x, output_weight, last)
            last = both[1]
        for (half, sign, moves), part in zip(pairs[0], both):
            arrived.setdefault((half, sign), []).append(lax.ppermute(part, "tp", moves))
    pages = adapter_page_table[jnp.concatenate([ids, ids_there])]
    places = pages % resident
    index, index_there = places[: ids.shape[0]], places[ids.shape[0] :]
    local = (pages[: ids.shape[0]] // resident == instance).astype(jnp.int32)
    last = collect(index_there, adapter_down_weight, last)
    got_down = lax.ppermute(last, "inst", SWAP)
    last = touch(last, *(arrived[half, sign][0] for half, sign, _ in pairs[0]))
    last = turn(1, last)
    last = collect(index_there, adapter_up_weight, last)
    got_up = lax.ppermute(last, "inst", SWAP)
    last = turn(2, last, got_down)
    side = (lax.axis_index("tp") & 1).reshape(1)
    low, give = low_rank(
        sizes, local, index, side, x, row_list_position, adapter_down_weight, got_down, last
    )
    last = touch(got_up, low)

    def over(value, apart):
        return lax.ppermute(value, "tp", [(i, i ^ apart) for i in range(size)])

    number, turns = 3, 2 * far - 1
    apart = 1
    while apart < size:
        sent = over(((give if apart == 1 else low) * LOW_SCALE).astype(jnp.float16), apart)
        until = turns - 1 if 2 * apart == size else number + 1
        while number < min(until, turns - 1):
            last = turn(number, last)
            if number == 3:
                own, up_pages = own_terms(
                    dests, local, index, x, output_weight, adapter_up_weight, got_up, last
                )
                last = own
            number += 1
        apart *= 2
        zero = touch(last)[0, 0]
        sent = sent.astype(jnp.float32) * (1.0 / LOW_SCALE) + zero
        low = last = add(low, sent, jnp.float32 if apart < size else jnp.bfloat16, last)
    other = over(low, 1)
    last = turn(number, last)
    own = add_delta(sizes, side, own, up_pages, row_list_position, low, other, last)
    own = join(own, arrived[0, -1][0], arrived[1, 1][0])
    result = finish(live_row_count.reshape(-1), own, arrived[0, 1][0], arrived[1, -1][0])
    return result.reshape(steps, row_count, -1)


def solution(mesh):
    in_specs = (
        P(None, ("grp", "inst"), "tp"),
        P("tp", None),
        P("inst", None, "tp"),
        P("inst", None, "tp"),
        P(),
        P(None, ("grp", "inst"), None),
        P(None, ("grp", "inst")),
        P(None, ("grp", "inst")),
    )
    out_specs = P(None, ("grp", "inst"), "tp")
    return jax.shard_map(
        functools.partial(per_device, mesh.shape["tp"]),
        mesh=mesh, in_specs=in_specs, out_specs=out_specs, check_vma=False,
    )
```

```python
import functools

import jax
import jax.numpy as jnp
from jax import lax
from jax.experimental import pallas as pl
from jax.experimental.pallas import tpu as pltpu
from jax.sharding import PartitionSpec as P

VMEM_LIMIT = 40 * 1024 * 1024
LOW_SCALE = 16.0
GRAIN = 16
SWAP = [(0, 1), (1, 0)]
WHOLE = pl.BlockSpec(memory_space=pltpu.VMEM)
ANYWHERE = pl.BlockSpec(memory_space=pl.ANY)


def serpentine(size):
    return size == 8


def ring_index(place, size):
    if not serpentine(size):
        return place
    return jnp.where(place < size // 2, 2 * place, 2 * (size - 1 - place) + 1)


def ring_place(index, size):
    if not serpentine(size):
        return index
    return jnp.where(index & 1 == 0, index >> 1, size - 1 - (index >> 1))


def ring_order(size):
    if not serpentine(size):
        return list(range(size))
    return list(range(0, size, 2)) + list(range(size - 1, 0, -2))


def params():
    return pltpu.CompilerParams(vmem_limit_bytes=VMEM_LIMIT)


def cost(flops, size):
    return pl.CostEstimate(flops=30 * flops, bytes_accessed=size, transcendentals=0)


def hop_kernel(pieces, dests, x_ref, w_ref, *refs):
    tile = w_ref.shape[1]
    now = pl.program_id(0)
    columns = pl.ds(pl.multiple_of(now * tile, tile), tile)
    total = jnp.dot(x_ref[...], w_ref[...], preferred_element_type=jnp.float32)
    out_ref = refs[-1]
    if len(pieces) == 1:
        out_ref[:, columns] = (total + refs[0][:, columns].astype(jnp.float32)).astype(
            out_ref.dtype
        )
    elif pieces:
        for piece, received_ref in zip(pieces, refs):

            @pl.when(now == piece)
            def _():
                out_ref[:, columns] = (total + received_ref[...].astype(jnp.float32)).astype(
                    out_ref.dtype
                )

    else:
        out_ref[:, columns] = total.astype(out_ref.dtype)


def tiling(dests, weight):
    half_cols = weight.shape[1] // dests.shape[0] // 2
    tile = min(256, half_cols)
    return half_cols, tile, half_cols // tile


def hop(dests, offset, half, x, weight, received, after):
    rows, depth = x.shape
    half_cols, tile, tiles = tiling(dests, weight)
    return pl.pallas_call(
        functools.partial(hop_kernel, tuple(range(len(received)))),
        grid_spec=pltpu.PrefetchScalarGridSpec(
            num_scalar_prefetch=1,
            grid=(tiles,),
            in_specs=[
                WHOLE,
                pl.BlockSpec(
                    (depth, tile), lambda j, d: (0, (d[offset] * 2 + half) * tiles + j)
                ),
            ]
            + [WHOLE] * len(received)
            + [ANYWHERE],
            out_specs=WHOLE,
        ),
        out_shape=jax.ShapeDtypeStruct((rows, half_cols), jnp.bfloat16),
        compiler_params=params(),
        cost_estimate=cost(
            2 * rows * depth * half_cols,
            2 * (rows * depth + depth * half_cols + 2 * rows * half_cols),
        ),
    )(dests, x, weight, *received, after)


def first_kernel(with_after, dests, x_ref, w_ref, *refs):
    total = jnp.dot(x_ref[...], w_ref[...], preferred_element_type=jnp.float32)
    refs[-1][...] = jnp.zeros_like(refs[-1])
    for chain, out_ref in enumerate(refs[-3:-1]):

        @pl.when(pl.program_id(0) == chain)
        def _():
            out_ref[...] = total.astype(out_ref.dtype)


def first_pieces(dests, offset, piece, x, weight, after):
    rows, depth = x.shape
    _, tile, tiles = tiling(dests, weight)
    size = dests.shape[0]

    def place(j, d):
        one = d[offset] * 2 * tiles + piece
        two = (d[(size - offset) % size] * 2 + 1) * tiles + piece
        return (0, jnp.where(j == 0, one, two))

    tail = [] if after is None else [after]
    return pl.pallas_call(
        functools.partial(first_kernel, after is not None),
        grid_spec=pltpu.PrefetchScalarGridSpec(
            num_scalar_prefetch=1,
            grid=(2,),
            in_specs=[
                WHOLE,
                pl.BlockSpec((depth, tile), place),
            ]
            + [ANYWHERE] * len(tail),
            out_specs=[WHOLE, WHOLE, pl.BlockSpec((8, 128), lambda j, d: (0, 0))],
        ),
        out_shape=[jax.ShapeDtypeStruct((rows, tile), jnp.bfloat16)] * 2
        + [jax.ShapeDtypeStruct((8, 128), jnp.float32)],
        compiler_params=params(),
        cost_estimate=cost(
            4 * rows * depth * tile, 2 * (rows * depth + 2 * depth * tile + 2 * rows * tile)
        ),
    )(dests, x, weight, *tail)


def touch_kernel(*refs):
    refs[-1][...] = jnp.zeros_like(refs[-1])


def touch(*arrays):
    return pl.pallas_call(
        touch_kernel,
        in_specs=[ANYWHERE] * len(arrays),
        out_specs=WHOLE,
        out_shape=jax.ShapeDtypeStruct((8, 128), jnp.float32),
        compiler_params=params(),
    )(*arrays)


def collect_kernel(count, index, table_ref, after_ref, out_ref, sems):
    copies = [
        pltpu.make_async_copy(table_ref.at[index[slot]], out_ref.at[slot], sems.at[slot])
        for slot in range(count)
    ]
    for copy in copies:
        copy.start()
    for copy in copies:
        copy.wait()


def collect(index, table, after):
    count = index.shape[0]
    shape = (count,) + table.shape[1:]
    return pl.pallas_call(
        functools.partial(collect_kernel, count),
        grid_spec=pltpu.PrefetchScalarGridSpec(
            num_scalar_prefetch=1,
            grid=(1,),
            in_specs=[ANYWHERE, ANYWHERE],
            out_specs=WHOLE,
            scratch_shapes=[pltpu.SemaphoreType.DMA((count,))],
        ),
        out_shape=jax.ShapeDtypeStruct(shape, table.dtype),
        compiler_params=params(),
        cost_estimate=cost(0, 4 * shape[0] * shape[1] * shape[2]),
    )(index, table, after)


def start_pages(count, local, index, table_ref, got_ref, pages, sems):
    for slot in range(count):
        own = local[slot] == 1

        @pl.when(own)
        def _():
            pltpu.make_async_copy(
                table_ref.at[index[slot]], pages.at[slot], sems.at[slot]
            ).start()

        @pl.when(jnp.logical_not(own))
        def _():
            pltpu.make_async_copy(got_ref.at[slot], pages.at[slot], sems.at[slot]).start()


def wait_pages(slots, got_ref, pages, sems):
    for slot in slots:
        pltpu.make_async_copy(got_ref.at[slot], pages.at[slot], sems.at[slot]).wait()


def low_kernel(
    sizes, local, index, side, x_ref, place_ref, table_ref, got_ref, after_ref, keep_ref, give_ref,
    pages, sems,
):
    steps, blocks, listed, rank, block_rows = sizes
    half = steps * blocks // 2
    start_pages(steps * blocks * listed, local, index, table_ref, got_ref, pages, sems)
    for step in range(steps):
        for block in range(blocks):
            at = step * blocks + block
            wait_pages(range(at * listed, (at + 1) * listed), got_ref, pages, sems)
            listing = pages[at * listed : (at + 1) * listed].reshape(listed * rank, -1)
            every = lax.dot_general(
                listing, x_ref[at * block_rows : (at + 1) * block_rows, :],
                (((1,), (1,)), ((), ())), preferred_element_type=jnp.float32,
            )
            place = place_ref[step : step + 1, block * block_rows : (block + 1) * block_rows]
            low = jnp.zeros((rank, block_rows), jnp.float32)
            for entry in range(listed):
                low = jnp.where(place == entry, every[entry * rank : (entry + 1) * rank], low)
            rows = slice(at % half * block_rows, (at % half + 1) * block_rows)
            mine = side[0] == at // half

            @pl.when(mine)
            def _():
                keep_ref[:, rows] = low

            @pl.when(jnp.logical_not(mine))
            def _():
                give_ref[:, rows] = low


def low_rank(sizes, local, index, side, x, place, table, got, after):
    steps, blocks, listed, rank, block_rows = sizes
    count = steps * blocks * listed
    rows, depth = x.shape
    return pl.pallas_call(
        functools.partial(low_kernel, sizes),
        grid_spec=pltpu.PrefetchScalarGridSpec(
            num_scalar_prefetch=3,
            grid=(1,),
            in_specs=[WHOLE, WHOLE, ANYWHERE, ANYWHERE, ANYWHERE],
            out_specs=[WHOLE, WHOLE],
            scratch_shapes=[
                pltpu.VMEM((count, rank, depth), table.dtype),
                pltpu.SemaphoreType.DMA((count,)),
            ],
        ),
        out_shape=[jax.ShapeDtypeStruct((rank, rows // 2), jnp.float32)] * 2,
        compiler_params=params(),
        cost_estimate=cost(
            2 * rows * depth * listed * rank, 2 * (rows * depth + count * rank * depth)
        ),
    )(local, index, side, x, place, table, got, after)


def add_kernel(low_ref, sent_ref, after_ref, out_ref):
    out_ref[...] = (low_ref[...] + sent_ref[...]).astype(out_ref.dtype)


def add(low, sent, dtype, after):
    return pl.pallas_call(
        add_kernel,
        in_specs=[WHOLE, WHOLE, ANYWHERE],
        out_specs=WHOLE,
        out_shape=jax.ShapeDtypeStruct(low.shape, dtype),
        compiler_params=params(),
        cost_estimate=cost(low.size, 12 * low.size),
    )(low, sent, after)


def own_kernel(
    local, index, dests, x_ref, w_ref, table_ref, got_ref, after_ref, out_ref, pages, sems
):
    tile = w_ref.shape[1]
    now = pl.program_id(0)
    count = pages.shape[0]

    @pl.when(now == 0)
    def _():
        start_pages(count, local, index, table_ref, got_ref, pages, sems)

    columns = pl.ds(pl.multiple_of(now * tile, tile), tile)
    out_ref[:, columns] = jnp.dot(x_ref[...], w_ref[...], preferred_element_type=jnp.float32)

    @pl.when(now == pl.num_programs(0) - 1)
    def _():
        wait_pages(range(count), got_ref, pages, sems)


def own_terms(dests, local, index, x, weight, table, got, after):
    count, rank, cols = got.shape
    rows, depth = x.shape
    tile = min(256, cols)
    tiles = cols // tile
    return pl.pallas_call(
        own_kernel,
        grid_spec=pltpu.PrefetchScalarGridSpec(
            num_scalar_prefetch=3,
            grid=(tiles,),
            in_specs=[
                WHOLE,
                pl.BlockSpec((depth, tile), lambda j, l, i, d: (0, d[0] * tiles + j)),
                ANYWHERE,
                ANYWHERE,
                ANYWHERE,
            ],
            out_specs=[WHOLE, WHOLE],
            scratch_shapes=[pltpu.SemaphoreType.DMA((count,))],
        ),
        out_shape=[
            jax.ShapeDtypeStruct((rows, cols), jnp.float32),
            jax.ShapeDtypeStruct((count, rank, cols), table.dtype),
        ],
        compiler_params=params(),
        cost_estimate=cost(
            2 * rows * cols * depth,
            2 * (rows * depth + depth * cols + 2 * count * rank * cols) + 4 * rows * cols,
        ),
    )(local, index, dests, x, weight, table, got, after)


def delta_kernel(
    sizes, side, own_ref, pages_ref, place_ref, low_ref, other_ref, after_ref, out_ref
):
    steps, blocks, listed, rank, block_rows = sizes
    half = steps * blocks // 2
    entry_of = lax.broadcasted_iota(jnp.int32, (listed * rank, block_rows), 0) // rank
    for step in range(steps):
        for block in range(blocks):
            at = step * blocks + block
            rows = slice(at * block_rows, (at + 1) * block_rows)
            in_half = slice(at % half * block_rows, (at % half + 1) * block_rows)
            low = jnp.where(
                side[0] == at // half,
                low_ref[:, in_half].astype(jnp.float32),
                other_ref[:, in_half].astype(jnp.float32),
            )
            spread = jnp.concatenate([low] * listed, axis=0)
            place = place_ref[step : step + 1, block * block_rows : (block + 1) * block_rows]
            spread = jnp.where(entry_of == place, spread, 0.0)
            listing = pages_ref[at * listed : (at + 1) * listed].reshape(listed * rank, -1)
            out_ref[rows, :] = own_ref[rows, :] + jnp.dot(
                spread.T.astype(jnp.bfloat16), listing, preferred_element_type=jnp.float32
            )


def add_delta(sizes, side, own, pages, place, low, other, after):
    rows, cols = own.shape
    return pl.pallas_call(
        functools.partial(delta_kernel, sizes),
        grid_spec=pltpu.PrefetchScalarGridSpec(
            num_scalar_prefetch=1,
            grid=(1,),
            in_specs=[WHOLE] * 5 + [ANYWHERE],
            out_specs=WHOLE,
        ),
        out_shape=jax.ShapeDtypeStruct(own.shape, own.dtype),
        compiler_params=params(),
        cost_estimate=cost(
            2 * rows * cols * sizes[2] * sizes[3], 8 * rows * cols + 2 * pages.size
        ),
    )(side, own, pages, place, low, other, after)


def chunks(count):
    size = 32 if count % 32 == 0 else GRAIN
    return [slice(at, at + size) for at in range(0, count, size)]


def join_kernel(own_ref, left_ref, right_ref, out_ref):
    cols = left_ref.shape[1]
    for rows in chunks(own_ref.shape[0]):
        for at, part_ref in ((0, left_ref), (cols, right_ref)):
            out_ref[rows, at : at + cols] = own_ref[rows, at : at + cols] + part_ref[
                rows, :
            ].astype(jnp.float32)


def join(own, left, right):
    return pl.pallas_call(
        join_kernel,
        in_specs=[WHOLE] * 3,
        out_specs=WHOLE,
        out_shape=jax.ShapeDtypeStruct(own.shape, own.dtype),
        compiler_params=params(),
        cost_estimate=cost(own.size, 10 * own.size),
    )(own, left, right)


def finish_kernel(half, live, own_ref, last_ref, *refs):
    out_ref, held, sems = refs[-3:]
    rows, cols = held.shape
    count = rows // live.shape[0]
    columns = slice(half * cols, (half + 1) * cols)
    part = rows // sems.shape[0]
    copies = []
    for at in range(sems.shape[0]):
        for chunk in chunks(part):
            here = slice(at * part + chunk.start, at * part + chunk.stop)
            total = own_ref[here, columns] + last_ref[here, :].astype(jnp.float32)
            row = here.start % count + lax.broadcasted_iota(jnp.int32, total.shape, 0)
            alive = row < live[here.start // count]
            held[here, :] = jnp.where(alive, total, 0.0).astype(held.dtype)
        rows_at = pl.ds(at * part, part)
        copies.append(
            pltpu.make_async_copy(held.at[rows_at], out_ref.at[rows_at, columns], sems.at[at])
        )
        copies[-1].start()
    for copy in copies:
        copy.wait()


def finish(live, half, own, last, result):
    rows, cols = own.shape
    steps = live.shape[0]
    in_specs = [WHOLE, WHOLE]
    operands = [own, last]
    aliases = {}
    if result is not None:
        in_specs.append(ANYWHERE)
        operands.append(result)
        aliases = {3: 0}
    return pl.pallas_call(
        functools.partial(finish_kernel, half),
        grid_spec=pltpu.PrefetchScalarGridSpec(
            num_scalar_prefetch=1,
            grid=(1,),
            in_specs=in_specs,
            out_specs=ANYWHERE,
            scratch_shapes=[
                pltpu.VMEM((rows, cols // 2), jnp.bfloat16),
                pltpu.SemaphoreType.DMA((2 * steps,)),
            ],
        ),
        out_shape=jax.ShapeDtypeStruct((rows, cols), jnp.bfloat16),
        input_output_aliases=aliases,
        compiler_params=params(),
        cost_estimate=cost(0, rows * cols * 5),
    )(live, *operands)


def per_device(
    size,
    attention_output,
    output_weight,
    adapter_down_weight,
    adapter_up_weight,
    adapter_page_table,
    block_adapter_ids,
    row_list_position,
    live_row_count,
):
    steps, row_count, depth = attention_output.shape
    resident, rank, _ = adapter_down_weight.shape
    _, blocks, listed = block_adapter_ids.shape
    sizes = (steps, blocks, listed, rank, row_count // blocks)
    x = attention_output.reshape(steps * row_count, depth)
    ring = ring_order(size)

    instance = lax.axis_index("inst")
    place = ring_place(lax.axis_index("tp"), size)
    dests = ring_index(lax.rem(place + jnp.arange(size, dtype=jnp.int32), size), size)

    forward = [(ring[i], ring[(i + 1) % size]) for i in range(size)]
    backward = [(ring[i], ring[i - 1]) for i in range(size)]
    far = size // 2
    pairs = [[(0, 1, forward), (1, -1, backward)], [(1, 1, forward), (0, -1, backward)]]
    arrived = {}

    def turn(number, last, between=None):
        left = far - (number + 1) // 2
        for half, sign, moves in pairs[number % 2]:
            last = hop(
                dests, (sign * left) % size, half, x, output_weight,
                arrived.get((half, sign), []), last,
            )
            arrived[half, sign] = [lax.ppermute(last, "tp", moves)]
            if between is not None:
                last, between = touch(*between, last), None
        return last

    ids = block_adapter_ids.reshape(-1)
    ids_there = lax.ppermute(block_adapter_ids, "inst", SWAP).reshape(-1)
    last = None
    for piece in range(tiling(dests, output_weight)[2]):
        *both, last = first_pieces(dests, far % size, piece, x, output_weight, last)
        for (half, sign, moves), part in zip(pairs[0], both):
            arrived.setdefault((half, sign), []).append(lax.ppermute(part, "tp", moves))
    pages = adapter_page_table[jnp.concatenate([ids, ids_there])]
    places = pages % resident
    index, index_there = places[: ids.shape[0]], places[ids.shape[0] :]
    local = (pages[: ids.shape[0]] // resident == instance).astype(jnp.int32)
    last = collect(index_there, adapter_down_weight, last)
    got_down = lax.ppermute(last, "inst", SWAP)
    last = turn(1, last, [arrived[half, sign][0] for half, sign, _ in pairs[0]])
    side = (lax.axis_index("tp") & 1).reshape(1)
    low, give = low_rank(
        sizes, local, index, side, x, row_list_position, adapter_down_weight, got_down, last
    )
    last = low

    def over(value, apart):
        return lax.ppermute(value, "tp", [(i, i ^ apart) for i in range(size)])

    number, turns = 2, 2 * far - 1
    apart = 1
    while apart < size:
        sent = over(((give if apart == 1 else low) * LOW_SCALE).astype(jnp.float16), apart)
        until = turns - 1 if 2 * apart == size else number + 1
        while number < min(until, turns - 1):
            last = turn(number, last)
            if number == 4:
                last = collect(index_there, adapter_up_weight, last)
                got_up = lax.ppermute(last, "inst", SWAP)
            if number == 5:
                own, up_pages = own_terms(
                    dests, local, index, x, output_weight, adapter_up_weight, got_up, last
                )
                last = own
            number += 1
        apart *= 2
        zero = touch(last)[0, 0]
        sent = sent.astype(jnp.float32) * (1.0 / LOW_SCALE) + zero
        low = last = add(low, sent, jnp.float32 if apart < size else jnp.bfloat16, last)
    other = over(low, 1)
    last = turn(number, last)
    own = add_delta(sizes, side, own, up_pages, row_list_position, low, other, last)
    own = join(own, arrived[0, -1][0], arrived[1, 1][0])
    result = None
    for half, sign, _ in pairs[0]:
        result = finish(live_row_count.reshape(-1), half, own, arrived[half, sign][0], result)
    return result.reshape(steps, row_count, -1)


def solution(mesh):
    in_specs = (
        P(None, ("grp", "inst"), "tp"),
        P("tp", None),
        P("inst", None, "tp"),
        P("inst", None, "tp"),
        P(),
        P(None, ("grp", "inst"), None),
        P(None, ("grp", "inst")),
        P(None, ("grp", "inst")),
    )
    out_specs = P(None, ("grp", "inst"), "tp")
    return jax.shard_map(
        functools.partial(per_device, mesh.shape["tp"]),
        mesh=mesh, in_specs=in_specs, out_specs=out_specs, check_vma=False,
    )
```

```python
import functools

import jax
import jax.numpy as jnp
from jax import lax
from jax.experimental import pallas as pl
from jax.experimental.pallas import tpu as pltpu
from jax.sharding import PartitionSpec as P

VMEM_LIMIT = 40 * 1024 * 1024
FIRST_VMEM_LIMIT = 52 * 1024 * 1024
LOW_SCALE = 16.0
GRAIN = 16
SWAP = [(0, 1), (1, 0)]
WHOLE = pl.BlockSpec(memory_space=pltpu.VMEM)
ANYWHERE = pl.BlockSpec(memory_space=pl.ANY)


def serpentine(size):
    return size == 8


def ring_index(place, size):
    if not serpentine(size):
        return place
    return jnp.where(place < size // 2, 2 * place, 2 * (size - 1 - place) + 1)


def ring_place(index, size):
    if not serpentine(size):
        return index
    return jnp.where(index & 1 == 0, index >> 1, size - 1 - (index >> 1))


def ring_order(size):
    if not serpentine(size):
        return list(range(size))
    return list(range(0, size, 2)) + list(range(size - 1, 0, -2))


def params(limit=VMEM_LIMIT):
    return pltpu.CompilerParams(vmem_limit_bytes=limit)


def cost(flops, size):
    return pl.CostEstimate(flops=30 * flops, bytes_accessed=size, transcendentals=0)


def hop_kernel(pieces, dests, x_ref, w_ref, *refs):
    tile = w_ref.shape[1]
    now = pl.program_id(0)
    columns = pl.ds(pl.multiple_of(now * tile, tile), tile)
    total = jnp.dot(x_ref[...], w_ref[...], preferred_element_type=jnp.float32)
    out_ref = refs[-1]
    if len(pieces) == 1:
        out_ref[:, columns] = (total + refs[0][:, columns].astype(jnp.float32)).astype(
            out_ref.dtype
        )
    elif pieces:
        for piece, received_ref in zip(pieces, refs):

            @pl.when(now == piece)
            def _():
                out_ref[:, columns] = (total + received_ref[...].astype(jnp.float32)).astype(
                    out_ref.dtype
                )

    else:
        out_ref[:, columns] = total.astype(out_ref.dtype)


def tiling(dests, weight):
    half_cols = weight.shape[1] // dests.shape[0] // 2
    tile = min(256, half_cols)
    return half_cols, tile, half_cols // tile


def hop(dests, offset, half, x, weight, received, after):
    rows, depth = x.shape
    half_cols, tile, tiles = tiling(dests, weight)
    return pl.pallas_call(
        functools.partial(hop_kernel, tuple(range(len(received)))),
        grid_spec=pltpu.PrefetchScalarGridSpec(
            num_scalar_prefetch=1,
            grid=(tiles,),
            in_specs=[
                WHOLE,
                pl.BlockSpec(
                    (depth, tile), lambda j, d: (0, (d[offset] * 2 + half) * tiles + j)
                ),
            ]
            + [WHOLE] * len(received)
            + [ANYWHERE],
            out_specs=WHOLE,
        ),
        out_shape=jax.ShapeDtypeStruct((rows, half_cols), jnp.bfloat16),
        compiler_params=params(),
        cost_estimate=cost(
            2 * rows * depth * half_cols,
            2 * (rows * depth + depth * half_cols + 2 * rows * half_cols),
        ),
    )(dests, x, weight, *received, after)


def first_kernel(with_after, dests, x_ref, w_ref, *refs):
    total = jnp.dot(x_ref[...], w_ref[...], preferred_element_type=jnp.float32)
    refs[-1][...] = jnp.zeros_like(refs[-1])
    for chain, out_ref in enumerate(refs[-3:-1]):

        @pl.when(pl.program_id(0) == chain)
        def _():
            out_ref[...] = total.astype(out_ref.dtype)


def first_pieces(dests, offset, piece, x, weight, after):
    rows, depth = x.shape
    _, tile, tiles = tiling(dests, weight)
    size = dests.shape[0]

    def place(j, d):
        one = d[offset] * 2 * tiles + piece
        two = (d[(size - offset) % size] * 2 + 1) * tiles + piece
        return (0, jnp.where(j == 0, one, two))

    tail = [] if after is None else [after]
    return pl.pallas_call(
        functools.partial(first_kernel, after is not None),
        grid_spec=pltpu.PrefetchScalarGridSpec(
            num_scalar_prefetch=1,
            grid=(2,),
            in_specs=[
                pl.BlockSpec((rows, depth), lambda j, d: (0, 0)) if after is None else WHOLE,
                pl.BlockSpec((depth, tile), place),
            ]
            + [ANYWHERE] * len(tail),
            out_specs=[WHOLE, WHOLE, pl.BlockSpec((8, 128), lambda j, d: (0, 0))],
        ),
        out_shape=[jax.ShapeDtypeStruct((rows, tile), jnp.bfloat16)] * 2
        + [jax.ShapeDtypeStruct((8, 128), jnp.float32)],
        compiler_params=params(FIRST_VMEM_LIMIT if after is None else VMEM_LIMIT),
        cost_estimate=cost(
            4 * rows * depth * tile, 2 * (rows * depth + 2 * depth * tile + 2 * rows * tile)
        ),
    )(dests, x, weight, *tail)


def touch_kernel(*refs):
    refs[-1][...] = jnp.zeros_like(refs[-1])


def touch(*arrays):
    return pl.pallas_call(
        touch_kernel,
        in_specs=[ANYWHERE] * len(arrays),
        out_specs=WHOLE,
        out_shape=jax.ShapeDtypeStruct((8, 128), jnp.float32),
        compiler_params=params(),
    )(*arrays)


def collect_kernel(count, index, table_ref, after_ref, out_ref, sems):
    copies = [
        pltpu.make_async_copy(table_ref.at[index[slot]], out_ref.at[slot], sems.at[slot])
        for slot in range(count)
    ]
    for copy in copies:
        copy.start()
    for copy in copies:
        copy.wait()


def collect(index, table, after):
    count = index.shape[0]
    shape = (count,) + table.shape[1:]
    return pl.pallas_call(
        functools.partial(collect_kernel, count),
        grid_spec=pltpu.PrefetchScalarGridSpec(
            num_scalar_prefetch=1,
            grid=(1,),
            in_specs=[ANYWHERE, ANYWHERE],
            out_specs=WHOLE,
            scratch_shapes=[pltpu.SemaphoreType.DMA((count,))],
        ),
        out_shape=jax.ShapeDtypeStruct(shape, table.dtype),
        compiler_params=params(),
        cost_estimate=cost(0, 4 * shape[0] * shape[1] * shape[2]),
    )(index, table, after)


def start_pages(count, local, index, table_ref, got_ref, pages, sems):
    for slot in range(count):
        own = local[slot] == 1

        @pl.when(own)
        def _():
            pltpu.make_async_copy(
                table_ref.at[index[slot]], pages.at[slot], sems.at[slot]
            ).start()

        @pl.when(jnp.logical_not(own))
        def _():
            pltpu.make_async_copy(got_ref.at[slot], pages.at[slot], sems.at[slot]).start()


def wait_pages(slots, got_ref, pages, sems):
    for slot in slots:
        pltpu.make_async_copy(got_ref.at[slot], pages.at[slot], sems.at[slot]).wait()


def low_kernel(
    sizes, local, index, side, x_ref, place_ref, table_ref, got_ref, after_ref, keep_ref, give_ref,
    pages, sems,
):
    steps, blocks, listed, rank, block_rows = sizes
    half = steps * blocks // 2
    start_pages(steps * blocks * listed, local, index, table_ref, got_ref, pages, sems)
    for step in range(steps):
        for block in range(blocks):
            at = step * blocks + block
            wait_pages(range(at * listed, (at + 1) * listed), got_ref, pages, sems)
            listing = pages[at * listed : (at + 1) * listed].reshape(listed * rank, -1)
            every = lax.dot_general(
                listing, x_ref[at * block_rows : (at + 1) * block_rows, :],
                (((1,), (1,)), ((), ())), preferred_element_type=jnp.float32,
            )
            place = place_ref[step : step + 1, block * block_rows : (block + 1) * block_rows]
            low = jnp.zeros((rank, block_rows), jnp.float32)
            for entry in range(listed):
                low = jnp.where(place == entry, every[entry * rank : (entry + 1) * rank], low)
            rows = slice(at % half * block_rows, (at % half + 1) * block_rows)
            mine = side[0] == at // half

            @pl.when(mine)
            def _():
                keep_ref[:, rows] = low

            @pl.when(jnp.logical_not(mine))
            def _():
                give_ref[:, rows] = low


def low_rank(sizes, local, index, side, x, place, table, got, after):
    steps, blocks, listed, rank, block_rows = sizes
    count = steps * blocks * listed
    rows, depth = x.shape
    return pl.pallas_call(
        functools.partial(low_kernel, sizes),
        grid_spec=pltpu.PrefetchScalarGridSpec(
            num_scalar_prefetch=3,
            grid=(1,),
            in_specs=[WHOLE, WHOLE, ANYWHERE, ANYWHERE, ANYWHERE],
            out_specs=[WHOLE, WHOLE],
            scratch_shapes=[
                pltpu.VMEM((count, rank, depth), table.dtype),
                pltpu.SemaphoreType.DMA((count,)),
            ],
        ),
        out_shape=[jax.ShapeDtypeStruct((rank, rows // 2), jnp.float32)] * 2,
        compiler_params=params(),
        cost_estimate=cost(
            2 * rows * depth * listed * rank, 2 * (rows * depth + count * rank * depth)
        ),
    )(local, index, side, x, place, table, got, after)


def add_kernel(low_ref, sent_ref, after_ref, out_ref):
    out_ref[...] = (low_ref[...] + sent_ref[...]).astype(out_ref.dtype)


def add(low, sent, dtype, after):
    return pl.pallas_call(
        add_kernel,
        in_specs=[WHOLE, WHOLE, ANYWHERE],
        out_specs=WHOLE,
        out_shape=jax.ShapeDtypeStruct(low.shape, dtype),
        compiler_params=params(),
        cost_estimate=cost(low.size, 12 * low.size),
    )(low, sent, after)


def own_kernel(
    local, index, dests, x_ref, w_ref, table_ref, got_ref, after_ref, out_ref, pages, sems
):
    tile = w_ref.shape[1]
    now = pl.program_id(0)
    count = pages.shape[0]

    @pl.when(now == 0)
    def _():
        start_pages(count, local, index, table_ref, got_ref, pages, sems)

    columns = pl.ds(pl.multiple_of(now * tile, tile), tile)
    out_ref[:, columns] = jnp.dot(x_ref[...], w_ref[...], preferred_element_type=jnp.float32)

    @pl.when(now == pl.num_programs(0) - 1)
    def _():
        wait_pages(range(count), got_ref, pages, sems)


def own_terms(dests, local, index, x, weight, table, got, after):
    count, rank, cols = got.shape
    rows, depth = x.shape
    tile = min(256, cols)
    tiles = cols // tile
    return pl.pallas_call(
        own_kernel,
        grid_spec=pltpu.PrefetchScalarGridSpec(
            num_scalar_prefetch=3,
            grid=(tiles,),
            in_specs=[
                WHOLE,
                pl.BlockSpec((depth, tile), lambda j, l, i, d: (0, d[0] * tiles + j)),
                ANYWHERE,
                ANYWHERE,
                ANYWHERE,
            ],
            out_specs=[WHOLE, WHOLE],
            scratch_shapes=[pltpu.SemaphoreType.DMA((count,))],
        ),
        out_shape=[
            jax.ShapeDtypeStruct((rows, cols), jnp.float32),
            jax.ShapeDtypeStruct((count, rank, cols), table.dtype),
        ],
        compiler_params=params(),
        cost_estimate=cost(
            2 * rows * cols * depth,
            2 * (rows * depth + depth * cols + 2 * count * rank * cols) + 4 * rows * cols,
        ),
    )(local, index, dests, x, weight, table, got, after)


def delta_kernel(
    sizes, side, own_ref, pages_ref, place_ref, low_ref, other_ref, after_ref, out_ref
):
    steps, blocks, listed, rank, block_rows = sizes
    half = steps * blocks // 2
    entry_of = lax.broadcasted_iota(jnp.int32, (listed * rank, block_rows), 0) // rank
    for step in range(steps):
        for block in range(blocks):
            at = step * blocks + block
            rows = slice(at * block_rows, (at + 1) * block_rows)
            in_half = slice(at % half * block_rows, (at % half + 1) * block_rows)
            low = jnp.where(
                side[0] == at // half,
                low_ref[:, in_half].astype(jnp.float32),
                other_ref[:, in_half].astype(jnp.float32),
            )
            spread = jnp.concatenate([low] * listed, axis=0)
            place = place_ref[step : step + 1, block * block_rows : (block + 1) * block_rows]
            spread = jnp.where(entry_of == place, spread, 0.0)
            listing = pages_ref[at * listed : (at + 1) * listed].reshape(listed * rank, -1)
            out_ref[rows, :] = own_ref[rows, :] + jnp.dot(
                spread.T.astype(jnp.bfloat16), listing, preferred_element_type=jnp.float32
            )


def add_delta(sizes, side, own, pages, place, low, other, after):
    rows, cols = own.shape
    return pl.pallas_call(
        functools.partial(delta_kernel, sizes),
        grid_spec=pltpu.PrefetchScalarGridSpec(
            num_scalar_prefetch=1,
            grid=(1,),
            in_specs=[WHOLE] * 5 + [ANYWHERE],
            out_specs=WHOLE,
        ),
        out_shape=jax.ShapeDtypeStruct(own.shape, own.dtype),
        compiler_params=params(),
        cost_estimate=cost(
            2 * rows * cols * sizes[2] * sizes[3], 8 * rows * cols + 2 * pages.size
        ),
    )(side, own, pages, place, low, other, after)


def chunks(count):
    size = 32 if count % 32 == 0 else GRAIN
    return [slice(at, at + size) for at in range(0, count, size)]


def join_kernel(own_ref, left_ref, right_ref, out_ref):
    cols = left_ref.shape[1]
    for rows in chunks(own_ref.shape[0]):
        for at, part_ref in ((0, left_ref), (cols, right_ref)):
            out_ref[rows, at : at + cols] = own_ref[rows, at : at + cols] + part_ref[
                rows, :
            ].astype(jnp.float32)


def join(own, left, right):
    return pl.pallas_call(
        join_kernel,
        in_specs=[WHOLE] * 3,
        out_specs=WHOLE,
        out_shape=jax.ShapeDtypeStruct(own.shape, own.dtype),
        compiler_params=params(),
        cost_estimate=cost(own.size, 10 * own.size),
    )(own, left, right)


def finish_kernel(half, live, own_ref, last_ref, *refs):
    out_ref, held, sems = refs[-3:]
    rows, cols = held.shape
    count = rows // live.shape[0]
    columns = slice(half * cols, (half + 1) * cols)
    part = rows // sems.shape[0]
    copies = []
    for at in range(sems.shape[0]):
        for chunk in chunks(part):
            here = slice(at * part + chunk.start, at * part + chunk.stop)
            total = own_ref[here, columns] + last_ref[here, :].astype(jnp.float32)
            row = here.start % count + lax.broadcasted_iota(jnp.int32, total.shape, 0)
            alive = row < live[here.start // count]
            held[here, :] = jnp.where(alive, total, 0.0).astype(held.dtype)
        rows_at = pl.ds(at * part, part)
        copies.append(
            pltpu.make_async_copy(held.at[rows_at], out_ref.at[rows_at, columns], sems.at[at])
        )
        copies[-1].start()
    for copy in copies:
        copy.wait()


def finish(live, half, own, last, result):
    rows, cols = own.shape
    steps = live.shape[0]
    in_specs = [WHOLE, WHOLE]
    operands = [own, last]
    aliases = {}
    if result is not None:
        in_specs.append(ANYWHERE)
        operands.append(result)
        aliases = {3: 0}
    return pl.pallas_call(
        functools.partial(finish_kernel, half),
        grid_spec=pltpu.PrefetchScalarGridSpec(
            num_scalar_prefetch=1,
            grid=(1,),
            in_specs=in_specs,
            out_specs=ANYWHERE,
            scratch_shapes=[
                pltpu.VMEM((rows, cols // 2), jnp.bfloat16),
                pltpu.SemaphoreType.DMA((2 * steps,)),
            ],
        ),
        out_shape=jax.ShapeDtypeStruct((rows, cols), jnp.bfloat16),
        input_output_aliases=aliases,
        compiler_params=params(),
        cost_estimate=cost(0, rows * cols * 5),
    )(live, *operands)


def per_device(
    size,
    attention_output,
    output_weight,
    adapter_down_weight,
    adapter_up_weight,
    adapter_page_table,
    block_adapter_ids,
    row_list_position,
    live_row_count,
):
    steps, row_count, depth = attention_output.shape
    resident, rank, _ = adapter_down_weight.shape
    _, blocks, listed = block_adapter_ids.shape
    sizes = (steps, blocks, listed, rank, row_count // blocks)
    x = attention_output.reshape(steps * row_count, depth)
    ring = ring_order(size)

    instance = lax.axis_index("inst")
    place = ring_place(lax.axis_index("tp"), size)
    dests = ring_index(lax.rem(place + jnp.arange(size, dtype=jnp.int32), size), size)

    forward = [(ring[i], ring[(i + 1) % size]) for i in range(size)]
    backward = [(ring[i], ring[i - 1]) for i in range(size)]
    far = size // 2
    pairs = [[(0, 1, forward), (1, -1, backward)], [(1, 1, forward), (0, -1, backward)]]
    arrived = {}

    def turn(number, last, between=None):
        left = far - (number + 1) // 2
        for half, sign, moves in pairs[number % 2]:
            last = hop(
                dests, (sign * left) % size, half, x, output_weight,
                arrived.get((half, sign), []), last,
            )
            arrived[half, sign] = [lax.ppermute(last, "tp", moves)]
            if between is not None:
                last, between = touch(between, last), None
        return last

    ids = block_adapter_ids.reshape(-1)
    ids_there = lax.ppermute(block_adapter_ids, "inst", SWAP).reshape(-1)
    last = None
    for piece in range(tiling(dests, output_weight)[2]):
        *both, last = first_pieces(dests, far % size, piece, x, output_weight, last)
        for (half, sign, moves), part in zip(pairs[0], both):
            arrived.setdefault((half, sign), []).append(lax.ppermute(part, "tp", moves))
    pages = adapter_page_table[jnp.concatenate([ids, ids_there])]
    places = pages % resident
    index, index_there = places[: ids.shape[0]], places[ids.shape[0] :]
    local = (pages[: ids.shape[0]] // resident == instance).astype(jnp.int32)
    last = collect(index_there, adapter_down_weight, last)
    got_down = lax.ppermute(last, "inst", SWAP)
    last = touch(last, *(arrived[half, sign][0] for half, sign, _ in pairs[0]))
    last = turn(1, last)
    last = collect(index_there, adapter_up_weight, last)
    got_up = lax.ppermute(last, "inst", SWAP)
    last = turn(2, last, got_down)
    side = (lax.axis_index("tp") & 1).reshape(1)
    low, give = low_rank(
        sizes, local, index, side, x, row_list_position, adapter_down_weight, got_down, last
    )
    last = touch(got_up, low)

    def over(value, apart):
        return lax.ppermute(value, "tp", [(i, i ^ apart) for i in range(size)])

    number, turns = 3, 2 * far - 1
    apart = 1
    while apart < size:
        sent = over(((give if apart == 1 else low) * LOW_SCALE).astype(jnp.float16), apart)
        until = turns - 1 if 2 * apart == size else number + 1
        while number < min(until, turns - 1):
            last = turn(number, last)
            if number == 3:
                own, up_pages = own_terms(
                    dests, local, index, x, output_weight, adapter_up_weight, got_up, last
                )
                last = own
            number += 1
        apart *= 2
        zero = touch(last)[0, 0]
        sent = sent.astype(jnp.float32) * (1.0 / LOW_SCALE) + zero
        low = last = add(low, sent, jnp.float32 if apart < size else jnp.bfloat16, last)
    other = over(low, 1)
    last = turn(number, last)
    own = add_delta(sizes, side, own, up_pages, row_list_position, low, other, last)
    own = join(own, arrived[0, -1][0], arrived[1, 1][0])
    result = None
    for half, sign, _ in pairs[0]:
        result = finish(live_row_count.reshape(-1), half, own, arrived[half, sign][0], result)
    return result.reshape(steps, row_count, -1)


def solution(mesh):
    in_specs = (
        P(None, ("grp", "inst"), "tp"),
        P("tp", None),
        P("inst", None, "tp"),
        P("inst", None, "tp"),
        P(),
        P(None, ("grp", "inst"), None),
        P(None, ("grp", "inst")),
        P(None, ("grp", "inst")),
    )
    out_specs = P(None, ("grp", "inst"), "tp")
    return jax.shard_map(
        functools.partial(per_device, mesh.shape["tp"]),
        mesh=mesh, in_specs=in_specs, out_specs=out_specs, check_vma=False,
    )
```

```python
import functools

import jax
import jax.numpy as jnp
from jax import lax
from jax.experimental import pallas as pl
from jax.experimental.pallas import tpu as pltpu
from jax.sharding import PartitionSpec as P

VMEM_LIMIT = 40 * 1024 * 1024
FIRST_VMEM_LIMIT = 52 * 1024 * 1024
LOW_SCALE = 16.0
GRAIN = 16
SWAP = [(0, 1), (1, 0)]
WHOLE = pl.BlockSpec(memory_space=pltpu.VMEM)
ANYWHERE = pl.BlockSpec(memory_space=pl.ANY)


def serpentine(size):
    return size == 8


def ring_index(place, size):
    if not serpentine(size):
        return place
    return jnp.where(place < size // 2, 2 * place, 2 * (size - 1 - place) + 1)


def ring_place(index, size):
    if not serpentine(size):
        return index
    return jnp.where(index & 1 == 0, index >> 1, size - 1 - (index >> 1))


def ring_order(size):
    if not serpentine(size):
        return list(range(size))
    return list(range(0, size, 2)) + list(range(size - 1, 0, -2))


def params(limit=VMEM_LIMIT):
    return pltpu.CompilerParams(vmem_limit_bytes=limit)


def cost(flops, size):
    return pl.CostEstimate(flops=30 * flops, bytes_accessed=size, transcendentals=0)


def hop_kernel(pieces, dests, x_ref, w_ref, *refs):
    tile = w_ref.shape[1]
    now = pl.program_id(0)
    columns = pl.ds(pl.multiple_of(now * tile, tile), tile)
    total = jnp.dot(x_ref[...], w_ref[...], preferred_element_type=jnp.float32)
    out_ref = refs[-1]
    if len(pieces) == 1:
        out_ref[:, columns] = (total + refs[0][:, columns].astype(jnp.float32)).astype(
            out_ref.dtype
        )
    elif pieces:
        for piece, received_ref in zip(pieces, refs):

            @pl.when(now == piece)
            def _():
                out_ref[:, columns] = (total + received_ref[...].astype(jnp.float32)).astype(
                    out_ref.dtype
                )

    else:
        out_ref[:, columns] = total.astype(out_ref.dtype)


def tiling(dests, weight):
    half_cols = weight.shape[1] // dests.shape[0] // 2
    tile = min(256, half_cols)
    return half_cols, tile, half_cols // tile


def hop(dests, offset, half, x, weight, received, after):
    rows, depth = x.shape
    half_cols, tile, tiles = tiling(dests, weight)
    return pl.pallas_call(
        functools.partial(hop_kernel, tuple(range(len(received)))),
        grid_spec=pltpu.PrefetchScalarGridSpec(
            num_scalar_prefetch=1,
            grid=(tiles,),
            in_specs=[
                WHOLE,
                pl.BlockSpec(
                    (depth, tile), lambda j, d: (0, (d[offset] * 2 + half) * tiles + j)
                ),
            ]
            + [WHOLE] * len(received)
            + [ANYWHERE],
            out_specs=WHOLE,
        ),
        out_shape=jax.ShapeDtypeStruct((rows, half_cols), jnp.bfloat16),
        compiler_params=params(),
        cost_estimate=cost(
            2 * rows * depth * half_cols,
            2 * (rows * depth + depth * half_cols + 2 * rows * half_cols),
        ),
    )(dests, x, weight, *received, after)


def first_kernel(with_after, dests, x_ref, w_ref, *refs):
    total = jnp.dot(x_ref[...], w_ref[...], preferred_element_type=jnp.float32)
    refs[-1][...] = jnp.zeros_like(refs[-1])
    for chain, out_ref in enumerate(refs[-3:-1]):

        @pl.when(pl.program_id(0) == chain)
        def _():
            out_ref[...] = total.astype(out_ref.dtype)


def first_pieces(dests, offset, piece, x, weight, after):
    rows, depth = x.shape
    _, tile, tiles = tiling(dests, weight)
    size = dests.shape[0]

    def place(j, d):
        one = d[offset] * 2 * tiles + piece
        two = (d[(size - offset) % size] * 2 + 1) * tiles + piece
        return (0, jnp.where(j == 0, one, two))

    tail = [] if after is None else [after]
    return pl.pallas_call(
        functools.partial(first_kernel, after is not None),
        grid_spec=pltpu.PrefetchScalarGridSpec(
            num_scalar_prefetch=1,
            grid=(2,),
            in_specs=[
                pl.BlockSpec((rows, depth), lambda j, d: (0, 0)) if after is None else WHOLE,
                pl.BlockSpec((depth, tile), place),
            ]
            + [ANYWHERE] * len(tail),
            out_specs=[WHOLE, WHOLE, pl.BlockSpec((8, 128), lambda j, d: (0, 0))],
        ),
        out_shape=[jax.ShapeDtypeStruct((rows, tile), jnp.bfloat16)] * 2
        + [jax.ShapeDtypeStruct((8, 128), jnp.float32)],
        compiler_params=params(FIRST_VMEM_LIMIT if after is None else VMEM_LIMIT),
        cost_estimate=cost(
            4 * rows * depth * tile, 2 * (rows * depth + 2 * depth * tile + 2 * rows * tile)
        ),
    )(dests, x, weight, *tail)


def touch_kernel(*refs):
    refs[-1][...] = jnp.zeros_like(refs[-1])


def touch(*arrays):
    return pl.pallas_call(
        touch_kernel,
        in_specs=[ANYWHERE] * len(arrays),
        out_specs=WHOLE,
        out_shape=jax.ShapeDtypeStruct((8, 128), jnp.float32),
        compiler_params=params(),
    )(*arrays)


def collect_kernel(count, index, table_ref, after_ref, out_ref, sems):
    copies = [
        pltpu.make_async_copy(table_ref.at[index[slot]], out_ref.at[slot], sems.at[slot])
        for slot in range(count)
    ]
    for copy in copies:
        copy.start()
    for copy in copies:
        copy.wait()


def collect(index, table, after):
    count = index.shape[0]
    shape = (count,) + table.shape[1:]
    return pl.pallas_call(
        functools.partial(collect_kernel, count),
        grid_spec=pltpu.PrefetchScalarGridSpec(
            num_scalar_prefetch=1,
            grid=(1,),
            in_specs=[ANYWHERE, ANYWHERE],
            out_specs=WHOLE,
            scratch_shapes=[pltpu.SemaphoreType.DMA((count,))],
        ),
        out_shape=jax.ShapeDtypeStruct(shape, table.dtype),
        compiler_params=params(),
        cost_estimate=cost(0, 4 * shape[0] * shape[1] * shape[2]),
    )(index, table, after)


def start_pages(count, local, index, table_ref, got_ref, pages, sems):
    for slot in range(count):
        own = local[slot] == 1

        @pl.when(own)
        def _():
            pltpu.make_async_copy(
                table_ref.at[index[slot]], pages.at[slot], sems.at[slot]
            ).start()

        @pl.when(jnp.logical_not(own))
        def _():
            pltpu.make_async_copy(got_ref.at[slot], pages.at[slot], sems.at[slot]).start()


def wait_pages(slots, got_ref, pages, sems):
    for slot in slots:
        pltpu.make_async_copy(got_ref.at[slot], pages.at[slot], sems.at[slot]).wait()


def low_kernel(
    sizes, local, index, side, x_ref, place_ref, table_ref, got_ref, after_ref, keep_ref, give_ref,
    pages, sems,
):
    steps, blocks, listed, rank, block_rows = sizes
    half = steps * blocks // 2
    start_pages(steps * blocks * listed, local, index, table_ref, got_ref, pages, sems)
    for step in range(steps):
        for block in range(blocks):
            at = step * blocks + block
            wait_pages(range(at * listed, (at + 1) * listed), got_ref, pages, sems)
            listing = pages[at * listed : (at + 1) * listed].reshape(listed * rank, -1)
            every = lax.dot_general(
                listing, x_ref[at * block_rows : (at + 1) * block_rows, :],
                (((1,), (1,)), ((), ())), preferred_element_type=jnp.float32,
            )
            place = place_ref[step : step + 1, block * block_rows : (block + 1) * block_rows]
            low = jnp.zeros((rank, block_rows), jnp.float32)
            for entry in range(listed):
                low = jnp.where(place == entry, every[entry * rank : (entry + 1) * rank], low)
            rows = slice(at % half * block_rows, (at % half + 1) * block_rows)
            mine = side[0] == at // half

            @pl.when(mine)
            def _():
                keep_ref[:, rows] = low

            @pl.when(jnp.logical_not(mine))
            def _():
                give_ref[:, rows] = low


def low_rank(sizes, local, index, side, x, place, table, got, after):
    steps, blocks, listed, rank, block_rows = sizes
    count = steps * blocks * listed
    rows, depth = x.shape
    return pl.pallas_call(
        functools.partial(low_kernel, sizes),
        grid_spec=pltpu.PrefetchScalarGridSpec(
            num_scalar_prefetch=3,
            grid=(1,),
            in_specs=[WHOLE, WHOLE, ANYWHERE, ANYWHERE, ANYWHERE],
            out_specs=[WHOLE, WHOLE],
            scratch_shapes=[
                pltpu.VMEM((count, rank, depth), table.dtype),
                pltpu.SemaphoreType.DMA((count,)),
            ],
        ),
        out_shape=[jax.ShapeDtypeStruct((rank, rows // 2), jnp.float32)] * 2,
        compiler_params=params(),
        cost_estimate=cost(
            2 * rows * depth * listed * rank, 2 * (rows * depth + count * rank * depth)
        ),
    )(local, index, side, x, place, table, got, after)


def add_kernel(low_ref, sent_ref, after_ref, out_ref):
    out_ref[...] = (low_ref[...] + sent_ref[...]).astype(out_ref.dtype)


def add(low, sent, dtype, after):
    return pl.pallas_call(
        add_kernel,
        in_specs=[WHOLE, WHOLE, ANYWHERE],
        out_specs=WHOLE,
        out_shape=jax.ShapeDtypeStruct(low.shape, dtype),
        compiler_params=params(),
        cost_estimate=cost(low.size, 12 * low.size),
    )(low, sent, after)


def own_kernel(
    local, index, dests, x_ref, w_ref, table_ref, got_ref, after_ref, out_ref, pages, sems
):
    tile = w_ref.shape[1]
    now = pl.program_id(0)
    count = pages.shape[0]

    @pl.when(now == 0)
    def _():
        start_pages(count, local, index, table_ref, got_ref, pages, sems)

    columns = pl.ds(pl.multiple_of(now * tile, tile), tile)
    out_ref[:, columns] = jnp.dot(x_ref[...], w_ref[...], preferred_element_type=jnp.float32)

    @pl.when(now == pl.num_programs(0) - 1)
    def _():
        wait_pages(range(count), got_ref, pages, sems)


def own_terms(dests, local, index, x, weight, table, got, after):
    count, rank, cols = got.shape
    rows, depth = x.shape
    tile = min(256, cols)
    tiles = cols // tile
    return pl.pallas_call(
        own_kernel,
        grid_spec=pltpu.PrefetchScalarGridSpec(
            num_scalar_prefetch=3,
            grid=(tiles,),
            in_specs=[
                WHOLE,
                pl.BlockSpec((depth, tile), lambda j, l, i, d: (0, d[0] * tiles + j)),
                ANYWHERE,
                ANYWHERE,
                ANYWHERE,
            ],
            out_specs=[WHOLE, WHOLE],
            scratch_shapes=[pltpu.SemaphoreType.DMA((count,))],
        ),
        out_shape=[
            jax.ShapeDtypeStruct((rows, cols), jnp.float32),
            jax.ShapeDtypeStruct((count, rank, cols), table.dtype),
        ],
        compiler_params=params(),
        cost_estimate=cost(
            2 * rows * cols * depth,
            2 * (rows * depth + depth * cols + 2 * count * rank * cols) + 4 * rows * cols,
        ),
    )(local, index, dests, x, weight, table, got, after)


def delta_kernel(
    sizes, side, own_ref, pages_ref, place_ref, low_ref, other_ref, after_ref, out_ref
):
    steps, blocks, listed, rank, block_rows = sizes
    half = steps * blocks // 2
    entry_of = lax.broadcasted_iota(jnp.int32, (listed * rank, block_rows), 0) // rank
    for step in range(steps):
        for block in range(blocks):
            at = step * blocks + block
            rows = slice(at * block_rows, (at + 1) * block_rows)
            in_half = slice(at % half * block_rows, (at % half + 1) * block_rows)
            low = jnp.where(
                side[0] == at // half,
                low_ref[:, in_half].astype(jnp.float32),
                other_ref[:, in_half].astype(jnp.float32),
            )
            spread = jnp.concatenate([low] * listed, axis=0)
            place = place_ref[step : step + 1, block * block_rows : (block + 1) * block_rows]
            spread = jnp.where(entry_of == place, spread, 0.0)
            listing = pages_ref[at * listed : (at + 1) * listed].reshape(listed * rank, -1)
            out_ref[rows, :] = own_ref[rows, :] + jnp.dot(
                spread.T.astype(jnp.bfloat16), listing, preferred_element_type=jnp.float32
            )


def add_delta(sizes, side, own, pages, place, low, other, after):
    rows, cols = own.shape
    return pl.pallas_call(
        functools.partial(delta_kernel, sizes),
        grid_spec=pltpu.PrefetchScalarGridSpec(
            num_scalar_prefetch=1,
            grid=(1,),
            in_specs=[WHOLE] * 5 + [ANYWHERE],
            out_specs=WHOLE,
        ),
        out_shape=jax.ShapeDtypeStruct(own.shape, own.dtype),
        compiler_params=params(),
        cost_estimate=cost(
            2 * rows * cols * sizes[2] * sizes[3], 8 * rows * cols + 2 * pages.size
        ),
    )(side, own, pages, place, low, other, after)


def chunks(count):
    size = 32 if count % 32 == 0 else GRAIN
    return [slice(at, at + size) for at in range(0, count, size)]


def join_kernel(own_ref, left_ref, right_ref, out_ref):
    cols = left_ref.shape[1]
    for rows in chunks(own_ref.shape[0]):
        for at, part_ref in ((0, left_ref), (cols, right_ref)):
            out_ref[rows, at : at + cols] = own_ref[rows, at : at + cols] + part_ref[
                rows, :
            ].astype(jnp.float32)


def join(own, left, right):
    return pl.pallas_call(
        join_kernel,
        in_specs=[WHOLE] * 3,
        out_specs=WHOLE,
        out_shape=jax.ShapeDtypeStruct(own.shape, own.dtype),
        compiler_params=params(),
        cost_estimate=cost(own.size, 10 * own.size),
    )(own, left, right)


def finish_kernel(half, live, own_ref, last_ref, *refs):
    out_ref, held, sems = refs[-3:]
    rows, cols = held.shape
    count = rows // live.shape[0]
    columns = slice(half * cols, (half + 1) * cols)
    part = rows // sems.shape[0]
    copies = []
    for at in range(sems.shape[0]):
        for chunk in chunks(part):
            here = slice(at * part + chunk.start, at * part + chunk.stop)
            total = own_ref[here, columns] + last_ref[here, :].astype(jnp.float32)
            row = here.start % count + lax.broadcasted_iota(jnp.int32, total.shape, 0)
            alive = row < live[here.start // count]
            held[here, :] = jnp.where(alive, total, 0.0).astype(held.dtype)
        rows_at = pl.ds(at * part, part)
        copies.append(
            pltpu.make_async_copy(held.at[rows_at], out_ref.at[rows_at, columns], sems.at[at])
        )
        copies[-1].start()
    for copy in copies:
        copy.wait()


def finish(live, half, own, last, result):
    rows, cols = own.shape
    steps = live.shape[0]
    in_specs = [WHOLE, WHOLE]
    operands = [own, last]
    aliases = {}
    if result is not None:
        in_specs.append(ANYWHERE)
        operands.append(result)
        aliases = {3: 0}
    return pl.pallas_call(
        functools.partial(finish_kernel, half),
        grid_spec=pltpu.PrefetchScalarGridSpec(
            num_scalar_prefetch=1,
            grid=(1,),
            in_specs=in_specs,
            out_specs=ANYWHERE,
            scratch_shapes=[
                pltpu.VMEM((rows, cols // 2), jnp.bfloat16),
                pltpu.SemaphoreType.DMA((2 * steps,)),
            ],
        ),
        out_shape=jax.ShapeDtypeStruct((rows, cols), jnp.bfloat16),
        input_output_aliases=aliases,
        compiler_params=params(),
        cost_estimate=cost(0, rows * cols * 5),
    )(live, *operands)


def per_device(
    size,
    attention_output,
    output_weight,
    adapter_down_weight,
    adapter_up_weight,
    adapter_page_table,
    block_adapter_ids,
    row_list_position,
    live_row_count,
):
    steps, row_count, depth = attention_output.shape
    resident, rank, _ = adapter_down_weight.shape
    _, blocks, listed = block_adapter_ids.shape
    sizes = (steps, blocks, listed, rank, row_count // blocks)
    x = attention_output.reshape(steps * row_count, depth)
    ring = ring_order(size)

    instance = lax.axis_index("inst")
    place = ring_place(lax.axis_index("tp"), size)
    steps_on = jnp.arange(size, dtype=jnp.int32)
    steps_on = jnp.where(instance == 0, steps_on, size - steps_on)
    dests = ring_index(lax.rem(place + steps_on, size), size)

    up = [(ring[i], ring[(i + 1) % size]) for i in range(size)]
    down = [(ring[i], ring[i - 1]) for i in range(size)]

    def both_instances(first, second):
        return first + [(size + source, size + target) for source, target in second]

    forward, backward = both_instances(up, down), both_instances(down, up)
    far = size // 2
    pairs = [[(0, 1, forward), (1, -1, backward)], [(1, 1, forward), (0, -1, backward)]]
    arrived = {}

    def turn(number, last, between=None):
        left = far - (number + 1) // 2
        for half, sign, moves in pairs[number % 2]:
            last = hop(
                dests, (sign * left) % size, half, x, output_weight,
                arrived.get((half, sign), []), last,
            )
            arrived[half, sign] = [lax.ppermute(last, ("inst", "tp"), moves)]
            if between is not None:
                last, between = touch(between, last), None
        return last

    ids = block_adapter_ids.reshape(-1)
    ids_there = lax.ppermute(block_adapter_ids, "inst", SWAP).reshape(-1)
    last = None
    for piece in range(tiling(dests, output_weight)[2]):
        *both, last = first_pieces(dests, far % size, piece, x, output_weight, last)
        for (half, sign, moves), part in zip(pairs[0], both):
            arrived.setdefault((half, sign), []).append(lax.ppermute(part, ("inst", "tp"), moves))
    pages = adapter_page_table[jnp.concatenate([ids, ids_there])]
    places = pages % resident
    index, index_there = places[: ids.shape[0]], places[ids.shape[0] :]
    local = (pages[: ids.shape[0]] // resident == instance).astype(jnp.int32)
    last = collect(index_there, adapter_down_weight, last)
    got_down = lax.ppermute(last, "inst", SWAP)
    last = touch(last, *(arrived[half, sign][0] for half, sign, _ in pairs[0]))
    last = turn(1, last)
    last = collect(index_there, adapter_up_weight, last)
    got_up = lax.ppermute(last, "inst", SWAP)
    last = turn(2, last, got_down)
    side = (lax.axis_index("tp") & 1).reshape(1)
    low, give = low_rank(
        sizes, local, index, side, x, row_list_position, adapter_down_weight, got_down, last
    )
    last = touch(got_up, low)

    def over(value, apart):
        return lax.ppermute(value, "tp", [(i, i ^ apart) for i in range(size)])

    number, turns = 3, 2 * far - 1
    apart = 1
    while apart < size:
        sent = over(((give if apart == 1 else low) * LOW_SCALE).astype(jnp.float16), apart)
        until = turns - 1 if 2 * apart == size else number + 1
        while number < min(until, turns - 1):
            last = turn(number, last)
            if number == 3:
                own, up_pages = own_terms(
                    dests, local, index, x, output_weight, adapter_up_weight, got_up, last
                )
                last = own
            number += 1
        apart *= 2
        zero = touch(last)[0, 0]
        sent = sent.astype(jnp.float32) * (1.0 / LOW_SCALE) + zero
        low = last = add(low, sent, jnp.float32 if apart < size else jnp.bfloat16, last)
    other = over(low, 1)
    last = turn(number, last)
    own = add_delta(sizes, side, own, up_pages, row_list_position, low, other, last)
    own = join(own, arrived[0, -1][0], arrived[1, 1][0])
    result = None
    for half, sign, _ in pairs[0]:
        result = finish(live_row_count.reshape(-1), half, own, arrived[half, sign][0], result)
    return result.reshape(steps, row_count, -1)


def solution(mesh):
    in_specs = (
        P(None, ("grp", "inst"), "tp"),
        P("tp", None),
        P("inst", None, "tp"),
        P("inst", None, "tp"),
        P(),
        P(None, ("grp", "inst"), None),
        P(None, ("grp", "inst")),
        P(None, ("grp", "inst")),
    )
    out_specs = P(None, ("grp", "inst"), "tp")
    return jax.shard_map(
        functools.partial(per_device, mesh.shape["tp"]),
        mesh=mesh, in_specs=in_specs, out_specs=out_specs, check_vma=False,
    )
```

```python
import functools

import jax
import jax.numpy as jnp
from jax import lax
from jax.experimental import pallas as pl
from jax.experimental.pallas import tpu as pltpu
from jax.sharding import PartitionSpec as P

VMEM_LIMIT = 40 * 1024 * 1024
FIRST_VMEM_LIMIT = 52 * 1024 * 1024
LOW_SCALE = 16.0
GRAIN = 16
SWAP = [(0, 1), (1, 0)]
WHOLE = pl.BlockSpec(memory_space=pltpu.VMEM)
ANYWHERE = pl.BlockSpec(memory_space=pl.ANY)


def serpentine(size):
    return size == 8


def ring_index(place, size):
    if not serpentine(size):
        return place
    return jnp.where(place < size // 2, 2 * place, 2 * (size - 1 - place) + 1)


def ring_place(index, size):
    if not serpentine(size):
        return index
    return jnp.where(index & 1 == 0, index >> 1, size - 1 - (index >> 1))


def ring_order(size):
    if not serpentine(size):
        return list(range(size))
    return list(range(0, size, 2)) + list(range(size - 1, 0, -2))


def params(limit=VMEM_LIMIT):
    return pltpu.CompilerParams(vmem_limit_bytes=limit)


def cost(flops, size):
    return pl.CostEstimate(flops=30 * flops, bytes_accessed=size, transcendentals=0)


def hop_kernel(pieces, dests, x_ref, w_ref, *refs):
    tile = w_ref.shape[1]
    now = pl.program_id(0)
    columns = pl.ds(pl.multiple_of(now * tile, tile), tile)
    total = jnp.dot(x_ref[...], w_ref[...], preferred_element_type=jnp.float32)
    out_ref = refs[-1]
    if len(pieces) == 1:
        out_ref[:, columns] = (total + refs[0][:, columns].astype(jnp.float32)).astype(
            out_ref.dtype
        )
    elif pieces:
        for piece, received_ref in zip(pieces, refs):

            @pl.when(now == piece)
            def _():
                out_ref[:, columns] = (total + received_ref[...].astype(jnp.float32)).astype(
                    out_ref.dtype
                )

    else:
        out_ref[:, columns] = total.astype(out_ref.dtype)


def tiling(dests, weight):
    half_cols = weight.shape[1] // dests.shape[0] // 2
    tile = min(256, half_cols)
    return half_cols, tile, half_cols // tile


def hop(dests, offset, half, x, weight, received, after):
    rows, depth = x.shape
    half_cols, tile, tiles = tiling(dests, weight)
    return pl.pallas_call(
        functools.partial(hop_kernel, tuple(range(len(received)))),
        grid_spec=pltpu.PrefetchScalarGridSpec(
            num_scalar_prefetch=1,
            grid=(tiles,),
            in_specs=[
                WHOLE,
                pl.BlockSpec(
                    (depth, tile), lambda j, d: (0, (d[offset] * 2 + half) * tiles + j)
                ),
            ]
            + [WHOLE] * len(received)
            + [ANYWHERE],
            out_specs=WHOLE,
        ),
        out_shape=jax.ShapeDtypeStruct((rows, half_cols), jnp.bfloat16),
        compiler_params=params(),
        cost_estimate=cost(
            2 * rows * depth * half_cols,
            2 * (rows * depth + depth * half_cols + 2 * rows * half_cols),
        ),
    )(dests, x, weight, *received, after)


def first_kernel(with_after, dests, x_ref, w_ref, *refs):
    total = jnp.dot(x_ref[...], w_ref[...], preferred_element_type=jnp.float32)
    refs[-1][...] = jnp.zeros_like(refs[-1])
    for chain, out_ref in enumerate(refs[-3:-1]):

        @pl.when(pl.program_id(0) == chain)
        def _():
            out_ref[...] = total.astype(out_ref.dtype)


def first_pieces(dests, offset, piece, x, weight, after):
    rows, depth = x.shape
    _, tile, tiles = tiling(dests, weight)
    size = dests.shape[0]

    def place(j, d):
        one = d[offset] * 2 * tiles + piece
        two = (d[(size - offset) % size] * 2 + 1) * tiles + piece
        return (0, jnp.where(j == 0, one, two))

    tail = [] if after is None else [after]
    return pl.pallas_call(
        functools.partial(first_kernel, after is not None),
        grid_spec=pltpu.PrefetchScalarGridSpec(
            num_scalar_prefetch=1,
            grid=(2,),
            in_specs=[
                pl.BlockSpec((rows, depth), lambda j, d: (0, 0)) if after is None else WHOLE,
                pl.BlockSpec((depth, tile), place),
            ]
            + [ANYWHERE] * len(tail),
            out_specs=[WHOLE, WHOLE, pl.BlockSpec((8, 128), lambda j, d: (0, 0))],
        ),
        out_shape=[jax.ShapeDtypeStruct((rows, tile), jnp.bfloat16)] * 2
        + [jax.ShapeDtypeStruct((8, 128), jnp.float32)],
        compiler_params=params(FIRST_VMEM_LIMIT if after is None else VMEM_LIMIT),
        cost_estimate=cost(
            4 * rows * depth * tile, 2 * (rows * depth + 2 * depth * tile + 2 * rows * tile)
        ),
    )(dests, x, weight, *tail)


def touch_kernel(*refs):
    refs[-1][...] = jnp.zeros_like(refs[-1])


def touch(*arrays):
    return pl.pallas_call(
        touch_kernel,
        in_specs=[ANYWHERE] * len(arrays),
        out_specs=WHOLE,
        out_shape=jax.ShapeDtypeStruct((8, 128), jnp.float32),
        compiler_params=params(),
    )(*arrays)


def collect_kernel(count, index, table_ref, after_ref, out_ref, sems):
    copies = [
        pltpu.make_async_copy(table_ref.at[index[slot]], out_ref.at[slot], sems.at[slot])
        for slot in range(count)
    ]
    for copy in copies:
        copy.start()
    for copy in copies:
        copy.wait()


def collect(index, table, after):
    count = index.shape[0]
    shape = (count,) + table.shape[1:]
    return pl.pallas_call(
        functools.partial(collect_kernel, count),
        grid_spec=pltpu.PrefetchScalarGridSpec(
            num_scalar_prefetch=1,
            grid=(1,),
            in_specs=[ANYWHERE, ANYWHERE],
            out_specs=WHOLE,
            scratch_shapes=[pltpu.SemaphoreType.DMA((count,))],
        ),
        out_shape=jax.ShapeDtypeStruct(shape, table.dtype),
        compiler_params=params(),
        cost_estimate=cost(0, 4 * shape[0] * shape[1] * shape[2]),
    )(index, table, after)


def start_pages(count, local, index, table_ref, got_ref, pages, sems):
    for slot in range(count):
        own = local[slot] == 1

        @pl.when(own)
        def _():
            pltpu.make_async_copy(
                table_ref.at[index[slot]], pages.at[slot], sems.at[slot]
            ).start()

        @pl.when(jnp.logical_not(own))
        def _():
            pltpu.make_async_copy(got_ref.at[slot], pages.at[slot], sems.at[slot]).start()


def wait_pages(slots, got_ref, pages, sems):
    for slot in slots:
        pltpu.make_async_copy(got_ref.at[slot], pages.at[slot], sems.at[slot]).wait()


def low_kernel(
    sizes, local, index, side, x_ref, place_ref, table_ref, got_ref, after_ref, keep_ref, give_ref,
    pages, sems,
):
    steps, blocks, listed, rank, block_rows = sizes
    half = steps * blocks // 2
    start_pages(steps * blocks * listed, local, index, table_ref, got_ref, pages, sems)
    for step in range(steps):
        for block in range(blocks):
            at = step * blocks + block
            wait_pages(range(at * listed, (at + 1) * listed), got_ref, pages, sems)
            listing = pages[at * listed : (at + 1) * listed].reshape(listed * rank, -1)
            every = lax.dot_general(
                listing, x_ref[at * block_rows : (at + 1) * block_rows, :],
                (((1,), (1,)), ((), ())), preferred_element_type=jnp.float32,
            )
            place = place_ref[step : step + 1, block * block_rows : (block + 1) * block_rows]
            low = jnp.zeros((rank, block_rows), jnp.float32)
            for entry in range(listed):
                low = jnp.where(place == entry, every[entry * rank : (entry + 1) * rank], low)
            rows = slice(at % half * block_rows, (at % half + 1) * block_rows)
            mine = side[0] == at // half

            @pl.when(mine)
            def _():
                keep_ref[:, rows] = low

            @pl.when(jnp.logical_not(mine))
            def _():
                give_ref[:, rows] = low


def low_rank(sizes, local, index, side, x, place, table, got, after):
    steps, blocks, listed, rank, block_rows = sizes
    count = steps * blocks * listed
    rows, depth = x.shape
    return pl.pallas_call(
        functools.partial(low_kernel, sizes),
        grid_spec=pltpu.PrefetchScalarGridSpec(
            num_scalar_prefetch=3,
            grid=(1,),
            in_specs=[WHOLE, WHOLE, ANYWHERE, ANYWHERE, ANYWHERE],
            out_specs=[WHOLE, WHOLE],
            scratch_shapes=[
                pltpu.VMEM((count, rank, depth), table.dtype),
                pltpu.SemaphoreType.DMA((count,)),
            ],
        ),
        out_shape=[jax.ShapeDtypeStruct((rank, rows // 2), jnp.float32)] * 2,
        compiler_params=params(),
        cost_estimate=cost(
            2 * rows * depth * listed * rank, 2 * (rows * depth + count * rank * depth)
        ),
    )(local, index, side, x, place, table, got, after)


def add_kernel(low_ref, sent_ref, after_ref, out_ref):
    out_ref[...] = (low_ref[...] + sent_ref[...]).astype(out_ref.dtype)


def add(low, sent, dtype, after):
    return pl.pallas_call(
        add_kernel,
        in_specs=[WHOLE, WHOLE, ANYWHERE],
        out_specs=WHOLE,
        out_shape=jax.ShapeDtypeStruct(low.shape, dtype),
        compiler_params=params(),
        cost_estimate=cost(low.size, 12 * low.size),
    )(low, sent, after)


def own_kernel(
    local, index, dests, x_ref, w_ref, table_ref, got_ref, after_ref, out_ref, pages, sems
):
    tile = w_ref.shape[1]
    now = pl.program_id(0)
    count = pages.shape[0]

    @pl.when(now == 0)
    def _():
        start_pages(count, local, index, table_ref, got_ref, pages, sems)

    columns = pl.ds(pl.multiple_of(now * tile, tile), tile)
    out_ref[:, columns] = jnp.dot(x_ref[...], w_ref[...], preferred_element_type=jnp.float32)

    @pl.when(now == pl.num_programs(0) - 1)
    def _():
        wait_pages(range(count), got_ref, pages, sems)


def own_terms(dests, local, index, x, weight, table, got, after):
    count, rank, cols = got.shape
    rows, depth = x.shape
    tile = min(256, cols)
    tiles = cols // tile
    return pl.pallas_call(
        own_kernel,
        grid_spec=pltpu.PrefetchScalarGridSpec(
            num_scalar_prefetch=3,
            grid=(tiles,),
            in_specs=[
                WHOLE,
                pl.BlockSpec((depth, tile), lambda j, l, i, d: (0, d[0] * tiles + j)),
                ANYWHERE,
                ANYWHERE,
                ANYWHERE,
            ],
            out_specs=[WHOLE, WHOLE],
            scratch_shapes=[pltpu.SemaphoreType.DMA((count,))],
        ),
        out_shape=[
            jax.ShapeDtypeStruct((rows, cols), jnp.float32),
            jax.ShapeDtypeStruct((count, rank, cols), table.dtype),
        ],
        compiler_params=params(),
        cost_estimate=cost(
            2 * rows * cols * depth,
            2 * (rows * depth + depth * cols + 2 * count * rank * cols) + 4 * rows * cols,
        ),
    )(local, index, dests, x, weight, table, got, after)


def delta_kernel(
    sizes, side, own_ref, pages_ref, place_ref, low_ref, other_ref, after_ref, out_ref
):
    steps, blocks, listed, rank, block_rows = sizes
    half = steps * blocks // 2
    entry_of = lax.broadcasted_iota(jnp.int32, (listed * rank, block_rows), 0) // rank
    for step in range(steps):
        for block in range(blocks):
            at = step * blocks + block
            rows = slice(at * block_rows, (at + 1) * block_rows)
            in_half = slice(at % half * block_rows, (at % half + 1) * block_rows)
            low = jnp.where(
                side[0] == at // half,
                low_ref[:, in_half].astype(jnp.float32),
                other_ref[:, in_half].astype(jnp.float32),
            )
            spread = jnp.concatenate([low] * listed, axis=0)
            place = place_ref[step : step + 1, block * block_rows : (block + 1) * block_rows]
            spread = jnp.where(entry_of == place, spread, 0.0)
            listing = pages_ref[at * listed : (at + 1) * listed].reshape(listed * rank, -1)
            out_ref[rows, :] = own_ref[rows, :] + jnp.dot(
                spread.T.astype(jnp.bfloat16), listing, preferred_element_type=jnp.float32
            )


def add_delta(sizes, side, own, pages, place, low, other, after):
    rows, cols = own.shape
    return pl.pallas_call(
        functools.partial(delta_kernel, sizes),
        grid_spec=pltpu.PrefetchScalarGridSpec(
            num_scalar_prefetch=1,
            grid=(1,),
            in_specs=[WHOLE] * 5 + [ANYWHERE],
            out_specs=WHOLE,
        ),
        out_shape=jax.ShapeDtypeStruct(own.shape, own.dtype),
        compiler_params=params(),
        cost_estimate=cost(
            2 * rows * cols * sizes[2] * sizes[3], 8 * rows * cols + 2 * pages.size
        ),
    )(side, own, pages, place, low, other, after)


def chunks(count):
    size = 32 if count % 32 == 0 else GRAIN
    return [slice(at, at + size) for at in range(0, count, size)]


def join_kernel(own_ref, left_ref, right_ref, out_ref):
    cols = left_ref.shape[1]
    for rows in chunks(own_ref.shape[0]):
        for at, part_ref in ((0, left_ref), (cols, right_ref)):
            out_ref[rows, at : at + cols] = own_ref[rows, at : at + cols] + part_ref[
                rows, :
            ].astype(jnp.float32)


def join(own, left, right):
    return pl.pallas_call(
        join_kernel,
        in_specs=[WHOLE] * 3,
        out_specs=WHOLE,
        out_shape=jax.ShapeDtypeStruct(own.shape, own.dtype),
        compiler_params=params(),
        cost_estimate=cost(own.size, 10 * own.size),
    )(own, left, right)


def finish_kernel(half, live, own_ref, last_ref, *refs):
    out_ref, held, sems = refs[-3:]
    rows, cols = held.shape
    count = rows // live.shape[0]
    columns = slice(half * cols, (half + 1) * cols)
    part = rows // sems.shape[0]
    copies = []
    for at in range(sems.shape[0]):
        for chunk in chunks(part):
            here = slice(at * part + chunk.start, at * part + chunk.stop)
            total = own_ref[here, columns] + last_ref[here, :].astype(jnp.float32)
            row = here.start % count + lax.broadcasted_iota(jnp.int32, total.shape, 0)
            alive = row < live[here.start // count]
            held[here, :] = jnp.where(alive, total, 0.0).astype(held.dtype)
        rows_at = pl.ds(at * part, part)
        copies.append(
            pltpu.make_async_copy(held.at[rows_at], out_ref.at[rows_at, columns], sems.at[at])
        )
        copies[-1].start()
    for copy in copies:
        copy.wait()


def finish(live, half, own, last, result):
    rows, cols = own.shape
    steps = live.shape[0]
    in_specs = [WHOLE, WHOLE]
    operands = [own, last]
    aliases = {}
    if result is not None:
        in_specs.append(ANYWHERE)
        operands.append(result)
        aliases = {3: 0}
    return pl.pallas_call(
        functools.partial(finish_kernel, half),
        grid_spec=pltpu.PrefetchScalarGridSpec(
            num_scalar_prefetch=1,
            grid=(1,),
            in_specs=in_specs,
            out_specs=ANYWHERE,
            scratch_shapes=[
                pltpu.VMEM((rows, cols // 2), jnp.bfloat16),
                pltpu.SemaphoreType.DMA((2 * steps,)),
            ],
        ),
        out_shape=jax.ShapeDtypeStruct((rows, cols), jnp.bfloat16),
        input_output_aliases=aliases,
        compiler_params=params(),
        cost_estimate=cost(0, rows * cols * 5),
    )(live, *operands)


def per_device(
    size,
    attention_output,
    output_weight,
    adapter_down_weight,
    adapter_up_weight,
    adapter_page_table,
    block_adapter_ids,
    row_list_position,
    live_row_count,
):
    steps, row_count, depth = attention_output.shape
    resident, rank, _ = adapter_down_weight.shape
    _, blocks, listed = block_adapter_ids.shape
    sizes = (steps, blocks, listed, rank, row_count // blocks)
    x = attention_output.reshape(steps * row_count, depth)
    ring = ring_order(size)

    instance = lax.axis_index("inst")
    place = ring_place(lax.axis_index("tp"), size)
    steps_on = jnp.arange(size, dtype=jnp.int32)
    steps_on = jnp.where(instance == 0, steps_on, size - steps_on)
    dests = ring_index(lax.rem(place + steps_on, size), size)

    up = [(ring[i], ring[(i + 1) % size]) for i in range(size)]
    down = [(ring[i], ring[i - 1]) for i in range(size)]

    def both_instances(first, second):
        return first + [(size + source, size + target) for source, target in second]

    forward, backward = both_instances(up, down), both_instances(down, up)
    far = size // 2
    pairs = [[(0, 1, forward), (1, -1, backward)], [(1, 1, forward), (0, -1, backward)]]
    arrived = {}

    def turn(number, last, between=None):
        left = far - (number + 1) // 2
        for half, sign, moves in pairs[number % 2]:
            last = hop(
                dests, (sign * left) % size, half, x, output_weight,
                arrived.get((half, sign), []), last,
            )
            arrived[half, sign] = [lax.ppermute(last, ("inst", "tp"), moves)]
            if between is not None:
                last, between = touch(*between, last), None
        return last

    ids = block_adapter_ids.reshape(-1)
    ids_there = lax.ppermute(block_adapter_ids, "inst", SWAP).reshape(-1)
    last = None
    for piece in range(tiling(dests, output_weight)[2]):
        *both, last = first_pieces(dests, far % size, piece, x, output_weight, last)
        for (half, sign, moves), part in zip(pairs[0], both):
            arrived.setdefault((half, sign), []).append(lax.ppermute(part, ("inst", "tp"), moves))
    pages = adapter_page_table[jnp.concatenate([ids, ids_there])]
    places = pages % resident
    index, index_there = places[: ids.shape[0]], places[ids.shape[0] :]
    local = (pages[: ids.shape[0]] // resident == instance).astype(jnp.int32)
    last = collect(index_there, adapter_down_weight, last)
    got_down = lax.ppermute(last, "inst", SWAP)
    last = turn(1, last, [arrived[half, sign][0] for half, sign, _ in pairs[0]])
    side = (lax.axis_index("tp") & 1).reshape(1)
    low, give = low_rank(
        sizes, local, index, side, x, row_list_position, adapter_down_weight, got_down, last
    )
    last = low

    def over(value, apart):
        return lax.ppermute(value, "tp", [(i, i ^ apart) for i in range(size)])

    number, turns = 2, 2 * far - 1
    apart = 1
    while apart < size:
        sent = over(((give if apart == 1 else low) * LOW_SCALE).astype(jnp.float16), apart)
        until = turns - 1 if 2 * apart == size else number + 1
        while number < min(until, turns - 1):
            last = turn(number, last)
            if number == 4:
                last = collect(index_there, adapter_up_weight, last)
                got_up = lax.ppermute(last, "inst", SWAP)
            if number == 5:
                own, up_pages = own_terms(
                    dests, local, index, x, output_weight, adapter_up_weight, got_up, last
                )
                last = own
            number += 1
        apart *= 2
        zero = touch(last)[0, 0]
        sent = sent.astype(jnp.float32) * (1.0 / LOW_SCALE) + zero
        low = last = add(low, sent, jnp.float32 if apart < size else jnp.bfloat16, last)
    other = over(low, 1)
    last = turn(number, last)
    own = add_delta(sizes, side, own, up_pages, row_list_position, low, other, last)
    own = join(own, arrived[0, -1][0], arrived[1, 1][0])
    result = None
    for half, sign, _ in pairs[0]:
        result = finish(live_row_count.reshape(-1), half, own, arrived[half, sign][0], result)
    return result.reshape(steps, row_count, -1)


def solution(mesh):
    in_specs = (
        P(None, ("grp", "inst"), "tp"),
        P("tp", None),
        P("inst", None, "tp"),
        P("inst", None, "tp"),
        P(),
        P(None, ("grp", "inst"), None),
        P(None, ("grp", "inst")),
        P(None, ("grp", "inst")),
    )
    out_specs = P(None, ("grp", "inst"), "tp")
    return jax.shard_map(
        functools.partial(per_device, mesh.shape["tp"]),
        mesh=mesh, in_specs=in_specs, out_specs=out_specs, check_vma=False,
    )
```

```python
import functools

import jax
import jax.numpy as jnp
from jax import lax
from jax.experimental import pallas as pl
from jax.experimental.pallas import tpu as pltpu
from jax.sharding import PartitionSpec as P

VMEM_LIMIT = 40 * 1024 * 1024
FIRST_VMEM_LIMIT = 52 * 1024 * 1024
LOW_SCALE = 16.0
GRAIN = 16
SWAP = [(0, 1), (1, 0)]
WHOLE = pl.BlockSpec(memory_space=pltpu.VMEM)
ANYWHERE = pl.BlockSpec(memory_space=pl.ANY)


def serpentine(size):
    return size == 8


def ring_index(place, size):
    if not serpentine(size):
        return place
    return jnp.where(place < size // 2, 2 * place, 2 * (size - 1 - place) + 1)


def ring_place(index, size):
    if not serpentine(size):
        return index
    return jnp.where(index & 1 == 0, index >> 1, size - 1 - (index >> 1))


def ring_order(size):
    if not serpentine(size):
        return list(range(size))
    return list(range(0, size, 2)) + list(range(size - 1, 0, -2))


def params(limit=VMEM_LIMIT):
    return pltpu.CompilerParams(vmem_limit_bytes=limit)


def cost(flops, size):
    return pl.CostEstimate(flops=30 * flops, bytes_accessed=size, transcendentals=0)


def hop_kernel(pieces, dests, x_ref, w_ref, *refs):
    tile = w_ref.shape[1]
    now = pl.program_id(0)
    columns = pl.ds(pl.multiple_of(now * tile, tile), tile)
    total = jnp.dot(x_ref[...], w_ref[...], preferred_element_type=jnp.float32)
    out_ref = refs[-1]
    if len(pieces) == 1:
        out_ref[:, columns] = (total + refs[0][:, columns].astype(jnp.float32)).astype(
            out_ref.dtype
        )
    elif pieces:
        for piece, received_ref in zip(pieces, refs):

            @pl.when(now == piece)
            def _():
                out_ref[:, columns] = (total + received_ref[...].astype(jnp.float32)).astype(
                    out_ref.dtype
                )

    else:
        out_ref[:, columns] = total.astype(out_ref.dtype)


def tiling(dests, weight):
    half_cols = weight.shape[1] // dests.shape[0] // 2
    tile = min(256, half_cols)
    return half_cols, tile, half_cols // tile


def hop(dests, offset, half, x, weight, received, after):
    rows, depth = x.shape
    half_cols, tile, tiles = tiling(dests, weight)
    return pl.pallas_call(
        functools.partial(hop_kernel, tuple(range(len(received)))),
        grid_spec=pltpu.PrefetchScalarGridSpec(
            num_scalar_prefetch=1,
            grid=(tiles,),
            in_specs=[
                WHOLE,
                pl.BlockSpec(
                    (depth, tile), lambda j, d: (0, (d[offset] * 2 + half) * tiles + j)
                ),
            ]
            + [WHOLE] * len(received)
            + [ANYWHERE],
            out_specs=WHOLE,
        ),
        out_shape=jax.ShapeDtypeStruct((rows, half_cols), jnp.bfloat16),
        compiler_params=params(),
        cost_estimate=cost(
            2 * rows * depth * half_cols,
            2 * (rows * depth + depth * half_cols + 2 * rows * half_cols),
        ),
    )(dests, x, weight, *received, after)


def first_kernel(with_after, dests, x_ref, w_ref, *refs):
    total = jnp.dot(x_ref[...], w_ref[...], preferred_element_type=jnp.float32)
    refs[-1][...] = jnp.zeros_like(refs[-1])
    for chain, out_ref in enumerate(refs[-3:-1]):

        @pl.when(pl.program_id(0) == chain)
        def _():
            out_ref[...] = total.astype(out_ref.dtype)


def first_pieces(dests, offset, piece, x, weight, after):
    rows, depth = x.shape
    _, tile, tiles = tiling(dests, weight)
    size = dests.shape[0]

    def place(j, d):
        one = d[offset] * 2 * tiles + piece
        two = (d[(size - offset) % size] * 2 + 1) * tiles + piece
        return (0, jnp.where(j == 0, one, two))

    tail = [] if after is None else [after]
    return pl.pallas_call(
        functools.partial(first_kernel, after is not None),
        grid_spec=pltpu.PrefetchScalarGridSpec(
            num_scalar_prefetch=1,
            grid=(2,),
            in_specs=[
                pl.BlockSpec((rows, depth), lambda j, d: (0, 0)) if after is None else WHOLE,
                pl.BlockSpec((depth, tile), place),
            ]
            + [ANYWHERE] * len(tail),
            out_specs=[WHOLE, WHOLE, pl.BlockSpec((8, 128), lambda j, d: (0, 0))],
        ),
        out_shape=[jax.ShapeDtypeStruct((rows, tile), jnp.bfloat16)] * 2
        + [jax.ShapeDtypeStruct((8, 128), jnp.float32)],
        compiler_params=params(FIRST_VMEM_LIMIT if after is None else VMEM_LIMIT),
        cost_estimate=cost(
            4 * rows * depth * tile, 2 * (rows * depth + 2 * depth * tile + 2 * rows * tile)
        ),
    )(dests, x, weight, *tail)


def touch_kernel(*refs):
    refs[-1][...] = jnp.zeros_like(refs[-1])


def touch(*arrays):
    return pl.pallas_call(
        touch_kernel,
        in_specs=[ANYWHERE] * len(arrays),
        out_specs=WHOLE,
        out_shape=jax.ShapeDtypeStruct((8, 128), jnp.float32),
        compiler_params=params(),
    )(*arrays)


def collect_kernel(count, index, table_ref, after_ref, out_ref, sems):
    copies = [
        pltpu.make_async_copy(table_ref.at[index[slot]], out_ref.at[slot], sems.at[slot])
        for slot in range(count)
    ]
    for copy in copies:
        copy.start()
    for copy in copies:
        copy.wait()


def collect(index, table, after):
    count = index.shape[0]
    shape = (count,) + table.shape[1:]
    return pl.pallas_call(
        functools.partial(collect_kernel, count),
        grid_spec=pltpu.PrefetchScalarGridSpec(
            num_scalar_prefetch=1,
            grid=(1,),
            in_specs=[ANYWHERE, ANYWHERE],
            out_specs=WHOLE,
            scratch_shapes=[pltpu.SemaphoreType.DMA((count,))],
        ),
        out_shape=jax.ShapeDtypeStruct(shape, table.dtype),
        compiler_params=params(),
        cost_estimate=cost(0, 4 * shape[0] * shape[1] * shape[2]),
    )(index, table, after)


def start_pages(count, local, index, table_ref, got_ref, pages, sems):
    for slot in range(count):
        own = local[slot] == 1

        @pl.when(own)
        def _():
            pltpu.make_async_copy(
                table_ref.at[index[slot]], pages.at[slot], sems.at[slot]
            ).start()

        @pl.when(jnp.logical_not(own))
        def _():
            pltpu.make_async_copy(got_ref.at[slot], pages.at[slot], sems.at[slot]).start()


def wait_pages(slots, got_ref, pages, sems):
    for slot in slots:
        pltpu.make_async_copy(got_ref.at[slot], pages.at[slot], sems.at[slot]).wait()


def low_kernel(
    sizes, local, index, side, x_ref, place_ref, table_ref, got_ref, after_ref, keep_ref, give_ref,
    pages, sems,
):
    steps, blocks, listed, rank, block_rows = sizes
    half = steps * blocks // 2
    start_pages(steps * blocks * listed, local, index, table_ref, got_ref, pages, sems)
    for step in range(steps):
        for block in range(blocks):
            at = step * blocks + block
            wait_pages(range(at * listed, (at + 1) * listed), got_ref, pages, sems)
            listing = pages[at * listed : (at + 1) * listed].reshape(listed * rank, -1)
            every = lax.dot_general(
                listing, x_ref[at * block_rows : (at + 1) * block_rows, :],
                (((1,), (1,)), ((), ())), preferred_element_type=jnp.float32,
            )
            place = place_ref[step : step + 1, block * block_rows : (block + 1) * block_rows]
            low = jnp.zeros((rank, block_rows), jnp.float32)
            for entry in range(listed):
                low = jnp.where(place == entry, every[entry * rank : (entry + 1) * rank], low)
            rows = slice(at % half * block_rows, (at % half + 1) * block_rows)
            mine = side[0] == at // half

            @pl.when(mine)
            def _():
                keep_ref[:, rows] = low

            @pl.when(jnp.logical_not(mine))
            def _():
                give_ref[:, rows] = low


def low_rank(sizes, local, index, side, x, place, table, got, after):
    steps, blocks, listed, rank, block_rows = sizes
    count = steps * blocks * listed
    rows, depth = x.shape
    return pl.pallas_call(
        functools.partial(low_kernel, sizes),
        grid_spec=pltpu.PrefetchScalarGridSpec(
            num_scalar_prefetch=3,
            grid=(1,),
            in_specs=[WHOLE, WHOLE, ANYWHERE, ANYWHERE, ANYWHERE],
            out_specs=[WHOLE, WHOLE],
            scratch_shapes=[
                pltpu.VMEM((count, rank, depth), table.dtype),
                pltpu.SemaphoreType.DMA((count,)),
            ],
        ),
        out_shape=[jax.ShapeDtypeStruct((rank, rows // 2), jnp.float32)] * 2,
        compiler_params=params(),
        cost_estimate=cost(
            2 * rows * depth * listed * rank, 2 * (rows * depth + count * rank * depth)
        ),
    )(local, index, side, x, place, table, got, after)


def add_kernel(low_ref, sent_ref, after_ref, out_ref):
    out_ref[...] = (low_ref[...] + sent_ref[...]).astype(out_ref.dtype)


def add(low, sent, dtype, after):
    return pl.pallas_call(
        add_kernel,
        in_specs=[WHOLE, WHOLE, ANYWHERE],
        out_specs=WHOLE,
        out_shape=jax.ShapeDtypeStruct(low.shape, dtype),
        compiler_params=params(),
        cost_estimate=cost(low.size, 12 * low.size),
    )(low, sent, after)


def own_kernel(
    local, index, dests, x_ref, w_ref, table_ref, got_ref, after_ref, out_ref, pages, sems
):
    tile = w_ref.shape[1]
    now = pl.program_id(0)
    count = pages.shape[0]

    @pl.when(now == 0)
    def _():
        start_pages(count, local, index, table_ref, got_ref, pages, sems)

    columns = pl.ds(pl.multiple_of(now * tile, tile), tile)
    out_ref[:, columns] = jnp.dot(x_ref[...], w_ref[...], preferred_element_type=jnp.float32)

    @pl.when(now == pl.num_programs(0) - 1)
    def _():
        wait_pages(range(count), got_ref, pages, sems)


def own_terms(dests, local, index, x, weight, table, got, after):
    count, rank, cols = got.shape
    rows, depth = x.shape
    tile = min(256, cols)
    tiles = cols // tile
    return pl.pallas_call(
        own_kernel,
        grid_spec=pltpu.PrefetchScalarGridSpec(
            num_scalar_prefetch=3,
            grid=(tiles,),
            in_specs=[
                WHOLE,
                pl.BlockSpec((depth, tile), lambda j, l, i, d: (0, d[0] * tiles + j)),
                ANYWHERE,
                ANYWHERE,
                ANYWHERE,
            ],
            out_specs=[WHOLE, WHOLE],
            scratch_shapes=[pltpu.SemaphoreType.DMA((count,))],
        ),
        out_shape=[
            jax.ShapeDtypeStruct((rows, cols), jnp.float32),
            jax.ShapeDtypeStruct((count, rank, cols), table.dtype),
        ],
        compiler_params=params(),
        cost_estimate=cost(
            2 * rows * cols * depth,
            2 * (rows * depth + depth * cols + 2 * count * rank * cols) + 4 * rows * cols,
        ),
    )(local, index, dests, x, weight, table, got, after)


def delta_kernel(
    sizes, side, own_ref, pages_ref, place_ref, low_ref, other_ref, after_ref, out_ref
):
    steps, blocks, listed, rank, block_rows = sizes
    half = steps * blocks // 2
    entry_of = lax.broadcasted_iota(jnp.int32, (listed * rank, block_rows), 0) // rank
    for step in range(steps):
        for block in range(blocks):
            at = step * blocks + block
            rows = slice(at * block_rows, (at + 1) * block_rows)
            in_half = slice(at % half * block_rows, (at % half + 1) * block_rows)
            low = jnp.where(
                side[0] == at // half,
                low_ref[:, in_half].astype(jnp.float32),
                other_ref[:, in_half].astype(jnp.float32),
            )
            spread = jnp.concatenate([low] * listed, axis=0)
            place = place_ref[step : step + 1, block * block_rows : (block + 1) * block_rows]
            spread = jnp.where(entry_of == place, spread, 0.0)
            listing = pages_ref[at * listed : (at + 1) * listed].reshape(listed * rank, -1)
            out_ref[rows, :] = own_ref[rows, :] + jnp.dot(
                spread.T.astype(jnp.bfloat16), listing, preferred_element_type=jnp.float32
            )


def add_delta(sizes, side, own, pages, place, low, other, after):
    rows, cols = own.shape
    return pl.pallas_call(
        functools.partial(delta_kernel, sizes),
        grid_spec=pltpu.PrefetchScalarGridSpec(
            num_scalar_prefetch=1,
            grid=(1,),
            in_specs=[WHOLE] * 5 + [ANYWHERE],
            out_specs=WHOLE,
        ),
        out_shape=jax.ShapeDtypeStruct(own.shape, own.dtype),
        compiler_params=params(),
        cost_estimate=cost(
            2 * rows * cols * sizes[2] * sizes[3], 8 * rows * cols + 2 * pages.size
        ),
    )(side, own, pages, place, low, other, after)


def chunks(count):
    size = 32 if count % 32 == 0 else GRAIN
    return [slice(at, at + size) for at in range(0, count, size)]


def join_kernel(own_ref, left_ref, right_ref, out_ref):
    cols = left_ref.shape[1]
    for rows in chunks(own_ref.shape[0]):
        for at, part_ref in ((0, left_ref), (cols, right_ref)):
            out_ref[rows, at : at + cols] = own_ref[rows, at : at + cols] + part_ref[
                rows, :
            ].astype(jnp.float32)


def join(own, left, right):
    return pl.pallas_call(
        join_kernel,
        in_specs=[WHOLE] * 3,
        out_specs=WHOLE,
        out_shape=jax.ShapeDtypeStruct(own.shape, own.dtype),
        compiler_params=params(),
        cost_estimate=cost(own.size, 10 * own.size),
    )(own, left, right)


def finish_kernel(live, own_ref, left_ref, right_ref, out_ref, held, sems):
    rows, cols = held.shape
    half = cols // 2
    count = rows // live.shape[0]
    part = rows // sems.shape[0]
    copies = []
    for at in range(sems.shape[0]):
        for chunk in chunks(part):
            here = slice(at * part + chunk.start, at * part + chunk.stop)
            row = here.start % count + lax.broadcasted_iota(
                jnp.int32, (here.stop - here.start, half), 0
            )
            alive = row < live[here.start // count]
            for columns, last_ref in ((slice(0, half), left_ref), (slice(half, cols), right_ref)):
                total = own_ref[here, columns] + last_ref[here, :].astype(jnp.float32)
                held[here, columns] = jnp.where(alive, total, 0.0).astype(held.dtype)
        rows_at = pl.ds(at * part, part)
        copies.append(pltpu.make_async_copy(held.at[rows_at], out_ref.at[rows_at], sems.at[at]))
        copies[-1].start()
    for copy in copies:
        copy.wait()


def finish(live, own, left, right):
    rows, cols = own.shape
    return pl.pallas_call(
        finish_kernel,
        grid_spec=pltpu.PrefetchScalarGridSpec(
            num_scalar_prefetch=1,
            grid=(1,),
            in_specs=[WHOLE] * 3,
            out_specs=ANYWHERE,
            scratch_shapes=[
                pltpu.VMEM((rows, cols), jnp.bfloat16),
                pltpu.SemaphoreType.DMA((4 * live.shape[0],)),
            ],
        ),
        out_shape=jax.ShapeDtypeStruct((rows, cols), jnp.bfloat16),
        compiler_params=params(),
        cost_estimate=cost(0, rows * cols * 10),
    )(live, own, left, right)


def per_device(
    size,
    attention_output,
    output_weight,
    adapter_down_weight,
    adapter_up_weight,
    adapter_page_table,
    block_adapter_ids,
    row_list_position,
    live_row_count,
):
    steps, row_count, depth = attention_output.shape
    resident, rank, _ = adapter_down_weight.shape
    _, blocks, listed = block_adapter_ids.shape
    sizes = (steps, blocks, listed, rank, row_count // blocks)
    x = attention_output.reshape(steps * row_count, depth)
    ring = ring_order(size)

    instance = lax.axis_index("inst")
    place = ring_place(lax.axis_index("tp"), size)
    steps_on = jnp.arange(size, dtype=jnp.int32)
    steps_on = jnp.where(instance == 0, steps_on, size - steps_on)
    dests = ring_index(lax.rem(place + steps_on, size), size)

    up = [(ring[i], ring[(i + 1) % size]) for i in range(size)]
    down = [(ring[i], ring[i - 1]) for i in range(size)]

    def both_instances(first, second):
        return first + [(size + source, size + target) for source, target in second]

    forward, backward = both_instances(up, down), both_instances(down, up)
    far = size // 2
    pairs = [[(0, 1, forward), (1, -1, backward)], [(1, 1, forward), (0, -1, backward)]]
    arrived = {}

    def turn(number, last, between=None):
        left = far - (number + 1) // 2
        for half, sign, moves in pairs[number % 2]:
            last = hop(
                dests, (sign * left) % size, half, x, output_weight,
                arrived.get((half, sign), []), last,
            )
            arrived[half, sign] = [lax.ppermute(last, ("inst", "tp"), moves)]
            if between is not None:
                last, between = touch(*between, last), None
        return last

    ids = block_adapter_ids.reshape(-1)
    ids_there = lax.ppermute(block_adapter_ids, "inst", SWAP).reshape(-1)
    last = None
    for piece in range(tiling(dests, output_weight)[2]):
        *both, last = first_pieces(dests, far % size, piece, x, output_weight, last)
        for (half, sign, moves), part in zip(pairs[0], both):
            arrived.setdefault((half, sign), []).append(lax.ppermute(part, ("inst", "tp"), moves))
    pages = adapter_page_table[jnp.concatenate([ids, ids_there])]
    places = pages % resident
    index, index_there = places[: ids.shape[0]], places[ids.shape[0] :]
    local = (pages[: ids.shape[0]] // resident == instance).astype(jnp.int32)
    last = collect(index_there, adapter_down_weight, last)
    got_down = lax.ppermute(last, "inst", SWAP)
    last = turn(1, last, [arrived[half, sign][0] for half, sign, _ in pairs[0]])
    side = (lax.axis_index("tp") & 1).reshape(1)
    low, give = low_rank(
        sizes, local, index, side, x, row_list_position, adapter_down_weight, got_down, last
    )
    last = low

    def over(value, apart):
        return lax.ppermute(value, "tp", [(i, i ^ apart) for i in range(size)])

    number, turns = 2, 2 * far - 1
    apart = 1
    while apart < size:
        sent = over(((give if apart == 1 else low) * LOW_SCALE).astype(jnp.float16), apart)
        until = turns - 1 if 2 * apart == size else number + 1
        while number < min(until, turns - 1):
            last = turn(number, last)
            if number == 4:
                last = collect(index_there, adapter_up_weight, last)
                got_up = lax.ppermute(last, "inst", SWAP)
            if number == 5:
                own, up_pages = own_terms(
                    dests, local, index, x, output_weight, adapter_up_weight, got_up, last
                )
                last = own
            number += 1
        apart *= 2
        zero = touch(last)[0, 0]
        sent = sent.astype(jnp.float32) * (1.0 / LOW_SCALE) + zero
        low = last = add(low, sent, jnp.float32 if apart < size else jnp.bfloat16, last)
    other = over(low, 1)
    last = turn(number, last)
    own = add_delta(sizes, side, own, up_pages, row_list_position, low, other, last)
    own = join(own, arrived[0, -1][0], arrived[1, 1][0])
    result = finish(live_row_count.reshape(-1), own, arrived[0, 1][0], arrived[1, -1][0])
    return result.reshape(steps, row_count, -1)


def solution(mesh):
    in_specs = (
        P(None, ("grp", "inst"), "tp"),
        P("tp", None),
        P("inst", None, "tp"),
        P("inst", None, "tp"),
        P(),
        P(None, ("grp", "inst"), None),
        P(None, ("grp", "inst")),
        P(None, ("grp", "inst")),
    )
    out_specs = P(None, ("grp", "inst"), "tp")
    return jax.shard_map(
        functools.partial(per_device, mesh.shape["tp"]),
        mesh=mesh, in_specs=in_specs, out_specs=out_specs, check_vma=False,
    )
```

```python
import functools

import jax
import jax.numpy as jnp
from jax import lax
from jax.experimental import pallas as pl
from jax.experimental.pallas import tpu as pltpu
from jax.sharding import PartitionSpec as P

VMEM_LIMIT = 40 * 1024 * 1024
FIRST_VMEM_LIMIT = 52 * 1024 * 1024
GRAIN = 16
SWAP = [(0, 1), (1, 0)]
WHOLE = pl.BlockSpec(memory_space=pltpu.VMEM)
ANYWHERE = pl.BlockSpec(memory_space=pl.ANY)


def serpentine(size):
    return size == 8


def ring_index(place, size):
    if not serpentine(size):
        return place
    return jnp.where(place < size // 2, 2 * place, 2 * (size - 1 - place) + 1)


def ring_place(index, size):
    if not serpentine(size):
        return index
    return jnp.where(index & 1 == 0, index >> 1, size - 1 - (index >> 1))


def ring_order(size):
    if not serpentine(size):
        return list(range(size))
    return list(range(0, size, 2)) + list(range(size - 1, 0, -2))


def params(limit=VMEM_LIMIT):
    return pltpu.CompilerParams(vmem_limit_bytes=limit)


def cost(flops, size):
    return pl.CostEstimate(flops=30 * flops, bytes_accessed=size, transcendentals=0)


def hop_kernel(pieces, dests, x_ref, w_ref, *refs):
    tile = w_ref.shape[1]
    now = pl.program_id(0)
    columns = pl.ds(pl.multiple_of(now * tile, tile), tile)
    total = jnp.dot(x_ref[...], w_ref[...], preferred_element_type=jnp.float32)
    out_ref = refs[-1]
    if len(pieces) == 1:
        out_ref[:, columns] = (total + refs[0][:, columns].astype(jnp.float32)).astype(
            out_ref.dtype
        )
    elif pieces:
        for piece, received_ref in zip(pieces, refs):

            @pl.when(now == piece)
            def _():
                out_ref[:, columns] = (total + received_ref[...].astype(jnp.float32)).astype(
                    out_ref.dtype
                )

    else:
        out_ref[:, columns] = total.astype(out_ref.dtype)


def tiling(dests, weight):
    half_cols = weight.shape[1] // dests.shape[0] // 2
    tile = min(256, half_cols)
    return half_cols, tile, half_cols // tile


def hop(dests, offset, half, x, weight, received, after):
    rows, depth = x.shape
    half_cols, tile, tiles = tiling(dests, weight)
    return pl.pallas_call(
        functools.partial(hop_kernel, tuple(range(len(received)))),
        grid_spec=pltpu.PrefetchScalarGridSpec(
            num_scalar_prefetch=1,
            grid=(tiles,),
            in_specs=[
                WHOLE,
                pl.BlockSpec(
                    (depth, tile), lambda j, d: (0, (d[offset] * 2 + half) * tiles + j)
                ),
            ]
            + [WHOLE] * len(received)
            + [ANYWHERE],
            out_specs=WHOLE,
        ),
        out_shape=jax.ShapeDtypeStruct((rows, half_cols), jnp.bfloat16),
        compiler_params=params(),
        cost_estimate=cost(
            2 * rows * depth * half_cols,
            2 * (rows * depth + depth * half_cols + 2 * rows * half_cols),
        ),
    )(dests, x, weight, *received, after)


def first_kernel(with_after, dests, x_ref, w_ref, *refs):
    total = jnp.dot(x_ref[...], w_ref[...], preferred_element_type=jnp.float32)
    refs[-1][...] = jnp.zeros_like(refs[-1])
    for chain, out_ref in enumerate(refs[-3:-1]):

        @pl.when(pl.program_id(0) == chain)
        def _():
            out_ref[...] = total.astype(out_ref.dtype)


def first_pieces(dests, offset, piece, x, weight, after):
    rows, depth = x.shape
    _, tile, tiles = tiling(dests, weight)
    size = dests.shape[0]

    def place(j, d):
        one = d[offset] * 2 * tiles + piece
        two = (d[(size - offset) % size] * 2 + 1) * tiles + piece
        return (0, jnp.where(j == 0, one, two))

    tail = [] if after is None else [after]
    return pl.pallas_call(
        functools.partial(first_kernel, after is not None),
        grid_spec=pltpu.PrefetchScalarGridSpec(
            num_scalar_prefetch=1,
            grid=(2,),
            in_specs=[
                pl.BlockSpec((rows, depth), lambda j, d: (0, 0)) if after is None else WHOLE,
                pl.BlockSpec((depth, tile), place),
            ]
            + [ANYWHERE] * len(tail),
            out_specs=[WHOLE, WHOLE, pl.BlockSpec((8, 128), lambda j, d: (0, 0))],
        ),
        out_shape=[jax.ShapeDtypeStruct((rows, tile), jnp.bfloat16)] * 2
        + [jax.ShapeDtypeStruct((8, 128), jnp.float32)],
        compiler_params=params(FIRST_VMEM_LIMIT if after is None else VMEM_LIMIT),
        cost_estimate=cost(
            4 * rows * depth * tile, 2 * (rows * depth + 2 * depth * tile + 2 * rows * tile)
        ),
    )(dests, x, weight, *tail)


def touch_kernel(*refs):
    refs[-1][...] = jnp.zeros_like(refs[-1])


def touch(*arrays):
    return pl.pallas_call(
        touch_kernel,
        in_specs=[ANYWHERE] * len(arrays),
        out_specs=WHOLE,
        out_shape=jax.ShapeDtypeStruct((8, 128), jnp.float32),
        compiler_params=params(),
    )(*arrays)


def collect_kernel(count, index, table_ref, after_ref, out_ref, sems):
    copies = [
        pltpu.make_async_copy(table_ref.at[index[slot]], out_ref.at[slot], sems.at[slot])
        for slot in range(count)
    ]
    for copy in copies:
        copy.start()
    for copy in copies:
        copy.wait()


def collect(index, table, after):
    count = index.shape[0]
    shape = (count,) + table.shape[1:]
    return pl.pallas_call(
        functools.partial(collect_kernel, count),
        grid_spec=pltpu.PrefetchScalarGridSpec(
            num_scalar_prefetch=1,
            grid=(1,),
            in_specs=[ANYWHERE, ANYWHERE],
            out_specs=WHOLE,
            scratch_shapes=[pltpu.SemaphoreType.DMA((count,))],
        ),
        out_shape=jax.ShapeDtypeStruct(shape, table.dtype),
        compiler_params=params(),
        cost_estimate=cost(0, 4 * shape[0] * shape[1] * shape[2]),
    )(index, table, after)


def start_pages(count, local, index, table_ref, got_ref, pages, sems):
    for slot in range(count):
        own = local[slot] == 1

        @pl.when(own)
        def _():
            pltpu.make_async_copy(
                table_ref.at[index[slot]], pages.at[slot], sems.at[slot]
            ).start()

        @pl.when(jnp.logical_not(own))
        def _():
            pltpu.make_async_copy(got_ref.at[slot], pages.at[slot], sems.at[slot]).start()


def wait_pages(slots, got_ref, pages, sems):
    for slot in slots:
        pltpu.make_async_copy(got_ref.at[slot], pages.at[slot], sems.at[slot]).wait()


def low_kernel(
    sizes, local, index, side, x_ref, place_ref, table_ref, got_ref, after_ref, keep_ref, give_ref,
    pages, sems,
):
    steps, blocks, listed, rank, block_rows = sizes
    half = steps * blocks // 2
    start_pages(steps * blocks * listed, local, index, table_ref, got_ref, pages, sems)
    for step in range(steps):
        for block in range(blocks):
            at = step * blocks + block
            wait_pages(range(at * listed, (at + 1) * listed), got_ref, pages, sems)
            listing = pages[at * listed : (at + 1) * listed].reshape(listed * rank, -1)
            every = lax.dot_general(
                listing, x_ref[at * block_rows : (at + 1) * block_rows, :],
                (((1,), (1,)), ((), ())), preferred_element_type=jnp.float32,
            )
            place = place_ref[step : step + 1, block * block_rows : (block + 1) * block_rows]
            low = jnp.zeros((rank, block_rows), jnp.float32)
            for entry in range(listed):
                low = jnp.where(place == entry, every[entry * rank : (entry + 1) * rank], low)
            rows = slice(at % half * block_rows, (at % half + 1) * block_rows)
            mine = side[0] == at // half

            @pl.when(mine)
            def _():
                keep_ref[:, rows] = low

            @pl.when(jnp.logical_not(mine))
            def _():
                give_ref[:, rows] = low


def low_rank(sizes, local, index, side, x, place, table, got, after):
    steps, blocks, listed, rank, block_rows = sizes
    count = steps * blocks * listed
    rows, depth = x.shape
    return pl.pallas_call(
        functools.partial(low_kernel, sizes),
        grid_spec=pltpu.PrefetchScalarGridSpec(
            num_scalar_prefetch=3,
            grid=(1,),
            in_specs=[WHOLE, WHOLE, ANYWHERE, ANYWHERE, ANYWHERE],
            out_specs=[WHOLE, WHOLE],
            scratch_shapes=[
                pltpu.VMEM((count, rank, depth), table.dtype),
                pltpu.SemaphoreType.DMA((count,)),
            ],
        ),
        out_shape=[jax.ShapeDtypeStruct((rank, rows // 2), jnp.float32)] * 2,
        compiler_params=params(),
        cost_estimate=cost(
            2 * rows * depth * listed * rank, 2 * (rows * depth + count * rank * depth)
        ),
    )(local, index, side, x, place, table, got, after)


def add_kernel(low_ref, sent_ref, after_ref, out_ref):
    out_ref[...] = (low_ref[...] + sent_ref[...]).astype(out_ref.dtype)


def add(low, sent, dtype, after):
    return pl.pallas_call(
        add_kernel,
        in_specs=[WHOLE, WHOLE, ANYWHERE],
        out_specs=WHOLE,
        out_shape=jax.ShapeDtypeStruct(low.shape, dtype),
        compiler_params=params(),
        cost_estimate=cost(low.size, 12 * low.size),
    )(low, sent, after)


def own_kernel(
    local, index, dests, x_ref, w_ref, table_ref, got_ref, after_ref, out_ref, pages, sems
):
    tile = w_ref.shape[1]
    now = pl.program_id(0)
    count = pages.shape[0]

    @pl.when(now == 0)
    def _():
        start_pages(count, local, index, table_ref, got_ref, pages, sems)

    columns = pl.ds(pl.multiple_of(now * tile, tile), tile)
    out_ref[:, columns] = jnp.dot(x_ref[...], w_ref[...], preferred_element_type=jnp.float32)

    @pl.when(now == pl.num_programs(0) - 1)
    def _():
        wait_pages(range(count), got_ref, pages, sems)


def own_terms(dests, local, index, x, weight, table, got, after):
    count, rank, cols = got.shape
    rows, depth = x.shape
    tile = min(256, cols)
    tiles = cols // tile
    return pl.pallas_call(
        own_kernel,
        grid_spec=pltpu.PrefetchScalarGridSpec(
            num_scalar_prefetch=3,
            grid=(tiles,),
            in_specs=[
                WHOLE,
                pl.BlockSpec((depth, tile), lambda j, l, i, d: (0, d[0] * tiles + j)),
                ANYWHERE,
                ANYWHERE,
                ANYWHERE,
            ],
            out_specs=[WHOLE, WHOLE],
            scratch_shapes=[pltpu.SemaphoreType.DMA((count,))],
        ),
        out_shape=[
            jax.ShapeDtypeStruct((rows, cols), jnp.float32),
            jax.ShapeDtypeStruct((count, rank, cols), table.dtype),
        ],
        compiler_params=params(),
        cost_estimate=cost(
            2 * rows * cols * depth,
            2 * (rows * depth + depth * cols + 2 * count * rank * cols) + 4 * rows * cols,
        ),
    )(local, index, dests, x, weight, table, got, after)


def delta_kernel(
    sizes, side, own_ref, pages_ref, place_ref, low_ref, other_ref, after_ref, out_ref
):
    steps, blocks, listed, rank, block_rows = sizes
    half = steps * blocks // 2
    entry_of = lax.broadcasted_iota(jnp.int32, (listed * rank, block_rows), 0) // rank
    for step in range(steps):
        for block in range(blocks):
            at = step * blocks + block
            rows = slice(at * block_rows, (at + 1) * block_rows)
            in_half = slice(at % half * block_rows, (at % half + 1) * block_rows)
            low = jnp.where(
                side[0] == at // half,
                low_ref[:, in_half].astype(jnp.float32),
                other_ref[:, in_half].astype(jnp.float32),
            )
            spread = jnp.concatenate([low] * listed, axis=0)
            place = place_ref[step : step + 1, block * block_rows : (block + 1) * block_rows]
            spread = jnp.where(entry_of == place, spread, 0.0)
            listing = pages_ref[at * listed : (at + 1) * listed].reshape(listed * rank, -1)
            out_ref[rows, :] = own_ref[rows, :] + jnp.dot(
                spread.T.astype(jnp.bfloat16), listing, preferred_element_type=jnp.float32
            )


def add_delta(sizes, side, own, pages, place, low, other, after):
    rows, cols = own.shape
    return pl.pallas_call(
        functools.partial(delta_kernel, sizes),
        grid_spec=pltpu.PrefetchScalarGridSpec(
            num_scalar_prefetch=1,
            grid=(1,),
            in_specs=[WHOLE] * 5 + [ANYWHERE],
            out_specs=WHOLE,
        ),
        out_shape=jax.ShapeDtypeStruct(own.shape, own.dtype),
        compiler_params=params(),
        cost_estimate=cost(
            2 * rows * cols * sizes[2] * sizes[3], 8 * rows * cols + 2 * pages.size
        ),
    )(side, own, pages, place, low, other, after)


def chunks(count):
    size = 32 if count % 32 == 0 else GRAIN
    return [slice(at, at + size) for at in range(0, count, size)]


def join_kernel(own_ref, left_ref, right_ref, out_ref):
    cols = left_ref.shape[1]
    for rows in chunks(own_ref.shape[0]):
        for at, part_ref in ((0, left_ref), (cols, right_ref)):
            out_ref[rows, at : at + cols] = own_ref[rows, at : at + cols] + part_ref[
                rows, :
            ].astype(jnp.float32)


def join(own, left, right):
    return pl.pallas_call(
        join_kernel,
        in_specs=[WHOLE] * 3,
        out_specs=WHOLE,
        out_shape=jax.ShapeDtypeStruct(own.shape, own.dtype),
        compiler_params=params(),
        cost_estimate=cost(own.size, 10 * own.size),
    )(own, left, right)


def finish_kernel(half, live, own_ref, last_ref, *refs):
    out_ref, held, sems = refs[-3:]
    rows, cols = held.shape
    count = rows // live.shape[0]
    columns = slice(half * cols, (half + 1) * cols)
    part = rows // sems.shape[0]
    copies = []
    for at in range(sems.shape[0]):
        for chunk in chunks(part):
            here = slice(at * part + chunk.start, at * part + chunk.stop)
            total = own_ref[here, columns] + last_ref[here, :].astype(jnp.float32)
            row = here.start % count + lax.broadcasted_iota(jnp.int32, total.shape, 0)
            alive = row < live[here.start // count]
            held[here, :] = jnp.where(alive, total, 0.0).astype(held.dtype)
        rows_at = pl.ds(at * part, part)
        copies.append(
            pltpu.make_async_copy(held.at[rows_at], out_ref.at[rows_at, columns], sems.at[at])
        )
        copies[-1].start()
    for copy in copies:
        copy.wait()


def finish(live, half, own, last, result):
    rows, cols = own.shape
    steps = live.shape[0]
    in_specs = [WHOLE, WHOLE]
    operands = [own, last]
    aliases = {}
    if result is not None:
        in_specs.append(ANYWHERE)
        operands.append(result)
        aliases = {3: 0}
    return pl.pallas_call(
        functools.partial(finish_kernel, half),
        grid_spec=pltpu.PrefetchScalarGridSpec(
            num_scalar_prefetch=1,
            grid=(1,),
            in_specs=in_specs,
            out_specs=ANYWHERE,
            scratch_shapes=[
                pltpu.VMEM((rows, cols // 2), jnp.bfloat16),
                pltpu.SemaphoreType.DMA((2 * steps,)),
            ],
        ),
        out_shape=jax.ShapeDtypeStruct((rows, cols), jnp.bfloat16),
        input_output_aliases=aliases,
        compiler_params=params(),
        cost_estimate=cost(0, rows * cols * 5),
    )(live, *operands)


def per_device(
    size,
    attention_output,
    output_weight,
    adapter_down_weight,
    adapter_up_weight,
    adapter_page_table,
    block_adapter_ids,
    row_list_position,
    live_row_count,
):
    steps, row_count, depth = attention_output.shape
    resident, rank, _ = adapter_down_weight.shape
    _, blocks, listed = block_adapter_ids.shape
    sizes = (steps, blocks, listed, rank, row_count // blocks)
    x = attention_output.reshape(steps * row_count, depth)
    ring = ring_order(size)

    instance = lax.axis_index("inst")
    place = ring_place(lax.axis_index("tp"), size)
    steps_on = jnp.arange(size, dtype=jnp.int32)
    steps_on = jnp.where(instance == 0, steps_on, size - steps_on)
    dests = ring_index(lax.rem(place + steps_on, size), size)

    up = [(ring[i], ring[(i + 1) % size]) for i in range(size)]
    down = [(ring[i], ring[i - 1]) for i in range(size)]

    def both_instances(first, second):
        return first + [(size + source, size + target) for source, target in second]

    forward, backward = both_instances(up, down), both_instances(down, up)
    far = size // 2
    pairs = [[(0, 1, forward), (1, -1, backward)], [(1, 1, forward), (0, -1, backward)]]
    arrived = {}

    def turn(number, last, between=None):
        left = far - (number + 1) // 2
        for half, sign, moves in pairs[number % 2]:
            last = hop(
                dests, (sign * left) % size, half, x, output_weight,
                arrived.get((half, sign), []), last,
            )
            arrived[half, sign] = [lax.ppermute(last, ("inst", "tp"), moves)]
            if between is not None:
                last, between = touch(*between, last), None
        return last

    ids = block_adapter_ids.reshape(-1)
    ids_there = lax.ppermute(block_adapter_ids, "inst", SWAP).reshape(-1)
    last = None
    for piece in range(tiling(dests, output_weight)[2]):
        *both, last = first_pieces(dests, far % size, piece, x, output_weight, last)
        for (half, sign, moves), part in zip(pairs[0], both):
            arrived.setdefault((half, sign), []).append(lax.ppermute(part, ("inst", "tp"), moves))
    pages = adapter_page_table[jnp.concatenate([ids, ids_there])]
    places = pages % resident
    index, index_there = places[: ids.shape[0]], places[ids.shape[0] :]
    local = (pages[: ids.shape[0]] // resident == instance).astype(jnp.int32)
    last = collect(index_there, adapter_down_weight, last)
    got_down = lax.ppermute(last, "inst", SWAP)
    last = turn(1, last, [arrived[half, sign][0] for half, sign, _ in pairs[0]])
    side = (lax.axis_index("tp") & 1).reshape(1)
    low, give = low_rank(
        sizes, local, index, side, x, row_list_position, adapter_down_weight, got_down, last
    )
    last = low

    def over(value, apart):
        return lax.ppermute(value, "tp", [(i, i ^ apart) for i in range(size)])

    number, turns = 2, 2 * far - 1
    apart = 1
    while apart < size:
        sent = over(give if apart == 1 else low, apart)
        until = turns - 1 if 2 * apart == size else number + 1
        while number < min(until, turns - 1):
            last = turn(number, last)
            if number == 4:
                last = collect(index_there, adapter_up_weight, last)
                got_up = lax.ppermute(last, "inst", SWAP)
            if number == 5:
                own, up_pages = own_terms(
                    dests, local, index, x, output_weight, adapter_up_weight, got_up, last
                )
                last = own
            number += 1
        apart *= 2
        low = last = add(low, sent, jnp.float32 if apart < size else jnp.bfloat16, last)
    other = over(low, 1)
    last = turn(number, last)
    own = add_delta(sizes, side, own, up_pages, row_list_position, low, other, last)
    own = join(own, arrived[0, -1][0], arrived[1, 1][0])
    result = None
    for half, sign, _ in pairs[0]:
        result = finish(live_row_count.reshape(-1), half, own, arrived[half, sign][0], result)
    return result.reshape(steps, row_count, -1)


def solution(mesh):
    in_specs = (
        P(None, ("grp", "inst"), "tp"),
        P("tp", None),
        P("inst", None, "tp"),
        P("inst", None, "tp"),
        P(),
        P(None, ("grp", "inst"), None),
        P(None, ("grp", "inst")),
        P(None, ("grp", "inst")),
    )
    out_specs = P(None, ("grp", "inst"), "tp")
    return jax.shard_map(
        functools.partial(per_device, mesh.shape["tp"]),
        mesh=mesh, in_specs=in_specs, out_specs=out_specs, check_vma=False,
    )
```

```python
import functools

import jax
import jax.numpy as jnp
from jax import lax
from jax.experimental import pallas as pl
from jax.experimental.pallas import tpu as pltpu
from jax.sharding import PartitionSpec as P

VMEM_LIMIT = 40 * 1024 * 1024
FIRST_VMEM_LIMIT = 52 * 1024 * 1024
LOW_SCALE = 16.0
GRAIN = 16
SWAP = [(0, 1), (1, 0)]
WHOLE = pl.BlockSpec(memory_space=pltpu.VMEM)
ANYWHERE = pl.BlockSpec(memory_space=pl.ANY)


def serpentine(size):
    return size == 8


def ring_index(place, size):
    if not serpentine(size):
        return place
    return jnp.where(place < size // 2, 2 * place, 2 * (size - 1 - place) + 1)


def ring_place(index, size):
    if not serpentine(size):
        return index
    return jnp.where(index & 1 == 0, index >> 1, size - 1 - (index >> 1))


def ring_order(size):
    if not serpentine(size):
        return list(range(size))
    return list(range(0, size, 2)) + list(range(size - 1, 0, -2))


def params(limit=VMEM_LIMIT):
    return pltpu.CompilerParams(vmem_limit_bytes=limit)


def cost(flops, size):
    return pl.CostEstimate(flops=30 * flops, bytes_accessed=size, transcendentals=0)


def hop_kernel(pieces, dests, x_ref, w_ref, *refs):
    tile = w_ref.shape[1]
    now = pl.program_id(0)
    columns = pl.ds(pl.multiple_of(now * tile, tile), tile)
    total = jnp.dot(x_ref[...], w_ref[...], preferred_element_type=jnp.float32)
    out_ref = refs[-1]
    if len(pieces) == 1:
        out_ref[:, columns] = (total + refs[0][:, columns].astype(jnp.float32)).astype(
            out_ref.dtype
        )
    elif pieces:
        for piece, received_ref in zip(pieces, refs):

            @pl.when(now == piece)
            def _():
                out_ref[:, columns] = (total + received_ref[...].astype(jnp.float32)).astype(
                    out_ref.dtype
                )

    else:
        out_ref[:, columns] = total.astype(out_ref.dtype)


def tiling(dests, weight):
    half_cols = weight.shape[1] // dests.shape[0] // 2
    tile = min(256, half_cols)
    return half_cols, tile, half_cols // tile


def hop(dests, offset, half, x, weight, received, after):
    rows, depth = x.shape
    half_cols, tile, tiles = tiling(dests, weight)
    return pl.pallas_call(
        functools.partial(hop_kernel, tuple(range(len(received)))),
        grid_spec=pltpu.PrefetchScalarGridSpec(
            num_scalar_prefetch=1,
            grid=(tiles,),
            in_specs=[
                WHOLE,
                pl.BlockSpec(
                    (depth, tile), lambda j, d: (0, (d[offset] * 2 + half) * tiles + j)
                ),
            ]
            + [WHOLE] * len(received)
            + [ANYWHERE],
            out_specs=WHOLE,
        ),
        out_shape=jax.ShapeDtypeStruct((rows, half_cols), jnp.bfloat16),
        compiler_params=params(),
        cost_estimate=cost(
            2 * rows * depth * half_cols,
            2 * (rows * depth + depth * half_cols + 2 * rows * half_cols),
        ),
    )(dests, x, weight, *received, after)


def first_kernel(with_after, dests, x_ref, w_ref, *refs):
    total = jnp.dot(x_ref[...], w_ref[...], preferred_element_type=jnp.float32)
    refs[-1][...] = jnp.zeros_like(refs[-1])
    for chain, out_ref in enumerate(refs[-3:-1]):

        @pl.when(pl.program_id(0) == chain)
        def _():
            out_ref[...] = total.astype(out_ref.dtype)


def first_pieces(dests, offset, piece, x, weight, after):
    rows, depth = x.shape
    _, tile, tiles = tiling(dests, weight)
    size = dests.shape[0]

    def place(j, d):
        one = d[offset] * 2 * tiles + piece
        two = (d[(size - offset) % size] * 2 + 1) * tiles + piece
        return (0, jnp.where(j == 0, one, two))

    tail = [] if after is None else [after]
    return pl.pallas_call(
        functools.partial(first_kernel, after is not None),
        grid_spec=pltpu.PrefetchScalarGridSpec(
            num_scalar_prefetch=1,
            grid=(2,),
            in_specs=[
                pl.BlockSpec((rows, depth), lambda j, d: (0, 0)) if after is None else WHOLE,
                pl.BlockSpec((depth, tile), place),
            ]
            + [ANYWHERE] * len(tail),
            out_specs=[WHOLE, WHOLE, pl.BlockSpec((8, 128), lambda j, d: (0, 0))],
        ),
        out_shape=[jax.ShapeDtypeStruct((rows, tile), jnp.bfloat16)] * 2
        + [jax.ShapeDtypeStruct((8, 128), jnp.float32)],
        compiler_params=params(FIRST_VMEM_LIMIT if after is None else VMEM_LIMIT),
        cost_estimate=cost(
            4 * rows * depth * tile, 2 * (rows * depth + 2 * depth * tile + 2 * rows * tile)
        ),
    )(dests, x, weight, *tail)


def touch_kernel(*refs):
    refs[-1][...] = jnp.zeros_like(refs[-1])


def touch(*arrays):
    return pl.pallas_call(
        touch_kernel,
        in_specs=[ANYWHERE] * len(arrays),
        out_specs=WHOLE,
        out_shape=jax.ShapeDtypeStruct((8, 128), jnp.float32),
        compiler_params=params(),
    )(*arrays)


def collect_kernel(count, index, table_ref, after_ref, out_ref, sems):
    copies = [
        pltpu.make_async_copy(table_ref.at[index[slot]], out_ref.at[slot], sems.at[slot])
        for slot in range(count)
    ]
    for copy in copies:
        copy.start()
    for copy in copies:
        copy.wait()


def collect(index, table, after):
    count = index.shape[0]
    shape = (count,) + table.shape[1:]
    return pl.pallas_call(
        functools.partial(collect_kernel, count),
        grid_spec=pltpu.PrefetchScalarGridSpec(
            num_scalar_prefetch=1,
            grid=(1,),
            in_specs=[ANYWHERE, ANYWHERE],
            out_specs=WHOLE,
            scratch_shapes=[pltpu.SemaphoreType.DMA((count,))],
        ),
        out_shape=jax.ShapeDtypeStruct(shape, table.dtype),
        compiler_params=params(),
        cost_estimate=cost(0, 4 * shape[0] * shape[1] * shape[2]),
    )(index, table, after)


def start_pages(count, local, index, table_ref, got_ref, pages, sems):
    for slot in range(count):
        own = local[slot] == 1

        @pl.when(own)
        def _():
            pltpu.make_async_copy(
                table_ref.at[index[slot]], pages.at[slot], sems.at[slot]
            ).start()

        @pl.when(jnp.logical_not(own))
        def _():
            pltpu.make_async_copy(got_ref.at[slot], pages.at[slot], sems.at[slot]).start()


def wait_pages(slots, got_ref, pages, sems):
    for slot in slots:
        pltpu.make_async_copy(got_ref.at[slot], pages.at[slot], sems.at[slot]).wait()


def low_kernel(
    sizes, local, index, side, x_ref, place_ref, table_ref, got_ref, after_ref, keep_ref, give_ref,
    pages, sems,
):
    steps, blocks, listed, rank, block_rows = sizes
    half = steps * blocks // 2
    start_pages(steps * blocks * listed, local, index, table_ref, got_ref, pages, sems)
    for step in range(steps):
        for block in range(blocks):
            at = step * blocks + block
            wait_pages(range(at * listed, (at + 1) * listed), got_ref, pages, sems)
            listing = pages[at * listed : (at + 1) * listed].reshape(listed * rank, -1)
            every = lax.dot_general(
                listing, x_ref[at * block_rows : (at + 1) * block_rows, :],
                (((1,), (1,)), ((), ())), preferred_element_type=jnp.float32,
            )
            place = place_ref[step : step + 1, block * block_rows : (block + 1) * block_rows]
            low = jnp.zeros((rank, block_rows), jnp.float32)
            for entry in range(listed):
                low = jnp.where(place == entry, every[entry * rank : (entry + 1) * rank], low)
            rows = slice(at % half * block_rows, (at % half + 1) * block_rows)
            mine = side[0] == at // half

            @pl.when(mine)
            def _():
                keep_ref[:, rows] = low

            @pl.when(jnp.logical_not(mine))
            def _():
                give_ref[:, rows] = low


def low_rank(sizes, local, index, side, x, place, table, got, after):
    steps, blocks, listed, rank, block_rows = sizes
    count = steps * blocks * listed
    rows, depth = x.shape
    return pl.pallas_call(
        functools.partial(low_kernel, sizes),
        grid_spec=pltpu.PrefetchScalarGridSpec(
            num_scalar_prefetch=3,
            grid=(1,),
            in_specs=[WHOLE, WHOLE, ANYWHERE, ANYWHERE, ANYWHERE],
            out_specs=[WHOLE, WHOLE],
            scratch_shapes=[
                pltpu.VMEM((count, rank, depth), table.dtype),
                pltpu.SemaphoreType.DMA((count,)),
            ],
        ),
        out_shape=[jax.ShapeDtypeStruct((rank, rows // 2), jnp.float32)] * 2,
        compiler_params=params(),
        cost_estimate=cost(
            2 * rows * depth * listed * rank, 2 * (rows * depth + count * rank * depth)
        ),
    )(local, index, side, x, place, table, got, after)


def add_kernel(low_ref, sent_ref, after_ref, out_ref):
    out_ref[...] = (low_ref[...] + sent_ref[...]).astype(out_ref.dtype)


def add(low, sent, dtype, after):
    return pl.pallas_call(
        add_kernel,
        in_specs=[WHOLE, WHOLE, ANYWHERE],
        out_specs=WHOLE,
        out_shape=jax.ShapeDtypeStruct(low.shape, dtype),
        compiler_params=params(),
        cost_estimate=cost(low.size, 12 * low.size),
    )(low, sent, after)


def own_kernel(
    local, index, dests, x_ref, w_ref, table_ref, got_ref, after_ref, out_ref, pages, sems
):
    tile = w_ref.shape[1]
    now = pl.program_id(0)
    count = pages.shape[0]

    @pl.when(now == 0)
    def _():
        start_pages(count, local, index, table_ref, got_ref, pages, sems)

    columns = pl.ds(pl.multiple_of(now * tile, tile), tile)
    out_ref[:, columns] = jnp.dot(x_ref[...], w_ref[...], preferred_element_type=jnp.float32)

    @pl.when(now == pl.num_programs(0) - 1)
    def _():
        wait_pages(range(count), got_ref, pages, sems)


def own_terms(dests, local, index, x, weight, table, got, after):
    count, rank, cols = got.shape
    rows, depth = x.shape
    tile = min(256, cols)
    tiles = cols // tile
    return pl.pallas_call(
        own_kernel,
        grid_spec=pltpu.PrefetchScalarGridSpec(
            num_scalar_prefetch=3,
            grid=(tiles,),
            in_specs=[
                WHOLE,
                pl.BlockSpec((depth, tile), lambda j, l, i, d: (0, d[0] * tiles + j)),
                ANYWHERE,
                ANYWHERE,
                ANYWHERE,
            ],
            out_specs=[WHOLE, WHOLE],
            scratch_shapes=[pltpu.SemaphoreType.DMA((count,))],
        ),
        out_shape=[
            jax.ShapeDtypeStruct((rows, cols), jnp.float32),
            jax.ShapeDtypeStruct((count, rank, cols), table.dtype),
        ],
        compiler_params=params(),
        cost_estimate=cost(
            2 * rows * cols * depth,
            2 * (rows * depth + depth * cols + 2 * count * rank * cols) + 4 * rows * cols,
        ),
    )(local, index, dests, x, weight, table, got, after)


def delta_kernel(
    sizes, side, own_ref, pages_ref, place_ref, low_ref, other_ref, after_ref, out_ref
):
    steps, blocks, listed, rank, block_rows = sizes
    half = steps * blocks // 2
    entry_of = lax.broadcasted_iota(jnp.int32, (listed * rank, block_rows), 0) // rank
    for step in range(steps):
        for block in range(blocks):
            at = step * blocks + block
            rows = slice(at * block_rows, (at + 1) * block_rows)
            in_half = slice(at % half * block_rows, (at % half + 1) * block_rows)
            low = jnp.where(
                side[0] == at // half,
                low_ref[:, in_half].astype(jnp.float32),
                other_ref[:, in_half].astype(jnp.float32),
            )
            spread = jnp.concatenate([low] * listed, axis=0)
            place = place_ref[step : step + 1, block * block_rows : (block + 1) * block_rows]
            spread = jnp.where(entry_of == place, spread, 0.0)
            listing = pages_ref[at * listed : (at + 1) * listed].reshape(listed * rank, -1)
            out_ref[rows, :] = own_ref[rows, :] + jnp.dot(
                spread.T.astype(jnp.bfloat16), listing, preferred_element_type=jnp.float32
            )


def add_delta(sizes, side, own, pages, place, low, other, after):
    rows, cols = own.shape
    return pl.pallas_call(
        functools.partial(delta_kernel, sizes),
        grid_spec=pltpu.PrefetchScalarGridSpec(
            num_scalar_prefetch=1,
            grid=(1,),
            in_specs=[WHOLE] * 5 + [ANYWHERE],
            out_specs=WHOLE,
        ),
        out_shape=jax.ShapeDtypeStruct(own.shape, own.dtype),
        compiler_params=params(),
        cost_estimate=cost(
            2 * rows * cols * sizes[2] * sizes[3], 8 * rows * cols + 2 * pages.size
        ),
    )(side, own, pages, place, low, other, after)


def chunks(count):
    size = 32 if count % 32 == 0 else GRAIN
    return [slice(at, at + size) for at in range(0, count, size)]


def join_kernel(own_ref, left_ref, right_ref, out_ref):
    cols = left_ref.shape[1]
    for rows in chunks(own_ref.shape[0]):
        for at, part_ref in ((0, left_ref), (cols, right_ref)):
            out_ref[rows, at : at + cols] = own_ref[rows, at : at + cols] + part_ref[
                rows, :
            ].astype(jnp.float32)


def join(own, left, right):
    return pl.pallas_call(
        join_kernel,
        in_specs=[WHOLE] * 3,
        out_specs=WHOLE,
        out_shape=jax.ShapeDtypeStruct(own.shape, own.dtype),
        compiler_params=params(),
        cost_estimate=cost(own.size, 10 * own.size),
    )(own, left, right)


def finish_kernel(live, own_ref, left_ref, right_ref, out_ref, held, sems):
    rows, cols = held.shape
    half = cols // 2
    count = rows // live.shape[0]
    part = rows // sems.shape[0]
    copies = []
    for at in range(sems.shape[0]):
        for chunk in chunks(part):
            here = slice(at * part + chunk.start, at * part + chunk.stop)
            row = here.start % count + lax.broadcasted_iota(
                jnp.int32, (here.stop - here.start, half), 0
            )
            alive = row < live[here.start // count]
            for columns, last_ref in ((slice(0, half), left_ref), (slice(half, cols), right_ref)):
                total = own_ref[here, columns] + last_ref[here, :].astype(jnp.float32)
                held[here, columns] = jnp.where(alive, total, 0.0).astype(held.dtype)
        rows_at = pl.ds(at * part, part)
        copies.append(pltpu.make_async_copy(held.at[rows_at], out_ref.at[rows_at], sems.at[at]))
        copies[-1].start()
    for copy in copies:
        copy.wait()


def finish(live, own, left, right):
    rows, cols = own.shape
    return pl.pallas_call(
        finish_kernel,
        grid_spec=pltpu.PrefetchScalarGridSpec(
            num_scalar_prefetch=1,
            grid=(1,),
            in_specs=[WHOLE] * 3,
            out_specs=ANYWHERE,
            scratch_shapes=[
                pltpu.VMEM((rows, cols), jnp.bfloat16),
                pltpu.SemaphoreType.DMA((4 * live.shape[0],)),
            ],
        ),
        out_shape=jax.ShapeDtypeStruct((rows, cols), jnp.bfloat16),
        compiler_params=params(),
        cost_estimate=cost(0, rows * cols * 10),
    )(live, own, left, right)


def per_device(
    size,
    attention_output,
    output_weight,
    adapter_down_weight,
    adapter_up_weight,
    adapter_page_table,
    block_adapter_ids,
    row_list_position,
    live_row_count,
):
    steps, row_count, depth = attention_output.shape
    resident, rank, _ = adapter_down_weight.shape
    _, blocks, listed = block_adapter_ids.shape
    sizes = (steps, blocks, listed, rank, row_count // blocks)
    x = attention_output.reshape(steps * row_count, depth)
    ring = ring_order(size)

    instance = lax.axis_index("inst")
    place = ring_place(lax.axis_index("tp"), size)
    steps_on = jnp.arange(size, dtype=jnp.int32)
    steps_on = jnp.where(instance == 0, steps_on, size - steps_on)
    dests = ring_index(lax.rem(place + steps_on, size), size)

    up = [(ring[i], ring[(i + 1) % size]) for i in range(size)]
    down = [(ring[i], ring[i - 1]) for i in range(size)]

    def both_instances(first, second):
        return first + [(size + source, size + target) for source, target in second]

    forward, backward = both_instances(up, down), both_instances(down, up)
    far = size // 2
    pairs = [[(0, 1, forward), (1, -1, backward)], [(1, 1, forward), (0, -1, backward)]]
    arrived = {}

    def turn(number, last, between=None, which=(0, 1)):
        left = far - (number + 1) // 2
        for half, sign, moves in [pairs[number % 2][side] for side in which]:
            last = hop(
                dests, (sign * left) % size, half, x, output_weight,
                arrived.get((half, sign), []), last,
            )
            arrived[half, sign] = [lax.ppermute(last, ("inst", "tp"), moves)]
            if between is not None:
                last, between = touch(*between, last), None
        return last

    ids = block_adapter_ids.reshape(-1)
    ids_there = lax.ppermute(block_adapter_ids, "inst", SWAP).reshape(-1)
    last = None
    for piece in range(tiling(dests, output_weight)[2]):
        *both, last = first_pieces(dests, far % size, piece, x, output_weight, last)
        for (half, sign, moves), part in zip(pairs[0], both):
            arrived.setdefault((half, sign), []).append(lax.ppermute(part, ("inst", "tp"), moves))
    pages = adapter_page_table[jnp.concatenate([ids, ids_there])]
    places = pages % resident
    index, index_there = places[: ids.shape[0]], places[ids.shape[0] :]
    local = (pages[: ids.shape[0]] // resident == instance).astype(jnp.int32)
    last = collect(index_there, adapter_down_weight, last)
    got_down = lax.ppermute(last, "inst", SWAP)
    last = turn(1, last, [arrived[half, sign][0] for half, sign, _ in pairs[0]])
    side = (lax.axis_index("tp") & 1).reshape(1)
    low, give = low_rank(
        sizes, local, index, side, x, row_list_position, adapter_down_weight, got_down, last
    )
    last = low

    def over(value, apart):
        return lax.ppermute(value, "tp", [(i, i ^ apart) for i in range(size)])

    number, turns, ahead = 2, 2 * far - 1, False
    apart = 1
    while apart < size:
        sent = over(((give if apart == 1 else low) * LOW_SCALE).astype(jnp.float16), apart)
        until = turns - 1 if 2 * apart == size else number + 1
        while number < min(until, turns - 1):
            last = turn(number, last, which=(1,) if number == 4 and ahead else (0, 1))
            if number == 5:
                last = collect(index_there, adapter_up_weight, last)
                got_up = lax.ppermute(last, "inst", SWAP)
            number += 1
        apart *= 2
        if number == 4 and not ahead and number < turns - 1:
            last, ahead = turn(number, last, which=(0,)), True
        zero = touch(last)[0, 0]
        sent = sent.astype(jnp.float32) * (1.0 / LOW_SCALE) + zero
        low = last = add(low, sent, jnp.float32 if apart < size else jnp.bfloat16, last)
    other = over(low, 1)
    last = turn(number, last)
    own, up_pages = own_terms(
        dests, local, index, x, output_weight, adapter_up_weight, got_up, last
    )
    last = own
    own = add_delta(sizes, side, own, up_pages, row_list_position, low, other, last)
    own = join(own, arrived[0, -1][0], arrived[1, 1][0])
    result = finish(live_row_count.reshape(-1), own, arrived[0, 1][0], arrived[1, -1][0])
    return result.reshape(steps, row_count, -1)


def solution(mesh):
    in_specs = (
        P(None, ("grp", "inst"), "tp"),
        P("tp", None),
        P("inst", None, "tp"),
        P("inst", None, "tp"),
        P(),
        P(None, ("grp", "inst"), None),
        P(None, ("grp", "inst")),
        P(None, ("grp", "inst")),
    )
    out_specs = P(None, ("grp", "inst"), "tp")
    return jax.shard_map(
        functools.partial(per_device, mesh.shape["tp"]),
        mesh=mesh, in_specs=in_specs, out_specs=out_specs, check_vma=False,
    )
```

```python
import functools

import jax
import jax.numpy as jnp
from jax import lax
from jax.experimental import pallas as pl
from jax.experimental.pallas import tpu as pltpu
from jax.sharding import PartitionSpec as P

VMEM_LIMIT = 40 * 1024 * 1024
FIRST_VMEM_LIMIT = 52 * 1024 * 1024
LOW_SCALE = 16.0
GRAIN = 16
SWAP = [(0, 1), (1, 0)]
WHOLE = pl.BlockSpec(memory_space=pltpu.VMEM)
ANYWHERE = pl.BlockSpec(memory_space=pl.ANY)


def serpentine(size):
    return size == 8


def ring_index(place, size):
    if not serpentine(size):
        return place
    return jnp.where(place < size // 2, 2 * place, 2 * (size - 1 - place) + 1)


def ring_place(index, size):
    if not serpentine(size):
        return index
    return jnp.where(index & 1 == 0, index >> 1, size - 1 - (index >> 1))


def ring_order(size):
    if not serpentine(size):
        return list(range(size))
    return list(range(0, size, 2)) + list(range(size - 1, 0, -2))


def params(limit=VMEM_LIMIT):
    return pltpu.CompilerParams(vmem_limit_bytes=limit)


def cost(flops, size):
    return pl.CostEstimate(flops=30 * flops, bytes_accessed=size, transcendentals=0)


def hop_kernel(pieces, dests, x_ref, w_ref, *refs):
    tile = w_ref.shape[1]
    now = pl.program_id(0)
    columns = pl.ds(pl.multiple_of(now * tile, tile), tile)
    total = jnp.dot(x_ref[...], w_ref[...], preferred_element_type=jnp.float32)
    out_ref = refs[-1]
    if len(pieces) == 1:
        out_ref[:, columns] = (total + refs[0][:, columns].astype(jnp.float32)).astype(
            out_ref.dtype
        )
    elif pieces:
        for piece, received_ref in zip(pieces, refs):

            @pl.when(now == piece)
            def _():
                out_ref[:, columns] = (total + received_ref[...].astype(jnp.float32)).astype(
                    out_ref.dtype
                )

    else:
        out_ref[:, columns] = total.astype(out_ref.dtype)


def tiling(dests, weight):
    half_cols = weight.shape[1] // dests.shape[0] // 2
    tile = min(256, half_cols)
    return half_cols, tile, half_cols // tile


def hop(dests, offset, half, x, weight, received, after):
    rows, depth = x.shape
    half_cols, tile, tiles = tiling(dests, weight)
    return pl.pallas_call(
        functools.partial(hop_kernel, tuple(range(len(received)))),
        grid_spec=pltpu.PrefetchScalarGridSpec(
            num_scalar_prefetch=1,
            grid=(tiles,),
            in_specs=[
                WHOLE,
                pl.BlockSpec(
                    (depth, tile), lambda j, d: (0, (d[offset] * 2 + half) * tiles + j)
                ),
            ]
            + [WHOLE] * len(received)
            + [ANYWHERE],
            out_specs=WHOLE,
        ),
        out_shape=jax.ShapeDtypeStruct((rows, half_cols), jnp.bfloat16),
        compiler_params=params(),
        cost_estimate=cost(
            2 * rows * depth * half_cols,
            2 * (rows * depth + depth * half_cols + 2 * rows * half_cols),
        ),
    )(dests, x, weight, *received, after)


def first_kernel(with_after, dests, x_ref, w_ref, *refs):
    total = jnp.dot(x_ref[...], w_ref[...], preferred_element_type=jnp.float32)
    refs[-1][...] = jnp.zeros_like(refs[-1])
    for chain, out_ref in enumerate(refs[-3:-1]):

        @pl.when(pl.program_id(0) == chain)
        def _():
            out_ref[...] = total.astype(out_ref.dtype)


def first_pieces(dests, offset, piece, x, weight, after):
    rows, depth = x.shape
    _, tile, tiles = tiling(dests, weight)
    size = dests.shape[0]

    def place(j, d):
        one = d[offset] * 2 * tiles + piece
        two = (d[(size - offset) % size] * 2 + 1) * tiles + piece
        return (0, jnp.where(j == 0, one, two))

    tail = [] if after is None else [after]
    return pl.pallas_call(
        functools.partial(first_kernel, after is not None),
        grid_spec=pltpu.PrefetchScalarGridSpec(
            num_scalar_prefetch=1,
            grid=(2,),
            in_specs=[
                pl.BlockSpec((rows, depth), lambda j, d: (0, 0)) if after is None else WHOLE,
                pl.BlockSpec((depth, tile), place),
            ]
            + [ANYWHERE] * len(tail),
            out_specs=[WHOLE, WHOLE, pl.BlockSpec((8, 128), lambda j, d: (0, 0))],
        ),
        out_shape=[jax.ShapeDtypeStruct((rows, tile), jnp.bfloat16)] * 2
        + [jax.ShapeDtypeStruct((8, 128), jnp.float32)],
        compiler_params=params(FIRST_VMEM_LIMIT if after is None else VMEM_LIMIT),
        cost_estimate=cost(
            4 * rows * depth * tile, 2 * (rows * depth + 2 * depth * tile + 2 * rows * tile)
        ),
    )(dests, x, weight, *tail)


def touch_kernel(*refs):
    refs[-1][...] = jnp.zeros_like(refs[-1])


def touch(*arrays):
    return pl.pallas_call(
        touch_kernel,
        in_specs=[ANYWHERE] * len(arrays),
        out_specs=WHOLE,
        out_shape=jax.ShapeDtypeStruct((8, 128), jnp.float32),
        compiler_params=params(),
    )(*arrays)


def collect_kernel(count, index, table_ref, after_ref, out_ref, sems):
    copies = [
        pltpu.make_async_copy(table_ref.at[index[slot]], out_ref.at[slot], sems.at[slot])
        for slot in range(count)
    ]
    for copy in copies:
        copy.start()
    for copy in copies:
        copy.wait()


def collect(index, table, after):
    count = index.shape[0]
    shape = (count,) + table.shape[1:]
    return pl.pallas_call(
        functools.partial(collect_kernel, count),
        grid_spec=pltpu.PrefetchScalarGridSpec(
            num_scalar_prefetch=1,
            grid=(1,),
            in_specs=[ANYWHERE, ANYWHERE],
            out_specs=WHOLE,
            scratch_shapes=[pltpu.SemaphoreType.DMA((count,))],
        ),
        out_shape=jax.ShapeDtypeStruct(shape, table.dtype),
        compiler_params=params(),
        cost_estimate=cost(0, 4 * shape[0] * shape[1] * shape[2]),
    )(index, table, after)


def start_pages(count, local, index, table_ref, got_ref, pages, sems):
    for slot in range(count):
        own = local[slot] == 1

        @pl.when(own)
        def _():
            pltpu.make_async_copy(
                table_ref.at[index[slot]], pages.at[slot], sems.at[slot]
            ).start()

        @pl.when(jnp.logical_not(own))
        def _():
            pltpu.make_async_copy(got_ref.at[slot], pages.at[slot], sems.at[slot]).start()


def wait_pages(slots, got_ref, pages, sems):
    for slot in slots:
        pltpu.make_async_copy(got_ref.at[slot], pages.at[slot], sems.at[slot]).wait()


def low_kernel(
    sizes, local, index, side, x_ref, place_ref, table_ref, got_ref, after_ref, keep_ref, give_ref,
    pages, sems,
):
    steps, blocks, listed, rank, block_rows = sizes
    half = steps * blocks // 2
    start_pages(steps * blocks * listed, local, index, table_ref, got_ref, pages, sems)
    for step in range(steps):
        for block in range(blocks):
            at = step * blocks + block
            wait_pages(range(at * listed, (at + 1) * listed), got_ref, pages, sems)
            listing = pages[at * listed : (at + 1) * listed].reshape(listed * rank, -1)
            every = lax.dot_general(
                listing, x_ref[at * block_rows : (at + 1) * block_rows, :],
                (((1,), (1,)), ((), ())), preferred_element_type=jnp.float32,
            )
            place = place_ref[step : step + 1, block * block_rows : (block + 1) * block_rows]
            low = jnp.zeros((rank, block_rows), jnp.float32)
            for entry in range(listed):
                low = jnp.where(place == entry, every[entry * rank : (entry + 1) * rank], low)
            rows = slice(at % half * block_rows, (at % half + 1) * block_rows)
            mine = side[0] == at // half

            @pl.when(mine)
            def _():
                keep_ref[:, rows] = low

            @pl.when(jnp.logical_not(mine))
            def _():
                give_ref[:, rows] = low


def low_rank(sizes, local, index, side, x, place, table, got, after):
    steps, blocks, listed, rank, block_rows = sizes
    count = steps * blocks * listed
    rows, depth = x.shape
    return pl.pallas_call(
        functools.partial(low_kernel, sizes),
        grid_spec=pltpu.PrefetchScalarGridSpec(
            num_scalar_prefetch=3,
            grid=(1,),
            in_specs=[WHOLE, WHOLE, ANYWHERE, ANYWHERE, ANYWHERE],
            out_specs=[WHOLE, WHOLE],
            scratch_shapes=[
                pltpu.VMEM((count, rank, depth), table.dtype),
                pltpu.SemaphoreType.DMA((count,)),
            ],
        ),
        out_shape=[jax.ShapeDtypeStruct((rank, rows // 2), jnp.float32)] * 2,
        compiler_params=params(),
        cost_estimate=cost(
            2 * rows * depth * listed * rank, 2 * (rows * depth + count * rank * depth)
        ),
    )(local, index, side, x, place, table, got, after)


def add_kernel(low_ref, sent_ref, after_ref, out_ref):
    out_ref[...] = (low_ref[...] + sent_ref[...]).astype(out_ref.dtype)


def add(low, sent, dtype, after):
    return pl.pallas_call(
        add_kernel,
        in_specs=[WHOLE, WHOLE, ANYWHERE],
        out_specs=WHOLE,
        out_shape=jax.ShapeDtypeStruct(low.shape, dtype),
        compiler_params=params(),
        cost_estimate=cost(low.size, 12 * low.size),
    )(low, sent, after)


def own_kernel(
    local, index, dests, x_ref, w_ref, table_ref, got_ref, after_ref, out_ref, pages, sems
):
    tile = w_ref.shape[1]
    now = pl.program_id(0)
    count = pages.shape[0]

    @pl.when(now == 0)
    def _():
        start_pages(count, local, index, table_ref, got_ref, pages, sems)

    columns = pl.ds(pl.multiple_of(now * tile, tile), tile)
    out_ref[:, columns] = jnp.dot(x_ref[...], w_ref[...], preferred_element_type=jnp.float32)

    @pl.when(now == pl.num_programs(0) - 1)
    def _():
        wait_pages(range(count), got_ref, pages, sems)


def own_terms(dests, local, index, x, weight, table, got, after):
    count, rank, cols = got.shape
    rows, depth = x.shape
    tile = min(256, cols)
    tiles = cols // tile
    return pl.pallas_call(
        own_kernel,
        grid_spec=pltpu.PrefetchScalarGridSpec(
            num_scalar_prefetch=3,
            grid=(tiles,),
            in_specs=[
                WHOLE,
                pl.BlockSpec((depth, tile), lambda j, l, i, d: (0, d[0] * tiles + j)),
                ANYWHERE,
                ANYWHERE,
                ANYWHERE,
            ],
            out_specs=[WHOLE, WHOLE],
            scratch_shapes=[pltpu.SemaphoreType.DMA((count,))],
        ),
        out_shape=[
            jax.ShapeDtypeStruct((rows, cols), jnp.float32),
            jax.ShapeDtypeStruct((count, rank, cols), table.dtype),
        ],
        compiler_params=params(),
        cost_estimate=cost(
            2 * rows * cols * depth,
            2 * (rows * depth + depth * cols + 2 * count * rank * cols) + 4 * rows * cols,
        ),
    )(local, index, dests, x, weight, table, got, after)


def delta_kernel(
    sizes, side, own_ref, pages_ref, place_ref, low_ref, other_ref, after_ref, out_ref
):
    steps, blocks, listed, rank, block_rows = sizes
    half = steps * blocks // 2
    entry_of = lax.broadcasted_iota(jnp.int32, (listed * rank, block_rows), 0) // rank
    for step in range(steps):
        for block in range(blocks):
            at = step * blocks + block
            rows = slice(at * block_rows, (at + 1) * block_rows)
            in_half = slice(at % half * block_rows, (at % half + 1) * block_rows)
            low = jnp.where(
                side[0] == at // half,
                low_ref[:, in_half].astype(jnp.float32),
                other_ref[:, in_half].astype(jnp.float32),
            )
            spread = jnp.concatenate([low] * listed, axis=0)
            place = place_ref[step : step + 1, block * block_rows : (block + 1) * block_rows]
            spread = jnp.where(entry_of == place, spread, 0.0)
            listing = pages_ref[at * listed : (at + 1) * listed].reshape(listed * rank, -1)
            out_ref[rows, :] = own_ref[rows, :] + jnp.dot(
                spread.T.astype(jnp.bfloat16), listing, preferred_element_type=jnp.float32
            )


def add_delta(sizes, side, own, pages, place, low, other, after):
    rows, cols = own.shape
    return pl.pallas_call(
        functools.partial(delta_kernel, sizes),
        grid_spec=pltpu.PrefetchScalarGridSpec(
            num_scalar_prefetch=1,
            grid=(1,),
            in_specs=[WHOLE] * 5 + [ANYWHERE],
            out_specs=WHOLE,
        ),
        out_shape=jax.ShapeDtypeStruct(own.shape, own.dtype),
        compiler_params=params(),
        cost_estimate=cost(
            2 * rows * cols * sizes[2] * sizes[3], 8 * rows * cols + 2 * pages.size
        ),
    )(side, own, pages, place, low, other, after)


def chunks(count):
    size = 32 if count % 32 == 0 else GRAIN
    return [slice(at, at + size) for at in range(0, count, size)]


def join_kernel(own_ref, left_ref, right_ref, out_ref):
    cols = left_ref.shape[1]
    for rows in chunks(own_ref.shape[0]):
        for at, part_ref in ((0, left_ref), (cols, right_ref)):
            out_ref[rows, at : at + cols] = own_ref[rows, at : at + cols] + part_ref[
                rows, :
            ].astype(jnp.float32)


def join(own, left, right):
    return pl.pallas_call(
        join_kernel,
        in_specs=[WHOLE] * 3,
        out_specs=WHOLE,
        out_shape=jax.ShapeDtypeStruct(own.shape, own.dtype),
        compiler_params=params(),
        cost_estimate=cost(own.size, 10 * own.size),
    )(own, left, right)


def finish_kernel(live, own_ref, left_ref, right_ref, out_ref, held, sems):
    rows, cols = held.shape
    half = cols // 2
    count = rows // live.shape[0]
    part = rows // sems.shape[0]
    copies = []
    for at in range(sems.shape[0]):
        for chunk in chunks(part):
            here = slice(at * part + chunk.start, at * part + chunk.stop)
            row = here.start % count + lax.broadcasted_iota(
                jnp.int32, (here.stop - here.start, half), 0
            )
            alive = row < live[here.start // count]
            for columns, last_ref in ((slice(0, half), left_ref), (slice(half, cols), right_ref)):
                total = own_ref[here, columns] + last_ref[here, :].astype(jnp.float32)
                held[here, columns] = jnp.where(alive, total, 0.0).astype(held.dtype)
        rows_at = pl.ds(at * part, part)
        copies.append(pltpu.make_async_copy(held.at[rows_at], out_ref.at[rows_at], sems.at[at]))
        copies[-1].start()
    for copy in copies:
        copy.wait()


def finish(live, own, left, right):
    rows, cols = own.shape
    return pl.pallas_call(
        finish_kernel,
        grid_spec=pltpu.PrefetchScalarGridSpec(
            num_scalar_prefetch=1,
            grid=(1,),
            in_specs=[WHOLE] * 3,
            out_specs=ANYWHERE,
            scratch_shapes=[
                pltpu.VMEM((rows, cols), jnp.bfloat16),
                pltpu.SemaphoreType.DMA((2 * live.shape[0],)),
            ],
        ),
        out_shape=jax.ShapeDtypeStruct((rows, cols), jnp.bfloat16),
        compiler_params=params(),
        cost_estimate=cost(0, rows * cols * 10),
    )(live, own, left, right)


def per_device(
    size,
    attention_output,
    output_weight,
    adapter_down_weight,
    adapter_up_weight,
    adapter_page_table,
    block_adapter_ids,
    row_list_position,
    live_row_count,
):
    steps, row_count, depth = attention_output.shape
    resident, rank, _ = adapter_down_weight.shape
    _, blocks, listed = block_adapter_ids.shape
    sizes = (steps, blocks, listed, rank, row_count // blocks)
    x = attention_output.reshape(steps * row_count, depth)
    ring = ring_order(size)

    instance = lax.axis_index("inst")
    place = ring_place(lax.axis_index("tp"), size)
    steps_on = jnp.arange(size, dtype=jnp.int32)
    steps_on = jnp.where(instance == 0, steps_on, size - steps_on)
    dests = ring_index(lax.rem(place + steps_on, size), size)

    up = [(ring[i], ring[(i + 1) % size]) for i in range(size)]
    down = [(ring[i], ring[i - 1]) for i in range(size)]

    def both_instances(first, second):
        return first + [(size + source, size + target) for source, target in second]

    forward, backward = both_instances(up, down), both_instances(down, up)
    far = size // 2
    pairs = [[(0, 1, forward), (1, -1, backward)], [(1, 1, forward), (0, -1, backward)]]
    arrived = {}

    def turn(number, last, between=None, which=(0, 1)):
        left = far - (number + 1) // 2
        for half, sign, moves in [pairs[number % 2][side] for side in which]:
            last = hop(
                dests, (sign * left) % size, half, x, output_weight,
                arrived.get((half, sign), []), last,
            )
            arrived[half, sign] = [lax.ppermute(last, ("inst", "tp"), moves)]
            if between is not None:
                last, between = touch(*between, last), None
        return last

    ids = block_adapter_ids.reshape(-1)
    ids_there = lax.ppermute(block_adapter_ids, "inst", SWAP).reshape(-1)
    last = None
    for piece in range(tiling(dests, output_weight)[2]):
        *both, last = first_pieces(dests, far % size, piece, x, output_weight, last)
        for (half, sign, moves), part in zip(pairs[0], both):
            arrived.setdefault((half, sign), []).append(lax.ppermute(part, ("inst", "tp"), moves))
    pages = adapter_page_table[jnp.concatenate([ids, ids_there])]
    places = pages % resident
    index, index_there = places[: ids.shape[0]], places[ids.shape[0] :]
    local = (pages[: ids.shape[0]] // resident == instance).astype(jnp.int32)
    last = collect(index_there, adapter_down_weight, last)
    got_down = lax.ppermute(last, "inst", SWAP)
    last = turn(1, last, [arrived[half, sign][0] for half, sign, _ in pairs[0]])
    side = (lax.axis_index("tp") & 1).reshape(1)
    low, give = low_rank(
        sizes, local, index, side, x, row_list_position, adapter_down_weight, got_down, last
    )
    last = low

    def over(value, apart):
        return lax.ppermute(value, "tp", [(i, i ^ apart) for i in range(size)])

    number, turns, ahead = 2, 2 * far - 1, False
    apart = 1
    while apart < size:
        sent = over(((give if apart == 1 else low) * LOW_SCALE).astype(jnp.float16), apart)
        until = turns - 1 if 2 * apart == size else number + 1
        while number < min(until, turns - 1):
            last = turn(number, last, which=(1,) if number == 4 and ahead else (0, 1))
            if number == 5:
                last = collect(index_there, adapter_up_weight, last)
                got_up = lax.ppermute(last, "inst", SWAP)
            number += 1
        apart *= 2
        if number == 4 and not ahead and number < turns - 1:
            last, ahead = turn(number, last, which=(0,)), True
        zero = touch(last)[0, 0]
        sent = sent.astype(jnp.float32) * (1.0 / LOW_SCALE) + zero
        low = last = add(low, sent, jnp.float32 if apart < size else jnp.bfloat16, last)
    other = over(low, 1)
    last = turn(number, last)
    own, up_pages = own_terms(
        dests, local, index, x, output_weight, adapter_up_weight, got_up, last
    )
    last = own
    own = add_delta(sizes, side, own, up_pages, row_list_position, low, other, last)
    own = join(own, arrived[0, -1][0], arrived[1, 1][0])
    result = finish(live_row_count.reshape(-1), own, arrived[0, 1][0], arrived[1, -1][0])
    return result.reshape(steps, row_count, -1)


def solution(mesh):
    in_specs = (
        P(None, ("grp", "inst"), "tp"),
        P("tp", None),
        P("inst", None, "tp"),
        P("inst", None, "tp"),
        P(),
        P(None, ("grp", "inst"), None),
        P(None, ("grp", "inst")),
        P(None, ("grp", "inst")),
    )
    out_specs = P(None, ("grp", "inst"), "tp")
    return jax.shard_map(
        functools.partial(per_device, mesh.shape["tp"]),
        mesh=mesh, in_specs=in_specs, out_specs=out_specs, check_vma=False,
    )
```
